32 devices in a mesh: grp: 2 (over y), blk: 4 (over z), sub: 2 (over x), pair: 2 (over core).
Axes of the slice: x: 2, y: 2, z: 4, core: 2. Of those that a mesh axis runs over, the one named last changes fastest.
Arguments:
- queries: bfloat16 [4096, 2048], P(('grp', 'blk', 'pair', 'sub')), parts along dimension 0, may hold values from -6 to 6
- keys: bfloat16 [4096, 2048], P(('grp', 'blk', 'pair', 'sub')), parts along dimension 0, may hold values from -6 to 6
- values: bfloat16 [4096, 2048], P(('grp', 'blk', 'pair', 'sub')), parts along dimension 0, may hold values from -6 to 6
- out_grad: bfloat16 [4096, 2048], P(('grp', 'blk', 'pair', 'sub')), parts along dimension 0, may hold values from -6 to 6
- session: int32 [4096], P('grp'), parts along dimension 0, may hold values from 0 to 7, never falling along the last dimension, each value on 1 to 512 neighbouring positions
Outputs:
- grad_queries: bfloat16 [4096, 2048], P(('grp', 'blk', 'pair', 'sub')), parts along dimension 0
- grad_keys: bfloat16 [4096, 2048], P(('grp', 'blk', 'pair', 'sub')), parts along dimension 0
- grad_values: bfloat16 [4096, 2048], P(('grp', 'blk', 'pair', 'sub')), parts along dimension 0
The draws below stay inside these ranges and needn't reach their ends.
There are 2 independent parts, one for each index of `grp`. The reference program is written for one: setup_inputs(seed, part) draws one part's arguments, and reference() takes and returns one part's arrays. A program takes and returns all parts, laid end to end along the dimension named above; each array names one. Nothing has to cross between parts.
Inputs may be any that keep to these rules, and one draw needn't show every extreme that they name: Session numbers never fall along the tokens; each session is 1 to 512 tokens long and one is exactly that long.
All inputs are finite; a program needn't handle non-finite values.
Results may differ from the reference program's by a relative error of at most 0.0094.
Values may be sent and summed in bfloat16 or wider, within the bound.
No kernel may reach another device: no remote copies, remote signals or barrier semaphores. Data moves between devices by JAX's collectives and lax.ppermute only.
A program may use at most 64 MiB of HBM per device.

```python
import math
import jax
import jax.numpy as jnp
import numpy as np
from jax import lax

H = 16
HD = 128
D = 2048
CYCLE = 2
BLOCK = 256
NBLOCKS = 8
TOKENS = 2048


def draw_queries(key, part):
    key = jax.random.fold_in(key, 11)
    base = jnp.clip(jax.random.normal(key, (TOKENS, D), jnp.float32), -6.0, 6.0)
    return base.astype(jnp.bfloat16)


def draw_keys(key, part):
    key = jax.random.fold_in(key, 23)
    base = jnp.clip(jax.random.normal(key, (TOKENS, D), jnp.float32), -6.0, 6.0)
    return base.astype(jnp.bfloat16)


def level_of(key, extent, shards, low, top_value):
    level = 1.0
    for axis_at, shards_of in shards:
        draws = jax.random.uniform(jax.random.fold_in(jax.random.fold_in(key, 6), axis_at), (shards_of,), jnp.float32, low / len(shards), top_value / len(shards))
        level = level * jnp.repeat(jnp.exp(draws), extent[axis_at] // shards_of).reshape((-1,) + (1,) * (len(extent) - 1 - axis_at))
    return level


def length_profile(number_of, total, reach, lean):
    weights = [(1 << 20) // math.isqrt(grade ** lean) + 1 for grade in range(2, number_of + 1)]
    rest, given = total - reach - (number_of - 1), [1] * (number_of - 1)
    while rest > 0:
        candidates = [i for i in range(number_of - 1) if given[i] < reach]
        whole, remaining = sum([weights[i] for i in candidates]), rest
        for i in candidates:
            addition = min(reach - given[i], max(1, remaining * weights[i] // whole), rest)
            given[i] = given[i] + addition
            rest = rest - addition
    return np.array([reach] + given)


def ragged_sizes(own_key, count, total, bound, slope):
    if count == 2:
        one = jax.random.randint(own_key, (), max(1, total - bound), min(bound, total - 1) + 1)
        return jnp.stack([one, total - one])
    lengths = jnp.asarray(length_profile(count, total, bound, slope), jnp.int32)
    couples = (count - 1) // 2
    giver, taker = lengths[1:1 + 2 * couples:2], lengths[2:2 + 2 * couples:2]
    room = jnp.minimum(giver - 1, bound - taker)
    shifted = jax.random.randint(jax.random.fold_in(own_key, 1), (couples,), 0, 1 << 20) % (room + 1)
    lengths = lengths.at[1:1 + 2 * couples:2].set(giver - shifted).at[2:2 + 2 * couples:2].set(taker + shifted)
    return lengths[jax.random.permutation(jax.random.fold_in(own_key, 2), count)]


def gaussian(key, shape, scale, limit, pieces=(), kind=jnp.bfloat16):
    result = scale * jax.random.normal(key, shape, jnp.float32)
    if pieces:
        result = result * level_of(key, shape, pieces, -0.22, 0.18)
    return jnp.clip(result, -limit, limit).astype(kind)


def setup_inputs(seed: int = 0, part: int = 0) -> dict:
    seeds = jax.random.split(jax.random.key(seed), 6)
    part_splits = jax.random.split(jax.random.fold_in(seeds[5], part), 6)
    queries = draw_queries(jax.random.fold_in(jax.random.fold_in(seeds[5], part), 71), part)
    keys = draw_keys(jax.random.fold_in(jax.random.fold_in(seeds[5], part), 71), part)
    values = gaussian(part_splits[2], (TOKENS, D), 1.0, 6.0, ((0, 16),))
    out_grad = gaussian(part_splits[3], (TOKENS, D), 1.0, 6.0, ((0, 16),))
    session = jnp.searchsorted(jnp.cumsum(ragged_sizes(part_splits[4], NBLOCKS, TOKENS, CYCLE * BLOCK, 2)), jnp.arange(TOKENS), side="right").astype(jnp.int32)
    return dict(queries=queries, keys=keys, values=values, out_grad=out_grad, session=session)


NEG_FILL = -1.0e30


def attend(operands):
    q_rows, k_rows, v_rows, g_rows, q_sess, k_sess, q_place, k_place = operands
    score_scale = HD ** -0.5
    q_heads = q_rows.astype(jnp.float32).reshape(-1, H, HD)
    k_heads = k_rows.astype(jnp.float32).reshape(-1, H, HD)
    v_heads = v_rows.astype(jnp.float32).reshape(-1, H, HD)
    g_heads = g_rows.astype(jnp.float32).reshape(-1, H, HD)
    allowed = (q_sess[:, None] == k_sess[None, :]) & (k_place[None, :] <= q_place[:, None])
    allowed = allowed & (k_place[None, :] >= 0)
    scores = jnp.einsum("qhd,khd->hqk", q_heads, k_heads) * score_scale
    scores = jnp.where(allowed[None], scores, NEG_FILL)
    row_peak = jnp.max(scores, axis=2, keepdims=True)
    log_total = row_peak + jnp.log(jnp.sum(jnp.exp(scores - row_peak), axis=2, keepdims=True))
    prob_full = jnp.where(allowed[None], jnp.exp(scores - log_total), 0.0)
    prob_low = lax.optimization_barrier(prob_full.astype(jnp.bfloat16))
    prob_wide = prob_low.astype(jnp.float32)
    output = jnp.einsum("hqk,khd->qhd", prob_wide, v_heads)
    row_dot = jnp.sum(g_heads * output, axis=2)
    grad_prob = jnp.einsum("qhd,khd->hqk", g_heads, v_heads)
    grad_score = prob_full * (grad_prob - row_dot.T[:, :, None])
    score_low = lax.optimization_barrier(grad_score.astype(jnp.bfloat16))
    score_wide = score_low.astype(jnp.float32)
    grad_q = jnp.einsum("hqk,khd->qhd", score_wide, k_heads) * score_scale
    grad_k = jnp.einsum("hqk,qhd->khd", score_wide, q_heads) * score_scale
    grad_v = jnp.einsum("hqk,qhd->khd", prob_wide, g_heads)
    return grad_q.reshape(-1, D).astype(jnp.bfloat16), grad_k.reshape(-1, D), grad_v.reshape(-1, D)


def reference(queries, keys, values, out_grad, session):
    def to_blocks(array):
        return array.reshape(NBLOCKS, BLOCK, D)

    def earlier(array, count):
        return jnp.concatenate([jnp.zeros_like(array[:count]), array[:-count]], axis=0)

    q_blocks = to_blocks(queries)
    k_blocks = to_blocks(keys)
    v_blocks = to_blocks(values)
    g_blocks = to_blocks(out_grad)
    s_blocks = session.reshape(NBLOCKS, BLOCK)
    places = jnp.arange(TOKENS, dtype=jnp.int32).reshape(NBLOCKS, BLOCK)
    back_steps = list(range(CYCLE, 0, -1))
    k_all = jnp.concatenate([earlier(k_blocks, r) for r in back_steps] + [k_blocks], axis=1)
    v_all = jnp.concatenate([earlier(v_blocks, r) for r in back_steps] + [v_blocks], axis=1)
    s_all = jnp.concatenate([earlier(s_blocks, r) for r in back_steps] + [s_blocks], axis=1)
    p_all = jnp.concatenate([places - r * BLOCK for r in back_steps] + [places], axis=1)
    grad_q, grad_k, grad_v = lax.map(attend, (q_blocks, k_all, v_all, g_blocks, s_blocks, s_all, places, p_all))

    def combine(grad):
        total = grad[:, CYCLE * BLOCK:]
        for r in range(1, CYCLE + 1):
            part = grad[:, (CYCLE - r) * BLOCK:(CYCLE - r + 1) * BLOCK]
            total = total + jnp.concatenate([part[r:], jnp.zeros_like(part[:r])], axis=0)
        return total.reshape(TOKENS, D).astype(jnp.bfloat16)

    return grad_q.reshape(TOKENS, D), combine(grad_k), combine(grad_v)
```

```python
import math

import jax
import jax.numpy as jnp
from jax import lax
from jax.experimental import pallas as pl
from jax.experimental.pallas import tpu as pltpu
from jax.sharding import PartitionSpec as P

HD = 128
CHUNKS = 2
NEG_FILL = -1e30
LOW = jnp.bfloat16
WIDE = jnp.float32
ROOM = 48 * 1024 * 1024


def along_blocks(value, by):
    peers = lax.axis_size("blk")
    pairs = [(i, i + by) for i in range(peers) if 0 <= i + by < peers]
    return lax.ppermute(value, "blk", pairs)


def round_sub(value, by):
    peers = lax.axis_size("sub")
    return lax.ppermute(value, "sub", [(i, (i + by) % peers) for i in range(peers)])


def swapped(value):
    return lax.ppermute(value, "pair", [(0, 1), (1, 0)])


def run_moves(moves, sems):
    copies = [pltpu.make_async_copy(src, dst, sems.at[at]) for at, (src, dst) in enumerate(moves)]
    for copy in copies:
        copy.start()
    for copy in copies:
        copy.wait()


def anywhere(count):
    return [pl.BlockSpec(memory_space=pl.ANY)] * count


def call(kernel, ins, outs, scratch, name, whole=False, flops=0):
    spec = (lambda n: [pl.BlockSpec(memory_space=pltpu.VMEM)] * n) if whole else anywhere
    moved = sum(math.prod(a.shape) * a.dtype.itemsize for a in list(ins) + list(outs))
    return pl.pallas_call(
        kernel,
        out_shape=outs,
        in_specs=spec(len(ins)),
        out_specs=spec(len(outs)),
        scratch_shapes=scratch,
        name=name,
        cost_estimate=pl.CostEstimate(flops=flops, bytes_accessed=moved, transcendentals=0),
        compiler_params=pltpu.CompilerParams(vmem_limit_bytes=ROOM),
    )(*ins)


def pair_part(arrays):
    count = len(arrays)
    rows, width = arrays[0].shape
    half = width // 2

    def kernel(*refs):
        ins, out, sems = refs[:count], refs[count], refs[count + 1]
        start = pl.multiple_of((1 - lax.axis_index("pair")) * half, half)
        run_moves([(ref.at[:, pl.ds(start, half)], out.at[i]) for i, ref in enumerate(ins)], sems)

    outs = [jax.ShapeDtypeStruct((count, rows, half), LOW)]
    return call(kernel, arrays, outs, [pltpu.SemaphoreType.DMA((count,))], "pair_part")[0]


def head_parts(arrays, received, chunk):
    count = len(arrays)
    rows, width = arrays[0].shape
    half = width // 2
    peers = lax.axis_size("sub")
    part = half // peers
    cut = part // CHUNKS

    def kernel(*refs):
        ins, rec, outs, sems = refs[:count], refs[count], refs[count + 1:-1], refs[-1]
        p, s = lax.axis_index("pair"), lax.axis_index("sub")
        moves = []
        for by, out in enumerate(outs):
            base = lax.rem(s + by, peers) * part + chunk * cut
            here = pl.multiple_of(p * half + base, cut)
            there = pl.multiple_of(base, cut)
            moves += [(ref.at[:, pl.ds(here, cut)], out.at[i, p]) for i, ref in enumerate(ins)]
            moves.append((rec.at[:, :, pl.ds(there, cut)], out.at[:, 1 - p]))
        run_moves(moves, sems)

    outs = [jax.ShapeDtypeStruct((count, 2, rows, cut), LOW)] * peers
    scratch = [pltpu.SemaphoreType.DMA((peers * (count + 1),))]
    return call(kernel, list(arrays) + [received], outs, scratch, "head_parts")


def attention_grads(bias, kv, kv_earlier, qg):
    peers = len(kv)
    _, _, rows, cut = kv[0].shape
    heads = cut // HD
    strip = rows * peers
    scale = HD ** (-0.5)
    to_bits = scale / math.log(2.0)

    def kernel(*refs):
        bias_ref = refs[0]
        kv_in, early_in, qg_in = refs[1:1 + peers], refs[1 + peers:1 + 2 * peers], refs[1 + 2 * peers:1 + 3 * peers]
        outs = refs[1 + 3 * peers:1 + 6 * peers]
        early_out, kv_out, dq_out = outs[:peers], outs[peers:2 * peers], outs[2 * peers:]
        bias_held, kv_all, qg_all, grads, early_low, dq_all, sems = refs[1 + 6 * peers:]
        s = lax.axis_index("sub")
        moves = [(bias_ref, bias_held)]
        for by in range(peers):
            at = lax.rem(s - by + peers, peers)
            moves += [
                (early_in[by], kv_all.at[:, 0:2, at]),
                (kv_in[by], kv_all.at[:, 2:4, at]),
                (qg_in[by], qg_all.at[:, :, at]),
            ]
        run_moves(moves, sems)
        for head in range(heads):
            columns = pl.ds(head * HD, HD)
            for tile in range(2):
                span = 3 * strip
                q = qg_all[0, tile, :, :, columns].reshape(strip, HD)
                g = qg_all[1, tile, :, :, columns].reshape(strip, HD)
                k = kv_all[0, tile:tile + 3, :, :, columns].reshape(span, HD)
                v = kv_all[1, tile:tile + 3, :, :, columns].reshape(span, HD)
                rows_by_rows = (((1,), (1,)), ((), ()))
                scores = lax.dot_general(k, q, rows_by_rows, preferred_element_type=WIDE) * to_bits + bias_held[tile]
                peak = jnp.max(scores, axis=0, keepdims=True)
                weight = jnp.exp2(scores - peak)
                prob = weight * (1.0 / jnp.sum(weight, axis=0, keepdims=True))
                prob_low = prob.astype(LOW)
                grad_prob = lax.dot_general(v, g, rows_by_rows, preferred_element_type=WIDE)
                row_dot = jnp.sum(prob_low.astype(WIDE) * grad_prob, axis=0, keepdims=True)
                score_low = (prob * (grad_prob - row_dot)).astype(LOW)
                dq = jnp.dot(k.T, score_low, preferred_element_type=WIDE) * scale
                dq_all[tile, :, :, columns] = dq.T.astype(LOW).reshape(peers, rows, HD)
                dk = jnp.dot(score_low, q, preferred_element_type=WIDE) * scale
                dv = jnp.dot(prob_low, g, preferred_element_type=WIDE)
                for which, term in ((0, dk), (1, dv)):
                    term = term.reshape(3, peers, rows, HD)
                    if tile == 0:
                        grads[which, 0:3, :, :, columns] = term
                    else:
                        grads[which, 1:3, :, :, columns] += term[0:2]
                        grads[which, 3:4, :, :, columns] = term[2:3]
        early_low[...] = grads[:, 0:2].astype(LOW)
        moves = []
        for by in range(peers):
            at = lax.rem(s + by, peers)
            moves += [
                (early_low.at[:, :, at], early_out[by]),
                (grads.at[:, 2:4, at], kv_out[by]),
                (dq_all.at[:, at], dq_out[by]),
            ]
        run_moves(moves, sems)

    outs = (
        [jax.ShapeDtypeStruct((2, 2, rows, cut), LOW)] * peers
        + [jax.ShapeDtypeStruct((2, 2, rows, cut), WIDE)] * peers
        + [jax.ShapeDtypeStruct((2, rows, cut), LOW)] * peers
    )
    scratch = [
        pltpu.VMEM(bias.shape, WIDE),
        pltpu.VMEM((2, 4, peers, rows, cut), LOW),
        pltpu.VMEM((2, 2, peers, rows, cut), LOW),
        pltpu.VMEM((2, 4, peers, rows, cut), WIDE),
        pltpu.VMEM((2, 2, peers, rows, cut), LOW),
        pltpu.VMEM((2, peers, rows, cut), LOW),
        pltpu.SemaphoreType.DMA((1 + 3 * peers,)),
    ]
    flops = heads * 2 * 5 * 2 * strip * 3 * strip * HD
    outs = call(kernel, [bias] + list(kv) + list(kv_earlier) + list(qg), outs, scratch, "attention_grads", flops=flops)
    return outs[:peers], outs[peers:2 * peers], outs[2 * peers:]


def summed(dq, own, later):
    _, rows, cut = dq.shape

    def kernel(dq_ref, own_ref, later_ref, out):
        out[0] = dq_ref[...]
        out[1:3] = (own_ref[...] + later_ref[...].astype(WIDE)).astype(LOW)

    outs = [jax.ShapeDtypeStruct((3, 2, rows, cut), LOW)]
    return call(kernel, [dq, own, later], outs, [], "summed", whole=True)[0]


def rows_for_pair(dq, own, later, received):
    peers = len(received) + 1
    _, rows, cut = dq.shape

    def kernel(dq_ref, own_ref, later_ref, *refs):
        rec, (send, keep) = refs[:peers - 1], refs[peers - 1:]
        p, s = lax.axis_index("pair"), lax.axis_index("sub")
        for out, row in ((send, 1 - p), (keep, p)):
            out[0, s] = dq_ref[row]
            for which in range(2):
                out[1 + which, s] = (own_ref[which, row] + later_ref[which, row].astype(WIDE)).astype(LOW)
            for by in range(1, peers):
                at = lax.rem(s - by + peers, peers)
                for which in range(3):
                    out[which, at] = rec[by - 1][which, row]

    outs = [jax.ShapeDtypeStruct((3, peers, rows, cut), LOW)] * 2
    return call(kernel, [dq, own, later] + list(received), outs, [], "rows_for_pair", whole=True)


def laid_out(kept, received):
    _, peers, rows, cut = kept[0].shape
    part = cut * CHUNKS
    half = part * peers

    def kernel(*refs):
        keep, rec, outs, sems = refs[:CHUNKS], refs[CHUNKS:2 * CHUNKS], refs[2 * CHUNKS:-1], refs[-1]
        p = lax.axis_index("pair")
        moves = []
        for chunk in range(CHUNKS):
            for source, side in ((keep[chunk], p), (rec[chunk], 1 - p)):
                for at in range(peers):
                    start = pl.multiple_of(side * half + at * part + chunk * cut, cut)
                    moves += [(source.at[which, at], out.at[:, pl.ds(start, cut)]) for which, out in enumerate(outs)]
        run_moves(moves, sems)

    outs = [jax.ShapeDtypeStruct((rows, 2 * half), LOW)] * 3
    return call(kernel, list(kept) + list(received), outs, [pltpu.SemaphoreType.DMA((6 * CHUNKS * peers,))], "laid_out")


def allowed_bias(session, rows):
    peers = lax.axis_size("sub")
    strip = rows * peers
    block = 2 * strip
    start = lax.axis_index("blk") * block
    padded = jnp.concatenate([jnp.zeros((block,), jnp.int32), session])
    sess = lax.dynamic_slice_in_dim(padded, start, 2 * block)
    place = start - block + jnp.arange(2 * block, dtype=jnp.int32)
    tiles = []
    for tile in range(2):
        q_at = slice(block + tile * strip, block + (tile + 1) * strip)
        k_at = slice(tile * strip, (tile + 3) * strip)
        allowed = (sess[None, q_at] == sess[k_at, None]) & (place[k_at, None] <= place[None, q_at])
        tiles.append(jnp.where(allowed & (place[k_at, None] >= 0), 0.0, NEG_FILL))
    return jnp.stack(tiles)


def shards(queries, keys, values, out_grad, session):
    peers = lax.axis_size("sub")
    kv_pair = swapped(pair_part([keys, values]))
    qg_pair = swapped(pair_part([queries, out_grad]))
    bias = allowed_bias(session, queries.shape[0])
    kept, paired = [], []
    for chunk in range(CHUNKS):
        kv = head_parts([keys, values], kv_pair, chunk)
        kv = [kv[0]] + [round_sub(kv[by], by) for by in range(1, peers)]
        kv_earlier = [along_blocks(value, 1) for value in kv]
        qg = head_parts([queries, out_grad], qg_pair, chunk)
        qg = [qg[0]] + [round_sub(qg[by], by) for by in range(1, peers)]
        early, own, dq = attention_grads(bias, kv, kv_earlier, qg)
        later = [along_blocks(early[by], -1) for by in list(range(1, peers)) + [0]]
        received = []
        for by in range(1, peers):
            received.append(round_sub(summed(dq[by], own[by], later[by - 1]), by))
        send, keep = rows_for_pair(dq[0], own[0], later[-1], received)
        kept.append(keep)
        paired.append(swapped(send))
    return tuple(laid_out(kept, paired))


def solution(mesh):
    spread = P(("grp", "blk", "pair", "sub"), None)
    return jax.shard_map(
        shards, mesh=mesh, in_specs=(spread,) * 4 + (P("grp"),), out_specs=(spread,) * 3, check_vma=False
    )
```

```python
import math

import jax
import jax.numpy as jnp
from jax import lax
from jax.experimental import pallas as pl
from jax.experimental.pallas import tpu as pltpu
from jax.sharding import PartitionSpec as P

HD = 128
CHUNKS = 2
NEG_FILL = -1e30
LOW = jnp.bfloat16
WIDE = jnp.float32
MIB = 1024 * 1024


def along_blocks(value, by):
    peers = lax.axis_size("blk")
    pairs = [(i, i + by) for i in range(peers) if 0 <= i + by < peers]
    return lax.ppermute(value, "blk", pairs)


def round_sub(value, by):
    peers = lax.axis_size("sub")
    return lax.ppermute(value, "sub", [(i, (i + by) % peers) for i in range(peers)])


def swapped(value):
    return lax.ppermute(value, "pair", [(0, 1), (1, 0)])


def run_moves(moves, sems):
    copies = [pltpu.make_async_copy(src, dst, sems.at[at]) for at, (src, dst) in enumerate(moves)]
    for copy in copies:
        copy.start()
    for copy in copies:
        copy.wait()


def anywhere(count):
    return [pl.BlockSpec(memory_space=pl.ANY)] * count


def call(kernel, ins, outs, scratch, name, whole=False, flops=0, room=8 * MIB):
    spec = (lambda n: [pl.BlockSpec(memory_space=pltpu.VMEM)] * n) if whole else anywhere
    moved = sum(math.prod(a.shape) * a.dtype.itemsize for a in list(ins) + list(outs))
    return pl.pallas_call(
        kernel,
        out_shape=outs,
        in_specs=spec(len(ins)),
        out_specs=spec(len(outs)),
        scratch_shapes=scratch,
        name=name,
        cost_estimate=pl.CostEstimate(flops=flops, bytes_accessed=moved, transcendentals=0),
        compiler_params=pltpu.CompilerParams(vmem_limit_bytes=room),
    )(*ins)


def corner(value):
    return value[0, 0, :16, :HD]


def first_parts(arrays, chunk, after):
    count = len(arrays)
    rows, width = arrays[0].shape
    half = width // 2
    peers = lax.axis_size("sub")
    part = half // peers
    cut = part // CHUNKS

    def kernel(*refs):
        ins, outs, sems = refs[:count], refs[-3:-1], refs[-1]
        p = lax.axis_index("pair")
        moves = []
        for side, out in zip((1 - p, p), outs):
            for at in range(peers):
                start = pl.multiple_of(side * half + at * part + chunk * cut, cut)
                moves += [(ref.at[:, pl.ds(start, cut)], out.at[i, at]) for i, ref in enumerate(ins)]
        run_moves(moves, sems)

    outs = [jax.ShapeDtypeStruct((count, peers, rows, cut), LOW)] * 2
    scratch = [pltpu.SemaphoreType.DMA((2 * peers * count,))]
    return call(kernel, arrays + after, outs, scratch, "first_parts", room=(8 if after else 62) * MIB)


def head_parts(own, received, turns, after=()):
    count, peers, rows, cut = own.shape

    def kernel(own_ref, rec_ref, *refs):
        outs, sems = refs[len(after):-1], refs[-1]
        p, s = lax.axis_index("pair"), lax.axis_index("sub")
        moves = []
        for by, out in zip(turns, outs):
            at = lax.rem(s + by, peers)
            moves += [(own_ref.at[:, at], out.at[:, p]), (rec_ref.at[:, at], out.at[:, 1 - p])]
        run_moves(moves, sems)

    outs = [jax.ShapeDtypeStruct((count, 2, rows, cut), LOW)] * len(turns)
    scratch = [pltpu.SemaphoreType.DMA((2 * len(turns),))]
    return call(kernel, [own, received] + list(after), outs, scratch, "head_parts")


def attention_grads(bias, kv, kv_earlier, qg):
    peers = len(kv)
    _, _, rows, cut = kv[0].shape
    heads = cut // HD
    strip = rows * peers
    scale = HD ** (-0.5)
    to_bits = scale / math.log(2.0)

    def kernel(*refs):
        bias_ref = refs[0]
        kv_in, early_in, qg_in = refs[1:1 + peers], refs[1 + peers:1 + 2 * peers], refs[1 + 2 * peers:1 + 3 * peers]
        early_out, kv_out, dq_out = refs[1 + 3 * peers:4 + 3 * peers]
        bias_held, kv_all, qg_all, grads, early_low, dq_all, sems = refs[4 + 3 * peers:]
        s = lax.axis_index("sub")
        moves = [(bias_ref, bias_held)]
        for by in range(peers):
            at = lax.rem(s - by + peers, peers)
            moves += [
                (early_in[by], kv_all.at[:, 0:2, at]),
                (kv_in[by], kv_all.at[:, 2:4, at]),
                (qg_in[by], qg_all.at[:, :, at]),
            ]
        run_moves(moves, sems)
        for head in range(heads):
            columns = pl.ds(head * HD, HD)
            for tile in range(2):
                span = 3 * strip
                q = qg_all[0, tile, :, :, columns].reshape(strip, HD)
                g = qg_all[1, tile, :, :, columns].reshape(strip, HD)
                k = kv_all[0, tile:tile + 3, :, :, columns].reshape(span, HD)
                v = kv_all[1, tile:tile + 3, :, :, columns].reshape(span, HD)
                rows_by_rows = (((1,), (1,)), ((), ()))
                scores = lax.dot_general(k, q, rows_by_rows, preferred_element_type=WIDE) * to_bits + bias_held[tile]
                peak = jnp.max(scores, axis=0, keepdims=True)
                weight = jnp.exp2(scores - peak)
                prob = weight * (1.0 / jnp.sum(weight, axis=0, keepdims=True))
                prob_low = prob.astype(LOW)
                grad_prob = lax.dot_general(v, g, rows_by_rows, preferred_element_type=WIDE)
                row_dot = jnp.sum(prob_low.astype(WIDE) * grad_prob, axis=0, keepdims=True)
                score_low = (prob * (grad_prob - row_dot)).astype(LOW)
                dq = jnp.dot(k.T, score_low, preferred_element_type=WIDE) * scale
                dq_all[tile, :, :, columns] = dq.T.astype(LOW).reshape(peers, rows, HD)
                dk = jnp.dot(score_low, q, preferred_element_type=WIDE) * scale
                dv = jnp.dot(prob_low, g, preferred_element_type=WIDE)
                for which, term in ((0, dk), (1, dv)):
                    term = term.reshape(3, peers, rows, HD)
                    if tile == 0:
                        grads[which, 0:3, :, :, columns] = term
                    else:
                        grads[which, 1:3, :, :, columns] += term[0:2]
                        grads[which, 3:4, :, :, columns] = term[2:3]
        early_low[...] = grads[:, 0:2].astype(LOW)
        run_moves([(early_low, early_out), (grads.at[:, 2:4], kv_out), (dq_all, dq_out)], sems)

    outs = [
        jax.ShapeDtypeStruct((2, 2, peers, rows, cut), LOW),
        jax.ShapeDtypeStruct((2, 2, peers, rows, cut), WIDE),
        jax.ShapeDtypeStruct((2, peers, rows, cut), LOW),
    ]
    scratch = [
        pltpu.VMEM(bias.shape, WIDE),
        pltpu.VMEM((2, 4, peers, rows, cut), LOW),
        pltpu.VMEM((2, 2, peers, rows, cut), LOW),
        pltpu.VMEM((2, 4, peers, rows, cut), WIDE),
        pltpu.VMEM((2, 2, peers, rows, cut), LOW),
        pltpu.VMEM((2, peers, rows, cut), LOW),
        pltpu.SemaphoreType.DMA((1 + 3 * peers,)),
    ]
    flops = heads * 2 * 5 * 2 * strip * 3 * strip * HD
    ins = [bias] + list(kv) + list(kv_earlier) + list(qg)
    return call(kernel, ins, outs, scratch, "attention_grads", flops=flops, room=44 * MIB)


def summed(dq, own, later):
    _, peers, rows, cut = dq.shape

    def kernel(dq_ref, own_ref, later_ref, *outs):
        s = lax.axis_index("sub")
        for by, out in enumerate(outs):
            at = lax.rem(s + by, peers)
            for row in range(2):
                out[0, row] = dq_ref[row, at]
                for which in range(2):
                    total = own_ref[which, row, at] + later_ref[which, row, at].astype(WIDE)
                    out[1 + which, row] = total.astype(LOW)

    outs = [jax.ShapeDtypeStruct((3, 2, rows, cut), LOW)] * peers
    return call(kernel, [dq, own, later], outs, [], "summed", whole=True)


def rows_for_pair(parts):
    peers = len(parts)
    _, _, rows, cut = parts[0].shape

    def kernel(*refs):
        ins, (send, keep), sems = refs[:peers], refs[peers:-1], refs[-1]
        p, s = lax.axis_index("pair"), lax.axis_index("sub")
        moves = []
        for by, ref in enumerate(ins):
            at = lax.rem(s - by + peers, peers)
            moves += [(ref.at[:, 1 - p], send.at[:, at]), (ref.at[:, p], keep.at[:, at])]
        run_moves(moves, sems)

    outs = [jax.ShapeDtypeStruct((3, peers, rows, cut), LOW)] * 2
    return call(kernel, parts, outs, [pltpu.SemaphoreType.DMA((2 * peers,))], "rows_for_pair")


def laid_out(kept, received):
    _, peers, rows, cut = kept[0].shape
    part = cut * CHUNKS
    half = part * peers

    def kernel(*refs):
        keep, rec, outs, sems = refs[:CHUNKS], refs[CHUNKS:2 * CHUNKS], refs[2 * CHUNKS:-1], refs[-1]
        p = lax.axis_index("pair")
        moves = []
        for chunk in range(CHUNKS):
            for source, side in ((keep[chunk], p), (rec[chunk], 1 - p)):
                for at in range(peers):
                    start = pl.multiple_of(side * half + at * part + chunk * cut, cut)
                    moves += [(source.at[which, at], out.at[:, pl.ds(start, cut)]) for which, out in enumerate(outs)]
        run_moves(moves, sems)

    outs = [jax.ShapeDtypeStruct((rows, 2 * half), LOW)] * 3
    return call(kernel, list(kept) + list(received), outs, [pltpu.SemaphoreType.DMA((6 * CHUNKS * peers,))], "laid_out")


def allowed_bias(session, rows):
    peers = lax.axis_size("sub")
    strip = rows * peers
    block = 2 * strip
    start = lax.axis_index("blk") * block
    padded = jnp.concatenate([jnp.zeros((block,), jnp.int32), session])
    sess = lax.dynamic_slice_in_dim(padded, start, 2 * block)
    place = start - block + jnp.arange(2 * block, dtype=jnp.int32)
    tiles = []
    for tile in range(2):
        q_at = slice(block + tile * strip, block + (tile + 1) * strip)
        k_at = slice(tile * strip, (tile + 3) * strip)
        allowed = (sess[None, q_at] == sess[k_at, None]) & (place[k_at, None] <= place[None, q_at])
        tiles.append(jnp.where(allowed & (place[k_at, None] >= 0), 0.0, NEG_FILL))
    return jnp.stack(tiles)


def shards(queries, keys, values, out_grad, session):
    others = range(1, lax.axis_size("sub"))
    bias = allowed_bias(session, queries.shape[0])
    kept, paired = [], []
    kv_turn, own_turn, qg_turn, first_turn = [], [], [], []
    for chunk in range(CHUNKS):
        send, own = first_parts([keys, values], chunk, first_turn)
        rec = swapped(send)
        sends = list(head_parts(own, rec, others, kv_turn))
        kv = [round_sub(part, by) for by, part in zip(others, sends)]
        kv_own = list(head_parts(own, rec, [0], own_turn))
        own_earlier = [along_blocks(kv_own[0], 1)]
        kv_earlier = [along_blocks(value, 1) for value in kv]
        kv_turn, own_turn = kv + own_earlier, kv_earlier
        send, own = first_parts([queries, out_grad], chunk, [corner(sends[0])])
        rec = swapped(send)
        sends = list(head_parts(own, rec, others, qg_turn))
        qg = [round_sub(part, by) for by, part in zip(others, sends)]
        qg_own = list(head_parts(own, rec, [0]))
        qg_turn, first_turn = qg, [corner(sends[0])]
        early, grads, dq = attention_grads(bias, kv_own + kv, own_earlier + kv_earlier, qg_own + qg)
        parts = summed(dq, grads, along_blocks(early, -1))
        send, keep = rows_for_pair([parts[0]] + [round_sub(parts[by], by) for by in others])
        kept.append(keep)
        paired.append(swapped(send))
    return tuple(laid_out(kept, paired))


def solution(mesh):
    spread = P(("grp", "blk", "pair", "sub"), None)
    return jax.shard_map(
        shards, mesh=mesh, in_specs=(spread,) * 4 + (P("grp"),), out_specs=(spread,) * 3, check_vma=False
    )
```

```python
import math

import jax
import jax.numpy as jnp
from jax import lax
from jax.experimental import pallas as pl
from jax.experimental.pallas import tpu as pltpu
from jax.sharding import PartitionSpec as P

HD = 128
NEG_FILL = -1e30
LOW = jnp.bfloat16
WIDE = jnp.float32
MIB = 1024 * 1024
TO_BITS = HD ** (-0.5) / math.log(2.0)
SCALE = HD ** (-0.5)
ROWS_BY_ROWS = (((1,), (1,)), ((), ()))


def chunks_of(heads):
    return [1] * heads


def neighbours(value, first):
    peers = lax.axis_size("blk")
    pairs = []
    for i in range(peers):
        other = i + 1 if (i % 2 == 0) == first else i - 1
        pairs.append((i, other if 0 <= other < peers else i))
    return lax.ppermute(value, "blk", pairs)


def from_later(value):
    peers = lax.axis_size("blk")
    return lax.ppermute(value, "blk", [(i, (i - 1) % peers) for i in range(peers)])


def round_sub(value, by):
    peers = lax.axis_size("sub")
    return lax.ppermute(value, "sub", [(i, (i + by) % peers) for i in range(peers)])


def swapped(value):
    return lax.ppermute(value, "pair", [(0, 1), (1, 0)])


def run_moves(moves, sems):
    copies = [pltpu.make_async_copy(src, dst, sems.at[at]) for at, (src, dst) in enumerate(moves)]
    for copy in copies:
        copy.start()
    for copy in copies:
        copy.wait()


def call(kernel, ins, outs, scratch, name, whole=False, flops=0, room=8 * MIB):
    spec = pl.BlockSpec(memory_space=pltpu.VMEM if whole else pl.ANY)
    moved = sum(math.prod(a.shape) * a.dtype.itemsize for a in list(ins) + list(outs))
    return list(
        pl.pallas_call(
            kernel,
            out_shape=outs,
            in_specs=[spec] * len(ins),
            out_specs=[spec] * len(outs),
            scratch_shapes=scratch,
            name=name,
            cost_estimate=pl.CostEstimate(flops=flops, bytes_accessed=moved, transcendentals=0),
            compiler_params=pltpu.CompilerParams(vmem_limit_bytes=room),
        )(*ins)
    )


def shape(*dims, dtype=LOW):
    return jax.ShapeDtypeStruct(dims, dtype)


def first_parts(arrays, low, high):
    count = len(arrays)
    rows, width = arrays[0].shape
    half = width // 2
    peers = lax.axis_size("sub")
    part = half // peers

    def kernel(*refs):
        ins, outs, sems = refs[:count], refs[count:-1], refs[-1]
        p = lax.axis_index("pair")
        moves = []
        for side, out in zip((1 - p, p), outs):
            for at in range(peers):
                start = pl.multiple_of(side * half + at * part + low, HD)
                moves += [(ref.at[:, pl.ds(start, high - low)], out.at[i, at]) for i, ref in enumerate(ins)]
        run_moves(moves, sems)

    outs = [pltpu.VMEM((count, peers, rows, high - low), LOW)] * 2
    spec = pl.BlockSpec(memory_space=pl.ANY)
    held = [pltpu.with_memory_space_constraint(array, pltpu.HBM) for array in arrays]
    return pl.pallas_call(
        kernel,
        out_shape=outs,
        in_specs=[spec] * count,
        out_specs=[spec] * 2,
        scratch_shapes=[pltpu.SemaphoreType.DMA((2 * peers * count,))],
        name="first_parts",
        compiler_params=pltpu.CompilerParams(vmem_limit_bytes=8 * MIB),
    )(*held)


def head_parts(own, paired, low, cut, after):
    count, peers, rows, _ = own.shape

    def kernel(own_ref, pair_ref, *refs):
        outs, sems = refs[len(after):-1], refs[-1]
        p, s = lax.axis_index("pair"), lax.axis_index("sub")
        columns = pl.ds(low, cut)
        moves = []
        for by, out in enumerate(outs, 1):
            at = lax.rem(s + by, peers)
            moves += [(own_ref.at[:, at, :, columns], out.at[:, p]), (pair_ref.at[:, at, :, columns], out.at[:, 1 - p])]
        run_moves(moves, sems)

    outs = [shape(count, 2, rows, cut)] * (peers - 1)
    scratch = [pltpu.SemaphoreType.DMA((2 * peers,))]
    return call(kernel, [own, paired] + after, outs, scratch, "head_parts")


def joined(own, paired, received, low, cut, after):
    count, peers, rows, _ = own.shape

    def kernel(own_ref, pair_ref, *refs):
        rec, (here, first, second), sems = refs[:peers - 1], refs[-4:-1], refs[-1]
        p, s = lax.axis_index("pair"), lax.axis_index("sub")
        odd = lax.rem(lax.axis_index("blk"), 2)
        columns = pl.ds(low, cut)
        moves = []
        for out, start, size in ((first, 2 * odd, 2), (second, 2 - 2 * odd, 2), (here, 0, 4)):
            which = pl.ds(start, size)
            moves.append((own_ref.at[which, s, :, columns], out.at[:, p, s]))
            moves.append((pair_ref.at[which, s, :, columns], out.at[:, 1 - p, s]))
            for by, ref in enumerate(rec, 1):
                moves.append((ref.at[which], out.at[:, :, lax.rem(s - by + peers, peers)]))
        run_moves(moves, sems)

    outs = [shape(count, 2, peers, rows, cut)] + [shape(2, 2, peers, rows, cut)] * 2
    scratch = [pltpu.SemaphoreType.DMA((3 * (peers + 1),))]
    return call(kernel, [own, paired] + received + after, outs, scratch, "joined")


def taken(odd, when_odd, otherwise, held, sem):
    @pl.when(odd == 1)
    def _():
        run_moves([(when_odd, held)], sem)

    @pl.when(odd == 0)
    def _():
        run_moves([(otherwise, held)], sem)


def query_grads(bias, here, first, second):
    _, _, peers, rows, cut = here.shape
    heads = cut // HD
    strip = rows * peers

    def kernel(bias_ref, here_ref, first_ref, second_ref, dq_out, kv_out, stats_out, early, sem):
        taken(lax.rem(lax.axis_index("blk"), 2), first_ref, second_ref, early, sem)
        stats_out[...] = jnp.zeros_like(stats_out)
        for head in range(heads):
            columns = pl.ds(head * HD, HD)

            def flat(ref, which, tiles):
                block = ref[which, tiles, :, :, columns]
                return block.reshape(block.shape[0] * strip, HD)

            own_terms = []
            for tile in range(2):
                before, upto, at = pl.ds(tile, 2 - tile), pl.ds(0, tile + 1), pl.ds(tile, 1)
                q, g = flat(here_ref, 2, at), flat(here_ref, 3, at)
                k = jnp.concatenate([flat(early, 0, before), flat(here_ref, 0, upto)], axis=0)
                v = jnp.concatenate([flat(early, 1, before), flat(here_ref, 1, upto)], axis=0)
                scores = lax.dot_general(k, q, ROWS_BY_ROWS, preferred_element_type=WIDE) * TO_BITS + bias_ref[tile]
                peak = jnp.max(scores, axis=0, keepdims=True)
                weight = jnp.exp2(scores - peak)
                total = jnp.sum(weight, axis=0, keepdims=True)
                prob = weight * (1.0 / total)
                prob_low = prob.astype(LOW)
                grad_prob = lax.dot_general(v, g, ROWS_BY_ROWS, preferred_element_type=WIDE)
                row_dot = jnp.sum(prob_low.astype(WIDE) * grad_prob, axis=0, keepdims=True)
                score_low = (prob * (grad_prob - row_dot)).astype(LOW)
                stats_out[head, 2 * tile:2 * tile + 1] = peak + jnp.log2(total)
                stats_out[head, 2 * tile + 1:2 * tile + 2] = row_dot
                dq = jnp.dot(k.T, score_low, preferred_element_type=WIDE) * SCALE
                dq_out[tile, :, :, columns] = dq.T.astype(LOW).reshape(peers, rows, HD)
                skip = (2 - tile) * strip
                dk = jnp.dot(score_low[skip:], q, preferred_element_type=WIDE)
                dv = jnp.dot(prob_low[skip:], g, preferred_element_type=WIDE)
                own_terms.append((dk, dv))
            for which in range(2):
                low, high = own_terms[0][which], own_terms[1][which]
                kv_out[which, 0, :, :, columns] = (low + high[:strip]).reshape(peers, rows, HD)
                kv_out[which, 1, :, :, columns] = high[strip:].reshape(peers, rows, HD)

    outs = [
        shape(2, peers, rows, cut),
        shape(2, 2, peers, rows, cut, dtype=WIDE),
        shape(heads, 8, strip, dtype=WIDE),
    ]
    scratch = [pltpu.VMEM((2, 2, peers, rows, cut), LOW), pltpu.SemaphoreType.DMA((1,))]
    flops = heads * 2 * 5 * 2 * strip * 3 * strip * HD
    ins = [bias, here, first, second]
    return call(kernel, ins, outs, scratch, "query_grads", whole=True, flops=flops, room=40 * MIB)


def key_grads(bias, here, first, second, stats, dq, own):
    _, _, peers, rows, cut = here.shape
    heads = cut // HD
    strip = rows * peers

    def kernel(bias_ref, here_ref, first_ref, second_ref, stats_ref, dq_ref, own_ref, *refs):
        outs, (later, grads, sem) = refs[:peers], refs[peers:]
        s = lax.axis_index("sub")
        taken(lax.rem(lax.axis_index("blk"), 2), second_ref, first_ref, later, sem)
        for head in range(heads):
            columns = pl.ds(head * HD, HD)

            def flat(ref, which, tiles):
                block = ref[which, tiles, :, :, columns]
                return block.reshape(block.shape[0] * strip, HD)

            terms = []
            for tile in range(2):
                span = (2 - tile) * strip
                tiles, at = pl.ds(tile, 2 - tile), pl.ds(tile, 1)
                q, g = flat(later, 0, at), flat(later, 1, at)
                k, v = flat(here_ref, 0, tiles), flat(here_ref, 1, tiles)
                scores = lax.dot_general(k, q, ROWS_BY_ROWS, preferred_element_type=WIDE) * TO_BITS
                prob = jnp.exp2(scores + bias_ref[tile, :span] - stats_ref[head, 2 * tile:2 * tile + 1])
                grad_prob = lax.dot_general(v, g, ROWS_BY_ROWS, preferred_element_type=WIDE)
                score_low = (prob * (grad_prob - stats_ref[head, 2 * tile + 1:2 * tile + 2])).astype(LOW)
                dk = jnp.dot(score_low, q, preferred_element_type=WIDE)
                dv = jnp.dot(prob.astype(LOW), g, preferred_element_type=WIDE)
                terms.append((dk, dv))
            for which in range(2):
                scale = SCALE if which == 0 else 1.0
                wide, narrow = terms[0][which], terms[1][which]
                for tile, term in ((0, wide[:strip]), (1, wide[strip:] + narrow)):
                    term = own_ref[which, tile, :, :, columns] + term.reshape(peers, rows, HD)
                    grads[which, tile, :, :, columns] = (term * scale).astype(LOW)
        for by, out in enumerate(outs):
            at = lax.rem(s + by, peers)
            for row in range(2):
                out[0, row] = dq_ref[row, at]
                for which in range(2):
                    out[1 + which, row] = grads[which, row, at]

    outs = [shape(3, 2, rows, cut)] * peers
    held = pltpu.VMEM((2, 2, peers, rows, cut), LOW)
    scratch = [held, held, pltpu.SemaphoreType.DMA((1,))]
    flops = heads * 4 * 2 * 3 * strip * strip * HD
    ins = [bias, here, first, second, stats, dq, own]
    return call(kernel, ins, outs, scratch, "key_grads", whole=True, flops=flops, room=40 * MIB)


def rows_for_pair(parts):
    peers = len(parts)
    _, _, rows, cut = parts[0].shape

    def kernel(*refs):
        ins, (send, keep), sems = refs[:peers], refs[peers:-1], refs[-1]
        p, s = lax.axis_index("pair"), lax.axis_index("sub")
        moves = []
        for by, ref in enumerate(ins):
            at = lax.rem(s - by + peers, peers)
            moves += [(ref.at[:, 1 - p], send.at[:, at]), (ref.at[:, p], keep.at[:, at])]
        run_moves(moves, sems)

    outs = [shape(3, peers, rows, cut)] * 2
    return call(kernel, parts, outs, [pltpu.SemaphoreType.DMA((2 * peers,))], "rows_for_pair")


def laid_out(kept, paired, spans):
    _, peers, rows, _ = kept[0].shape
    part = spans[-1][1]
    half = part * peers
    count = len(spans)

    def kernel(*refs):
        keep, rec, outs, sems = refs[:count], refs[count:2 * count], refs[2 * count:-1], refs[-1]
        p = lax.axis_index("pair")
        moves = []
        for mine, theirs, (low, high) in zip(keep, rec, spans):
            for source, side in ((mine, p), (theirs, 1 - p)):
                for at in range(peers):
                    columns = pl.ds(pl.multiple_of(side * half + at * part + low, HD), high - low)
                    moves += [(source.at[which, at], out.at[:, columns]) for which, out in enumerate(outs)]
        run_moves(moves, sems)

    outs = [shape(rows, 2 * half)] * 3
    return call(kernel, kept + paired, outs, [pltpu.SemaphoreType.DMA((6 * count * peers,))], "laid_out")


def allowed_bias(session, rows):
    strip = rows * lax.axis_size("sub")
    block = 2 * strip
    at_block = lax.axis_index("blk")
    margin = jnp.zeros((block,), jnp.int32)
    window = jnp.concatenate([margin, session, margin])
    sess = lax.dynamic_slice_in_dim(window, at_block * block, 3 * block)
    place = (at_block - 1) * block + jnp.arange(3 * block, dtype=jnp.int32)

    def tile_bias(q_tile, k_tile, tiles):
        q_at = slice(q_tile * strip, (q_tile + 1) * strip)
        k_at = slice(k_tile * strip, (k_tile + tiles) * strip)
        k_place, q_place = place[k_at, None], place[None, q_at]
        allowed = (sess[None, q_at] == sess[k_at, None]) & (k_place <= q_place)
        allowed = allowed & (k_place >= 0) & (q_place < session.shape[0])
        return jnp.where(allowed, 0.0, NEG_FILL)

    for_queries = jnp.stack([tile_bias(2, 0, 3), tile_bias(3, 1, 3)])
    for_keys = jnp.stack([tile_bias(4, 2, 2), tile_bias(5, 3, 2)])
    return for_queries, for_keys


def shards(queries, keys, values, out_grad, session):
    peers = lax.axis_size("sub")
    others = range(1, peers)
    arrays = [keys, values, queries, out_grad]
    part = queries.shape[1] // (2 * peers)
    spans, at = [], 0
    for heads in chunks_of(part // HD):
        spans.append((at, at + heads * HD))
        at += heads * HD
    split = spans[0][1]
    fetched = []
    for low, high in ((0, split), (split, part)):
        send, own = first_parts(arrays, low, high)
        fetched.append((low, own, swapped(send)))
    query_bias, key_bias = allowed_bias(session, queries.shape[0])
    kept, paired = [], []
    arrived, exchanged, totals = [[], []], [[], [], []], [[], []]
    for index, (low, high) in enumerate(spans):
        base, own, pair_own = fetched[min(index, 1)]
        low, cut = low - base, high - low
        sends = head_parts(own, pair_own, low, cut, arrived[index] + exchanged[index])
        received = [round_sub(value, by) for by, value in zip(others, sends)]
        arrived.append(received)
        here, first, second = joined(own, pair_own, received, low, cut, totals[index])
        first, second = neighbours(first, True), neighbours(second, False)
        exchanged.append([first, second])
        dq, grads, stats = query_grads(query_bias, here, first, second)
        totals.append([stats])
        parts = key_grads(key_bias, here, first, second, from_later(stats), dq, grads)
        send, keep = rows_for_pair([parts[0]] + [round_sub(parts[by], by) for by in others])
        kept.append(keep)
        paired.append(swapped(send))
    return tuple(laid_out(kept, paired, spans))


def solution(mesh):
    spread = P(("grp", "blk", "pair", "sub"), None)
    return jax.shard_map(
        shards, mesh=mesh, in_specs=(spread,) * 4 + (P("grp"),), out_specs=(spread,) * 3, check_vma=False
    )
```

```python
import math

import jax
import jax.numpy as jnp
from jax import lax
from jax.experimental import pallas as pl
from jax.experimental.pallas import tpu as pltpu
from jax.sharding import PartitionSpec as P

HD = 128
NEG_FILL = -1e30
LOW = jnp.bfloat16
WIDE = jnp.float32
MIB = 1024 * 1024
TO_BITS = HD ** (-0.5) / math.log(2.0)
SCALE = HD ** (-0.5)
ROWS_BY_ROWS = (((1,), (1,)), ((), ()))


def chunks_of(heads):
    return [heads // 2, heads - heads // 2]


def along_blocks(value, by):
    peers = lax.axis_size("blk")
    return lax.ppermute(value, "blk", [(i, (i + by) % peers) for i in range(peers)])


def round_sub(value, by):
    peers = lax.axis_size("sub")
    return lax.ppermute(value, "sub", [(i, (i + by) % peers) for i in range(peers)])


def swapped(value):
    return lax.ppermute(value, "pair", [(0, 1), (1, 0)])


def run_moves(moves, sems):
    copies = [pltpu.make_async_copy(src, dst, sems.at[at]) for at, (src, dst) in enumerate(moves)]
    for copy in copies:
        copy.start()
    for copy in copies:
        copy.wait()


def call(kernel, ins, outs, scratch, name, whole=False, flops=0, room=8 * MIB):
    spec = pl.BlockSpec(memory_space=pltpu.VMEM if whole else pl.ANY)
    moved = sum(math.prod(a.shape) * a.dtype.itemsize for a in list(ins) + list(outs))
    return list(
        pl.pallas_call(
            kernel,
            out_shape=outs,
            in_specs=[spec] * len(ins),
            out_specs=[spec] * len(outs),
            scratch_shapes=scratch,
            name=name,
            cost_estimate=pl.CostEstimate(flops=flops, bytes_accessed=moved, transcendentals=0),
            compiler_params=pltpu.CompilerParams(vmem_limit_bytes=room),
        )(*ins)
    )


def shape(*dims, dtype=LOW):
    return jax.ShapeDtypeStruct(dims, dtype)


def first_parts(arrays, low, high, after):
    count = len(arrays)
    rows, width = arrays[0].shape
    half = width // 2
    peers = lax.axis_size("sub")
    part = half // peers

    def kernel(*refs):
        ins, outs, sems = refs[:count], refs[-3:-1], refs[-1]
        p = lax.axis_index("pair")
        moves = []
        for side, out in zip((1 - p, p), outs):
            for at in range(peers):
                start = pl.multiple_of(side * half + at * part + low, HD)
                moves += [(ref.at[:, pl.ds(start, high - low)], out.at[i, at]) for i, ref in enumerate(ins)]
        run_moves(moves, sems)

    outs = [pltpu.VMEM((count, peers, rows, high - low), LOW)] * 2
    spec = pl.BlockSpec(memory_space=pl.ANY)
    held = [pltpu.with_memory_space_constraint(array, pltpu.HBM) for array in arrays]
    return pl.pallas_call(
        kernel,
        out_shape=outs,
        in_specs=[spec] * (count + len(after)),
        out_specs=[spec] * 2,
        scratch_shapes=[pltpu.SemaphoreType.DMA((2 * peers * count,))],
        name="first_parts",
        compiler_params=pltpu.CompilerParams(vmem_limit_bytes=8 * MIB),
    )(*held, *after)


def head_parts(own, paired, turns, after):
    count, peers, rows, cut = own.shape

    def kernel(own_ref, pair_ref, *refs):
        outs, sems = refs[len(after):-1], refs[-1]
        p, s = lax.axis_index("pair"), lax.axis_index("sub")
        moves = []
        for by, out in zip(turns, outs):
            at = lax.rem(s + by, peers)
            moves += [(own_ref.at[:, at], out.at[:, p]), (pair_ref.at[:, at], out.at[:, 1 - p])]
        run_moves(moves, sems)

    outs = [shape(count, 2, rows, cut)] * len(turns)
    scratch = [pltpu.SemaphoreType.DMA((2 * len(turns),))]
    return call(kernel, [own, paired] + after, outs, scratch, "head_parts")


def attention_grads(bias, kv, kv_earlier, qg, split):
    peers = len(kv)
    _, _, rows, cut = kv[0].shape
    heads = cut // HD
    strip = rows * peers
    early_count = peers if split else 1

    def kernel(*refs):
        bias_ref = refs[0]
        kv_in, early_in, qg_in = refs[1:1 + peers], refs[1 + peers:1 + 2 * peers], refs[1 + 2 * peers:1 + 3 * peers]
        outs = refs[1 + 3 * peers:-5]
        own_out, dq_outs, early_outs = outs[0], outs[1:1 + peers], outs[1 + peers:]
        kv_all, qg_all, early, dq_all, sems = refs[-5:]
        s = lax.axis_index("sub")
        moves = []
        for by in range(peers):
            at = lax.rem(s - by + peers, peers)
            moves += [
                (early_in[by], kv_all.at[:, 0:2, at]),
                (kv_in[by], kv_all.at[:, 2:4, at]),
                (qg_in[by], qg_all.at[:, :, at]),
            ]
        run_moves(moves, sems)
        for head in range(heads):
            columns = pl.ds(head * HD, HD)

            def flat(ref, which, tiles):
                block = ref[which, tiles, :, :, columns]
                return block.reshape(block.shape[0] * strip, HD)

            terms = []
            for tile in range(2):
                at, span = pl.ds(tile, 1), pl.ds(tile, 3)
                q, g = flat(qg_all, 0, at), flat(qg_all, 1, at)
                k, v = flat(kv_all, 0, span), flat(kv_all, 1, span)
                scores = lax.dot_general(k, q, ROWS_BY_ROWS, preferred_element_type=WIDE) * TO_BITS + bias_ref[tile]
                peak = jnp.max(scores, axis=0, keepdims=True)
                weight = jnp.exp2(scores - peak)
                prob = weight * (1.0 / jnp.sum(weight, axis=0, keepdims=True))
                prob_low = prob.astype(LOW)
                grad_prob = lax.dot_general(v, g, ROWS_BY_ROWS, preferred_element_type=WIDE)
                row_dot = jnp.sum(prob_low.astype(WIDE) * grad_prob, axis=0, keepdims=True)
                score_low = (prob * (grad_prob - row_dot)).astype(LOW)
                dq = jnp.dot(k.T, score_low, preferred_element_type=WIDE) * SCALE
                dq_all[tile, :, :, columns] = dq.T.astype(LOW).reshape(peers, rows, HD)
                dk = jnp.dot(score_low, q, preferred_element_type=WIDE) * SCALE
                dv = jnp.dot(prob_low, g, preferred_element_type=WIDE)
                terms.append((dk, dv))
            for which in range(2):
                low, high = terms[0][which], terms[1][which]
                sums = (
                    low[:strip],
                    low[strip:2 * strip] + high[:strip],
                    low[2 * strip:] + high[strip:2 * strip],
                    high[2 * strip:],
                )
                for tile, total in enumerate(sums):
                    total = total.reshape(peers, rows, HD)
                    if tile < 2:
                        early[which, tile, :, :, columns] = total.astype(LOW)
                    else:
                        own_out[which, tile - 2, :, :, columns] = total
        moves = [] if split else [(early, early_outs[0])]
        for by in range(peers):
            at = lax.rem(s + by, peers)
            moves.append((dq_all.at[:, at], dq_outs[by]))
            if split:
                moves.append((early.at[:, :, at], early_outs[by]))
        run_moves(moves, sems)

    outs = [shape(2, 2, peers, rows, cut, dtype=WIDE)] + [shape(2, rows, cut)] * peers
    outs += [shape(2, 2, rows, cut)] * peers if split else [shape(2, 2, peers, rows, cut)]
    scratch = [
        pltpu.VMEM((2, 4, peers, rows, cut), LOW),
        pltpu.VMEM((2, 2, peers, rows, cut), LOW),
        pltpu.VMEM((2, 2, peers, rows, cut), LOW),
        pltpu.VMEM((2, peers, rows, cut), LOW),
        pltpu.SemaphoreType.DMA((3 * peers,)),
    ]
    flops = heads * 2 * 5 * 2 * strip * 3 * strip * HD
    ins = [bias] + kv + kv_earlier + qg
    outs = call(kernel, ins, outs, scratch, "attention_grads", whole=True, flops=flops, room=40 * MIB)
    return outs[0], outs[1:1 + peers], outs[1 + peers:]


def summed(own, later, turns, after):
    _, _, peers, rows, cut = own.shape
    split = len(later) > 1 or later[0].ndim == 4

    def kernel(own_ref, *refs):
        later_refs, outs = refs[:len(later)], refs[len(later) + len(after):]
        s = lax.axis_index("sub")
        for place, (by, out) in enumerate(zip(turns, outs)):
            at = lax.rem(s + by, peers)
            for which in range(2):
                for row in range(2):
                    term = later_refs[place][which, row] if split else later_refs[0][which, row, at]
                    out[which, row] = (own_ref[which, row, at] + term.astype(WIDE)).astype(LOW)

    outs = [shape(2, 2, rows, cut)] * len(turns)
    return call(kernel, [own] + later + after, outs, [], "summed", whole=True)


def rows_for_pair(dq, dkv):
    peers = len(dq)
    _, rows, cut = dq[0].shape

    def kernel(*refs):
        dq_refs, dkv_refs, (send, keep), sems = refs[:peers], refs[peers:2 * peers], refs[-3:-1], refs[-1]
        p, s = lax.axis_index("pair"), lax.axis_index("sub")
        moves = []
        for by in range(peers):
            at = lax.rem(s - by + peers, peers)
            for out, row in ((send, 1 - p), (keep, p)):
                moves += [(dq_refs[by].at[row], out.at[0, at]), (dkv_refs[by].at[:, row], out.at[1:3, at])]
        run_moves(moves, sems)

    outs = [shape(3, peers, rows, cut)] * 2
    return call(kernel, dq + dkv, outs, [pltpu.SemaphoreType.DMA((4 * peers,))], "rows_for_pair")


def laid_out(kept, paired, spans):
    _, peers, rows, _ = kept[0].shape
    part = spans[-1][1]
    half = part * peers
    count = len(spans)

    def kernel(*refs):
        keep, rec, outs, sems = refs[:count], refs[count:2 * count], refs[2 * count:-1], refs[-1]
        p = lax.axis_index("pair")
        moves = []
        for mine, theirs, (low, high) in zip(keep, rec, spans):
            for source, side in ((mine, p), (theirs, 1 - p)):
                for at in range(peers):
                    columns = pl.ds(pl.multiple_of(side * half + at * part + low, HD), high - low)
                    moves += [(source.at[which, at], out.at[:, columns]) for which, out in enumerate(outs)]
        run_moves(moves, sems)

    outs = [shape(rows, 2 * half)] * 3
    return call(kernel, kept + paired, outs, [pltpu.SemaphoreType.DMA((6 * count * peers,))], "laid_out")


def allowed_bias(session, rows):
    strip = rows * lax.axis_size("sub")
    block = 2 * strip
    at_block = lax.axis_index("blk")
    window = jnp.concatenate([jnp.zeros((block,), jnp.int32), session])
    sess = lax.dynamic_slice_in_dim(window, at_block * block, 2 * block)
    place = (at_block - 1) * block + jnp.arange(2 * block, dtype=jnp.int32)

    def tile_bias(tile):
        q_at = slice(block + tile * strip, block + (tile + 1) * strip)
        k_at = slice(tile * strip, (tile + 3) * strip)
        k_place, q_place = place[k_at, None], place[None, q_at]
        allowed = (sess[None, q_at] == sess[k_at, None]) & (k_place <= q_place) & (k_place >= 0)
        return jnp.where(allowed, 0.0, NEG_FILL)

    return jnp.stack([tile_bias(0), tile_bias(1)])


def shards(queries, keys, values, out_grad, session):
    peers = lax.axis_size("sub")
    others = list(range(1, peers))
    part = queries.shape[1] // (2 * peers)
    spans, at = [], 0
    for heads in chunks_of(part // HD):
        spans.append((at, at + heads * HD))
        at += heads * HD
    bias = allowed_bias(session, queries.shape[0])
    kept, paired = [], []
    first_turn, kv_turn, own_turn, qg_turn = [], [], [], []
    for index, (low, high) in enumerate(spans):
        last = index == len(spans) - 1
        send, own = first_parts([keys, values], low, high, first_turn)
        rec = swapped(send)
        sends = head_parts(own, rec, others, kv_turn)
        kv = [round_sub(value, by) for by, value in zip(others, sends)]
        kv_own = head_parts(own, rec, [0], own_turn)
        earlier = [along_blocks(kv_own[0], 1)]
        own_turn = earlier[:]
        earlier += [along_blocks(value, 1) for value in kv]
        send, own = first_parts([queries, out_grad], low, high, [own])
        rec = swapped(send)
        sends = head_parts(own, rec, others, qg_turn)
        qg = [round_sub(value, by) for by, value in zip(others, sends)]
        qg_own = head_parts(own, rec, [0], [])
        first_turn, kv_turn, qg_turn = sends, kv, qg
        grads, dq, early = attention_grads(bias, kv_own + kv, earlier, qg_own + qg, last)
        dq = [dq[0]] + [round_sub(dq[by], by) for by in others]
        if last:
            later = [along_blocks(value, -1) for value in early]
            dkv = summed(grads, later[1:], others, dq[1:])
            dkv = summed(grads, later[:1], [0], []) + [round_sub(value, by) for by, value in zip(others, dkv)]
        else:
            dkv = summed(grads, [along_blocks(early[0], -1)], [0] + others, dq[1:])
            dkv = [dkv[0]] + [round_sub(dkv[by], by) for by in others]
        send, keep = rows_for_pair(dq, dkv)
        kept.append(keep)
        paired.append(swapped(send))
    return tuple(laid_out(kept, paired, spans))


def solution(mesh):
    spread = P(("grp", "blk", "pair", "sub"), None)
    return jax.shard_map(
        shards, mesh=mesh, in_specs=(spread,) * 4 + (P("grp"),), out_specs=(spread,) * 3, check_vma=False
    )
```

```python
import math

import jax
import jax.numpy as jnp
from jax import lax
from jax.experimental import pallas as pl
from jax.experimental.pallas import tpu as pltpu
from jax.sharding import PartitionSpec as P

HD = 128
NEG_FILL = -1e30
LOW = jnp.bfloat16
WIDE = jnp.float32
MIB = 1024 * 1024
TO_BITS = HD ** (-0.5) / math.log(2.0)
SCALE = HD ** (-0.5)
ROWS_BY_ROWS = (((1,), (1,)), ((), ()))


def chunks_of(heads):
    return [heads // 2, heads - heads // 2]


def along_blocks(value, by, ring):
    peers = lax.axis_size("blk")
    pairs = [(i, (i + by) % peers) for i in range(peers) if ring or 0 <= i + by < peers]
    return lax.ppermute(value, "blk", pairs)


def round_sub(value, by):
    peers = lax.axis_size("sub")
    return lax.ppermute(value, "sub", [(i, (i + by) % peers) for i in range(peers)])


def swapped(value):
    return lax.ppermute(value, "pair", [(0, 1), (1, 0)])


def run_moves(moves, sems):
    copies = [pltpu.make_async_copy(src, dst, sems.at[at]) for at, (src, dst) in enumerate(moves)]
    for copy in copies:
        copy.start()
    for copy in copies:
        copy.wait()


def call(kernel, ins, outs, scratch, name, whole=False, flops=0, room=8 * MIB):
    spec = pl.BlockSpec(memory_space=pltpu.VMEM if whole else pl.ANY)
    moved = sum(math.prod(a.shape) * a.dtype.itemsize for a in list(ins) + list(outs))
    return list(
        pl.pallas_call(
            kernel,
            out_shape=outs,
            in_specs=[spec] * len(ins),
            out_specs=[spec] * len(outs),
            scratch_shapes=scratch,
            name=name,
            cost_estimate=pl.CostEstimate(flops=flops, bytes_accessed=moved, transcendentals=0),
            compiler_params=pltpu.CompilerParams(vmem_limit_bytes=room),
        )(*ins)
    )


def shape(*dims, dtype=LOW):
    return jax.ShapeDtypeStruct(dims, dtype)


def first_parts(arrays, low, high, after):
    count = len(arrays)
    rows, width = arrays[0].shape
    half = width // 2
    peers = lax.axis_size("sub")
    part = half // peers

    def kernel(*refs):
        ins, outs, sems = refs[:count], refs[-3:-1], refs[-1]
        p = lax.axis_index("pair")
        moves = []
        for side, out in zip((1 - p, p), outs):
            for at in range(peers):
                start = pl.multiple_of(side * half + at * part + low, HD)
                moves += [(ref.at[:, pl.ds(start, high - low)], out.at[i, at]) for i, ref in enumerate(ins)]
        run_moves(moves, sems)

    outs = [pltpu.VMEM((count, peers, rows, high - low), LOW)] * 2
    spec = pl.BlockSpec(memory_space=pl.ANY)
    held = [pltpu.with_memory_space_constraint(array, pltpu.HBM) for array in arrays]
    return pl.pallas_call(
        kernel,
        out_shape=outs,
        in_specs=[spec] * (count + len(after)),
        out_specs=[spec] * 2,
        scratch_shapes=[pltpu.SemaphoreType.DMA((2 * peers * count,))],
        name="first_parts",
        compiler_params=pltpu.CompilerParams(vmem_limit_bytes=8 * MIB),
    )(*held, *after)


def head_parts(own, paired, turns, after):
    count, peers, rows, cut = own.shape

    def kernel(own_ref, pair_ref, *refs):
        outs, sems = refs[len(after):-1], refs[-1]
        p, s = lax.axis_index("pair"), lax.axis_index("sub")
        moves = []
        for by, out in zip(turns, outs):
            at = lax.rem(s + by, peers)
            moves += [(own_ref.at[:, at], out.at[:, p]), (pair_ref.at[:, at], out.at[:, 1 - p])]
        run_moves(moves, sems)

    outs = [shape(count, 2, rows, cut)] * len(turns)
    scratch = [pltpu.SemaphoreType.DMA((2 * len(turns),))]
    return call(kernel, [own, paired] + after, outs, scratch, "head_parts")


def relayed(value, after):
    def kernel(value_ref, *refs):
        run_moves([(value_ref, refs[-2])], refs[-1])

    scratch = [pltpu.SemaphoreType.DMA((1,))]
    return call(kernel, [value] + after, [shape(*value.shape)], scratch, "relayed")[0]


def attention_grads(bias, kv, kv_earlier, qg, split):
    peers = len(kv)
    _, _, rows, cut = kv[0].shape
    heads = cut // HD
    strip = rows * peers
    early_count = peers if split else 1

    def kernel(*refs):
        bias_ref = refs[0]
        kv_in, early_in, qg_in = refs[1:1 + peers], refs[1 + peers:1 + 2 * peers], refs[1 + 2 * peers:1 + 3 * peers]
        outs = refs[1 + 3 * peers:-5]
        own_out, dq_outs, early_outs = outs[0], outs[1:1 + peers], outs[1 + peers:]
        kv_all, qg_all, early, dq_all, sems = refs[-5:]
        s = lax.axis_index("sub")
        moves = []
        for by in range(peers):
            at = lax.rem(s - by + peers, peers)
            moves += [
                (early_in[by], kv_all.at[:, 0:2, at]),
                (kv_in[by], kv_all.at[:, 2:4, at]),
                (qg_in[by], qg_all.at[:, :, at]),
            ]
        run_moves(moves, sems)
        for head in range(heads):
            columns = pl.ds(head * HD, HD)

            def flat(ref, which, tiles):
                block = ref[which, tiles, :, :, columns]
                return block.reshape(block.shape[0] * strip, HD)

            terms = []
            for tile in range(2):
                at, span = pl.ds(tile, 1), pl.ds(tile, 3)
                q, g = flat(qg_all, 0, at), flat(qg_all, 1, at)
                k, v = flat(kv_all, 0, span), flat(kv_all, 1, span)
                scores = lax.dot_general(k, q, ROWS_BY_ROWS, preferred_element_type=WIDE) * TO_BITS + bias_ref[tile]
                peak = jnp.max(scores, axis=0, keepdims=True)
                weight = jnp.exp2(scores - peak)
                prob = weight * (1.0 / jnp.sum(weight, axis=0, keepdims=True))
                prob_low = prob.astype(LOW)
                grad_prob = lax.dot_general(v, g, ROWS_BY_ROWS, preferred_element_type=WIDE)
                row_dot = jnp.sum(prob_low.astype(WIDE) * grad_prob, axis=0, keepdims=True)
                score_low = (prob * (grad_prob - row_dot)).astype(LOW)
                dq = jnp.dot(k.T, score_low, preferred_element_type=WIDE) * SCALE
                dq_all[tile, :, :, columns] = dq.T.astype(LOW).reshape(peers, rows, HD)
                dk = jnp.dot(score_low, q, preferred_element_type=WIDE) * SCALE
                dv = jnp.dot(prob_low, g, preferred_element_type=WIDE)
                terms.append((dk, dv))
            for which in range(2):
                low, high = terms[0][which], terms[1][which]
                sums = (
                    low[:strip],
                    low[strip:2 * strip] + high[:strip],
                    low[2 * strip:] + high[strip:2 * strip],
                    high[2 * strip:],
                )
                for tile, total in enumerate(sums):
                    total = total.reshape(peers, rows, HD)
                    if tile < 2:
                        early[which, tile, :, :, columns] = total.astype(LOW)
                    else:
                        own_out[which, tile - 2, :, :, columns] = total
        moves = [] if split else [(early, early_outs[0])]
        for by in range(peers):
            at = lax.rem(s + by, peers)
            moves.append((dq_all.at[:, at], dq_outs[by]))
            if split:
                moves.append((early.at[:, :, at], early_outs[by]))
        run_moves(moves, sems)

    outs = [shape(2, 2, peers, rows, cut, dtype=WIDE)] + [shape(2, rows, cut)] * peers
    outs += [shape(2, 2, rows, cut)] * peers if split else [shape(2, 2, peers, rows, cut)]
    scratch = [
        pltpu.VMEM((2, 4, peers, rows, cut), LOW),
        pltpu.VMEM((2, 2, peers, rows, cut), LOW),
        pltpu.VMEM((2, 2, peers, rows, cut), LOW),
        pltpu.VMEM((2, peers, rows, cut), LOW),
        pltpu.SemaphoreType.DMA((3 * peers,)),
    ]
    flops = heads * 2 * 5 * 2 * strip * 3 * strip * HD
    ins = [bias] + kv + kv_earlier + qg
    outs = call(kernel, ins, outs, scratch, "attention_grads", whole=True, flops=flops, room=40 * MIB)
    return outs[0], outs[1:1 + peers], outs[1 + peers:]


def summed(own, later, turns, after):
    _, _, peers, rows, cut = own.shape
    split = len(later) > 1 or later[0].ndim == 4

    def kernel(own_ref, *refs):
        later_refs, outs = refs[:len(later)], refs[len(later) + len(after):]
        s = lax.axis_index("sub")
        for place, (by, out) in enumerate(zip(turns, outs)):
            at = lax.rem(s + by, peers)
            for which in range(2):
                for row in range(2):
                    term = later_refs[place][which, row] if split else later_refs[0][which, row, at]
                    out[which, row] = (own_ref[which, row, at] + term.astype(WIDE)).astype(LOW)

    outs = [shape(2, 2, rows, cut)] * len(turns)
    return call(kernel, [own] + later + after, outs, [], "summed", whole=True)


def rows_for_pair(dq, dkv):
    peers = len(dq)
    _, rows, cut = dq[0].shape

    def kernel(*refs):
        dq_refs, dkv_refs, (send, keep), sems = refs[:peers], refs[peers:2 * peers], refs[-3:-1], refs[-1]
        p, s = lax.axis_index("pair"), lax.axis_index("sub")
        moves = []
        for by in range(peers):
            at = lax.rem(s - by + peers, peers)
            for out, row in ((send, 1 - p), (keep, p)):
                moves += [(dq_refs[by].at[row], out.at[0, at]), (dkv_refs[by].at[:, row], out.at[1:3, at])]
        run_moves(moves, sems)

    outs = [shape(3, peers, rows, cut)] * 2
    return call(kernel, dq + dkv, outs, [pltpu.SemaphoreType.DMA((4 * peers,))], "rows_for_pair")


def laid_out(kept, paired, spans):
    _, peers, rows, _ = kept[0].shape
    part = spans[-1][1]
    half = part * peers
    count = len(spans)

    def kernel(*refs):
        keep, rec, outs, sems = refs[:count], refs[count:2 * count], refs[2 * count:-1], refs[-1]
        p = lax.axis_index("pair")
        moves = []
        for mine, theirs, (low, high) in zip(keep, rec, spans):
            for source, side in ((mine, p), (theirs, 1 - p)):
                for at in range(peers):
                    columns = pl.ds(pl.multiple_of(side * half + at * part + low, HD), high - low)
                    moves += [(source.at[which, at], out.at[:, columns]) for which, out in enumerate(outs)]
        run_moves(moves, sems)

    outs = [shape(rows, 2 * half)] * 3
    return call(kernel, kept + paired, outs, [pltpu.SemaphoreType.DMA((6 * count * peers,))], "laid_out")


def allowed_bias(session, rows):
    strip = rows * lax.axis_size("sub")
    block = 2 * strip
    at_block = lax.axis_index("blk")
    window = jnp.concatenate([jnp.zeros((block,), jnp.int32), session])
    sess = lax.dynamic_slice_in_dim(window, at_block * block, 2 * block)
    place = (at_block - 1) * block + jnp.arange(2 * block, dtype=jnp.int32)

    def tile_bias(tile):
        q_at = slice(block + tile * strip, block + (tile + 1) * strip)
        k_at = slice(tile * strip, (tile + 3) * strip)
        k_place, q_place = place[k_at, None], place[None, q_at]
        allowed = (sess[None, q_at] == sess[k_at, None]) & (k_place <= q_place) & (k_place >= 0)
        return jnp.where(allowed, 0.0, NEG_FILL)

    return jnp.stack([tile_bias(0), tile_bias(1)])


def shards(queries, keys, values, out_grad, session):
    peers = lax.axis_size("sub")
    others = list(range(1, peers))
    part = queries.shape[1] // (2 * peers)
    spans, at = [], 0
    for heads in chunks_of(part // HD):
        spans.append((at, at + heads * HD))
        at += heads * HD
    bias = allowed_bias(session, queries.shape[0])
    kept, paired = [], []
    first_turn, kv_turn, own_turn, qg_turn, last_turn = [], [], [], [], []
    for index, (low, high) in enumerate(spans):
        last = index == len(spans) - 1
        send, own = first_parts([keys, values], low, high, first_turn)
        rec = swapped(send)
        sends = head_parts(own, rec, others, kv_turn)
        kv = [round_sub(value, by) for by, value in zip(others, sends)]
        kv_own = head_parts(own, rec, [0], own_turn)
        earlier = [along_blocks(kv_own[0], 1, True)]
        own_turn = earlier[:]
        if last:
            earlier += [along_blocks(relayed(value, last_turn), 1, False) for value in kv]
        else:
            earlier += [along_blocks(value, 1, True) for value in kv]
        send, own = first_parts([queries, out_grad], low, high, [own])
        rec = swapped(send)
        sends = head_parts(own, rec, others, qg_turn)
        qg = [round_sub(value, by) for by, value in zip(others, sends)]
        qg_own = head_parts(own, rec, [0], [])
        first_turn, kv_turn, qg_turn = sends, kv, qg
        grads, dq, early = attention_grads(bias, kv_own + kv, earlier, qg_own + qg, last)
        last_turn = [dq[0]]
        dq = [dq[0]] + [round_sub(dq[by], by) for by in others]
        if last:
            later = [along_blocks(value, -1, False) for value in early]
            dkv = summed(grads, later[1:], others, dq[1:])
            dkv = summed(grads, later[:1], [0], []) + [round_sub(value, by) for by, value in zip(others, dkv)]
        else:
            dkv = summed(grads, [along_blocks(early[0], -1, False)], [0] + others, dq[1:])
            dkv = [dkv[0]] + [round_sub(dkv[by], by) for by in others]
        send, keep = rows_for_pair(dq, dkv)
        kept.append(keep)
        paired.append(swapped(send))
    return tuple(laid_out(kept, paired, spans))


def solution(mesh):
    spread = P(("grp", "blk", "pair", "sub"), None)
    return jax.shard_map(
        shards, mesh=mesh, in_specs=(spread,) * 4 + (P("grp"),), out_specs=(spread,) * 3, check_vma=False
    )
```

```python
import math

import jax
import jax.numpy as jnp
from jax import lax
from jax.experimental import pallas as pl
from jax.experimental.pallas import tpu as pltpu
from jax.sharding import PartitionSpec as P

HD = 128
NEG_FILL = -1e30
LOW = jnp.bfloat16
WIDE = jnp.float32
MIB = 1024 * 1024
TO_BITS = HD ** (-0.5) / math.log(2.0)
SCALE = HD ** (-0.5)
ROWS_BY_ROWS = (((1,), (1,)), ((), ()))


def chunks_of(heads):
    return [heads // 2, heads - heads // 2]


def along_blocks(value, by, ring):
    peers = lax.axis_size("blk")
    pairs = [(i, (i + by) % peers) for i in range(peers) if ring or 0 <= i + by < peers]
    return lax.ppermute(value, "blk", pairs)


def round_sub(value, by):
    peers = lax.axis_size("sub")
    return lax.ppermute(value, "sub", [(i, (i + by) % peers) for i in range(peers)])


def swapped(value):
    return lax.ppermute(value, "pair", [(0, 1), (1, 0)])


def run_moves(moves, sems):
    copies = [pltpu.make_async_copy(src, dst, sems.at[at]) for at, (src, dst) in enumerate(moves)]
    for copy in copies:
        copy.start()
    for copy in copies:
        copy.wait()


def call(kernel, ins, outs, scratch, name, whole=False, flops=0, room=8 * MIB):
    spec = pl.BlockSpec(memory_space=pltpu.VMEM if whole else pl.ANY)
    moved = sum(math.prod(a.shape) * a.dtype.itemsize for a in list(ins) + list(outs))
    return list(
        pl.pallas_call(
            kernel,
            out_shape=outs,
            in_specs=[spec] * len(ins),
            out_specs=[spec] * len(outs),
            scratch_shapes=scratch,
            name=name,
            cost_estimate=pl.CostEstimate(flops=flops, bytes_accessed=moved, transcendentals=0),
            compiler_params=pltpu.CompilerParams(vmem_limit_bytes=room),
        )(*ins)
    )


def shape(*dims, dtype=LOW):
    return jax.ShapeDtypeStruct(dims, dtype)


def first_parts(groups, after):
    held, wanted, outs = [], [], []
    for arrays, low, high in groups:
        rows, width = arrays[0].shape
        peers = lax.axis_size("sub")
        half = width // 2
        part = half // peers
        wanted.append((len(held), len(arrays), low, high))
        held += [pltpu.with_memory_space_constraint(array, pltpu.HBM) for array in arrays]
        outs += [pltpu.VMEM((len(arrays), peers, rows, high - low), LOW)] * 2

    def kernel(*refs):
        out_refs, sems = refs[-1 - len(outs):-1], refs[-1]
        p = lax.axis_index("pair")
        moves = []
        for group, (first, count, low, high) in enumerate(wanted):
            for side, out in zip((1 - p, p), out_refs[2 * group:2 * group + 2]):
                for at in range(peers):
                    start = pl.multiple_of(side * half + at * part + low, HD)
                    for i in range(count):
                        moves.append((refs[first + i].at[:, pl.ds(start, high - low)], out.at[i, at]))
        run_moves(moves, sems)

    spec = pl.BlockSpec(memory_space=pl.ANY)
    parts = pl.pallas_call(
        kernel,
        out_shape=outs,
        in_specs=[spec] * (len(held) + len(after)),
        out_specs=[spec] * len(outs),
        scratch_shapes=[pltpu.SemaphoreType.DMA((2 * peers * len(held),))],
        name="first_parts",
        compiler_params=pltpu.CompilerParams(vmem_limit_bytes=8 * MIB),
    )(*held, *after)
    return [(parts[2 * i], parts[2 * i + 1]) for i in range(len(groups))]


def head_parts(own, paired, which, turns, after):
    _, peers, rows, cut = own.shape
    chosen = pl.ds(which, 2)

    def kernel(own_ref, pair_ref, *refs):
        outs, sems = refs[len(after):-1], refs[-1]
        p, s = lax.axis_index("pair"), lax.axis_index("sub")
        moves = []
        for by, out in zip(turns, outs):
            at = lax.rem(s + by, peers)
            moves += [(own_ref.at[chosen, at], out.at[:, p]), (pair_ref.at[chosen, at], out.at[:, 1 - p])]
        run_moves(moves, sems)

    outs = [shape(2, 2, rows, cut)] * len(turns)
    scratch = [pltpu.SemaphoreType.DMA((2 * len(turns),))]
    return call(kernel, [own, paired] + after, outs, scratch, "head_parts")


def attention_grads(bias, kv, kv_earlier, qg, split, after):
    peers = len(kv)
    _, _, rows, cut = kv[0].shape
    heads = cut // HD
    strip = rows * peers
    early_count = peers if split else 1

    def kernel(*refs):
        bias_ref = refs[0]
        kv_in, early_in, qg_in = refs[1:1 + peers], refs[1 + peers:1 + 2 * peers], refs[1 + 2 * peers:1 + 3 * peers]
        outs = refs[1 + 3 * peers + len(after):-5]
        own_out, dq_outs, early_outs = outs[0], outs[1:1 + peers], outs[1 + peers:]
        kv_all, qg_all, early, dq_all, sems = refs[-5:]
        s = lax.axis_index("sub")
        moves = []
        for by in range(peers):
            at = lax.rem(s - by + peers, peers)
            moves += [
                (early_in[by], kv_all.at[:, 0:2, at]),
                (kv_in[by], kv_all.at[:, 2:4, at]),
                (qg_in[by], qg_all.at[:, :, at]),
            ]
        run_moves(moves, sems)
        strips = [(head, tile) for head in range(heads) for tile in range(2)]
        products, terms = {}, {}

        def flat(ref, which, tiles, head):
            block = ref[which, tiles, :, :, pl.ds(head * HD, HD)]
            return block.reshape(block.shape[0] * strip, HD)

        def multiply(head, tile):
            at, span = pl.ds(tile, 1), pl.ds(tile, 3)
            q, g = flat(qg_all, 0, at, head), flat(qg_all, 1, at, head)
            k, v = flat(kv_all, 0, span, head), flat(kv_all, 1, span, head)
            scores = lax.dot_general(k, q, ROWS_BY_ROWS, preferred_element_type=WIDE)
            grad_prob = lax.dot_general(v, g, ROWS_BY_ROWS, preferred_element_type=WIDE)
            products[head, tile] = q, g, k, scores, grad_prob

        def finish(head, tile):
            q, g, k, scores, grad_prob = products.pop((head, tile))
            scores = scores * TO_BITS + bias_ref[tile]
            peak = jnp.max(scores, axis=0, keepdims=True)
            weight = jnp.exp2(scores - peak)
            prob = weight * (1.0 / jnp.sum(weight, axis=0, keepdims=True))
            prob_low = prob.astype(LOW)
            row_dot = jnp.sum(prob_low.astype(WIDE) * grad_prob, axis=0, keepdims=True)
            score_low = (prob * (grad_prob - row_dot)).astype(LOW)
            dq = jnp.dot(k.T, score_low, preferred_element_type=WIDE) * SCALE
            dq_all[tile, :, :, pl.ds(head * HD, HD)] = dq.T.astype(LOW).reshape(peers, rows, HD)
            dk = jnp.dot(score_low, q, preferred_element_type=WIDE) * SCALE
            dv = jnp.dot(prob_low, g, preferred_element_type=WIDE)
            terms[head, tile] = dk, dv

        def gather(head):
            for which in range(2):
                low, high = terms[head, 0][which], terms[head, 1][which]
                sums = (
                    low[:strip],
                    low[strip:2 * strip] + high[:strip],
                    low[2 * strip:] + high[strip:2 * strip],
                    high[2 * strip:],
                )
                for tile, total in enumerate(sums):
                    total = total.reshape(peers, rows, HD)
                    if tile < 2:
                        early[which, tile, :, :, pl.ds(head * HD, HD)] = total.astype(LOW)
                    else:
                        own_out[which, tile - 2, :, :, pl.ds(head * HD, HD)] = total

        multiply(*strips[0])
        for at, (head, tile) in enumerate(strips):
            if at + 1 < len(strips):
                multiply(*strips[at + 1])
            finish(head, tile)
            if tile == 1:
                gather(head)
        moves = [] if split else [(early, early_outs[0])]
        for by in range(peers):
            at = lax.rem(s + by, peers)
            moves.append((dq_all.at[:, at], dq_outs[by]))
            if split:
                moves.append((early.at[:, :, at], early_outs[by]))
        run_moves(moves, sems)

    outs = [shape(2, 2, peers, rows, cut, dtype=WIDE)] + [shape(2, rows, cut)] * peers
    outs += [shape(2, 2, rows, cut)] * peers if split else [shape(2, 2, peers, rows, cut)]
    scratch = [
        pltpu.VMEM((2, 4, peers, rows, cut), LOW),
        pltpu.VMEM((2, 2, peers, rows, cut), LOW),
        pltpu.VMEM((2, 2, peers, rows, cut), LOW),
        pltpu.VMEM((2, peers, rows, cut), LOW),
        pltpu.SemaphoreType.DMA((3 * peers,)),
    ]
    flops = heads * 2 * 5 * 2 * strip * 3 * strip * HD
    ins = [bias] + kv + kv_earlier + qg + after
    outs = call(kernel, ins, outs, scratch, "attention_grads", whole=True, flops=flops, room=40 * MIB)
    return outs[0], outs[1:1 + peers], outs[1 + peers:]


def summed(own, later, turns, after):
    _, _, peers, rows, cut = own.shape
    split = len(later) > 1 or later[0].ndim == 4

    def kernel(own_ref, *refs):
        later_refs, outs = refs[:len(later)], refs[len(later) + len(after):]
        s = lax.axis_index("sub")
        for place, (by, out) in enumerate(zip(turns, outs)):
            at = lax.rem(s + by, peers)
            for which in range(2):
                for row in range(2):
                    term = later_refs[place][which, row] if split else later_refs[0][which, row, at]
                    out[which, row] = (own_ref[which, row, at] + term.astype(WIDE)).astype(LOW)

    outs = [shape(2, 2, rows, cut)] * len(turns)
    return call(kernel, [own] + later + after, outs, [], "summed", whole=True)


def rows_for_pair(dq, dkv):
    peers = len(dq)
    _, rows, cut = dq[0].shape

    def kernel(*refs):
        dq_refs, dkv_refs, (send, keep) = refs[:peers], refs[peers:2 * peers], refs[-2:]
        p, s = lax.axis_index("pair"), lax.axis_index("sub")
        for by in range(peers):
            at = lax.rem(s - by + peers, peers)
            for out, row in ((send, 1 - p), (keep, p)):
                out[0, at] = dq_refs[by][row]
                for which in range(2):
                    out[1 + which, at] = dkv_refs[by][which, row]

    outs = [shape(3, peers, rows, cut)] * 2
    return call(kernel, dq + dkv, outs, [], "rows_for_pair", whole=True)


def laid_out(kept, paired, spans):
    _, peers, rows, _ = kept[0].shape
    part = spans[-1][1]
    half = part * peers
    count = len(spans)

    def kernel(*refs):
        keep, rec, outs, sems = refs[:count], refs[count:2 * count], refs[2 * count:-1], refs[-1]
        p = lax.axis_index("pair")
        moves = []
        for mine, theirs, (low, high) in zip(keep, rec, spans):
            for source, side in ((mine, p), (theirs, 1 - p)):
                for at in range(peers):
                    columns = pl.ds(pl.multiple_of(side * half + at * part + low, HD), high - low)
                    moves += [(source.at[which, at], out.at[:, columns]) for which, out in enumerate(outs)]
        run_moves(moves, sems)

    outs = [shape(rows, 2 * half)] * 3
    return call(kernel, kept + paired, outs, [pltpu.SemaphoreType.DMA((6 * count * peers,))], "laid_out")


def allowed_bias(session, rows):
    strip = rows * lax.axis_size("sub")
    block = 2 * strip
    at_block = lax.axis_index("blk")
    window = jnp.concatenate([jnp.zeros((block,), jnp.int32), session])
    sess = lax.dynamic_slice_in_dim(window, at_block * block, 2 * block)
    place = (at_block - 1) * block + jnp.arange(2 * block, dtype=jnp.int32)

    def tile_bias(tile):
        q_at = slice(block + tile * strip, block + (tile + 1) * strip)
        k_at = slice(tile * strip, (tile + 3) * strip)
        k_place, q_place = place[k_at, None], place[None, q_at]
        allowed = (sess[None, q_at] == sess[k_at, None]) & (k_place <= q_place) & (k_place >= 0)
        return jnp.where(allowed, 0.0, NEG_FILL)

    return jnp.stack([tile_bias(0), tile_bias(1)])


def shards(queries, keys, values, out_grad, session):
    peers = lax.axis_size("sub")
    others = list(range(1, peers))
    part = queries.shape[1] // (2 * peers)
    spans, at = [], 0
    for heads in chunks_of(part // HD):
        spans.append((at, at + heads * HD))
        at += heads * HD
    bias = allowed_bias(session, queries.shape[0])
    (kv_send, kv_first), = first_parts([([keys, values], *spans[0])], [])
    rest = [([queries, out_grad], *spans[0])] + [([keys, values, queries, out_grad], *span) for span in spans[1:]]
    rest = first_parts(rest, [kv_first])
    kv_parts = [(kv_first, swapped(kv_send), 0)]
    qg_parts = [(rest[0][1], swapped(rest[0][0]), 0)]
    for send, own in rest[1:]:
        paired = swapped(send)
        kv_parts.append((own, paired, 0))
        qg_parts.append((own, paired, 2))
    count = len(spans)
    kv_sends, qg_sends, kv, qg, kv_own, own_earlier = [], [], [], [], [], []
    for index in range(count):
        kv_sends.append(head_parts(*kv_parts[index], others, kv[index - 1] if index else []))
        kv.append([round_sub(value, by) for by, value in zip(others, kv_sends[index])])
        kv_own.append(head_parts(*kv_parts[index], [0], own_earlier[index - 1:index]))
        own_earlier.append(along_blocks(kv_own[index][0], 1, True))
        qg_sends.append(head_parts(*qg_parts[index], others, qg[index - 1] if index else []))
        qg.append([round_sub(value, by) for by, value in zip(others, qg_sends[index])])
    kept, paired = [], []
    for index in range(count):
        last = index == count - 1
        earlier = [own_earlier[index]] + [along_blocks(value, 1, not last) for value in kv[index]]
        qg_all = head_parts(*qg_parts[index], [0], []) + qg[index]
        grads, dq, early = attention_grads(bias, kv_own[index] + kv[index], earlier, qg_all, last, [])
        dq = [dq[0]] + [round_sub(dq[by], by) for by in others]
        later = [along_blocks(value, -1, False) for value in early]
        if last:
            dkv = summed(grads, later[1:], others, dq[1:])
            dkv = summed(grads, later[:1], [0], dkv[:1]) + [round_sub(value, by) for by, value in zip(others, dkv)]
        else:
            dkv = summed(grads, later, [0] + others, dq[1:])
            dkv = [dkv[0]] + [round_sub(dkv[by], by) for by in others]
        send, keep = rows_for_pair(dq, dkv)
        kept.append(keep)
        paired.append(swapped(send))
    return tuple(laid_out(kept, paired, spans))


def solution(mesh):
    spread = P(("grp", "blk", "pair", "sub"), None)
    return jax.shard_map(
        shards, mesh=mesh, in_specs=(spread,) * 4 + (P("grp"),), out_specs=(spread,) * 3, check_vma=False
    )
```

```python
import math

import jax
import jax.numpy as jnp
from jax import lax
from jax.experimental import pallas as pl
from jax.experimental.pallas import tpu as pltpu
from jax.sharding import PartitionSpec as P

HD = 128
NEG_FILL = -1e30
LOW = jnp.bfloat16
WIDE = jnp.float32
MIB = 1024 * 1024
TO_BITS = HD ** (-0.5) / math.log(2.0)
SCALE = HD ** (-0.5)
ROWS_BY_ROWS = (((1,), (1,)), ((), ()))


def chunks_of(heads):
    return [heads // 2, heads - heads // 2]


def along_blocks(value, by):
    peers = lax.axis_size("blk")
    return lax.ppermute(value, "blk", [(i, i + by) for i in range(peers) if 0 <= i + by < peers])


def neighbours(value, first):
    peers = lax.axis_size("blk")
    pairs = []
    for i in range(peers):
        other = i + 1 if (i % 2 == 0) == first else i - 1
        pairs.append((i, other if 0 <= other < peers else i))
    return lax.ppermute(value, "blk", pairs)


def round_sub(value, by):
    peers = lax.axis_size("sub")
    return lax.ppermute(value, "sub", [(i, (i + by) % peers) for i in range(peers)])


def swapped(value):
    return lax.ppermute(value, "pair", [(0, 1), (1, 0)])


def run_moves(moves, sems):
    copies = [pltpu.make_async_copy(src, dst, sems.at[at]) for at, (src, dst) in enumerate(moves)]
    for copy in copies:
        copy.start()
    for copy in copies:
        copy.wait()


def call(kernel, ins, outs, scratch, name, whole=False, flops=0, room=8 * MIB):
    spec = pl.BlockSpec(memory_space=pltpu.VMEM if whole else pl.ANY)
    moved = sum(math.prod(a.shape) * a.dtype.itemsize for a in list(ins) + list(outs))
    return list(
        pl.pallas_call(
            kernel,
            out_shape=outs,
            in_specs=[spec] * len(ins),
            out_specs=[spec] * len(outs),
            scratch_shapes=scratch,
            name=name,
            cost_estimate=pl.CostEstimate(flops=flops, bytes_accessed=moved, transcendentals=0),
            compiler_params=pltpu.CompilerParams(vmem_limit_bytes=room),
        )(*ins)
    )


def shape(*dims, dtype=LOW):
    return jax.ShapeDtypeStruct(dims, dtype)


def first_parts(groups, after):
    held, wanted, outs = [], [], []
    for arrays, low, high in groups:
        rows, width = arrays[0].shape
        peers = lax.axis_size("sub")
        half = width // 2
        part = half // peers
        wanted.append((len(held), len(arrays), low, high))
        held += [pltpu.with_memory_space_constraint(array, pltpu.HBM) for array in arrays]
        outs += [pltpu.VMEM((len(arrays), peers, rows, high - low), LOW)] * 2

    def kernel(*refs):
        out_refs, sems = refs[-1 - len(outs):-1], refs[-1]
        p = lax.axis_index("pair")
        moves = []
        for group, (first, count, low, high) in enumerate(wanted):
            for side, out in zip((1 - p, p), out_refs[2 * group:2 * group + 2]):
                for at in range(peers):
                    start = pl.multiple_of(side * half + at * part + low, HD)
                    for i in range(count):
                        moves.append((refs[first + i].at[:, pl.ds(start, high - low)], out.at[i, at]))
        run_moves(moves, sems)

    spec = pl.BlockSpec(memory_space=pl.ANY)
    parts = pl.pallas_call(
        kernel,
        out_shape=outs,
        in_specs=[spec] * (len(held) + len(after)),
        out_specs=[spec] * len(outs),
        scratch_shapes=[pltpu.SemaphoreType.DMA((2 * peers * len(held),))],
        name="first_parts",
        compiler_params=pltpu.CompilerParams(vmem_limit_bytes=8 * MIB),
    )(*held, *after)
    return [(parts[2 * i], parts[2 * i + 1]) for i in range(len(groups))]


def head_parts(own, paired, which, turns, after):
    _, peers, rows, cut = own.shape
    chosen = pl.ds(which, 2)

    def kernel(own_ref, pair_ref, *refs):
        outs, sems = refs[len(after):-1], refs[-1]
        p, s = lax.axis_index("pair"), lax.axis_index("sub")
        moves = []
        for by, out in zip(turns, outs):
            at = lax.rem(s + by, peers)
            moves += [(own_ref.at[chosen, at], out.at[:, p]), (pair_ref.at[chosen, at], out.at[:, 1 - p])]
        run_moves(moves, sems)

    outs = [shape(2, 2, rows, cut)] * len(turns)
    scratch = [pltpu.SemaphoreType.DMA((2 * len(turns),))]
    return call(kernel, [own, paired] + after, outs, scratch, "head_parts")


def relayed(value, after):
    def kernel(value_ref, *refs):
        run_moves([(value_ref, refs[-2])], refs[-1])

    scratch = [pltpu.SemaphoreType.DMA((1,))]
    return call(kernel, [value] + after, [shape(*value.shape)], scratch, "relayed")[0]


def near_exchange(kv_parts, qg_parts, spans):
    _, _, rows, _ = kv_parts[0][0].shape
    ins = [array for parts in kv_parts + qg_parts for array in parts[:2]]

    def kernel(*refs):
        outs, sems = refs[-3:-1], refs[-1]
        p, s = lax.axis_index("pair"), lax.axis_index("sub")
        count = len(spans)

        def fill(out, parts, first):
            moves = []
            for chunk, (low, high) in enumerate(spans):
                which = pl.ds(parts[chunk][2], 2)
                for side, ref in zip((p, 1 - p), refs[2 * (first + chunk):]):
                    moves.append((ref.at[which, s], out.at[:, side, :, pl.ds(low, high - low)]))
            return moves

        for odd, order in ((0, outs), (1, outs[::-1])):
            @pl.when(lax.rem(lax.axis_index("blk"), 2) == odd)
            def _():
                run_moves(fill(order[0], kv_parts, 0) + fill(order[1], qg_parts, count), sems)

    outs = [shape(2, 2, rows, spans[-1][1])] * 2
    scratch = [pltpu.SemaphoreType.DMA((4 * len(spans),))]
    return call(kernel, ins, outs, scratch, "near_exchange")


def either(condition, when_true, otherwise, held, sem):
    @pl.when(condition)
    def _():
        run_moves([(when_true, held)], sem)

    @pl.when(jnp.logical_not(condition))
    def _():
        run_moves([(otherwise, held)], sem)


def query_grads(bias, kv, near, far, qg, span):
    peers = len(kv)
    _, _, rows, cut = kv[0].shape
    heads = cut // HD
    strip = rows * peers

    def kernel(*refs):
        bias_ref, first, second = refs[:3]
        kv_in, far_in, qg_in = refs[3:3 + peers], refs[3 + peers:2 + 2 * peers], refs[2 + 2 * peers:2 + 3 * peers]
        own_out, stats_out, *dq_outs = refs[2 + 3 * peers:-4]
        kv_all, qg_all, dq_all, sems = refs[-4:]
        s = lax.axis_index("sub")
        odd = lax.rem(lax.axis_index("blk"), 2) == 1
        columns = pl.ds(span[0], cut)
        either(odd, first.at[:, :, :, columns], second.at[:, :, :, columns], kv_all.at[:, 0:2, s], sems)
        moves = []
        for by in range(peers):
            at = lax.rem(s - by + peers, peers)
            moves += [(kv_in[by], kv_all.at[:, 2:4, at]), (qg_in[by], qg_all.at[:, :, at])]
            if by:
                moves.append((far_in[by - 1], kv_all.at[:, 0:2, at]))
        run_moves(moves, sems)
        strips = [(head, tile) for head in range(heads) for tile in range(2)]
        products, terms = {}, {}
        stats_out[...] = jnp.zeros_like(stats_out)

        def flat(ref, which, tiles, head):
            block = ref[which, tiles, :, :, pl.ds(head * HD, HD)]
            return block.reshape(block.shape[0] * strip, HD)

        def multiply(head, tile):
            at, reach = pl.ds(tile, 1), pl.ds(tile, 3)
            q, g = flat(qg_all, 0, at, head), flat(qg_all, 1, at, head)
            k, v = flat(kv_all, 0, reach, head), flat(kv_all, 1, reach, head)
            scores = lax.dot_general(k, q, ROWS_BY_ROWS, preferred_element_type=WIDE)
            grad_prob = lax.dot_general(v, g, ROWS_BY_ROWS, preferred_element_type=WIDE)
            products[head, tile] = q, g, k, scores, grad_prob

        def finish(head, tile):
            q, g, k, scores, grad_prob = products.pop((head, tile))
            scores = scores * TO_BITS + bias_ref[tile]
            peak = jnp.max(scores, axis=0, keepdims=True)
            weight = jnp.exp2(scores - peak)
            total = jnp.sum(weight, axis=0, keepdims=True)
            prob = weight * (1.0 / total)
            prob_low = prob.astype(LOW)
            row_dot = jnp.sum(prob_low.astype(WIDE) * grad_prob, axis=0, keepdims=True)
            score_low = (prob * (grad_prob - row_dot)).astype(LOW)
            stats_out[head, 2 * tile:2 * tile + 1] = peak + jnp.log2(total)
            stats_out[head, 2 * tile + 1:2 * tile + 2] = row_dot
            dq = jnp.dot(k.T, score_low, preferred_element_type=WIDE) * SCALE
            dq_all[tile, :, :, pl.ds(head * HD, HD)] = dq.T.astype(LOW).reshape(peers, rows, HD)
            skip = (2 - tile) * strip
            dk = jnp.dot(score_low[skip:], q, preferred_element_type=WIDE)
            dv = jnp.dot(prob_low[skip:], g, preferred_element_type=WIDE)
            terms[head, tile] = dk, dv

        def gather(head):
            for which in range(2):
                low, high = terms[head, 0][which], terms[head, 1][which]
                for tile, total in enumerate((low + high[:strip], high[strip:])):
                    own_out[which, tile, :, :, pl.ds(head * HD, HD)] = total.reshape(peers, rows, HD)

        multiply(*strips[0])
        for at, (head, tile) in enumerate(strips):
            if at + 1 < len(strips):
                multiply(*strips[at + 1])
            finish(head, tile)
            if tile == 1:
                gather(head)
        run_moves([(dq_all.at[:, lax.rem(s + by, peers)], dq_outs[by]) for by in range(peers)], sems)

    outs = [shape(2, 2, peers, rows, cut, dtype=WIDE), shape(heads, 8, strip, dtype=WIDE)]
    outs += [shape(2, rows, cut)] * peers
    scratch = [
        pltpu.VMEM((2, 4, peers, rows, cut), LOW),
        pltpu.VMEM((2, 2, peers, rows, cut), LOW),
        pltpu.VMEM((2, peers, rows, cut), LOW),
        pltpu.SemaphoreType.DMA((3 * peers,)),
    ]
    flops = heads * 2 * 5 * 2 * strip * 3 * strip * HD
    ins = [bias] + near + kv + far + qg
    outs = call(kernel, ins, outs, scratch, "query_grads", whole=True, flops=flops, room=40 * MIB)
    return outs[0], outs[1], outs[2:]


def key_grads(bias, kv, near, far, stats, own, span, after):
    peers = len(kv)
    _, _, rows, cut = kv[0].shape
    heads = cut // HD
    strip = rows * peers

    def kernel(*refs):
        bias_ref, first, second, stats_ref, own_ref = refs[:5]
        kv_in, far_in = refs[5:5 + peers], refs[5 + peers:4 + 2 * peers]
        outs = refs[4 + 2 * peers + len(after):-4]
        kv_all, later, grads, sems = refs[-4:]
        s = lax.axis_index("sub")
        odd = lax.rem(lax.axis_index("blk"), 2) == 1
        columns = pl.ds(span[0], cut)
        either(odd, second.at[:, :, :, columns], first.at[:, :, :, columns], later.at[:, :, s], sems)
        moves = []
        for by in range(peers):
            at = lax.rem(s - by + peers, peers)
            moves.append((kv_in[by], kv_all.at[:, :, at]))
            if by:
                moves.append((far_in[by - 1], later.at[:, :, at]))
        run_moves(moves, sems)
        strips = [(head, tile) for head in range(heads) for tile in range(2)]
        products, terms = {}, {}

        def flat(ref, which, tiles, head):
            block = ref[which, tiles, :, :, pl.ds(head * HD, HD)]
            return block.reshape(block.shape[0] * strip, HD)

        def multiply(head, tile):
            at, reach = pl.ds(tile, 1), pl.ds(tile, 2 - tile)
            q, g = flat(later, 0, at, head), flat(later, 1, at, head)
            k, v = flat(kv_all, 0, reach, head), flat(kv_all, 1, reach, head)
            scores = lax.dot_general(k, q, ROWS_BY_ROWS, preferred_element_type=WIDE)
            grad_prob = lax.dot_general(v, g, ROWS_BY_ROWS, preferred_element_type=WIDE)
            products[head, tile] = q, g, scores, grad_prob

        def finish(head, tile):
            q, g, scores, grad_prob = products.pop((head, tile))
            scores = scores * TO_BITS + bias_ref[tile, :(2 - tile) * strip]
            prob = jnp.exp2(scores - stats_ref[head, 2 * tile:2 * tile + 1])
            score_low = (prob * (grad_prob - stats_ref[head, 2 * tile + 1:2 * tile + 2])).astype(LOW)
            dk = jnp.dot(score_low, q, preferred_element_type=WIDE)
            dv = jnp.dot(prob.astype(LOW), g, preferred_element_type=WIDE)
            terms[head, tile] = dk, dv

        def gather(head):
            for which in range(2):
                scale = SCALE if which == 0 else 1.0
                wide, narrow = terms[head, 0][which], terms[head, 1][which]
                for tile, term in ((0, wide[:strip]), (1, wide[strip:] + narrow)):
                    here = pl.ds(head * HD, HD)
                    term = own_ref[which, tile, :, :, here] + term.reshape(peers, rows, HD)
                    grads[which, tile, :, :, here] = (term * scale).astype(LOW)

        multiply(*strips[0])
        for at, (head, tile) in enumerate(strips):
            if at + 1 < len(strips):
                multiply(*strips[at + 1])
            finish(head, tile)
            if tile == 1:
                gather(head)
        run_moves([(grads.at[:, :, lax.rem(s + by, peers)], outs[by]) for by in range(peers)], sems)

    outs = [shape(2, 2, rows, cut)] * peers
    held = pltpu.VMEM((2, 2, peers, rows, cut), LOW)
    scratch = [held, held, held, pltpu.SemaphoreType.DMA((3 * peers,))]
    flops = heads * 4 * 2 * 3 * strip * strip * HD
    ins = [bias] + near + [stats, own] + kv + far + after
    return call(kernel, ins, outs, scratch, "key_grads", whole=True, flops=flops, room=40 * MIB)


def rows_for_pair(dq, dkv):
    peers = len(dq)
    _, rows, cut = dq[0].shape

    def kernel(*refs):
        dq_refs, dkv_refs, (send, keep) = refs[:peers], refs[peers:2 * peers], refs[-2:]
        p, s = lax.axis_index("pair"), lax.axis_index("sub")
        for by in range(peers):
            at = lax.rem(s - by + peers, peers)
            for out, row in ((send, 1 - p), (keep, p)):
                out[0, at] = dq_refs[by][row]
                for which in range(2):
                    out[1 + which, at] = dkv_refs[by][which, row]

    outs = [shape(3, peers, rows, cut)] * 2
    return call(kernel, dq + dkv, outs, [], "rows_for_pair", whole=True)


def laid_out(kept, paired, spans):
    _, peers, rows, _ = kept[0].shape
    part = spans[-1][1]
    half = part * peers
    count = len(spans)

    def kernel(*refs):
        keep, rec, outs, sems = refs[:count], refs[count:2 * count], refs[2 * count:-1], refs[-1]
        p = lax.axis_index("pair")
        moves = []
        for mine, theirs, (low, high) in zip(keep, rec, spans):
            for source, side in ((mine, p), (theirs, 1 - p)):
                for at in range(peers):
                    columns = pl.ds(pl.multiple_of(side * half + at * part + low, HD), high - low)
                    moves += [(source.at[which, at], out.at[:, columns]) for which, out in enumerate(outs)]
        run_moves(moves, sems)

    outs = [shape(rows, 2 * half)] * 3
    return call(kernel, kept + paired, outs, [pltpu.SemaphoreType.DMA((6 * count * peers,))], "laid_out")


def allowed_bias(session, rows):
    strip = rows * lax.axis_size("sub")
    block = 2 * strip
    at_block = lax.axis_index("blk")
    margin = jnp.zeros((block,), jnp.int32)
    window = jnp.concatenate([margin, session, margin])
    sess = lax.dynamic_slice_in_dim(window, at_block * block, 3 * block)
    place = (at_block - 1) * block + jnp.arange(3 * block, dtype=jnp.int32)

    def tile_bias(q_tile, k_tile, tiles):
        q_at = slice(q_tile * strip, (q_tile + 1) * strip)
        k_at = slice(k_tile * strip, (k_tile + tiles) * strip)
        k_place, q_place = place[k_at, None], place[None, q_at]
        allowed = (sess[None, q_at] == sess[k_at, None]) & (k_place <= q_place)
        allowed = allowed & (k_place >= 0) & (q_place < session.shape[0])
        return jnp.where(allowed, 0.0, NEG_FILL)

    for_queries = jnp.stack([tile_bias(2, 0, 3), tile_bias(3, 1, 3)])
    for_keys = jnp.stack([tile_bias(4, 2, 2), tile_bias(5, 3, 2)])
    return for_queries, for_keys


def shards(queries, keys, values, out_grad, session):
    peers = lax.axis_size("sub")
    others = list(range(1, peers))
    part = queries.shape[1] // (2 * peers)
    spans, at = [], 0
    for heads in chunks_of(part // HD):
        spans.append((at, at + heads * HD))
        at += heads * HD
    query_bias, key_bias = allowed_bias(session, queries.shape[0])
    (kv_send, kv_first), = first_parts([([keys, values], *spans[0])], [])
    rest = [([queries, out_grad], *spans[0])] + [([keys, values, queries, out_grad], *span) for span in spans[1:]]
    rest = first_parts(rest, [kv_first])
    kv_parts = [(kv_first, swapped(kv_send), 0)]
    qg_parts = [(rest[0][1], swapped(rest[0][0]), 0)]
    for send, own in rest[1:]:
        paired = swapped(send)
        kv_parts.append((own, paired, 0))
        qg_parts.append((own, paired, 2))
    count = len(spans)
    near = near_exchange(kv_parts, qg_parts, spans)
    near = [neighbours(near[0], True), neighbours(near[1], False)]
    kv_sends, qg_sends, kv, qg = [], [], [], []
    for index in range(count):
        kv_sends.append(head_parts(*kv_parts[index], others, kv[index - 1] if index else []))
        kv.append([round_sub(value, by) for by, value in zip(others, kv_sends[index])])
        qg_sends.append(head_parts(*qg_parts[index], others, qg[index - 1] if index else []))
        qg.append([round_sub(value, by) for by, value in zip(others, qg_sends[index])])
    kept, paired = [], []
    query_turn, key_turn = [], []
    for index, span in enumerate(spans):
        kv_all = head_parts(*kv_parts[index], [0], []) + kv[index]
        qg_all = head_parts(*qg_parts[index], [0], []) + qg[index]
        upward = [relayed(value, query_turn) if index else value for value in kv[index]]
        downward = [relayed(value, key_turn) if index else value for value in qg[index]]
        earlier = [along_blocks(value, 1) for value in upward]
        later = [along_blocks(value, -1) for value in downward]
        grads, stats, dq = query_grads(query_bias, kv_all, near, earlier, qg_all, span)
        query_turn = [dq[0]]
        dq = [dq[0]] + [round_sub(dq[by], by) for by in others]
        dkv = key_grads(key_bias, kv_all, near, later, along_blocks(stats, -1), grads, span, dq[1:])
        key_turn = [dkv[0]]
        dkv = [dkv[0]] + [round_sub(dkv[by], by) for by in others]
        send, keep = rows_for_pair(dq, dkv)
        kept.append(keep)
        paired.append(swapped(send))
    return tuple(laid_out(kept, paired, spans))


def solution(mesh):
    spread = P(("grp", "blk", "pair", "sub"), None)
    return jax.shard_map(
        shards, mesh=mesh, in_specs=(spread,) * 4 + (P("grp"),), out_specs=(spread,) * 3, check_vma=False
    )
```

```python
import math

import jax
import jax.numpy as jnp
from jax import lax
from jax.experimental import pallas as pl
from jax.experimental.pallas import tpu as pltpu
from jax.sharding import PartitionSpec as P

HD = 128
NEG_FILL = -1e30
LOW = jnp.bfloat16
WIDE = jnp.float32
MIB = 1024 * 1024
TO_BITS = HD ** (-0.5) / math.log(2.0)
SCALE = HD ** (-0.5)
ROWS_BY_ROWS = (((1,), (1,)), ((), ()))


def chunks_of(heads):
    return [heads // 2, heads - heads // 2]


def along_blocks(value, by, ring):
    peers = lax.axis_size("blk")
    pairs = [(i, (i + by) % peers) for i in range(peers) if ring or 0 <= i + by < peers]
    return lax.ppermute(value, "blk", pairs)


def round_sub(value, by):
    peers = lax.axis_size("sub")
    return lax.ppermute(value, "sub", [(i, (i + by) % peers) for i in range(peers)])


def swapped(value):
    return lax.ppermute(value, "pair", [(0, 1), (1, 0)])


def run_moves(moves, sems):
    copies = [pltpu.make_async_copy(src, dst, sems.at[at]) for at, (src, dst) in enumerate(moves)]
    for copy in copies:
        copy.start()
    for copy in copies:
        copy.wait()


def call(kernel, ins, outs, scratch, name, whole=False, flops=0, room=8 * MIB):
    spec = pl.BlockSpec(memory_space=pltpu.VMEM if whole else pl.ANY)
    moved = sum(math.prod(a.shape) * a.dtype.itemsize for a in list(ins) + list(outs))
    return list(
        pl.pallas_call(
            kernel,
            out_shape=outs,
            in_specs=[spec] * len(ins),
            out_specs=[spec] * len(outs),
            scratch_shapes=scratch,
            name=name,
            cost_estimate=pl.CostEstimate(flops=flops, bytes_accessed=moved, transcendentals=0),
            compiler_params=pltpu.CompilerParams(vmem_limit_bytes=room),
        )(*ins)
    )


def shape(*dims, dtype=LOW):
    return jax.ShapeDtypeStruct(dims, dtype)


def first_parts(groups, after):
    held, wanted, outs = [], [], []
    for arrays, low, high in groups:
        rows, width = arrays[0].shape
        peers = lax.axis_size("sub")
        half = width // 2
        part = half // peers
        wanted.append((len(held), len(arrays), low, high))
        held += [pltpu.with_memory_space_constraint(array, pltpu.HBM) for array in arrays]
        outs += [pltpu.VMEM((len(arrays), peers, rows, high - low), LOW)] * 2

    def kernel(*refs):
        out_refs, sems = refs[-1 - len(outs):-1], refs[-1]
        p = lax.axis_index("pair")
        moves = []
        for group, (first, count, low, high) in enumerate(wanted):
            for side, out in zip((1 - p, p), out_refs[2 * group:2 * group + 2]):
                for at in range(peers):
                    start = pl.multiple_of(side * half + at * part + low, HD)
                    for i in range(count):
                        moves.append((refs[first + i].at[:, pl.ds(start, high - low)], out.at[i, at]))
        run_moves(moves, sems)

    spec = pl.BlockSpec(memory_space=pl.ANY)
    parts = pl.pallas_call(
        kernel,
        out_shape=outs,
        in_specs=[spec] * (len(held) + len(after)),
        out_specs=[spec] * len(outs),
        scratch_shapes=[pltpu.SemaphoreType.DMA((2 * peers * len(held),))],
        name="first_parts",
        compiler_params=pltpu.CompilerParams(vmem_limit_bytes=8 * MIB),
    )(*held, *after)
    return [(parts[2 * i], parts[2 * i + 1]) for i in range(len(groups))]


def head_parts(own, paired, which, turns, after):
    _, peers, rows, cut = own.shape
    chosen = pl.ds(which, 2)

    def kernel(own_ref, pair_ref, *refs):
        outs, sems = refs[len(after):-1], refs[-1]
        p, s = lax.axis_index("pair"), lax.axis_index("sub")
        moves = []
        for by, out in zip(turns, outs):
            at = lax.rem(s + by, peers)
            moves += [(own_ref.at[chosen, at], out.at[:, p]), (pair_ref.at[chosen, at], out.at[:, 1 - p])]
        run_moves(moves, sems)

    outs = [shape(2, 2, rows, cut)] * len(turns)
    scratch = [pltpu.SemaphoreType.DMA((2 * len(turns),))]
    return call(kernel, [own, paired] + after, outs, scratch, "head_parts")


def relayed(value, after):
    def kernel(value_ref, *refs):
        run_moves([(value_ref, refs[-2])], refs[-1])

    scratch = [pltpu.SemaphoreType.DMA((1,))]
    return call(kernel, [value] + after, [shape(*value.shape)], scratch, "relayed")[0]


def attention_grads(bias, kv, kv_earlier, qg, split, after):
    peers = len(kv)
    _, _, rows, cut = kv[0].shape
    heads = cut // HD
    strip = rows * peers
    early_count = peers if split else 1

    def kernel(*refs):
        bias_ref = refs[0]
        kv_in, early_in, qg_in = refs[1:1 + peers], refs[1 + peers:1 + 2 * peers], refs[1 + 2 * peers:1 + 3 * peers]
        outs = refs[1 + 3 * peers + len(after):-5]
        own_out, dq_outs, early_outs = outs[0], outs[1:1 + peers], outs[1 + peers:]
        kv_all, qg_all, early, dq_all, sems = refs[-5:]
        s = lax.axis_index("sub")
        moves = []
        for by in range(peers):
            at = lax.rem(s - by + peers, peers)
            moves += [
                (early_in[by], kv_all.at[:, 0:2, at]),
                (kv_in[by], kv_all.at[:, 2:4, at]),
                (qg_in[by], qg_all.at[:, :, at]),
            ]
        run_moves(moves, sems)
        strips = [(head, tile) for head in range(heads) for tile in range(2)]
        products, terms = {}, {}

        def flat(ref, which, tiles, head):
            block = ref[which, tiles, :, :, pl.ds(head * HD, HD)]
            return block.reshape(block.shape[0] * strip, HD)

        def multiply(head, tile):
            at, span = pl.ds(tile, 1), pl.ds(tile, 3)
            q, g = flat(qg_all, 0, at, head), flat(qg_all, 1, at, head)
            k, v = flat(kv_all, 0, span, head), flat(kv_all, 1, span, head)
            scores = lax.dot_general(k, q, ROWS_BY_ROWS, preferred_element_type=WIDE)
            grad_prob = lax.dot_general(v, g, ROWS_BY_ROWS, preferred_element_type=WIDE)
            products[head, tile] = q, g, k, scores, grad_prob

        def finish(head, tile):
            q, g, k, scores, grad_prob = products.pop((head, tile))
            scores = scores * TO_BITS + bias_ref[tile]
            peak = jnp.max(scores, axis=0, keepdims=True)
            weight = jnp.exp2(scores - peak)
            prob = weight * (1.0 / jnp.sum(weight, axis=0, keepdims=True))
            prob_low = prob.astype(LOW)
            row_dot = jnp.sum(prob_low.astype(WIDE) * grad_prob, axis=0, keepdims=True)
            score_low = (prob * (grad_prob - row_dot)).astype(LOW)
            dq = jnp.dot(k.T, score_low, preferred_element_type=WIDE) * SCALE
            dq_all[tile, :, :, pl.ds(head * HD, HD)] = dq.T.astype(LOW).reshape(peers, rows, HD)
            dk = jnp.dot(score_low, q, preferred_element_type=WIDE) * SCALE
            dv = jnp.dot(prob_low, g, preferred_element_type=WIDE)
            terms[head, tile] = dk, dv

        def gather(head):
            for which in range(2):
                low, high = terms[head, 0][which], terms[head, 1][which]
                sums = (
                    low[:strip],
                    low[strip:2 * strip] + high[:strip],
                    low[2 * strip:] + high[strip:2 * strip],
                    high[2 * strip:],
                )
                for tile, total in enumerate(sums):
                    total = total.reshape(peers, rows, HD)
                    if tile < 2:
                        early[which, tile, :, :, pl.ds(head * HD, HD)] = total.astype(LOW)
                    else:
                        own_out[which, tile - 2, :, :, pl.ds(head * HD, HD)] = total

        multiply(*strips[0])
        for at, (head, tile) in enumerate(strips):
            if at + 1 < len(strips):
                multiply(*strips[at + 1])
            finish(head, tile)
            if tile == 1:
                gather(head)
        moves = [] if split else [(early, early_outs[0])]
        for by in range(peers):
            at = lax.rem(s + by, peers)
            moves.append((dq_all.at[:, at], dq_outs[by]))
            if split:
                moves.append((early.at[:, :, at], early_outs[by]))
        run_moves(moves, sems)

    outs = [shape(2, 2, peers, rows, cut, dtype=WIDE)] + [shape(2, rows, cut)] * peers
    outs += [shape(2, 2, rows, cut)] * peers if split else [shape(2, 2, peers, rows, cut)]
    scratch = [
        pltpu.VMEM((2, 4, peers, rows, cut), LOW),
        pltpu.VMEM((2, 2, peers, rows, cut), LOW),
        pltpu.VMEM((2, 2, peers, rows, cut), LOW),
        pltpu.VMEM((2, peers, rows, cut), LOW),
        pltpu.SemaphoreType.DMA((3 * peers,)),
    ]
    flops = heads * 2 * 5 * 2 * strip * 3 * strip * HD
    ins = [bias] + kv + kv_earlier + qg + after
    outs = call(kernel, ins, outs, scratch, "attention_grads", whole=True, flops=flops, room=40 * MIB)
    return outs[0], outs[1:1 + peers], outs[1 + peers:]


def summed(own, later, turns, after):
    _, _, peers, rows, cut = own.shape
    split = len(later) > 1 or later[0].ndim == 4

    def kernel(own_ref, *refs):
        later_refs, outs = refs[:len(later)], refs[len(later) + len(after):]
        s = lax.axis_index("sub")
        for place, (by, out) in enumerate(zip(turns, outs)):
            at = lax.rem(s + by, peers)
            for which in range(2):
                for row in range(2):
                    term = later_refs[place][which, row] if split else later_refs[0][which, row, at]
                    out[which, row] = (own_ref[which, row, at] + term.astype(WIDE)).astype(LOW)

    outs = [shape(2, 2, rows, cut)] * len(turns)
    return call(kernel, [own] + later + after, outs, [], "summed", whole=True)


def rows_for_pair(dq, dkv):
    peers = len(dq)
    _, rows, cut = dq[0].shape

    def kernel(*refs):
        dq_refs, dkv_refs, (send, keep) = refs[:peers], refs[peers:2 * peers], refs[-2:]
        p, s = lax.axis_index("pair"), lax.axis_index("sub")
        for by in range(peers):
            at = lax.rem(s - by + peers, peers)
            for out, row in ((send, 1 - p), (keep, p)):
                out[0, at] = dq_refs[by][row]
                for which in range(2):
                    out[1 + which, at] = dkv_refs[by][which, row]

    outs = [shape(3, peers, rows, cut)] * 2
    return call(kernel, dq + dkv, outs, [], "rows_for_pair", whole=True)


def laid_out(kept, paired, spans):
    _, peers, rows, _ = kept[0].shape
    part = spans[-1][1]
    half = part * peers
    count = len(spans)

    def kernel(*refs):
        keep, rec, outs, sems = refs[:count], refs[count:2 * count], refs[2 * count:-1], refs[-1]
        p = lax.axis_index("pair")
        moves = []
        for mine, theirs, (low, high) in zip(keep, rec, spans):
            for source, side in ((mine, p), (theirs, 1 - p)):
                for at in range(peers):
                    columns = pl.ds(pl.multiple_of(side * half + at * part + low, HD), high - low)
                    moves += [(source.at[which, at], out.at[:, columns]) for which, out in enumerate(outs)]
        run_moves(moves, sems)

    outs = [shape(rows, 2 * half)] * 3
    return call(kernel, kept + paired, outs, [pltpu.SemaphoreType.DMA((6 * count * peers,))], "laid_out")


def allowed_bias(session, rows):
    strip = rows * lax.axis_size("sub")
    block = 2 * strip
    at_block = lax.axis_index("blk")
    window = jnp.concatenate([jnp.zeros((block,), jnp.int32), session])
    sess = lax.dynamic_slice_in_dim(window, at_block * block, 2 * block)
    place = (at_block - 1) * block + jnp.arange(2 * block, dtype=jnp.int32)

    def tile_bias(tile):
        q_at = slice(block + tile * strip, block + (tile + 1) * strip)
        k_at = slice(tile * strip, (tile + 3) * strip)
        k_place, q_place = place[k_at, None], place[None, q_at]
        allowed = (sess[None, q_at] == sess[k_at, None]) & (k_place <= q_place) & (k_place >= 0)
        return jnp.where(allowed, 0.0, NEG_FILL)

    return jnp.stack([tile_bias(0), tile_bias(1)])


def shards(queries, keys, values, out_grad, session):
    peers = lax.axis_size("sub")
    others = list(range(1, peers))
    part = queries.shape[1] // (2 * peers)
    spans, at = [], 0
    for heads in chunks_of(part // HD):
        spans.append((at, at + heads * HD))
        at += heads * HD
    bias = allowed_bias(session, queries.shape[0])
    (kv_send, kv_first), = first_parts([([keys, values], *spans[0])], [])
    rest = [([queries, out_grad], *spans[0])] + [([keys, values, queries, out_grad], *span) for span in spans[1:]]
    rest = first_parts(rest, [kv_first])
    kv_parts = [(kv_first, swapped(kv_send), 0)]
    qg_parts = [(rest[0][1], swapped(rest[0][0]), 0)]
    for send, own in rest[1:]:
        paired = swapped(send)
        kv_parts.append((own, paired, 0))
        qg_parts.append((own, paired, 2))
    count = len(spans)
    kv, qg, kept, paired = [], [], [], []
    kv_turn, own_turn, far_turn = [], [], []
    for index in range(count):
        last = index == count - 1
        sends = head_parts(*kv_parts[index], others, kv_turn)
        kv = [round_sub(value, by) for by, value in zip(others, sends)]
        kv_own = head_parts(*kv_parts[index], [0], own_turn)
        own_earlier = along_blocks(kv_own[0], 1, True)
        sends = head_parts(*qg_parts[index], others, sends if last else kv)
        qg = [round_sub(value, by) for by, value in zip(others, sends)]
        forward = [relayed(value, far_turn if index else [own_earlier]) for value in kv]
        far_earlier = [along_blocks(value, 1, not last) for value in forward]
        kv_turn, own_turn = qg, far_earlier
        qg_all = head_parts(*qg_parts[index], [0], []) + qg
        grads, dq, early = attention_grads(bias, kv_own + kv, [own_earlier] + far_earlier, qg_all, last, [])
        far_turn = [dq[0]]
        dq = [dq[0]] + [round_sub(dq[by], by) for by in others]
        if last:
            later = [along_blocks(value, -1, False) for value in early[1:]]
            dkv = summed(grads, later, others, dq[1:])
            near = along_blocks(relayed(early[0], later), -1, False)
            dkv = summed(grads, [near], [0], []) + [round_sub(value, by) for by, value in zip(others, dkv)]
        else:
            dkv = summed(grads, [along_blocks(early[0], -1, False)], [0] + others, dq[1:])
            dkv = [dkv[0]] + [round_sub(dkv[by], by) for by in others]
        send, keep = rows_for_pair(dq, dkv)
        kept.append(keep)
        paired.append(swapped(send))
    return tuple(laid_out(kept, paired, spans))


def solution(mesh):
    spread = P(("grp", "blk", "pair", "sub"), None)
    return jax.shard_map(
        shards, mesh=mesh, in_specs=(spread,) * 4 + (P("grp"),), out_specs=(spread,) * 3, check_vma=False
    )
```

```python
import math

import jax
import jax.numpy as jnp
from jax import lax
from jax.experimental import pallas as pl
from jax.experimental.pallas import tpu as pltpu
from jax.sharding import PartitionSpec as P

HD = 128
NEG_FILL = -1e30
LOW = jnp.bfloat16
WIDE = jnp.float32
MIB = 1024 * 1024
TO_BITS = HD ** (-0.5) / math.log(2.0)
SCALE = HD ** (-0.5)
ROWS_BY_ROWS = (((1,), (1,)), ((), ()))


def chunks_of(heads):
    return [heads // 2, heads - heads // 2]


def along_blocks(value, by, ring):
    peers = lax.axis_size("blk")
    pairs = [(i, (i + by) % peers) for i in range(peers) if ring or 0 <= i + by < peers]
    return lax.ppermute(value, "blk", pairs)


def round_sub(value, by):
    peers = lax.axis_size("sub")
    return lax.ppermute(value, "sub", [(i, (i + by) % peers) for i in range(peers)])


def swapped(value):
    return lax.ppermute(value, "pair", [(0, 1), (1, 0)])


def run_moves(moves, sems):
    copies = [pltpu.make_async_copy(src, dst, sems.at[at]) for at, (src, dst) in enumerate(moves)]
    for copy in copies:
        copy.start()
    for copy in copies:
        copy.wait()


def call(kernel, ins, outs, scratch, name, whole=False, flops=0, room=8 * MIB):
    spec = pl.BlockSpec(memory_space=pltpu.VMEM if whole else pl.ANY)
    moved = sum(math.prod(a.shape) * a.dtype.itemsize for a in list(ins) + list(outs))
    return list(
        pl.pallas_call(
            kernel,
            out_shape=outs,
            in_specs=[spec] * len(ins),
            out_specs=[spec] * len(outs),
            scratch_shapes=scratch,
            name=name,
            cost_estimate=pl.CostEstimate(flops=flops, bytes_accessed=moved, transcendentals=0),
            compiler_params=pltpu.CompilerParams(vmem_limit_bytes=room),
        )(*ins)
    )


def shape(*dims, dtype=LOW):
    return jax.ShapeDtypeStruct(dims, dtype)


def first_parts(groups, after):
    held, wanted, outs = [], [], []
    for arrays, low, high in groups:
        rows, width = arrays[0].shape
        peers = lax.axis_size("sub")
        half = width // 2
        part = half // peers
        wanted.append((len(held), len(arrays), low, high))
        held += [pltpu.with_memory_space_constraint(array, pltpu.HBM) for array in arrays]
        outs += [pltpu.VMEM((len(arrays), peers, rows, high - low), LOW)] * 2

    def kernel(*refs):
        out_refs, sems = refs[-1 - len(outs):-1], refs[-1]
        p = lax.axis_index("pair")
        moves = []
        for group, (first, count, low, high) in enumerate(wanted):
            for side, out in zip((1 - p, p), out_refs[2 * group:2 * group + 2]):
                for at in range(peers):
                    start = pl.multiple_of(side * half + at * part + low, HD)
                    for i in range(count):
                        moves.append((refs[first + i].at[:, pl.ds(start, high - low)], out.at[i, at]))
        run_moves(moves, sems)

    spec = pl.BlockSpec(memory_space=pl.ANY)
    parts = pl.pallas_call(
        kernel,
        out_shape=outs,
        in_specs=[spec] * (len(held) + len(after)),
        out_specs=[spec] * len(outs),
        scratch_shapes=[pltpu.SemaphoreType.DMA((2 * peers * len(held),))],
        name="first_parts",
        compiler_params=pltpu.CompilerParams(vmem_limit_bytes=8 * MIB),
    )(*held, *after)
    return [(parts[2 * i], parts[2 * i + 1]) for i in range(len(groups))]


def head_parts(own, paired, which, turns, after):
    _, peers, rows, cut = own.shape
    chosen = pl.ds(which, 2)

    def kernel(own_ref, pair_ref, *refs):
        outs, sems = refs[len(after):-1], refs[-1]
        p, s = lax.axis_index("pair"), lax.axis_index("sub")
        moves = []
        for by, out in zip(turns, outs):
            at = lax.rem(s + by, peers)
            moves += [(own_ref.at[chosen, at], out.at[:, p]), (pair_ref.at[chosen, at], out.at[:, 1 - p])]
        run_moves(moves, sems)

    outs = [shape(2, 2, rows, cut)] * len(turns)
    scratch = [pltpu.SemaphoreType.DMA((2 * len(turns),))]
    return call(kernel, [own, paired] + after, outs, scratch, "head_parts")


def relayed(value, after):
    def kernel(value_ref, *refs):
        run_moves([(value_ref, refs[-2])], refs[-1])

    scratch = [pltpu.SemaphoreType.DMA((1,))]
    return call(kernel, [value] + after, [shape(*value.shape)], scratch, "relayed")[0]


def attention_grads(bias, kv, kv_earlier, qg, split, after):
    peers = len(kv)
    _, _, rows, cut = kv[0].shape
    heads = cut // HD
    strip = rows * peers
    early_count = peers if split else 1

    def kernel(*refs):
        bias_ref = refs[0]
        kv_in, early_in, qg_in = refs[1:1 + peers], refs[1 + peers:1 + 2 * peers], refs[1 + 2 * peers:1 + 3 * peers]
        outs = refs[1 + 3 * peers + len(after):-5]
        own_out, dq_outs, early_outs = outs[0], outs[1:1 + peers], outs[1 + peers:]
        kv_all, qg_all, early, dq_all, sems = refs[-5:]
        s = lax.axis_index("sub")
        moves = []
        for by in range(peers):
            at = lax.rem(s - by + peers, peers)
            moves += [
                (early_in[by], kv_all.at[:, 0:2, at]),
                (kv_in[by], kv_all.at[:, 2:4, at]),
                (qg_in[by], qg_all.at[:, :, at]),
            ]
        run_moves(moves, sems)
        strips = [(head, tile) for head in range(heads) for tile in range(2)]
        products, terms = {}, {}

        def flat(ref, which, tiles, head):
            block = ref[which, tiles, :, :, pl.ds(head * HD, HD)]
            return block.reshape(block.shape[0] * strip, HD)

        def multiply(head, tile):
            at, span = pl.ds(tile, 1), pl.ds(tile, 3)
            q, g = flat(qg_all, 0, at, head), flat(qg_all, 1, at, head)
            k, v = flat(kv_all, 0, span, head), flat(kv_all, 1, span, head)
            scores = lax.dot_general(k, q, ROWS_BY_ROWS, preferred_element_type=WIDE)
            grad_prob = lax.dot_general(v, g, ROWS_BY_ROWS, preferred_element_type=WIDE)
            products[head, tile] = q, g, k, scores, grad_prob

        def finish(head, tile):
            q, g, k, scores, grad_prob = products.pop((head, tile))
            scores = scores * TO_BITS + bias_ref[tile]
            peak = jnp.max(scores, axis=0, keepdims=True)
            weight = jnp.exp2(scores - peak)
            prob = weight * (1.0 / jnp.sum(weight, axis=0, keepdims=True))
            prob_low = prob.astype(LOW)
            row_dot = jnp.sum(prob_low.astype(WIDE) * grad_prob, axis=0, keepdims=True)
            score_low = (prob * (grad_prob - row_dot)).astype(LOW)
            dq = jnp.dot(k.T, score_low, preferred_element_type=WIDE) * SCALE
            dq_all[tile, :, :, pl.ds(head * HD, HD)] = dq.T.astype(LOW).reshape(peers, rows, HD)
            dk = jnp.dot(score_low, q, preferred_element_type=WIDE) * SCALE
            dv = jnp.dot(prob_low, g, preferred_element_type=WIDE)
            terms[head, tile] = dk, dv

        def gather(head):
            for which in range(2):
                low, high = terms[head, 0][which], terms[head, 1][which]
                sums = (
                    low[:strip],
                    low[strip:2 * strip] + high[:strip],
                    low[2 * strip:] + high[strip:2 * strip],
                    high[2 * strip:],
                )
                for tile, total in enumerate(sums):
                    total = total.reshape(peers, rows, HD)
                    if tile < 2:
                        early[which, tile, :, :, pl.ds(head * HD, HD)] = total.astype(LOW)
                    else:
                        own_out[which, tile - 2, :, :, pl.ds(head * HD, HD)] = total

        multiply(*strips[0])
        for at, (head, tile) in enumerate(strips):
            if at + 1 < len(strips):
                multiply(*strips[at + 1])
            finish(head, tile)
            if tile == 1:
                gather(head)
        moves = [] if split else [(early, early_outs[0])]
        for by in range(peers):
            at = lax.rem(s + by, peers)
            moves.append((dq_all.at[:, at], dq_outs[by]))
            if split:
                moves.append((early.at[:, :, at], early_outs[by]))
        run_moves(moves, sems)

    outs = [shape(2, 2, peers, rows, cut, dtype=WIDE)] + [shape(2, rows, cut)] * peers
    outs += [shape(2, 2, rows, cut)] * peers if split else [shape(2, 2, peers, rows, cut)]
    scratch = [
        pltpu.VMEM((2, 4, peers, rows, cut), LOW),
        pltpu.VMEM((2, 2, peers, rows, cut), LOW),
        pltpu.VMEM((2, 2, peers, rows, cut), LOW),
        pltpu.VMEM((2, peers, rows, cut), LOW),
        pltpu.SemaphoreType.DMA((3 * peers,)),
    ]
    flops = heads * 2 * 5 * 2 * strip * 3 * strip * HD
    ins = [bias] + kv + kv_earlier + qg + after
    outs = call(kernel, ins, outs, scratch, "attention_grads", whole=True, flops=flops, room=40 * MIB)
    return outs[0], outs[1:1 + peers], outs[1 + peers:]


def summed(own, later, turns, after):
    _, _, peers, rows, cut = own.shape
    split = len(later) > 1 or later[0].ndim == 4

    def kernel(own_ref, *refs):
        later_refs, outs = refs[:len(later)], refs[len(later) + len(after):]
        s = lax.axis_index("sub")
        for place, (by, out) in enumerate(zip(turns, outs)):
            at = lax.rem(s + by, peers)
            for which in range(2):
                for row in range(2):
                    term = later_refs[place][which, row] if split else later_refs[0][which, row, at]
                    out[which, row] = (own_ref[which, row, at] + term.astype(WIDE)).astype(LOW)

    outs = [shape(2, 2, rows, cut)] * len(turns)
    return call(kernel, [own] + later + after, outs, [], "summed", whole=True)


def rows_for_pair(dq, dkv):
    peers = len(dq)
    _, rows, cut = dq[0].shape

    def kernel(*refs):
        dq_refs, dkv_refs, (send, keep) = refs[:peers], refs[peers:2 * peers], refs[-2:]
        p, s = lax.axis_index("pair"), lax.axis_index("sub")
        for by in range(peers):
            at = lax.rem(s - by + peers, peers)
            for out, row in ((send, 1 - p), (keep, p)):
                out[0, at] = dq_refs[by][row]
                for which in range(2):
                    out[1 + which, at] = dkv_refs[by][which, row]

    outs = [shape(3, peers, rows, cut)] * 2
    return call(kernel, dq + dkv, outs, [], "rows_for_pair", whole=True)


def laid_out(kept, paired, spans):
    _, peers, rows, _ = kept[0].shape
    part = spans[-1][1]
    half = part * peers
    count = len(spans)

    def kernel(*refs):
        keep, rec, outs, sems = refs[:count], refs[count:2 * count], refs[2 * count:-1], refs[-1]
        p = lax.axis_index("pair")
        moves = []
        for mine, theirs, (low, high) in zip(keep, rec, spans):
            for source, side in ((mine, p), (theirs, 1 - p)):
                for at in range(peers):
                    columns = pl.ds(pl.multiple_of(side * half + at * part + low, HD), high - low)
                    moves += [(source.at[which, at], out.at[:, columns]) for which, out in enumerate(outs)]
        run_moves(moves, sems)

    outs = [shape(rows, 2 * half)] * 3
    return call(kernel, kept + paired, outs, [pltpu.SemaphoreType.DMA((6 * count * peers,))], "laid_out")


def allowed_bias(session, rows):
    strip = rows * lax.axis_size("sub")
    block = 2 * strip
    at_block = lax.axis_index("blk")
    window = jnp.concatenate([jnp.zeros((block,), jnp.int32), session])
    sess = lax.dynamic_slice_in_dim(window, at_block * block, 2 * block)
    place = (at_block - 1) * block + jnp.arange(2 * block, dtype=jnp.int32)

    def tile_bias(tile):
        q_at = slice(block + tile * strip, block + (tile + 1) * strip)
        k_at = slice(tile * strip, (tile + 3) * strip)
        k_place, q_place = place[k_at, None], place[None, q_at]
        allowed = (sess[None, q_at] == sess[k_at, None]) & (k_place <= q_place) & (k_place >= 0)
        return jnp.where(allowed, 0.0, NEG_FILL)

    return jnp.stack([tile_bias(0), tile_bias(1)])


def shards(queries, keys, values, out_grad, session):
    peers = lax.axis_size("sub")
    others = list(range(1, peers))
    part = queries.shape[1] // (2 * peers)
    spans, at = [], 0
    for heads in chunks_of(part // HD):
        spans.append((at, at + heads * HD))
        at += heads * HD
    bias = allowed_bias(session, queries.shape[0])
    (kv_send, kv_first), = first_parts([([keys, values], *spans[0])], [])
    rest = [([queries, out_grad], *spans[0])] + [([keys, values, queries, out_grad], *span) for span in spans[1:]]
    rest = first_parts(rest, [kv_first])
    kv_parts = [(kv_first, swapped(kv_send), 0)]
    qg_parts = [(rest[0][1], swapped(rest[0][0]), 0)]
    for send, own in rest[1:]:
        paired = swapped(send)
        kv_parts.append((own, paired, 0))
        qg_parts.append((own, paired, 2))
    count = len(spans)
    kv_sends, qg_sends, kv, qg, kv_own, own_earlier = [], [], [], [], [], []
    for index in range(count):
        kv_sends.append(head_parts(*kv_parts[index], others, kv[index - 1] if index else []))
        kv.append([round_sub(value, by) for by, value in zip(others, kv_sends[index])])
        kv_own.append(head_parts(*kv_parts[index], [0], own_earlier[index - 1:index]))
        own_earlier.append(along_blocks(kv_own[index][0], 1, True))
        qg_sends.append(head_parts(*qg_parts[index], others, qg[index - 1] if index else []))
        qg.append([round_sub(value, by) for by, value in zip(others, qg_sends[index])])
    kept, paired = [], []
    for index in range(count):
        last = index == count - 1
        forward = [relayed(value, [first_dq]) if index else value for value in kv[index]]
        earlier = [own_earlier[index]] + [along_blocks(value, 1, not last) for value in forward]
        qg_all = head_parts(*qg_parts[index], [0], []) + qg[index]
        grads, dq, early = attention_grads(bias, kv_own[index] + kv[index], earlier, qg_all, last, [])
        first_dq = dq[0]
        dq = [dq[0]] + [round_sub(dq[by], by) for by in others]
        if last:
            later = [along_blocks(value, -1, False) for value in early[1:]]
            dkv = summed(grads, later, others, dq[1:])
            near = along_blocks(relayed(early[0], dkv), -1, False)
            dkv = summed(grads, [near], [0], []) + [round_sub(value, by) for by, value in zip(others, dkv)]
        else:
            dkv = summed(grads, [along_blocks(early[0], -1, False)], [0] + others, dq[1:])
            dkv = [dkv[0]] + [round_sub(dkv[by], by) for by in others]
        send, keep = rows_for_pair(dq, dkv)
        kept.append(keep)
        paired.append(swapped(send))
    return tuple(laid_out(kept, paired, spans))


def solution(mesh):
    spread = P(("grp", "blk", "pair", "sub"), None)
    return jax.shard_map(
        shards, mesh=mesh, in_specs=(spread,) * 4 + (P("grp"),), out_specs=(spread,) * 3, check_vma=False
    )
```

```python
import math

import jax
import jax.numpy as jnp
from jax import lax
from jax.experimental import pallas as pl
from jax.experimental.pallas import tpu as pltpu
from jax.sharding import PartitionSpec as P

HD = 128
NEG_FILL = -1e30
LOW = jnp.bfloat16
WIDE = jnp.float32
MIB = 1024 * 1024
TO_BITS = HD ** (-0.5) / math.log(2.0)
SCALE = HD ** (-0.5)
ROWS_BY_ROWS = (((1,), (1,)), ((), ()))


def chunks_of(heads):
    return [heads // 2, heads - heads // 2]


def along_blocks(value, by, ring):
    peers = lax.axis_size("blk")
    pairs = [(i, (i + by) % peers) for i in range(peers) if ring or 0 <= i + by < peers]
    return lax.ppermute(value, "blk", pairs)


def round_sub(value, by):
    peers = lax.axis_size("sub")
    return lax.ppermute(value, "sub", [(i, (i + by) % peers) for i in range(peers)])


def swapped(value):
    return lax.ppermute(value, "pair", [(0, 1), (1, 0)])


def run_moves(moves, sems):
    copies = [pltpu.make_async_copy(src, dst, sems.at[at]) for at, (src, dst) in enumerate(moves)]
    for copy in copies:
        copy.start()
    for copy in copies:
        copy.wait()


def call(kernel, ins, outs, scratch, name, whole=False, flops=0, room=8 * MIB):
    spec = pl.BlockSpec(memory_space=pltpu.VMEM if whole else pl.ANY)
    moved = sum(math.prod(a.shape) * a.dtype.itemsize for a in list(ins) + list(outs))
    return list(
        pl.pallas_call(
            kernel,
            out_shape=outs,
            in_specs=[spec] * len(ins),
            out_specs=[spec] * len(outs),
            scratch_shapes=scratch,
            name=name,
            cost_estimate=pl.CostEstimate(flops=flops, bytes_accessed=moved, transcendentals=0),
            compiler_params=pltpu.CompilerParams(vmem_limit_bytes=room),
        )(*ins)
    )


def shape(*dims, dtype=LOW):
    return jax.ShapeDtypeStruct(dims, dtype)


def first_parts(groups, after):
    held, wanted, outs = [], [], []
    for arrays, low, high in groups:
        rows, width = arrays[0].shape
        peers = lax.axis_size("sub")
        half = width // 2
        part = half // peers
        wanted.append((len(held), len(arrays), low, high))
        held += [pltpu.with_memory_space_constraint(array, pltpu.HBM) for array in arrays]
        outs += [pltpu.VMEM((len(arrays), peers, rows, high - low), LOW)] * 2

    def kernel(*refs):
        out_refs, sems = refs[-1 - len(outs):-1], refs[-1]
        p = lax.axis_index("pair")
        moves = []
        for group, (first, count, low, high) in enumerate(wanted):
            for side, out in zip((1 - p, p), out_refs[2 * group:2 * group + 2]):
                for at in range(peers):
                    start = pl.multiple_of(side * half + at * part + low, HD)
                    for i in range(count):
                        moves.append((refs[first + i].at[:, pl.ds(start, high - low)], out.at[i, at]))
        run_moves(moves, sems)

    spec = pl.BlockSpec(memory_space=pl.ANY)
    parts = pl.pallas_call(
        kernel,
        out_shape=outs,
        in_specs=[spec] * (len(held) + len(after)),
        out_specs=[spec] * len(outs),
        scratch_shapes=[pltpu.SemaphoreType.DMA((2 * peers * len(held),))],
        name="first_parts",
        compiler_params=pltpu.CompilerParams(vmem_limit_bytes=8 * MIB),
    )(*held, *after)
    return [(parts[2 * i], parts[2 * i + 1]) for i in range(len(groups))]


def head_parts(own, paired, which, turns, after):
    _, peers, rows, cut = own.shape
    chosen = pl.ds(which, 2)

    def kernel(own_ref, pair_ref, *refs):
        outs, sems = refs[len(after):-1], refs[-1]
        p, s = lax.axis_index("pair"), lax.axis_index("sub")
        moves = []
        for by, out in zip(turns, outs):
            at = lax.rem(s + by, peers)
            moves += [(own_ref.at[chosen, at], out.at[:, p]), (pair_ref.at[chosen, at], out.at[:, 1 - p])]
        run_moves(moves, sems)

    outs = [shape(2, 2, rows, cut)] * len(turns)
    scratch = [pltpu.SemaphoreType.DMA((2 * len(turns),))]
    return call(kernel, [own, paired] + after, outs, scratch, "head_parts")


def near_keys(kv_parts, spans):
    _, _, rows, _ = kv_parts[0][0].shape
    ins = [array for parts in kv_parts for array in parts[:2]]

    def kernel(*refs):
        out, sems = refs[-2:]
        p, s = lax.axis_index("pair"), lax.axis_index("sub")
        moves = []
        for chunk, (low, high) in enumerate(spans):
            which = pl.ds(kv_parts[chunk][2], 2)
            for side, ref in zip((p, 1 - p), refs[2 * chunk:]):
                moves.append((ref.at[which, s], out.at[:, side, :, pl.ds(low, high - low)]))
        run_moves(moves, sems)

    outs = [shape(2, 2, rows, spans[-1][1])]
    scratch = [pltpu.SemaphoreType.DMA((2 * len(spans),))]
    return call(kernel, ins, outs, scratch, "near_keys")[0]


def attention_grads(bias, kv, kv_earlier, qg, split, low):
    peers = len(kv)
    _, _, rows, cut = kv[0].shape
    heads = cut // HD
    strip = rows * peers
    early_count = peers if split else 1

    def kernel(*refs):
        bias_ref = refs[0]
        kv_in, early_in, qg_in = refs[1:1 + peers], refs[1 + peers:1 + 2 * peers], refs[1 + 2 * peers:1 + 3 * peers]
        outs = refs[1 + 3 * peers:-5]
        own_out, dq_outs, early_outs = outs[0], outs[1:1 + peers], outs[1 + peers:]
        kv_all, qg_all, early, dq_all, sems = refs[-5:]
        s = lax.axis_index("sub")
        moves = []
        for by in range(peers):
            at = lax.rem(s - by + peers, peers)
            moves += [
                (early_in[by] if by else early_in[0].at[:, :, :, pl.ds(low, cut)], kv_all.at[:, 0:2, at]),
                (kv_in[by], kv_all.at[:, 2:4, at]),
                (qg_in[by], qg_all.at[:, :, at]),
            ]
        run_moves(moves, sems)
        strips = [(head, tile) for head in range(heads) for tile in range(2)]
        products, terms = {}, {}

        def flat(ref, which, tiles, head):
            block = ref[which, tiles, :, :, pl.ds(head * HD, HD)]
            return block.reshape(block.shape[0] * strip, HD)

        def multiply(head, tile):
            at, span = pl.ds(tile, 1), pl.ds(tile, 3)
            q, g = flat(qg_all, 0, at, head), flat(qg_all, 1, at, head)
            k, v = flat(kv_all, 0, span, head), flat(kv_all, 1, span, head)
            scores = lax.dot_general(k, q, ROWS_BY_ROWS, preferred_element_type=WIDE)
            grad_prob = lax.dot_general(v, g, ROWS_BY_ROWS, preferred_element_type=WIDE)
            products[head, tile] = q, g, k, scores, grad_prob

        def finish(head, tile):
            q, g, k, scores, grad_prob = products.pop((head, tile))
            scores = scores * TO_BITS + bias_ref[tile]
            peak = jnp.max(scores, axis=0, keepdims=True)
            weight = jnp.exp2(scores - peak)
            prob = weight * (1.0 / jnp.sum(weight, axis=0, keepdims=True))
            prob_low = prob.astype(LOW)
            row_dot = jnp.sum(prob_low.astype(WIDE) * grad_prob, axis=0, keepdims=True)
            score_low = (prob * (grad_prob - row_dot)).astype(LOW)
            dq = jnp.dot(k.T, score_low, preferred_element_type=WIDE) * SCALE
            dq_all[tile, :, :, pl.ds(head * HD, HD)] = dq.T.astype(LOW).reshape(peers, rows, HD)
            dk = jnp.dot(score_low, q, preferred_element_type=WIDE) * SCALE
            dv = jnp.dot(prob_low, g, preferred_element_type=WIDE)
            terms[head, tile] = dk, dv

        def gather(head):
            for which in range(2):
                low, high = terms[head, 0][which], terms[head, 1][which]
                sums = (
                    low[:strip],
                    low[strip:2 * strip] + high[:strip],
                    low[2 * strip:] + high[strip:2 * strip],
                    high[2 * strip:],
                )
                for tile, total in enumerate(sums):
                    total = total.reshape(peers, rows, HD)
                    if tile < 2:
                        early[which, tile, :, :, pl.ds(head * HD, HD)] = total.astype(LOW)
                    else:
                        own_out[which, tile - 2, :, :, pl.ds(head * HD, HD)] = total

        multiply(*strips[0])
        for at, (head, tile) in enumerate(strips):
            if at + 1 < len(strips):
                multiply(*strips[at + 1])
            finish(head, tile)
            if tile == 1:
                gather(head)
        moves = [] if split else [(early, early_outs[0])]
        for by in range(peers):
            at = lax.rem(s + by, peers)
            moves.append((dq_all.at[:, at], dq_outs[by]))
            if split:
                moves.append((early.at[:, :, at], early_outs[by]))
        run_moves(moves, sems)

    outs = [shape(2, 2, peers, rows, cut, dtype=WIDE)] + [shape(2, rows, cut)] * peers
    outs += [shape(2, 2, rows, cut)] * peers if split else [shape(2, 2, peers, rows, cut)]
    scratch = [
        pltpu.VMEM((2, 4, peers, rows, cut), LOW),
        pltpu.VMEM((2, 2, peers, rows, cut), LOW),
        pltpu.VMEM((2, 2, peers, rows, cut), LOW),
        pltpu.VMEM((2, peers, rows, cut), LOW),
        pltpu.SemaphoreType.DMA((3 * peers,)),
    ]
    flops = heads * 2 * 5 * 2 * strip * 3 * strip * HD
    ins = [bias] + kv + kv_earlier + qg
    outs = call(kernel, ins, outs, scratch, "attention_grads", whole=True, flops=flops, room=40 * MIB)
    return outs[0], outs[1:1 + peers], outs[1 + peers:]


def summed(own, later, turns, after):
    _, _, peers, rows, cut = own.shape
    split = len(later) > 1 or later[0].ndim == 4

    def kernel(own_ref, *refs):
        later_refs, outs = refs[:len(later)], refs[len(later) + len(after):]
        s = lax.axis_index("sub")
        for place, (by, out) in enumerate(zip(turns, outs)):
            at = lax.rem(s + by, peers)
            for which in range(2):
                for row in range(2):
                    term = later_refs[place][which, row] if split else later_refs[0][which, row, at]
                    out[which, row] = (own_ref[which, row, at] + term.astype(WIDE)).astype(LOW)

    outs = [shape(2, 2, rows, cut)] * len(turns)
    return call(kernel, [own] + later + after, outs, [], "summed", whole=True)


def rows_for_pair(dq, dkv):
    peers = len(dq)
    _, rows, cut = dq[0].shape

    def kernel(*refs):
        dq_refs, dkv_refs, (send, keep) = refs[:peers], refs[peers:2 * peers], refs[-2:]
        p, s = lax.axis_index("pair"), lax.axis_index("sub")
        for by in range(peers):
            at = lax.rem(s - by + peers, peers)
            for out, row in ((send, 1 - p), (keep, p)):
                out[0, at] = dq_refs[by][row]
                for which in range(2):
                    out[1 + which, at] = dkv_refs[by][which, row]

    outs = [shape(3, peers, rows, cut)] * 2
    return call(kernel, dq + dkv, outs, [], "rows_for_pair", whole=True)


def laid_out(kept, paired, spans):
    _, peers, rows, _ = kept[0].shape
    part = spans[-1][1]
    half = part * peers
    count = len(spans)

    def kernel(*refs):
        keep, rec, outs, sems = refs[:count], refs[count:2 * count], refs[2 * count:-1], refs[-1]
        p = lax.axis_index("pair")
        moves = []
        for mine, theirs, (low, high) in zip(keep, rec, spans):
            for source, side in ((mine, p), (theirs, 1 - p)):
                for at in range(peers):
                    columns = pl.ds(pl.multiple_of(side * half + at * part + low, HD), high - low)
                    moves += [(source.at[which, at], out.at[:, columns]) for which, out in enumerate(outs)]
        run_moves(moves, sems)

    outs = [shape(rows, 2 * half)] * 3
    return call(kernel, kept + paired, outs, [pltpu.SemaphoreType.DMA((6 * count * peers,))], "laid_out")


def allowed_bias(session, rows):
    strip = rows * lax.axis_size("sub")
    block = 2 * strip
    at_block = lax.axis_index("blk")
    window = jnp.concatenate([jnp.zeros((block,), jnp.int32), session])
    sess = lax.dynamic_slice_in_dim(window, at_block * block, 2 * block)
    place = (at_block - 1) * block + jnp.arange(2 * block, dtype=jnp.int32)

    def tile_bias(tile):
        q_at = slice(block + tile * strip, block + (tile + 1) * strip)
        k_at = slice(tile * strip, (tile + 3) * strip)
        k_place, q_place = place[k_at, None], place[None, q_at]
        allowed = (sess[None, q_at] == sess[k_at, None]) & (k_place <= q_place) & (k_place >= 0)
        return jnp.where(allowed, 0.0, NEG_FILL)

    return jnp.stack([tile_bias(0), tile_bias(1)])


def shards(queries, keys, values, out_grad, session):
    peers = lax.axis_size("sub")
    others = list(range(1, peers))
    part = queries.shape[1] // (2 * peers)
    spans, at = [], 0
    for heads in chunks_of(part // HD):
        spans.append((at, at + heads * HD))
        at += heads * HD
    bias = allowed_bias(session, queries.shape[0])
    (kv_send, kv_first), = first_parts([([keys, values], *spans[0])], [])
    rest = [([queries, out_grad], *spans[0])] + [([keys, values, queries, out_grad], *span) for span in spans[1:]]
    rest = first_parts(rest, [kv_first])
    kv_parts = [(kv_first, swapped(kv_send), 0)]
    qg_parts = [(rest[0][1], swapped(rest[0][0]), 0)]
    for send, own in rest[1:]:
        paired = swapped(send)
        kv_parts.append((own, paired, 0))
        qg_parts.append((own, paired, 2))
    count = len(spans)
    near = along_blocks(near_keys(kv_parts, spans), 1, True)
    kv, qg = [], []
    for index in range(count):
        sends = head_parts(*kv_parts[index], others, kv[index - 2] if index > 1 else [])
        kv.append([round_sub(value, by) for by, value in zip(others, sends)])
    for index in range(count):
        sends = head_parts(*qg_parts[index], others, kv[index])
        qg.append([round_sub(value, by) for by, value in zip(others, sends)])
    kept, paired, sums = [], [], []
    for index in range(count):
        last = index == count - 1
        earlier = [near] + [along_blocks(value, 1, True) for value in kv[index]]
        kv_all = head_parts(*kv_parts[index], [0], []) + kv[index]
        qg_all = head_parts(*qg_parts[index], [0], []) + qg[index]
        grads, dq, early = attention_grads(bias, kv_all, earlier, qg_all, last, spans[index][0])
        dq = [dq[0]] + [round_sub(dq[by], by) for by in others]
        later = [along_blocks(value, -1, False) for value in early]
        if last:
            dkv = summed(grads, later[1:], others, dq[1:] + sums)
            dkv = summed(grads, later[:1], [0], dkv[:1]) + [round_sub(value, by) for by, value in zip(others, dkv)]
        else:
            dkv = summed(grads, later, [0] + others, dq[1:])
            sums = dkv[:1]
            dkv = [dkv[0]] + [round_sub(dkv[by], by) for by in others]
        send, keep = rows_for_pair(dq, dkv)
        kept.append(keep)
        paired.append(swapped(send))
    return tuple(laid_out(kept, paired, spans))


def solution(mesh):
    spread = P(("grp", "blk", "pair", "sub"), None)
    return jax.shard_map(
        shards, mesh=mesh, in_specs=(spread,) * 4 + (P("grp"),), out_specs=(spread,) * 3, check_vma=False
    )
```

```python
import math

import jax
import jax.numpy as jnp
from jax import lax
from jax.experimental import pallas as pl
from jax.experimental.pallas import tpu as pltpu
from jax.sharding import PartitionSpec as P

HD = 128
NEG_FILL = -1e30
LOW = jnp.bfloat16
WIDE = jnp.float32
MIB = 1024 * 1024
TO_BITS = HD ** (-0.5) / math.log(2.0)
SCALE = HD ** (-0.5)
ROWS_BY_ROWS = (((1,), (1,)), ((), ()))


def chunks_of(heads):
    return [heads // 2, heads - heads // 2]


def along_blocks(value, by, ring):
    peers = lax.axis_size("blk")
    pairs = [(i, (i + by) % peers) for i in range(peers) if ring or 0 <= i + by < peers]
    return lax.ppermute(value, "blk", pairs)


def round_sub(value, by):
    peers = lax.axis_size("sub")
    return lax.ppermute(value, "sub", [(i, (i + by) % peers) for i in range(peers)])


def swapped(value):
    return lax.ppermute(value, "pair", [(0, 1), (1, 0)])


def run_moves(moves, sems):
    copies = [pltpu.make_async_copy(src, dst, sems.at[at]) for at, (src, dst) in enumerate(moves)]
    for copy in copies:
        copy.start()
    for copy in copies:
        copy.wait()


def call(kernel, ins, outs, scratch, name, whole=False, flops=0, room=8 * MIB):
    spec = pl.BlockSpec(memory_space=pltpu.VMEM if whole else pl.ANY)
    moved = sum(math.prod(a.shape) * a.dtype.itemsize for a in list(ins) + list(outs))
    return list(
        pl.pallas_call(
            kernel,
            out_shape=outs,
            in_specs=[spec] * len(ins),
            out_specs=[spec] * len(outs),
            scratch_shapes=scratch,
            name=name,
            cost_estimate=pl.CostEstimate(flops=flops, bytes_accessed=moved, transcendentals=0),
            compiler_params=pltpu.CompilerParams(vmem_limit_bytes=room),
        )(*ins)
    )


def shape(*dims, dtype=LOW):
    return jax.ShapeDtypeStruct(dims, dtype)


def first_parts(groups, after):
    held, wanted, outs = [], [], []
    for arrays, low, high in groups:
        rows, width = arrays[0].shape
        peers = lax.axis_size("sub")
        half = width // 2
        part = half // peers
        wanted.append((len(held), len(arrays), low, high))
        held += [pltpu.with_memory_space_constraint(array, pltpu.HBM) for array in arrays]
        outs += [pltpu.VMEM((len(arrays), peers, rows, high - low), LOW)] * 2

    def kernel(*refs):
        out_refs, sems = refs[-1 - len(outs):-1], refs[-1]
        p = lax.axis_index("pair")
        moves = []
        for group, (first, count, low, high) in enumerate(wanted):
            for side, out in zip((1 - p, p), out_refs[2 * group:2 * group + 2]):
                for at in range(peers):
                    start = pl.multiple_of(side * half + at * part + low, HD)
                    for i in range(count):
                        moves.append((refs[first + i].at[:, pl.ds(start, high - low)], out.at[i, at]))
        run_moves(moves, sems)

    spec = pl.BlockSpec(memory_space=pl.ANY)
    parts = pl.pallas_call(
        kernel,
        out_shape=outs,
        in_specs=[spec] * (len(held) + len(after)),
        out_specs=[spec] * len(outs),
        scratch_shapes=[pltpu.SemaphoreType.DMA((2 * peers * len(held),))],
        name="first_parts",
        compiler_params=pltpu.CompilerParams(vmem_limit_bytes=8 * MIB),
    )(*held, *after)
    return [(parts[2 * i], parts[2 * i + 1]) for i in range(len(groups))]


def head_parts(own, paired, which, turns, after):
    _, peers, rows, cut = own.shape
    chosen = pl.ds(which, 2)

    def kernel(own_ref, pair_ref, *refs):
        outs, sems = refs[len(after):-1], refs[-1]
        p, s = lax.axis_index("pair"), lax.axis_index("sub")
        moves = []
        for by, out in zip(turns, outs):
            at = lax.rem(s + by, peers)
            moves += [(own_ref.at[chosen, at], out.at[:, p]), (pair_ref.at[chosen, at], out.at[:, 1 - p])]
        run_moves(moves, sems)

    outs = [shape(2, 2, rows, cut)] * len(turns)
    scratch = [pltpu.SemaphoreType.DMA((2 * len(turns),))]
    return call(kernel, [own, paired] + after, outs, scratch, "head_parts")


def relayed(value, after):
    def kernel(value_ref, *refs):
        run_moves([(value_ref, refs[-2])], refs[-1])

    scratch = [pltpu.SemaphoreType.DMA((1,))]
    return call(kernel, [value] + after, [shape(*value.shape)], scratch, "relayed")[0]


def attention_grads(bias, kv, kv_earlier, qg, split, after):
    peers = len(kv)
    _, _, rows, cut = kv[0].shape
    heads = cut // HD
    strip = rows * peers
    early_count = peers if split else 1

    def kernel(*refs):
        bias_ref = refs[0]
        kv_in, early_in, qg_in = refs[1:1 + peers], refs[1 + peers:1 + 2 * peers], refs[1 + 2 * peers:1 + 3 * peers]
        outs = refs[1 + 3 * peers + len(after):-5]
        own_out, dq_outs, early_outs = outs[0], outs[1:1 + peers], outs[1 + peers:]
        kv_all, qg_all, early, dq_all, sems = refs[-5:]
        s = lax.axis_index("sub")
        moves = []
        for by in range(peers):
            at = lax.rem(s - by + peers, peers)
            moves += [
                (early_in[by], kv_all.at[:, 0:2, at]),
                (kv_in[by], kv_all.at[:, 2:4, at]),
                (qg_in[by], qg_all.at[:, :, at]),
            ]
        run_moves(moves, sems)
        strips = [(head, tile) for head in range(heads) for tile in range(2)]
        products, terms = {}, {}

        def flat(ref, which, tiles, head):
            block = ref[which, tiles, :, :, pl.ds(head * HD, HD)]
            return block.reshape(block.shape[0] * strip, HD)

        def multiply(head, tile):
            at, span = pl.ds(tile, 1), pl.ds(tile, 3)
            q, g = flat(qg_all, 0, at, head), flat(qg_all, 1, at, head)
            k, v = flat(kv_all, 0, span, head), flat(kv_all, 1, span, head)
            scores = lax.dot_general(k, q, ROWS_BY_ROWS, preferred_element_type=WIDE)
            grad_prob = lax.dot_general(v, g, ROWS_BY_ROWS, preferred_element_type=WIDE)
            products[head, tile] = q, g, k, scores, grad_prob

        def finish(head, tile):
            q, g, k, scores, grad_prob = products.pop((head, tile))
            scores = scores * TO_BITS + bias_ref[tile]
            peak = jnp.max(scores, axis=0, keepdims=True)
            weight = jnp.exp2(scores - peak)
            prob = weight * (1.0 / jnp.sum(weight, axis=0, keepdims=True))
            prob_low = prob.astype(LOW)
            row_dot = jnp.sum(prob_low.astype(WIDE) * grad_prob, axis=0, keepdims=True)
            score_low = (prob * (grad_prob - row_dot)).astype(LOW)
            dq = jnp.dot(k.T, score_low, preferred_element_type=WIDE) * SCALE
            dq_all[tile, :, :, pl.ds(head * HD, HD)] = dq.T.astype(LOW).reshape(peers, rows, HD)
            dk = jnp.dot(score_low, q, preferred_element_type=WIDE) * SCALE
            dv = jnp.dot(prob_low, g, preferred_element_type=WIDE)
            terms[head, tile] = dk, dv

        def gather(head):
            for which in range(2):
                low, high = terms[head, 0][which], terms[head, 1][which]
                sums = (
                    low[:strip],
                    low[strip:2 * strip] + high[:strip],
                    low[2 * strip:] + high[strip:2 * strip],
                    high[2 * strip:],
                )
                for tile, total in enumerate(sums):
                    total = total.reshape(peers, rows, HD)
                    if tile < 2:
                        early[which, tile, :, :, pl.ds(head * HD, HD)] = total.astype(LOW)
                    else:
                        own_out[which, tile - 2, :, :, pl.ds(head * HD, HD)] = total

        multiply(*strips[0])
        for at, (head, tile) in enumerate(strips):
            if at + 1 < len(strips):
                multiply(*strips[at + 1])
            finish(head, tile)
            if tile == 1:
                gather(head)
        moves = [] if split else [(early, early_outs[0])]
        for by in range(peers):
            at = lax.rem(s + by, peers)
            moves.append((dq_all.at[:, at], dq_outs[by]))
            if split:
                moves.append((early.at[:, :, at], early_outs[by]))
        run_moves(moves, sems)

    outs = [shape(2, 2, peers, rows, cut, dtype=WIDE)] + [shape(2, rows, cut)] * peers
    outs += [shape(2, 2, rows, cut)] * peers if split else [shape(2, 2, peers, rows, cut)]
    scratch = [
        pltpu.VMEM((2, 4, peers, rows, cut), LOW),
        pltpu.VMEM((2, 2, peers, rows, cut), LOW),
        pltpu.VMEM((2, 2, peers, rows, cut), LOW),
        pltpu.VMEM((2, peers, rows, cut), LOW),
        pltpu.SemaphoreType.DMA((3 * peers,)),
    ]
    flops = heads * 2 * 5 * 2 * strip * 3 * strip * HD
    ins = [bias] + kv + kv_earlier + qg + after
    outs = call(kernel, ins, outs, scratch, "attention_grads", whole=True, flops=flops, room=40 * MIB)
    return outs[0], outs[1:1 + peers], outs[1 + peers:]


def summed(own, later, turns, after):
    _, _, peers, rows, cut = own.shape
    split = len(later) > 1 or later[0].ndim == 4

    def kernel(own_ref, *refs):
        later_refs, outs = refs[:len(later)], refs[len(later) + len(after):]
        s = lax.axis_index("sub")
        for place, (by, out) in enumerate(zip(turns, outs)):
            at = lax.rem(s + by, peers)
            for which in range(2):
                for row in range(2):
                    term = later_refs[place][which, row] if split else later_refs[0][which, row, at]
                    out[which, row] = (own_ref[which, row, at] + term.astype(WIDE)).astype(LOW)

    outs = [shape(2, 2, rows, cut)] * len(turns)
    return call(kernel, [own] + later + after, outs, [], "summed", whole=True)


def rows_for_pair(dq, dkv):
    peers = len(dq)
    _, rows, cut = dq[0].shape

    def kernel(*refs):
        dq_refs, dkv_refs, (send, keep) = refs[:peers], refs[peers:2 * peers], refs[-2:]
        p, s = lax.axis_index("pair"), lax.axis_index("sub")
        for by in range(peers):
            at = lax.rem(s - by + peers, peers)
            for out, row in ((send, 1 - p), (keep, p)):
                out[0, at] = dq_refs[by][row]
                for which in range(2):
                    out[1 + which, at] = dkv_refs[by][which, row]

    outs = [shape(3, peers, rows, cut)] * 2
    return call(kernel, dq + dkv, outs, [], "rows_for_pair", whole=True)


def laid_out(kept, paired, spans):
    _, peers, rows, _ = kept[0].shape
    part = spans[-1][1]
    half = part * peers
    count = len(spans)

    def kernel(*refs):
        keep, rec, outs, sems = refs[:count], refs[count:2 * count], refs[2 * count:-1], refs[-1]
        p = lax.axis_index("pair")
        moves = []
        for mine, theirs, (low, high) in zip(keep, rec, spans):
            for source, side in ((mine, p), (theirs, 1 - p)):
                for at in range(peers):
                    columns = pl.ds(pl.multiple_of(side * half + at * part + low, HD), high - low)
                    moves += [(source.at[which, at], out.at[:, columns]) for which, out in enumerate(outs)]
        run_moves(moves, sems)

    outs = [shape(rows, 2 * half)] * 3
    return call(kernel, kept + paired, outs, [pltpu.SemaphoreType.DMA((6 * count * peers,))], "laid_out")


def allowed_bias(session, rows):
    strip = rows * lax.axis_size("sub")
    block = 2 * strip
    at_block = lax.axis_index("blk")
    window = jnp.concatenate([jnp.zeros((block,), jnp.int32), session])
    sess = lax.dynamic_slice_in_dim(window, at_block * block, 2 * block)
    place = (at_block - 1) * block + jnp.arange(2 * block, dtype=jnp.int32)

    def tile_bias(tile):
        q_at = slice(block + tile * strip, block + (tile + 1) * strip)
        k_at = slice(tile * strip, (tile + 3) * strip)
        k_place, q_place = place[k_at, None], place[None, q_at]
        allowed = (sess[None, q_at] == sess[k_at, None]) & (k_place <= q_place) & (k_place >= 0)
        return jnp.where(allowed, 0.0, NEG_FILL)

    return jnp.stack([tile_bias(0), tile_bias(1)])


def shards(queries, keys, values, out_grad, session):
    peers = lax.axis_size("sub")
    others = list(range(1, peers))
    part = queries.shape[1] // (2 * peers)
    spans, at = [], 0
    for heads in chunks_of(part // HD):
        spans.append((at, at + heads * HD))
        at += heads * HD
    bias = allowed_bias(session, queries.shape[0])
    (kv_send, kv_first), = first_parts([([keys, values], *spans[0])], [])
    rest = [([queries, out_grad], *spans[0])] + [([keys, values, queries, out_grad], *span) for span in spans[1:]]
    rest = first_parts(rest, [kv_first])
    kv_parts = [(kv_first, swapped(kv_send), 0)]
    qg_parts = [(rest[0][1], swapped(rest[0][0]), 0)]
    for send, own in rest[1:]:
        paired = swapped(send)
        kv_parts.append((own, paired, 0))
        qg_parts.append((own, paired, 2))
    count = len(spans)
    kv_sends, qg_sends, kv, qg, kv_own, own_earlier = [], [], [], [], [], []
    for index in range(count):
        kv_sends.append(head_parts(*kv_parts[index], others, kv[index - 1] if index else []))
        kv.append([round_sub(value, by) for by, value in zip(others, kv_sends[index])])
        kv_own.append(head_parts(*kv_parts[index], [0], own_earlier[index - 1:index]))
        own_earlier.append(along_blocks(kv_own[index][0], 1, True))
        qg_sends.append(head_parts(*qg_parts[index], others, qg[index - 1] if index else []))
        qg.append([round_sub(value, by) for by, value in zip(others, qg_sends[index])])
    kept, paired = [], []
    for index in range(count):
        last = index == count - 1
        forward = [relayed(value, [first_dq]) if index else value for value in kv[index]]
        earlier = [own_earlier[index]] + [along_blocks(value, 1, not last) for value in forward]
        qg_all = head_parts(*qg_parts[index], [0], []) + qg[index]
        grads, dq, early = attention_grads(bias, kv_own[index] + kv[index], earlier, qg_all, last, [])
        first_dq = dq[0]
        dq = [dq[0]] + [round_sub(dq[by], by) for by in others]
        if last:
            later = [along_blocks(value, -1, True) for value in early[1:]]
            dkv = summed(grads, later, others, dq[1:])
            near = along_blocks(relayed(early[0], dkv), -1, True)
            dkv = summed(grads, [near], [0], []) + [round_sub(value, by) for by, value in zip(others, dkv)]
        else:
            dkv = summed(grads, [along_blocks(early[0], -1, False)], [0] + others, dq[1:])
            dkv = [dkv[0]] + [round_sub(dkv[by], by) for by in others]
        send, keep = rows_for_pair(dq, dkv)
        kept.append(keep)
        paired.append(swapped(send))
    return tuple(laid_out(kept, paired, spans))


def solution(mesh):
    spread = P(("grp", "blk", "pair", "sub"), None)
    return jax.shard_map(
        shards, mesh=mesh, in_specs=(spread,) * 4 + (P("grp"),), out_specs=(spread,) * 3, check_vma=False
    )
```

```python
import math

import jax
import jax.numpy as jnp
from jax import lax
from jax.experimental import pallas as pl
from jax.experimental.pallas import tpu as pltpu
from jax.sharding import PartitionSpec as P

HD = 128
NEG_FILL = -1e30
LOW = jnp.bfloat16
WIDE = jnp.float32
MIB = 1024 * 1024
TO_BITS = HD ** (-0.5) / math.log(2.0)
SCALE = HD ** (-0.5)
ROWS_BY_ROWS = (((1,), (1,)), ((), ()))


def chunks_of(heads):
    return [heads // 2, heads - heads // 2]


def along_blocks(value, by, ring):
    peers = lax.axis_size("blk")
    pairs = [(i, (i + by) % peers) for i in range(peers) if ring or 0 <= i + by < peers]
    return lax.ppermute(value, "blk", pairs)


def round_sub(value, by):
    peers = lax.axis_size("sub")
    return lax.ppermute(value, "sub", [(i, (i + by) % peers) for i in range(peers)])


def swapped(value):
    return lax.ppermute(value, "pair", [(0, 1), (1, 0)])


def run_moves(moves, sems):
    copies = [pltpu.make_async_copy(src, dst, sems.at[at]) for at, (src, dst) in enumerate(moves)]
    for copy in copies:
        copy.start()
    for copy in copies:
        copy.wait()


def call(kernel, ins, outs, scratch, name, whole=False, flops=0, room=8 * MIB):
    spec = pl.BlockSpec(memory_space=pltpu.VMEM if whole else pl.ANY)
    moved = sum(math.prod(a.shape) * a.dtype.itemsize for a in list(ins) + list(outs))
    return list(
        pl.pallas_call(
            kernel,
            out_shape=outs,
            in_specs=[spec] * len(ins),
            out_specs=[spec] * len(outs),
            scratch_shapes=scratch,
            name=name,
            cost_estimate=pl.CostEstimate(flops=flops, bytes_accessed=moved, transcendentals=0),
            compiler_params=pltpu.CompilerParams(vmem_limit_bytes=room),
        )(*ins)
    )


def shape(*dims, dtype=LOW):
    return jax.ShapeDtypeStruct(dims, dtype)


def first_parts(groups, after):
    held, wanted, outs = [], [], []
    for arrays, low, high in groups:
        rows, width = arrays[0].shape
        peers = lax.axis_size("sub")
        half = width // 2
        part = half // peers
        wanted.append((len(held), len(arrays), low, high))
        held += [pltpu.with_memory_space_constraint(array, pltpu.HBM) for array in arrays]
        outs += [pltpu.VMEM((len(arrays), peers, rows, high - low), LOW)] * 2

    def kernel(*refs):
        out_refs, sems = refs[-1 - len(outs):-1], refs[-1]
        p = lax.axis_index("pair")
        moves = []
        for group, (first, count, low, high) in enumerate(wanted):
            for side, out in zip((1 - p, p), out_refs[2 * group:2 * group + 2]):
                for at in range(peers):
                    start = pl.multiple_of(side * half + at * part + low, HD)
                    for i in range(count):
                        moves.append((refs[first + i].at[:, pl.ds(start, high - low)], out.at[i, at]))
        run_moves(moves, sems)

    spec = pl.BlockSpec(memory_space=pl.ANY)
    parts = pl.pallas_call(
        kernel,
        out_shape=outs,
        in_specs=[spec] * (len(held) + len(after)),
        out_specs=[spec] * len(outs),
        scratch_shapes=[pltpu.SemaphoreType.DMA((2 * peers * len(held),))],
        name="first_parts",
        compiler_params=pltpu.CompilerParams(vmem_limit_bytes=8 * MIB),
    )(*held, *after)
    return [(parts[2 * i], parts[2 * i + 1]) for i in range(len(groups))]


def first_keys(arrays, low, high):
    rows, width = arrays[0].shape
    half = width // 2
    peers = lax.axis_size("sub")
    part = half // peers
    cut = high - low

    def kernel(*refs):
        ins, far, (send, keep), sems = refs[:2], refs[2:1 + peers], refs[1 + peers:-1], refs[-1]
        p, s = lax.axis_index("pair"), lax.axis_index("sub")
        moves = []
        for i, ref in enumerate(ins):
            for by in range(1, peers):
                for side in range(2):
                    start = pl.multiple_of(side * half + lax.rem(s + by, peers) * part + low, HD)
                    moves.append((ref.at[:, pl.ds(start, cut)], far[by - 1].at[i, side]))
            for out, side in ((send, 1 - p), (keep, p)):
                start = pl.multiple_of(side * half + s * part + low, HD)
                moves.append((ref.at[:, pl.ds(start, cut)], out.at[i]))
        run_moves(moves, sems)

    spec = pl.BlockSpec(memory_space=pl.ANY)
    outs = [pltpu.VMEM((2, 2, rows, cut), LOW)] * (peers - 1) + [pltpu.VMEM((2, rows, cut), LOW)] * 2
    parts = pl.pallas_call(
        kernel,
        out_shape=outs,
        in_specs=[spec] * 2,
        out_specs=[spec] * len(outs),
        scratch_shapes=[pltpu.SemaphoreType.DMA((4 * peers,))],
        name="first_keys",
        compiler_params=pltpu.CompilerParams(vmem_limit_bytes=8 * MIB),
    )(*[pltpu.with_memory_space_constraint(array, pltpu.HBM) for array in arrays])
    return list(parts[:-2]), parts[-2], parts[-1]


def other_side(received):
    count = len(received)

    def kernel(*refs):
        p = lax.axis_index("pair")
        run_moves([(ref.at[:, 1 - p], refs[-2].at[by]) for by, ref in enumerate(refs[:count])], refs[-1])

    _, _, rows, cut = received[0].shape
    scratch = [pltpu.SemaphoreType.DMA((count,))]
    return call(kernel, received, [shape(count, 2, rows, cut)], scratch, "other_side")[0]


def both_rows(mine, theirs):
    count = len(mine)
    _, _, rows, cut = theirs.shape

    def kernel(*refs):
        ins, theirs_ref, outs, sems = refs[:count], refs[count], refs[count + 1:-1], refs[-1]
        p = lax.axis_index("pair")
        moves = []
        for by, (ref, out) in enumerate(zip(ins, outs)):
            source = ref.at[:, p] if len(ref.shape) == 4 else ref
            moves += [(source, out.at[:, p]), (theirs_ref.at[by], out.at[:, 1 - p])]
        run_moves(moves, sems)

    outs = [shape(2, 2, rows, cut)] * count
    scratch = [pltpu.SemaphoreType.DMA((2 * count,))]
    return call(kernel, mine + [theirs], outs, scratch, "both_rows")


def head_parts(own, paired, which, turns, after):
    _, peers, rows, cut = own.shape
    chosen = pl.ds(which, 2)

    def kernel(own_ref, pair_ref, *refs):
        outs, sems = refs[len(after):-1], refs[-1]
        p, s = lax.axis_index("pair"), lax.axis_index("sub")
        moves = []
        for by, out in zip(turns, outs):
            at = lax.rem(s + by, peers)
            moves += [(own_ref.at[chosen, at], out.at[:, p]), (pair_ref.at[chosen, at], out.at[:, 1 - p])]
        run_moves(moves, sems)

    outs = [shape(2, 2, rows, cut)] * len(turns)
    scratch = [pltpu.SemaphoreType.DMA((2 * len(turns),))]
    return call(kernel, [own, paired] + after, outs, scratch, "head_parts")


def relayed(value, after):
    def kernel(value_ref, *refs):
        run_moves([(value_ref, refs[-2])], refs[-1])

    scratch = [pltpu.SemaphoreType.DMA((1,))]
    return call(kernel, [value] + after, [shape(*value.shape)], scratch, "relayed")[0]


def attention_grads(bias, kv, kv_earlier, qg, split, after):
    peers = len(kv)
    _, _, rows, cut = kv[0].shape
    heads = cut // HD
    strip = rows * peers
    early_count = peers if split else 1

    def kernel(*refs):
        bias_ref = refs[0]
        kv_in, early_in, qg_in = refs[1:1 + peers], refs[1 + peers:1 + 2 * peers], refs[1 + 2 * peers:1 + 3 * peers]
        outs = refs[1 + 3 * peers + len(after):-5]
        own_out, dq_outs, early_outs = outs[0], outs[1:1 + peers], outs[1 + peers:]
        kv_all, qg_all, early, dq_all, sems = refs[-5:]
        s = lax.axis_index("sub")
        moves = []
        for by in range(peers):
            at = lax.rem(s - by + peers, peers)
            moves += [
                (early_in[by], kv_all.at[:, 0:2, at]),
                (kv_in[by], kv_all.at[:, 2:4, at]),
                (qg_in[by], qg_all.at[:, :, at]),
            ]
        run_moves(moves, sems)
        strips = [(head, tile) for head in range(heads) for tile in range(2)]
        products, terms = {}, {}

        def flat(ref, which, tiles, head):
            block = ref[which, tiles, :, :, pl.ds(head * HD, HD)]
            return block.reshape(block.shape[0] * strip, HD)

        def multiply(head, tile):
            at, span = pl.ds(tile, 1), pl.ds(tile, 3)
            q, g = flat(qg_all, 0, at, head), flat(qg_all, 1, at, head)
            k, v = flat(kv_all, 0, span, head), flat(kv_all, 1, span, head)
            scores = lax.dot_general(k, q, ROWS_BY_ROWS, preferred_element_type=WIDE)
            grad_prob = lax.dot_general(v, g, ROWS_BY_ROWS, preferred_element_type=WIDE)
            products[head, tile] = q, g, k, scores, grad_prob

        def finish(head, tile):
            q, g, k, scores, grad_prob = products.pop((head, tile))
            scores = scores * TO_BITS + bias_ref[tile]
            peak = jnp.max(scores, axis=0, keepdims=True)
            weight = jnp.exp2(scores - peak)
            prob = weight * (1.0 / jnp.sum(weight, axis=0, keepdims=True))
            prob_low = prob.astype(LOW)
            row_dot = jnp.sum(prob_low.astype(WIDE) * grad_prob, axis=0, keepdims=True)
            score_low = (prob * (grad_prob - row_dot)).astype(LOW)
            dq = jnp.dot(k.T, score_low, preferred_element_type=WIDE) * SCALE
            dq_all[tile, :, :, pl.ds(head * HD, HD)] = dq.T.astype(LOW).reshape(peers, rows, HD)
            dk = jnp.dot(score_low, q, preferred_element_type=WIDE) * SCALE
            dv = jnp.dot(prob_low, g, preferred_element_type=WIDE)
            terms[head, tile] = dk, dv

        def gather(head):
            for which in range(2):
                low, high = terms[head, 0][which], terms[head, 1][which]
                sums = (
                    low[:strip],
                    low[strip:2 * strip] + high[:strip],
                    low[2 * strip:] + high[strip:2 * strip],
                    high[2 * strip:],
                )
                for tile, total in enumerate(sums):
                    total = total.reshape(peers, rows, HD)
                    if tile < 2:
                        early[which, tile, :, :, pl.ds(head * HD, HD)] = total.astype(LOW)
                    else:
                        own_out[which, tile - 2, :, :, pl.ds(head * HD, HD)] = total

        multiply(*strips[0])
        for at, (head, tile) in enumerate(strips):
            if at + 1 < len(strips):
                multiply(*strips[at + 1])
            finish(head, tile)
            if tile == 1:
                gather(head)
        moves = [] if split else [(early, early_outs[0])]
        for by in range(peers):
            at = lax.rem(s + by, peers)
            moves.append((dq_all.at[:, at], dq_outs[by]))
            if split:
                moves.append((early.at[:, :, at], early_outs[by]))
        run_moves(moves, sems)

    outs = [shape(2, 2, peers, rows, cut, dtype=WIDE)] + [shape(2, rows, cut)] * peers
    outs += [shape(2, 2, rows, cut)] * peers if split else [shape(2, 2, peers, rows, cut)]
    scratch = [
        pltpu.VMEM((2, 4, peers, rows, cut), LOW),
        pltpu.VMEM((2, 2, peers, rows, cut), LOW),
        pltpu.VMEM((2, 2, peers, rows, cut), LOW),
        pltpu.VMEM((2, peers, rows, cut), LOW),
        pltpu.SemaphoreType.DMA((3 * peers,)),
    ]
    flops = heads * 2 * 5 * 2 * strip * 3 * strip * HD
    ins = [bias] + kv + kv_earlier + qg + after
    outs = call(kernel, ins, outs, scratch, "attention_grads", whole=True, flops=flops, room=40 * MIB)
    return outs[0], outs[1:1 + peers], outs[1 + peers:]


def summed(own, later, turns, after):
    _, _, peers, rows, cut = own.shape
    split = len(later) > 1 or later[0].ndim == 4

    def kernel(own_ref, *refs):
        later_refs, outs = refs[:len(later)], refs[len(later) + len(after):]
        s = lax.axis_index("sub")
        for place, (by, out) in enumerate(zip(turns, outs)):
            at = lax.rem(s + by, peers)
            for which in range(2):
                for row in range(2):
                    term = later_refs[place][which, row] if split else later_refs[0][which, row, at]
                    out[which, row] = (own_ref[which, row, at] + term.astype(WIDE)).astype(LOW)

    outs = [shape(2, 2, rows, cut)] * len(turns)
    return call(kernel, [own] + later + after, outs, [], "summed", whole=True)


def rows_for_pair(dq, dkv):
    peers = len(dq)
    _, rows, cut = dq[0].shape

    def kernel(*refs):
        dq_refs, dkv_refs, (send, keep) = refs[:peers], refs[peers:2 * peers], refs[-2:]
        p, s = lax.axis_index("pair"), lax.axis_index("sub")
        for by in range(peers):
            at = lax.rem(s - by + peers, peers)
            for out, row in ((send, 1 - p), (keep, p)):
                out[0, at] = dq_refs[by][row]
                for which in range(2):
                    out[1 + which, at] = dkv_refs[by][which, row]

    outs = [shape(3, peers, rows, cut)] * 2
    return call(kernel, dq + dkv, outs, [], "rows_for_pair", whole=True)


def laid_out(kept, paired, spans):
    _, peers, rows, _ = kept[0].shape
    part = spans[-1][1]
    half = part * peers
    count = len(spans)

    def kernel(*refs):
        keep, rec, outs, sems = refs[:count], refs[count:2 * count], refs[2 * count:-1], refs[-1]
        p = lax.axis_index("pair")
        moves = []
        for mine, theirs, (low, high) in zip(keep, rec, spans):
            for source, side in ((mine, p), (theirs, 1 - p)):
                for at in range(peers):
                    columns = pl.ds(pl.multiple_of(side * half + at * part + low, HD), high - low)
                    moves += [(source.at[which, at], out.at[:, columns]) for which, out in enumerate(outs)]
        run_moves(moves, sems)

    outs = [shape(rows, 2 * half)] * 3
    return call(kernel, kept + paired, outs, [pltpu.SemaphoreType.DMA((6 * count * peers,))], "laid_out")


def allowed_bias(session, rows):
    strip = rows * lax.axis_size("sub")
    block = 2 * strip
    at_block = lax.axis_index("blk")
    window = jnp.concatenate([jnp.zeros((block,), jnp.int32), session])
    sess = lax.dynamic_slice_in_dim(window, at_block * block, 2 * block)
    place = (at_block - 1) * block + jnp.arange(2 * block, dtype=jnp.int32)

    def tile_bias(tile):
        q_at = slice(block + tile * strip, block + (tile + 1) * strip)
        k_at = slice(tile * strip, (tile + 3) * strip)
        k_place, q_place = place[k_at, None], place[None, q_at]
        allowed = (sess[None, q_at] == sess[k_at, None]) & (k_place <= q_place) & (k_place >= 0)
        return jnp.where(allowed, 0.0, NEG_FILL)

    return jnp.stack([tile_bias(0), tile_bias(1)])


def shards(queries, keys, values, out_grad, session):
    peers = lax.axis_size("sub")
    others = list(range(1, peers))
    part = queries.shape[1] // (2 * peers)
    spans, at = [], 0
    for heads in chunks_of(part // HD):
        spans.append((at, at + heads * HD))
        at += heads * HD
    bias = allowed_bias(session, queries.shape[0])
    kv_far, near_send, near_keep = first_keys([keys, values], *spans[0])
    kv_far = [round_sub(value, by) for by, value in zip(others, kv_far)]
    rest = [([queries, out_grad], *spans[0])] + [([keys, values, queries, out_grad], *span) for span in spans[1:]]
    rest = first_parts(rest, [near_keep])
    near_theirs = swapped(near_send)
    kv_parts = [None]
    qg_parts = [(rest[0][1], swapped(rest[0][0]), 0)]
    for send, own in rest[1:]:
        paired = swapped(send)
        kv_parts.append((own, paired, 0))
        qg_parts.append((own, paired, 2))
    count = len(spans)
    kv_sends, qg_sends, kv, qg, kv_own, own_earlier = [], [], [], [], [], []
    for index in range(count):
        if index:
            kv_sends.append(head_parts(*kv_parts[index], others, kv[index - 1] + own_earlier[index - 1:index]))
            kv.append([round_sub(value, by) for by, value in zip(others, kv_sends[index])])
            kv_own.append(head_parts(*kv_parts[index], [0], own_earlier[index - 1:index]))
        else:
            kv_sends.append([])
            kv_own.append(both_rows([near_keep], near_theirs.reshape(1, *near_theirs.shape)))
            kv.append(both_rows(kv_far, swapped(other_side(kv_far))))
        own_earlier.append(along_blocks(kv_own[index][0], 1, True))
        qg_sends.append(head_parts(*qg_parts[index], others, qg[index - 1] if index else []))
        qg.append([round_sub(value, by) for by, value in zip(others, qg_sends[index])])
    kept, paired = [], []
    for index in range(count):
        last = index == count - 1
        forward = [relayed(value, [first_dq]) if index else value for value in kv[index]]
        earlier = [own_earlier[index]] + [along_blocks(value, 1, not last) for value in forward]
        qg_all = head_parts(*qg_parts[index], [0], []) + qg[index]
        grads, dq, early = attention_grads(bias, kv_own[index] + kv[index], earlier, qg_all, last, [])
        first_dq = dq[0]
        dq = [dq[0]] + [round_sub(dq[by], by) for by in others]
        if last:
            later = [along_blocks(value, -1, False) for value in early[1:]]
            dkv = summed(grads, later, others, dq[1:])
            near = along_blocks(relayed(early[0], dkv), -1, False)
            dkv = summed(grads, [near], [0], []) + [round_sub(value, by) for by, value in zip(others, dkv)]
        else:
            dkv = summed(grads, [along_blocks(early[0], -1, False)], [0] + others, dq[1:])
            dkv = [dkv[0]] + [round_sub(dkv[by], by) for by in others]
        send, keep = rows_for_pair(dq, dkv)
        kept.append(keep)
        paired.append(swapped(send))
    return tuple(laid_out(kept, paired, spans))


def solution(mesh):
    spread = P(("grp", "blk", "pair", "sub"), None)
    return jax.shard_map(
        shards, mesh=mesh, in_specs=(spread,) * 4 + (P("grp"),), out_specs=(spread,) * 3, check_vma=False
    )
```

```python
import math

import jax
import jax.numpy as jnp
from jax import lax
from jax.experimental import pallas as pl
from jax.experimental.pallas import tpu as pltpu
from jax.sharding import PartitionSpec as P

HD = 128
NEG_FILL = -1e30
LOW = jnp.bfloat16
WIDE = jnp.float32
MIB = 1024 * 1024
TO_BITS = HD ** (-0.5) / math.log(2.0)
SCALE = HD ** (-0.5)
ROWS_BY_ROWS = (((1,), (1,)), ((), ()))


def chunks_of(heads):
    return [heads // 2, heads - heads // 2]


def along_blocks(value, by, ring):
    peers = lax.axis_size("blk")
    pairs = [(i, (i + by) % peers) for i in range(peers) if ring or 0 <= i + by < peers]
    return lax.ppermute(value, "blk", pairs)


def round_sub(value, by):
    peers = lax.axis_size("sub")
    return lax.ppermute(value, "sub", [(i, (i + by) % peers) for i in range(peers)])


def swapped(value):
    return lax.ppermute(value, "pair", [(0, 1), (1, 0)])


def run_moves(moves, sems):
    copies = [pltpu.make_async_copy(src, dst, sems.at[at]) for at, (src, dst) in enumerate(moves)]
    for copy in copies:
        copy.start()
    for copy in copies:
        copy.wait()


def call(kernel, ins, outs, scratch, name, whole=False, flops=0, room=8 * MIB):
    spec = pl.BlockSpec(memory_space=pltpu.VMEM if whole else pl.ANY)
    moved = sum(math.prod(a.shape) * a.dtype.itemsize for a in list(ins) + list(outs))
    return list(
        pl.pallas_call(
            kernel,
            out_shape=outs,
            in_specs=[spec] * len(ins),
            out_specs=[spec] * len(outs),
            scratch_shapes=scratch,
            name=name,
            cost_estimate=pl.CostEstimate(flops=flops, bytes_accessed=moved, transcendentals=0),
            compiler_params=pltpu.CompilerParams(vmem_limit_bytes=room),
        )(*ins)
    )


def shape(*dims, dtype=LOW):
    return jax.ShapeDtypeStruct(dims, dtype)


def first_parts(groups, after):
    held, wanted, outs = [], [], []
    for arrays, low, high in groups:
        rows, width = arrays[0].shape
        peers = lax.axis_size("sub")
        half = width // 2
        part = half // peers
        wanted.append((len(held), len(arrays), low, high))
        held += [pltpu.with_memory_space_constraint(array, pltpu.HBM) for array in arrays]
        outs += [pltpu.VMEM((len(arrays), peers, rows, high - low), LOW)] * 2

    def kernel(*refs):
        out_refs, sems = refs[-1 - len(outs):-1], refs[-1]
        p = lax.axis_index("pair")
        moves = []
        for group, (first, count, low, high) in enumerate(wanted):
            for side, out in zip((1 - p, p), out_refs[2 * group:2 * group + 2]):
                for at in range(peers):
                    start = pl.multiple_of(side * half + at * part + low, HD)
                    for i in range(count):
                        moves.append((refs[first + i].at[:, pl.ds(start, high - low)], out.at[i, at]))
        run_moves(moves, sems)

    spec = pl.BlockSpec(memory_space=pl.ANY)
    parts = pl.pallas_call(
        kernel,
        out_shape=outs,
        in_specs=[spec] * (len(held) + len(after)),
        out_specs=[spec] * len(outs),
        scratch_shapes=[pltpu.SemaphoreType.DMA((2 * peers * len(held),))],
        name="first_parts",
        compiler_params=pltpu.CompilerParams(vmem_limit_bytes=8 * MIB),
    )(*held, *after)
    return [(parts[2 * i], parts[2 * i + 1]) for i in range(len(groups))]


def first_keys(arrays, low, high):
    rows, width = arrays[0].shape
    half = width // 2
    peers = lax.axis_size("sub")
    part = half // peers
    cut = high - low

    def kernel(*refs):
        ins, far, (send, keep), sems = refs[:2], refs[2:1 + peers], refs[1 + peers:-1], refs[-1]
        p, s = lax.axis_index("pair"), lax.axis_index("sub")
        moves = []
        for i, ref in enumerate(ins):
            for by in range(1, peers):
                for side in range(2):
                    start = pl.multiple_of(side * half + lax.rem(s + by, peers) * part + low, HD)
                    moves.append((ref.at[:, pl.ds(start, cut)], far[by - 1].at[i, side]))
            for out, side in ((send, 1 - p), (keep, p)):
                start = pl.multiple_of(side * half + s * part + low, HD)
                moves.append((ref.at[:, pl.ds(start, cut)], out.at[i]))
        run_moves(moves, sems)

    spec = pl.BlockSpec(memory_space=pl.ANY)
    outs = [pltpu.VMEM((2, 2, rows, cut), LOW)] * (peers - 1) + [pltpu.VMEM((2, rows, cut), LOW)] * 2
    parts = pl.pallas_call(
        kernel,
        out_shape=outs,
        in_specs=[spec] * 2,
        out_specs=[spec] * len(outs),
        scratch_shapes=[pltpu.SemaphoreType.DMA((4 * peers,))],
        name="first_keys",
        compiler_params=pltpu.CompilerParams(vmem_limit_bytes=8 * MIB),
    )(*[pltpu.with_memory_space_constraint(array, pltpu.HBM) for array in arrays])
    return list(parts[:-2]), parts[-2], parts[-1]


def other_side(received):
    count = len(received)

    def kernel(*refs):
        p = lax.axis_index("pair")
        run_moves([(ref.at[:, 1 - p], refs[-2].at[by]) for by, ref in enumerate(refs[:count])], refs[-1])

    _, _, rows, cut = received[0].shape
    scratch = [pltpu.SemaphoreType.DMA((count,))]
    return call(kernel, received, [shape(count, 2, rows, cut)], scratch, "other_side")[0]


def both_rows(mine, theirs):
    count = len(mine)
    _, _, rows, cut = theirs.shape

    def kernel(*refs):
        ins, theirs_ref, outs, sems = refs[:count], refs[count], refs[count + 1:-1], refs[-1]
        p = lax.axis_index("pair")
        moves = []
        for by, (ref, out) in enumerate(zip(ins, outs)):
            source = ref.at[:, p] if len(ref.shape) == 4 else ref
            moves += [(source, out.at[:, p]), (theirs_ref.at[by], out.at[:, 1 - p])]
        run_moves(moves, sems)

    outs = [shape(2, 2, rows, cut)] * count
    scratch = [pltpu.SemaphoreType.DMA((2 * count,))]
    return call(kernel, mine + [theirs], outs, scratch, "both_rows")


def head_parts(own, paired, which, turns, after):
    _, peers, rows, cut = own.shape
    chosen = pl.ds(which, 2)

    def kernel(own_ref, pair_ref, *refs):
        outs, sems = refs[len(after):-1], refs[-1]
        p, s = lax.axis_index("pair"), lax.axis_index("sub")
        moves = []
        for by, out in zip(turns, outs):
            at = lax.rem(s + by, peers)
            moves += [(own_ref.at[chosen, at], out.at[:, p]), (pair_ref.at[chosen, at], out.at[:, 1 - p])]
        run_moves(moves, sems)

    outs = [shape(2, 2, rows, cut)] * len(turns)
    scratch = [pltpu.SemaphoreType.DMA((2 * len(turns),))]
    return call(kernel, [own, paired] + after, outs, scratch, "head_parts")


def relayed(value, after):
    def kernel(value_ref, *refs):
        run_moves([(value_ref, refs[-2])], refs[-1])

    scratch = [pltpu.SemaphoreType.DMA((1,))]
    return call(kernel, [value] + after, [shape(*value.shape)], scratch, "relayed")[0]


def attention_grads(bias, kv, kv_earlier, qg, split, after):
    peers = len(kv)
    _, _, rows, cut = kv[0].shape
    heads = cut // HD
    strip = rows * peers
    early_count = peers if split else 1

    def kernel(*refs):
        bias_ref = refs[0]
        kv_in, early_in, qg_in = refs[1:1 + peers], refs[1 + peers:1 + 2 * peers], refs[1 + 2 * peers:1 + 3 * peers]
        outs = refs[1 + 3 * peers + len(after):-5]
        own_out, dq_outs, early_outs = outs[0], outs[1:1 + peers], outs[1 + peers:]
        kv_all, qg_all, early, dq_all, sems = refs[-5:]
        s = lax.axis_index("sub")
        moves = []
        for by in range(peers):
            at = lax.rem(s - by + peers, peers)
            moves += [
                (early_in[by], kv_all.at[:, 0:2, at]),
                (kv_in[by], kv_all.at[:, 2:4, at]),
                (qg_in[by], qg_all.at[:, :, at]),
            ]
        run_moves(moves, sems)
        strips = [(head, tile) for head in range(heads) for tile in range(2)]
        products, terms = {}, {}

        def flat(ref, which, tiles, head):
            block = ref[which, tiles, :, :, pl.ds(head * HD, HD)]
            return block.reshape(block.shape[0] * strip, HD)

        def multiply(head, tile):
            at, span = pl.ds(tile, 1), pl.ds(tile, 3)
            q, g = flat(qg_all, 0, at, head), flat(qg_all, 1, at, head)
            k, v = flat(kv_all, 0, span, head), flat(kv_all, 1, span, head)
            scores = lax.dot_general(k, q, ROWS_BY_ROWS, preferred_element_type=WIDE)
            grad_prob = lax.dot_general(v, g, ROWS_BY_ROWS, preferred_element_type=WIDE)
            products[head, tile] = q, g, k, scores, grad_prob

        def finish(head, tile):
            q, g, k, scores, grad_prob = products.pop((head, tile))
            scores = scores * TO_BITS + bias_ref[tile]
            peak = jnp.max(scores, axis=0, keepdims=True)
            weight = jnp.exp2(scores - peak)
            prob = weight * (1.0 / jnp.sum(weight, axis=0, keepdims=True))
            prob_low = prob.astype(LOW)
            row_dot = jnp.sum(prob_low.astype(WIDE) * grad_prob, axis=0, keepdims=True)
            score_low = (prob * (grad_prob - row_dot)).astype(LOW)
            dq = jnp.dot(k.T, score_low, preferred_element_type=WIDE) * SCALE
            dq_all[tile, :, :, pl.ds(head * HD, HD)] = dq.T.astype(LOW).reshape(peers, rows, HD)
            dk = jnp.dot(score_low, q, preferred_element_type=WIDE) * SCALE
            dv = jnp.dot(prob_low, g, preferred_element_type=WIDE)
            terms[head, tile] = dk, dv

        def gather(head):
            for which in range(2):
                low, high = terms[head, 0][which], terms[head, 1][which]
                sums = (
                    low[:strip],
                    low[strip:2 * strip] + high[:strip],
                    low[2 * strip:] + high[strip:2 * strip],
                    high[2 * strip:],
                )
                for tile, total in enumerate(sums):
                    total = total.reshape(peers, rows, HD)
                    if tile < 2:
                        early[which, tile, :, :, pl.ds(head * HD, HD)] = total.astype(LOW)
                    else:
                        own_out[which, tile - 2, :, :, pl.ds(head * HD, HD)] = total

        multiply(*strips[0])
        for at, (head, tile) in enumerate(strips):
            if at + 1 < len(strips):
                multiply(*strips[at + 1])
            finish(head, tile)
            if tile == 1:
                gather(head)
        moves = [] if split else [(early, early_outs[0])]
        for by in range(peers):
            at = lax.rem(s + by, peers)
            moves.append((dq_all.at[:, at], dq_outs[by]))
            if split:
                moves.append((early.at[:, :, at], early_outs[by]))
        run_moves(moves, sems)

    outs = [shape(2, 2, peers, rows, cut, dtype=WIDE)] + [shape(2, rows, cut)] * peers
    outs += [shape(2, 2, rows, cut)] * peers if split else [shape(2, 2, peers, rows, cut)]
    scratch = [
        pltpu.VMEM((2, 4, peers, rows, cut), LOW),
        pltpu.VMEM((2, 2, peers, rows, cut), LOW),
        pltpu.VMEM((2, 2, peers, rows, cut), LOW),
        pltpu.VMEM((2, peers, rows, cut), LOW),
        pltpu.SemaphoreType.DMA((3 * peers,)),
    ]
    flops = heads * 2 * 5 * 2 * strip * 3 * strip * HD
    ins = [bias] + kv + kv_earlier + qg + after
    outs = call(kernel, ins, outs, scratch, "attention_grads", whole=True, flops=flops, room=40 * MIB)
    return outs[0], outs[1:1 + peers], outs[1 + peers:]


def summed(own, later, turns, after):
    _, _, peers, rows, cut = own.shape
    split = len(later) > 1 or later[0].ndim == 4

    def kernel(own_ref, *refs):
        later_refs, outs = refs[:len(later)], refs[len(later) + len(after):]
        s = lax.axis_index("sub")
        for place, (by, out) in enumerate(zip(turns, outs)):
            at = lax.rem(s + by, peers)
            for which in range(2):
                for row in range(2):
                    term = later_refs[place][which, row] if split else later_refs[0][which, row, at]
                    out[which, row] = (own_ref[which, row, at] + term.astype(WIDE)).astype(LOW)

    outs = [shape(2, 2, rows, cut)] * len(turns)
    return call(kernel, [own] + later + after, outs, [], "summed", whole=True)


def rows_for_pair(dq, dkv):
    peers = len(dq)
    _, rows, cut = dq[0].shape

    def kernel(*refs):
        dq_refs, dkv_refs, (send, keep) = refs[:peers], refs[peers:2 * peers], refs[-2:]
        p, s = lax.axis_index("pair"), lax.axis_index("sub")
        for by in range(peers):
            at = lax.rem(s - by + peers, peers)
            for out, row in ((send, 1 - p), (keep, p)):
                out[0, at] = dq_refs[by][row]
                for which in range(2):
                    out[1 + which, at] = dkv_refs[by][which, row]

    outs = [shape(3, peers, rows, cut)] * 2
    return call(kernel, dq + dkv, outs, [], "rows_for_pair", whole=True)


def laid_out(kept, paired, spans):
    _, peers, rows, _ = kept[0].shape
    part = spans[-1][1]
    half = part * peers
    count = len(spans)

    def kernel(*refs):
        keep, rec, outs, sems = refs[:count], refs[count:2 * count], refs[2 * count:-1], refs[-1]
        p = lax.axis_index("pair")
        moves = []
        for mine, theirs, (low, high) in zip(keep, rec, spans):
            for source, side in ((mine, p), (theirs, 1 - p)):
                for at in range(peers):
                    columns = pl.ds(pl.multiple_of(side * half + at * part + low, HD), high - low)
                    moves += [(source.at[which, at], out.at[:, columns]) for which, out in enumerate(outs)]
        run_moves(moves, sems)

    outs = [shape(rows, 2 * half)] * 3
    return call(kernel, kept + paired, outs, [pltpu.SemaphoreType.DMA((6 * count * peers,))], "laid_out")


def allowed_bias(session, rows):
    strip = rows * lax.axis_size("sub")
    block = 2 * strip
    at_block = lax.axis_index("blk")
    window = jnp.concatenate([jnp.zeros((block,), jnp.int32), session])
    sess = lax.dynamic_slice_in_dim(window, at_block * block, 2 * block)
    place = (at_block - 1) * block + jnp.arange(2 * block, dtype=jnp.int32)

    def tile_bias(tile):
        q_at = slice(block + tile * strip, block + (tile + 1) * strip)
        k_at = slice(tile * strip, (tile + 3) * strip)
        k_place, q_place = place[k_at, None], place[None, q_at]
        allowed = (sess[None, q_at] == sess[k_at, None]) & (k_place <= q_place) & (k_place >= 0)
        return jnp.where(allowed, 0.0, NEG_FILL)

    return jnp.stack([tile_bias(0), tile_bias(1)])


def shards(queries, keys, values, out_grad, session):
    peers = lax.axis_size("sub")
    others = list(range(1, peers))
    part = queries.shape[1] // (2 * peers)
    spans, at = [], 0
    for heads in chunks_of(part // HD):
        spans.append((at, at + heads * HD))
        at += heads * HD
    bias = allowed_bias(session, queries.shape[0])
    kv_far, near_send, near_keep = first_keys([keys, values], *spans[0])
    kv_far = [round_sub(value, by) for by, value in zip(others, kv_far)]
    rest = [([queries, out_grad], *spans[0])] + [([keys, values, queries, out_grad], *span) for span in spans[1:]]
    rest = first_parts(rest, [near_keep])
    near_theirs = swapped(near_send)
    kv_parts = [None]
    qg_parts = [(rest[0][1], swapped(rest[0][0]), 0)]
    for send, own in rest[1:]:
        paired = swapped(send)
        kv_parts.append((own, paired, 0))
        qg_parts.append((own, paired, 2))
    count = len(spans)
    kv_sends, qg_sends, kv, qg, kv_own, own_earlier = [], [], [], [], [], []
    for index in range(count):
        if index:
            kv_sends.append(head_parts(*kv_parts[index], others, kv_far))
            kv.append([round_sub(value, by) for by, value in zip(others, kv_sends[index])])
            kv_own.append(head_parts(*kv_parts[index], [0], own_earlier[index - 1:index]))
        else:
            kv_sends.append([])
            kv_own.append(both_rows([near_keep], near_theirs.reshape(1, *near_theirs.shape)))
            kv.append(both_rows(kv_far, swapped(other_side(kv_far))))
        own_earlier.append(along_blocks(kv_own[index][0], 1, True))
    for index in range(count):
        turn = kv[index] if index else kv_sends[-1] + own_earlier[:1]
        qg_sends.append(head_parts(*qg_parts[index], others, turn))
        qg.append([round_sub(value, by) for by, value in zip(others, qg_sends[index])])
    kept, paired = [], []
    for index in range(count):
        last = index == count - 1
        earlier = [own_earlier[index]] + [along_blocks(value, 1, not last) for value in kv[index]]
        qg_all = head_parts(*qg_parts[index], [0], []) + qg[index]
        grads, dq, early = attention_grads(bias, kv_own[index] + kv[index], earlier, qg_all, last, [])
        dq = [dq[0]] + [round_sub(dq[by], by) for by in others]
        if last:
            later = [along_blocks(value, -1, False) for value in early[1:]]
            dkv = summed(grads, later, others, dq[1:])
            near = along_blocks(relayed(early[0], dkv), -1, False)
            dkv = summed(grads, [near], [0], []) + [round_sub(value, by) for by, value in zip(others, dkv)]
        else:
            dkv = summed(grads, [along_blocks(early[0], -1, False)], [0] + others, dq[1:])
            dkv = [dkv[0]] + [round_sub(dkv[by], by) for by in others]
        send, keep = rows_for_pair(dq, dkv)
        kept.append(keep)
        paired.append(swapped(send))
    return tuple(laid_out(kept, paired, spans))


def solution(mesh):
    spread = P(("grp", "blk", "pair", "sub"), None)
    return jax.shard_map(
        shards, mesh=mesh, in_specs=(spread,) * 4 + (P("grp"),), out_specs=(spread,) * 3, check_vma=False
    )
```

```python
import math

import jax
import jax.numpy as jnp
from jax import lax
from jax.experimental import pallas as pl
from jax.experimental.pallas import tpu as pltpu
from jax.sharding import PartitionSpec as P

HD = 128
NEG_FILL = -1e30
LOW = jnp.bfloat16
WIDE = jnp.float32
MIB = 1024 * 1024
TO_BITS = HD ** (-0.5) / math.log(2.0)
SCALE = HD ** (-0.5)
ROWS_BY_ROWS = (((1,), (1,)), ((), ()))


def chunks_of(heads):
    return [heads // 2, heads - heads // 2]


def along_blocks(value, by, ring):
    peers = lax.axis_size("blk")
    pairs = [(i, (i + by) % peers) for i in range(peers) if ring or 0 <= i + by < peers]
    return lax.ppermute(value, "blk", pairs)


def round_sub(value, by):
    peers = lax.axis_size("sub")
    return lax.ppermute(value, "sub", [(i, (i + by) % peers) for i in range(peers)])


def swapped(value):
    return lax.ppermute(value, "pair", [(0, 1), (1, 0)])


def run_moves(moves, sems):
    copies = [pltpu.make_async_copy(src, dst, sems.at[at]) for at, (src, dst) in enumerate(moves)]
    for copy in copies:
        copy.start()
    for copy in copies:
        copy.wait()


def call(kernel, ins, outs, scratch, name, whole=False, flops=0, room=8 * MIB):
    spec = pl.BlockSpec(memory_space=pltpu.VMEM if whole else pl.ANY)
    moved = sum(math.prod(a.shape) * a.dtype.itemsize for a in list(ins) + list(outs))
    return list(
        pl.pallas_call(
            kernel,
            out_shape=outs,
            in_specs=[spec] * len(ins),
            out_specs=[spec] * len(outs),
            scratch_shapes=scratch,
            name=name,
            cost_estimate=pl.CostEstimate(flops=flops, bytes_accessed=moved, transcendentals=0),
            compiler_params=pltpu.CompilerParams(vmem_limit_bytes=room),
        )(*ins)
    )


def shape(*dims, dtype=LOW):
    return jax.ShapeDtypeStruct(dims, dtype)


def first_parts(groups, after):
    held, wanted, outs = [], [], []
    for arrays, low, high in groups:
        rows, width = arrays[0].shape
        peers = lax.axis_size("sub")
        half = width // 2
        part = half // peers
        wanted.append((len(held), len(arrays), low, high))
        held += [pltpu.with_memory_space_constraint(array, pltpu.HBM) for array in arrays]
        outs += [pltpu.VMEM((len(arrays), peers, rows, high - low), LOW)] * 2

    def kernel(*refs):
        out_refs, sems = refs[-1 - len(outs):-1], refs[-1]
        p = lax.axis_index("pair")
        moves = []
        for group, (first, count, low, high) in enumerate(wanted):
            for side, out in zip((1 - p, p), out_refs[2 * group:2 * group + 2]):
                for at in range(peers):
                    start = pl.multiple_of(side * half + at * part + low, HD)
                    for i in range(count):
                        moves.append((refs[first + i].at[:, pl.ds(start, high - low)], out.at[i, at]))
        run_moves(moves, sems)

    spec = pl.BlockSpec(memory_space=pl.ANY)
    parts = pl.pallas_call(
        kernel,
        out_shape=outs,
        in_specs=[spec] * (len(held) + len(after)),
        out_specs=[spec] * len(outs),
        scratch_shapes=[pltpu.SemaphoreType.DMA((2 * peers * len(held),))],
        name="first_parts",
        compiler_params=pltpu.CompilerParams(vmem_limit_bytes=8 * MIB),
    )(*held, *after)
    return [(parts[2 * i], parts[2 * i + 1]) for i in range(len(groups))]


def first_keys(arrays, low, high):
    rows, width = arrays[0].shape
    half = width // 2
    peers = lax.axis_size("sub")
    part = half // peers
    cut = high - low

    def kernel(*refs):
        ins, far, (send, keep), sems = refs[:2], refs[2:1 + peers], refs[1 + peers:-1], refs[-1]
        p, s = lax.axis_index("pair"), lax.axis_index("sub")
        moves = []
        for i, ref in enumerate(ins):
            for by in range(1, peers):
                for side in range(2):
                    start = pl.multiple_of(side * half + lax.rem(s + by, peers) * part + low, HD)
                    moves.append((ref.at[:, pl.ds(start, cut)], far[by - 1].at[i, side]))
            for out, side in ((send, 1 - p), (keep, p)):
                start = pl.multiple_of(side * half + s * part + low, HD)
                moves.append((ref.at[:, pl.ds(start, cut)], out.at[i]))
        run_moves(moves, sems)

    spec = pl.BlockSpec(memory_space=pl.ANY)
    outs = [pltpu.VMEM((2, 2, rows, cut), LOW)] * (peers - 1) + [pltpu.VMEM((2, rows, cut), LOW)] * 2
    parts = pl.pallas_call(
        kernel,
        out_shape=outs,
        in_specs=[spec] * 2,
        out_specs=[spec] * len(outs),
        scratch_shapes=[pltpu.SemaphoreType.DMA((4 * peers,))],
        name="first_keys",
        compiler_params=pltpu.CompilerParams(vmem_limit_bytes=8 * MIB),
    )(*[pltpu.with_memory_space_constraint(array, pltpu.HBM) for array in arrays])
    return list(parts[:-2]), parts[-2], parts[-1]


def other_side(received):
    count = len(received)

    def kernel(*refs):
        p = lax.axis_index("pair")
        run_moves([(ref.at[:, 1 - p], refs[-2].at[by]) for by, ref in enumerate(refs[:count])], refs[-1])

    _, _, rows, cut = received[0].shape
    scratch = [pltpu.SemaphoreType.DMA((count,))]
    return call(kernel, received, [shape(count, 2, rows, cut)], scratch, "other_side")[0]


def both_rows(mine, theirs):
    count = len(mine)
    _, _, rows, cut = theirs.shape

    def kernel(*refs):
        ins, theirs_ref, outs, sems = refs[:count], refs[count], refs[count + 1:-1], refs[-1]
        p = lax.axis_index("pair")
        moves = []
        for by, (ref, out) in enumerate(zip(ins, outs)):
            source = ref.at[:, p] if len(ref.shape) == 4 else ref
            moves += [(source, out.at[:, p]), (theirs_ref.at[by], out.at[:, 1 - p])]
        run_moves(moves, sems)

    outs = [shape(2, 2, rows, cut)] * count
    scratch = [pltpu.SemaphoreType.DMA((2 * count,))]
    return call(kernel, mine + [theirs], outs, scratch, "both_rows")


def head_parts(own, paired, which, turns, after):
    _, peers, rows, cut = own.shape
    chosen = pl.ds(which, 2)

    def kernel(own_ref, pair_ref, *refs):
        outs, sems = refs[len(after):-1], refs[-1]
        p, s = lax.axis_index("pair"), lax.axis_index("sub")
        moves = []
        for by, out in zip(turns, outs):
            at = lax.rem(s + by, peers)
            moves += [(own_ref.at[chosen, at], out.at[:, p]), (pair_ref.at[chosen, at], out.at[:, 1 - p])]
        run_moves(moves, sems)

    outs = [shape(2, 2, rows, cut)] * len(turns)
    scratch = [pltpu.SemaphoreType.DMA((2 * len(turns),))]
    return call(kernel, [own, paired] + after, outs, scratch, "head_parts")


def relayed(value, after):
    def kernel(value_ref, *refs):
        run_moves([(value_ref, refs[-2])], refs[-1])

    scratch = [pltpu.SemaphoreType.DMA((1,))]
    return call(kernel, [value] + after, [shape(*value.shape)], scratch, "relayed")[0]


def attention_grads(bias, kv, kv_earlier, qg, split, first, heads, after):
    peers = len(kv)
    rows, cut = kv[0].shape[2], heads * HD
    chosen = pl.ds(first * HD, cut)
    strip = rows * peers
    early_count = peers if split else 1

    def kernel(*refs):
        bias_ref = refs[0]
        kv_in, early_in, qg_in = refs[1:1 + peers], refs[1 + peers:1 + 2 * peers], refs[1 + 2 * peers:1 + 3 * peers]
        outs = refs[1 + 3 * peers + len(after):-5]
        own_out, dq_outs, early_outs = outs[0], outs[1:1 + peers], outs[1 + peers:]
        kv_all, qg_all, early, dq_all, sems = refs[-5:]
        s = lax.axis_index("sub")
        moves = []
        for by in range(peers):
            at = lax.rem(s - by + peers, peers)
            moves += [
                (early_in[by].at[:, :, :, chosen], kv_all.at[:, 0:2, at]),
                (kv_in[by].at[:, :, :, chosen], kv_all.at[:, 2:4, at]),
                (qg_in[by].at[:, :, :, chosen], qg_all.at[:, :, at]),
            ]
        run_moves(moves, sems)
        strips = [(head, tile) for head in range(heads) for tile in range(2)]
        products, terms = {}, {}

        def flat(ref, which, tiles, head):
            block = ref[which, tiles, :, :, pl.ds(head * HD, HD)]
            return block.reshape(block.shape[0] * strip, HD)

        def multiply(head, tile):
            at, span = pl.ds(tile, 1), pl.ds(tile, 3)
            q, g = flat(qg_all, 0, at, head), flat(qg_all, 1, at, head)
            k, v = flat(kv_all, 0, span, head), flat(kv_all, 1, span, head)
            scores = lax.dot_general(k, q, ROWS_BY_ROWS, preferred_element_type=WIDE)
            grad_prob = lax.dot_general(v, g, ROWS_BY_ROWS, preferred_element_type=WIDE)
            products[head, tile] = q, g, k, scores, grad_prob

        def finish(head, tile):
            q, g, k, scores, grad_prob = products.pop((head, tile))
            scores = scores * TO_BITS + bias_ref[tile]
            peak = jnp.max(scores, axis=0, keepdims=True)
            weight = jnp.exp2(scores - peak)
            prob = weight * (1.0 / jnp.sum(weight, axis=0, keepdims=True))
            prob_low = prob.astype(LOW)
            row_dot = jnp.sum(prob_low.astype(WIDE) * grad_prob, axis=0, keepdims=True)
            score_low = (prob * (grad_prob - row_dot)).astype(LOW)
            dq = jnp.dot(k.T, score_low, preferred_element_type=WIDE) * SCALE
            dq_all[tile, :, :, pl.ds(head * HD, HD)] = dq.T.astype(LOW).reshape(peers, rows, HD)
            dk = jnp.dot(score_low, q, preferred_element_type=WIDE) * SCALE
            dv = jnp.dot(prob_low, g, preferred_element_type=WIDE)
            terms[head, tile] = dk, dv

        def gather(head):
            for which in range(2):
                low, high = terms[head, 0][which], terms[head, 1][which]
                sums = (
                    low[:strip],
                    low[strip:2 * strip] + high[:strip],
                    low[2 * strip:] + high[strip:2 * strip],
                    high[2 * strip:],
                )
                for tile, total in enumerate(sums):
                    total = total.reshape(peers, rows, HD)
                    if tile < 2:
                        early[which, tile, :, :, pl.ds(head * HD, HD)] = total.astype(LOW)
                    else:
                        own_out[which, tile - 2, :, :, pl.ds(head * HD, HD)] = total

        multiply(*strips[0])
        for at, (head, tile) in enumerate(strips):
            if at + 1 < len(strips):
                multiply(*strips[at + 1])
            finish(head, tile)
            if tile == 1:
                gather(head)
        moves = [] if split else [(early, early_outs[0])]
        for by in range(peers):
            at = lax.rem(s + by, peers)
            moves.append((dq_all.at[:, at], dq_outs[by]))
            if split:
                moves.append((early.at[:, :, at], early_outs[by]))
        run_moves(moves, sems)

    outs = [shape(2, 2, peers, rows, cut, dtype=WIDE)] + [shape(2, rows, cut)] * peers
    outs += [shape(2, 2, rows, cut)] * peers if split else [shape(2, 2, peers, rows, cut)]
    scratch = [
        pltpu.VMEM((2, 4, peers, rows, cut), LOW),
        pltpu.VMEM((2, 2, peers, rows, cut), LOW),
        pltpu.VMEM((2, 2, peers, rows, cut), LOW),
        pltpu.VMEM((2, peers, rows, cut), LOW),
        pltpu.SemaphoreType.DMA((3 * peers,)),
    ]
    flops = heads * 2 * 5 * 2 * strip * 3 * strip * HD
    ins = [bias] + kv + kv_earlier + qg + after
    outs = call(kernel, ins, outs, scratch, "attention_grads", whole=True, flops=flops, room=40 * MIB)
    return outs[0], outs[1:1 + peers], outs[1 + peers:]


def summed(own, later, turns, after):
    _, _, peers, rows, _ = own[0].shape
    widths = [array.shape[-1] for array in own]
    split = later[0].ndim == 4

    def kernel(*refs):
        own_refs, later_refs = refs[:len(own)], refs[len(own):len(own) + len(later)]
        outs = refs[len(own) + len(later) + len(after):]
        s = lax.axis_index("sub")
        for place, (by, out) in enumerate(zip(turns, outs)):
            at = lax.rem(s + by, peers)
            start = 0
            for group, width in enumerate(widths):
                for which in range(2):
                    for row in range(2):
                        term = later_refs[place][which, row] if split else later_refs[group][which, row, at]
                        total = own_refs[group][which, row, at] + term.astype(WIDE)
                        out[which, row, :, pl.ds(start, width)] = total.astype(LOW)
                start += width

    outs = [shape(2, 2, rows, sum(widths))] * len(turns)
    return call(kernel, own + later + after, outs, [], "summed", whole=True)


def side_by_side(groups):
    count, peers = len(groups), len(groups[0])
    _, rows, _ = groups[0][0].shape
    widths = [group[0].shape[-1] for group in groups]

    def kernel(*refs):
        for by in range(peers):
            start = 0
            for group, width in enumerate(widths):
                refs[count * peers + by][:, :, pl.ds(start, width)] = refs[group * peers + by][...]
                start += width

    ins = [array for group in groups for array in group]
    return call(kernel, ins, [shape(2, rows, sum(widths))] * peers, [], "side_by_side", whole=True)


def rows_for_pair(dq, dkv):
    peers = len(dq)
    _, rows, cut = dq[0].shape

    def kernel(*refs):
        dq_refs, dkv_refs, (send, keep) = refs[:peers], refs[peers:2 * peers], refs[-2:]
        p, s = lax.axis_index("pair"), lax.axis_index("sub")
        for by in range(peers):
            at = lax.rem(s - by + peers, peers)
            for out, row in ((send, 1 - p), (keep, p)):
                out[0, at] = dq_refs[by][row]
                for which in range(2):
                    out[1 + which, at] = dkv_refs[by][which, row]

    outs = [shape(3, peers, rows, cut)] * 2
    return call(kernel, dq + dkv, outs, [], "rows_for_pair", whole=True)


def laid_out(kept, paired, spans):
    _, peers, rows, _ = kept[0].shape
    part = spans[-1][1]
    half = part * peers
    count = len(spans)

    def kernel(*refs):
        keep, rec, outs, sems = refs[:count], refs[count:2 * count], refs[2 * count:-1], refs[-1]
        p = lax.axis_index("pair")
        moves = []
        for mine, theirs, (low, high) in zip(keep, rec, spans):
            for source, side in ((mine, p), (theirs, 1 - p)):
                for at in range(peers):
                    columns = pl.ds(pl.multiple_of(side * half + at * part + low, HD), high - low)
                    moves += [(source.at[which, at], out.at[:, columns]) for which, out in enumerate(outs)]
        run_moves(moves, sems)

    outs = [shape(rows, 2 * half)] * 3
    return call(kernel, kept + paired, outs, [pltpu.SemaphoreType.DMA((6 * count * peers,))], "laid_out")


def allowed_bias(session, rows):
    strip = rows * lax.axis_size("sub")
    block = 2 * strip
    at_block = lax.axis_index("blk")
    window = jnp.concatenate([jnp.zeros((block,), jnp.int32), session])
    sess = lax.dynamic_slice_in_dim(window, at_block * block, 2 * block)
    place = (at_block - 1) * block + jnp.arange(2 * block, dtype=jnp.int32)

    def tile_bias(tile):
        q_at = slice(block + tile * strip, block + (tile + 1) * strip)
        k_at = slice(tile * strip, (tile + 3) * strip)
        k_place, q_place = place[k_at, None], place[None, q_at]
        allowed = (sess[None, q_at] == sess[k_at, None]) & (k_place <= q_place) & (k_place >= 0)
        return jnp.where(allowed, 0.0, NEG_FILL)

    return jnp.stack([tile_bias(0), tile_bias(1)])


def shards(queries, keys, values, out_grad, session):
    peers = lax.axis_size("sub")
    others = list(range(1, peers))
    part = queries.shape[1] // (2 * peers)
    spans, at = [], 0
    for heads in chunks_of(part // HD):
        spans.append((at, at + heads * HD))
        at += heads * HD
    bias = allowed_bias(session, queries.shape[0])
    kv_far, near_send, near_keep = first_keys([keys, values], *spans[0])
    kv_far = [round_sub(value, by) for by, value in zip(others, kv_far)]
    rest = [([queries, out_grad], *spans[0])] + [([keys, values, queries, out_grad], *span) for span in spans[1:]]
    rest = first_parts(rest, [near_keep])
    near_theirs = swapped(near_send)
    kv_parts = [None]
    qg_parts = [(rest[0][1], swapped(rest[0][0]), 0)]
    for send, own in rest[1:]:
        paired = swapped(send)
        kv_parts.append((own, paired, 0))
        qg_parts.append((own, paired, 2))
    count = len(spans)
    kv_sends, qg_sends, kv, qg, kv_own, own_earlier = [], [], [], [], [], []
    for index in range(count):
        if index:
            kv_sends.append(head_parts(*kv_parts[index], others, kv[index - 1] + own_earlier[index - 1:index]))
            kv.append([round_sub(value, by) for by, value in zip(others, kv_sends[index])])
            kv_own.append(head_parts(*kv_parts[index], [0], own_earlier[index - 1:index]))
        else:
            kv_sends.append([])
            kv_own.append(both_rows([near_keep], near_theirs.reshape(1, *near_theirs.shape)))
            kv.append(both_rows(kv_far, swapped(other_side(kv_far))))
        own_earlier.append(along_blocks(kv_own[index][0], 1, True))
        qg_sends.append(head_parts(*qg_parts[index], others, qg[index - 1] if index else []))
        qg.append([round_sub(value, by) for by, value in zip(others, qg_sends[index])])
    kept, paired, first_dq, back = [], [], [], []
    for index, (low, high) in enumerate(spans):
        last = index == count - 1
        forward = [relayed(value, first_dq) if index else value for value in kv[index]]
        earlier = [own_earlier[index]] + [along_blocks(value, 1, not last) for value in forward]
        qg_all = head_parts(*qg_parts[index], [0], []) + qg[index]
        kv_all = kv_own[index] + kv[index]
        heads = (high - low) // HD
        if last:
            grads, dq, early = attention_grads(bias, kv_all, earlier, qg_all, True, 0, heads, back)
            dq = [dq[0]] + [round_sub(dq[by], by) for by in others]
            later = [along_blocks(value, -1, False) for value in early[1:]]
            dkv = summed([grads], later, others, dq[1:])
            near = along_blocks(relayed(early[0], dq[1:]), -1, False)
            dkv = summed([grads], [near], [0], []) + [round_sub(value, by) for by, value in zip(others, dkv)]
        else:
            groups, turn = [], []
            for head in range(heads):
                groups.append(attention_grads(bias, kv_all, earlier, qg_all, False, head, 1, turn))
                turn = groups[-1][1][:1]
                first_dq = first_dq or turn
            later = [along_blocks(early[0], -1, False) for _, _, early in groups]
            back = later[:1]
            dq = side_by_side([dq for _, dq, _ in groups]) if heads > 1 else groups[0][1]
            dq = [dq[0]] + [round_sub(dq[by], by) for by in others]
            dkv = summed([grads for grads, _, _ in groups], later, [0] + others, dq[1:])
            dkv = [dkv[0]] + [round_sub(dkv[by], by) for by in others]
        send, keep = rows_for_pair(dq, dkv)
        kept.append(keep)
        paired.append(swapped(send))
    return tuple(laid_out(kept, paired, spans))


def solution(mesh):
    spread = P(("grp", "blk", "pair", "sub"), None)
    return jax.shard_map(
        shards, mesh=mesh, in_specs=(spread,) * 4 + (P("grp"),), out_specs=(spread,) * 3, check_vma=False
    )
```

```python
import math

import jax
import jax.numpy as jnp
from jax import lax
from jax.experimental import pallas as pl
from jax.experimental.pallas import tpu as pltpu
from jax.sharding import PartitionSpec as P

HD = 128
NEG_FILL = -1e30
LOW = jnp.bfloat16
WIDE = jnp.float32
MIB = 1024 * 1024
TO_BITS = HD ** (-0.5) / math.log(2.0)
SCALE = HD ** (-0.5)
ROWS_BY_ROWS = (((1,), (1,)), ((), ()))


def chunks_of(heads):
    return [heads // 2, heads - heads // 2]


def along_blocks(value, by, ring):
    peers = lax.axis_size("blk")
    pairs = [(i, (i + by) % peers) for i in range(peers) if ring or 0 <= i + by < peers]
    return lax.ppermute(value, "blk", pairs)


def round_sub(value, by):
    peers = lax.axis_size("sub")
    return lax.ppermute(value, "sub", [(i, (i + by) % peers) for i in range(peers)])


def swapped(value):
    return lax.ppermute(value, "pair", [(0, 1), (1, 0)])


def run_moves(moves, sems):
    copies = [pltpu.make_async_copy(src, dst, sems.at[at]) for at, (src, dst) in enumerate(moves)]
    for copy in copies:
        copy.start()
    for copy in copies:
        copy.wait()


def call(kernel, ins, outs, scratch, name, whole=False, flops=0, room=8 * MIB):
    spec = pl.BlockSpec(memory_space=pltpu.VMEM if whole else pl.ANY)
    moved = sum(math.prod(a.shape) * a.dtype.itemsize for a in list(ins) + list(outs))
    return list(
        pl.pallas_call(
            kernel,
            out_shape=outs,
            in_specs=[spec] * len(ins),
            out_specs=[spec] * len(outs),
            scratch_shapes=scratch,
            name=name,
            cost_estimate=pl.CostEstimate(flops=flops, bytes_accessed=moved, transcendentals=0),
            compiler_params=pltpu.CompilerParams(vmem_limit_bytes=room),
        )(*ins)
    )


def shape(*dims, dtype=LOW):
    return jax.ShapeDtypeStruct(dims, dtype)


def first_parts(groups, after):
    held, wanted, outs = [], [], []
    for arrays, low, high in groups:
        rows, width = arrays[0].shape
        peers = lax.axis_size("sub")
        half = width // 2
        part = half // peers
        wanted.append((len(held), len(arrays), low, high))
        held += [pltpu.with_memory_space_constraint(array, pltpu.HBM) for array in arrays]
        outs += [pltpu.VMEM((len(arrays), peers, rows, high - low), LOW)] * 2

    def kernel(*refs):
        out_refs, sems = refs[-1 - len(outs):-1], refs[-1]
        p = lax.axis_index("pair")
        moves = []
        for group, (first, count, low, high) in enumerate(wanted):
            for side, out in zip((1 - p, p), out_refs[2 * group:2 * group + 2]):
                for at in range(peers):
                    start = pl.multiple_of(side * half + at * part + low, HD)
                    for i in range(count):
                        moves.append((refs[first + i].at[:, pl.ds(start, high - low)], out.at[i, at]))
        run_moves(moves, sems)

    spec = pl.BlockSpec(memory_space=pl.ANY)
    parts = pl.pallas_call(
        kernel,
        out_shape=outs,
        in_specs=[spec] * (len(held) + len(after)),
        out_specs=[spec] * len(outs),
        scratch_shapes=[pltpu.SemaphoreType.DMA((2 * peers * len(held),))],
        name="first_parts",
        compiler_params=pltpu.CompilerParams(vmem_limit_bytes=8 * MIB),
    )(*held, *after)
    return [(parts[2 * i], parts[2 * i + 1]) for i in range(len(groups))]


def first_keys(arrays, low, high):
    rows, width = arrays[0].shape
    half = width // 2
    peers = lax.axis_size("sub")
    part = half // peers
    cut = high - low

    def kernel(*refs):
        ins, far, (send, keep), sems = refs[:2], refs[2:1 + peers], refs[1 + peers:-1], refs[-1]
        p, s = lax.axis_index("pair"), lax.axis_index("sub")
        moves = []
        for i, ref in enumerate(ins):
            for by in range(1, peers):
                for side in range(2):
                    start = pl.multiple_of(side * half + lax.rem(s + by, peers) * part + low, HD)
                    moves.append((ref.at[:, pl.ds(start, cut)], far[by - 1].at[i, side]))
            for out, side in ((send, 1 - p), (keep, p)):
                start = pl.multiple_of(side * half + s * part + low, HD)
                moves.append((ref.at[:, pl.ds(start, cut)], out.at[i]))
        run_moves(moves, sems)

    spec = pl.BlockSpec(memory_space=pl.ANY)
    outs = [pltpu.VMEM((2, 2, rows, cut), LOW)] * (peers - 1) + [pltpu.VMEM((2, rows, cut), LOW)] * 2
    parts = pl.pallas_call(
        kernel,
        out_shape=outs,
        in_specs=[spec] * 2,
        out_specs=[spec] * len(outs),
        scratch_shapes=[pltpu.SemaphoreType.DMA((4 * peers,))],
        name="first_keys",
        compiler_params=pltpu.CompilerParams(vmem_limit_bytes=8 * MIB),
    )(*[pltpu.with_memory_space_constraint(array, pltpu.HBM) for array in arrays])
    return list(parts[:-2]), parts[-2], parts[-1]


def other_side(received):
    count = len(received)

    def kernel(*refs):
        p = lax.axis_index("pair")
        run_moves([(ref.at[:, 1 - p], refs[-2].at[by]) for by, ref in enumerate(refs[:count])], refs[-1])

    _, _, rows, cut = received[0].shape
    scratch = [pltpu.SemaphoreType.DMA((count,))]
    return call(kernel, received, [shape(count, 2, rows, cut)], scratch, "other_side")[0]


def both_rows(mine, theirs):
    count = len(mine)
    _, _, rows, cut = theirs.shape

    def kernel(*refs):
        ins, theirs_ref, outs, sems = refs[:count], refs[count], refs[count + 1:-1], refs[-1]
        p = lax.axis_index("pair")
        moves = []
        for by, (ref, out) in enumerate(zip(ins, outs)):
            source = ref.at[:, p] if len(ref.shape) == 4 else ref
            moves += [(source, out.at[:, p]), (theirs_ref.at[by], out.at[:, 1 - p])]
        run_moves(moves, sems)

    outs = [shape(2, 2, rows, cut)] * count
    scratch = [pltpu.SemaphoreType.DMA((2 * count,))]
    return call(kernel, mine + [theirs], outs, scratch, "both_rows")


def head_parts(own, paired, which, turns, after):
    _, peers, rows, cut = own.shape
    chosen = pl.ds(which, 2)

    def kernel(own_ref, pair_ref, *refs):
        outs, sems = refs[len(after):-1], refs[-1]
        p, s = lax.axis_index("pair"), lax.axis_index("sub")
        moves = []
        for by, out in zip(turns, outs):
            at = lax.rem(s + by, peers)
            moves += [(own_ref.at[chosen, at], out.at[:, p]), (pair_ref.at[chosen, at], out.at[:, 1 - p])]
        run_moves(moves, sems)

    outs = [shape(2, 2, rows, cut)] * len(turns)
    scratch = [pltpu.SemaphoreType.DMA((2 * len(turns),))]
    return call(kernel, [own, paired] + after, outs, scratch, "head_parts")


def relayed(value, after):
    def kernel(value_ref, *refs):
        run_moves([(value_ref, refs[-2])], refs[-1])

    scratch = [pltpu.SemaphoreType.DMA((1,))]
    return call(kernel, [value] + after, [shape(*value.shape)], scratch, "relayed")[0]


def attention_grads(bias, kv, kv_earlier, qg, split, first, heads, after):
    peers = len(kv)
    rows, cut = kv[0].shape[2], heads * HD
    chosen = pl.ds(first * HD, cut)
    strip = rows * peers
    early_count = peers if split else 1

    def kernel(*refs):
        bias_ref = refs[0]
        kv_in, early_in, qg_in = refs[1:1 + peers], refs[1 + peers:1 + 2 * peers], refs[1 + 2 * peers:1 + 3 * peers]
        outs = refs[1 + 3 * peers + len(after):-5]
        own_out, dq_outs, early_outs = outs[0], outs[1:1 + peers], outs[1 + peers:]
        kv_all, qg_all, early, dq_all, sems = refs[-5:]
        s = lax.axis_index("sub")
        moves = []
        for by in range(peers):
            at = lax.rem(s - by + peers, peers)
            moves += [
                (early_in[by].at[:, :, :, chosen], kv_all.at[:, 0:2, at]),
                (kv_in[by].at[:, :, :, chosen], kv_all.at[:, 2:4, at]),
                (qg_in[by].at[:, :, :, chosen], qg_all.at[:, :, at]),
            ]
        run_moves(moves, sems)
        strips = [(head, tile) for head in range(heads) for tile in range(2)]
        products, terms = {}, {}

        def flat(ref, which, tiles, head):
            block = ref[which, tiles, :, :, pl.ds(head * HD, HD)]
            return block.reshape(block.shape[0] * strip, HD)

        def multiply(head, tile):
            at, span = pl.ds(tile, 1), pl.ds(tile, 3)
            q, g = flat(qg_all, 0, at, head), flat(qg_all, 1, at, head)
            k, v = flat(kv_all, 0, span, head), flat(kv_all, 1, span, head)
            scores = lax.dot_general(k, q, ROWS_BY_ROWS, preferred_element_type=WIDE)
            grad_prob = lax.dot_general(v, g, ROWS_BY_ROWS, preferred_element_type=WIDE)
            products[head, tile] = q, g, k, scores, grad_prob

        def finish(head, tile):
            q, g, k, scores, grad_prob = products.pop((head, tile))
            scores = scores * TO_BITS + bias_ref[tile]
            peak = jnp.max(scores, axis=0, keepdims=True)
            weight = jnp.exp2(scores - peak)
            prob = weight * (1.0 / jnp.sum(weight, axis=0, keepdims=True))
            prob_low = prob.astype(LOW)
            row_dot = jnp.sum(prob_low.astype(WIDE) * grad_prob, axis=0, keepdims=True)
            score_low = (prob * (grad_prob - row_dot)).astype(LOW)
            dq = jnp.dot(k.T, score_low, preferred_element_type=WIDE) * SCALE
            dq_all[tile, :, :, pl.ds(head * HD, HD)] = dq.T.astype(LOW).reshape(peers, rows, HD)
            dk = jnp.dot(score_low, q, preferred_element_type=WIDE) * SCALE
            dv = jnp.dot(prob_low, g, preferred_element_type=WIDE)
            terms[head, tile] = dk, dv

        def gather(head):
            for which in range(2):
                low, high = terms[head, 0][which], terms[head, 1][which]
                sums = (
                    low[:strip],
                    low[strip:2 * strip] + high[:strip],
                    low[2 * strip:] + high[strip:2 * strip],
                    high[2 * strip:],
                )
                for tile, total in enumerate(sums):
                    total = total.reshape(peers, rows, HD)
                    if tile < 2:
                        early[which, tile, :, :, pl.ds(head * HD, HD)] = total.astype(LOW)
                    else:
                        own_out[which, tile - 2, :, :, pl.ds(head * HD, HD)] = total

        multiply(*strips[0])
        for at, (head, tile) in enumerate(strips):
            if at + 1 < len(strips):
                multiply(*strips[at + 1])
            finish(head, tile)
            if tile == 1:
                gather(head)
        moves = [] if split else [(early, early_outs[0])]
        for by in range(peers):
            at = lax.rem(s + by, peers)
            moves.append((dq_all.at[:, at], dq_outs[by]))
            if split:
                moves.append((early.at[:, :, at], early_outs[by]))
        run_moves(moves, sems)

    outs = [shape(2, 2, peers, rows, cut, dtype=WIDE)] + [shape(2, rows, cut)] * peers
    outs += [shape(2, 2, rows, cut)] * peers if split else [shape(2, 2, peers, rows, cut)]
    scratch = [
        pltpu.VMEM((2, 4, peers, rows, cut), LOW),
        pltpu.VMEM((2, 2, peers, rows, cut), LOW),
        pltpu.VMEM((2, 2, peers, rows, cut), LOW),
        pltpu.VMEM((2, peers, rows, cut), LOW),
        pltpu.SemaphoreType.DMA((3 * peers,)),
    ]
    flops = heads * 2 * 5 * 2 * strip * 3 * strip * HD
    ins = [bias] + kv + kv_earlier + qg + after
    outs = call(kernel, ins, outs, scratch, "attention_grads", whole=True, flops=flops, room=40 * MIB)
    return outs[0], outs[1:1 + peers], outs[1 + peers:]


def summed(own, later, turns, after):
    _, _, peers, rows, _ = own[0].shape
    widths = [array.shape[-1] for array in own]
    split = later[0].ndim == 4

    def kernel(*refs):
        own_refs, later_refs = refs[:len(own)], refs[len(own):len(own) + len(later)]
        outs = refs[len(own) + len(later) + len(after):]
        s = lax.axis_index("sub")
        for place, (by, out) in enumerate(zip(turns, outs)):
            at = lax.rem(s + by, peers)
            start = 0
            for group, width in enumerate(widths):
                for which in range(2):
                    for row in range(2):
                        term = later_refs[place][which, row] if split else later_refs[group][which, row, at]
                        total = own_refs[group][which, row, at] + term.astype(WIDE)
                        out[which, row, :, pl.ds(start, width)] = total.astype(LOW)
                start += width

    outs = [shape(2, 2, rows, sum(widths))] * len(turns)
    return call(kernel, own + later + after, outs, [], "summed", whole=True)


def side_by_side(groups):
    count, peers = len(groups), len(groups[0])
    _, rows, _ = groups[0][0].shape
    widths = [group[0].shape[-1] for group in groups]

    def kernel(*refs):
        for by in range(peers):
            start = 0
            for group, width in enumerate(widths):
                refs[count * peers + by][:, :, pl.ds(start, width)] = refs[group * peers + by][...]
                start += width

    ins = [array for group in groups for array in group]
    return call(kernel, ins, [shape(2, rows, sum(widths))] * peers, [], "side_by_side", whole=True)


def rows_for_pair(dq, dkv):
    peers = len(dq)
    _, rows, cut = dq[0].shape

    def kernel(*refs):
        dq_refs, dkv_refs, (send, keep) = refs[:peers], refs[peers:2 * peers], refs[-2:]
        p, s = lax.axis_index("pair"), lax.axis_index("sub")
        for by in range(peers):
            at = lax.rem(s - by + peers, peers)
            for out, row in ((send, 1 - p), (keep, p)):
                out[0, at] = dq_refs[by][row]
                for which in range(2):
                    out[1 + which, at] = dkv_refs[by][which, row]

    outs = [shape(3, peers, rows, cut)] * 2
    return call(kernel, dq + dkv, outs, [], "rows_for_pair", whole=True)


def laid_out(kept, paired, spans):
    _, peers, rows, _ = kept[0].shape
    part = spans[-1][1]
    half = part * peers
    count = len(spans)

    def kernel(*refs):
        keep, rec, outs, sems = refs[:count], refs[count:2 * count], refs[2 * count:-1], refs[-1]
        p = lax.axis_index("pair")
        moves = []
        for mine, theirs, (low, high) in zip(keep, rec, spans):
            for source, side in ((mine, p), (theirs, 1 - p)):
                for at in range(peers):
                    columns = pl.ds(pl.multiple_of(side * half + at * part + low, HD), high - low)
                    moves += [(source.at[which, at], out.at[:, columns]) for which, out in enumerate(outs)]
        run_moves(moves, sems)

    outs = [shape(rows, 2 * half)] * 3
    return call(kernel, kept + paired, outs, [pltpu.SemaphoreType.DMA((6 * count * peers,))], "laid_out")


def allowed_bias(session, rows):
    strip = rows * lax.axis_size("sub")
    block = 2 * strip
    at_block = lax.axis_index("blk")
    window = jnp.concatenate([jnp.zeros((block,), jnp.int32), session])
    sess = lax.dynamic_slice_in_dim(window, at_block * block, 2 * block)
    place = (at_block - 1) * block + jnp.arange(2 * block, dtype=jnp.int32)

    def tile_bias(tile):
        q_at = slice(block + tile * strip, block + (tile + 1) * strip)
        k_at = slice(tile * strip, (tile + 3) * strip)
        k_place, q_place = place[k_at, None], place[None, q_at]
        allowed = (sess[None, q_at] == sess[k_at, None]) & (k_place <= q_place) & (k_place >= 0)
        return jnp.where(allowed, 0.0, NEG_FILL)

    return jnp.stack([tile_bias(0), tile_bias(1)])


def shards(queries, keys, values, out_grad, session):
    peers = lax.axis_size("sub")
    others = list(range(1, peers))
    part = queries.shape[1] // (2 * peers)
    spans, at = [], 0
    for heads in chunks_of(part // HD):
        spans.append((at, at + heads * HD))
        at += heads * HD
    bias = allowed_bias(session, queries.shape[0])
    kv_far, near_send, near_keep = first_keys([keys, values], *spans[0])
    kv_far = [round_sub(value, by) for by, value in zip(others, kv_far)]
    rest = [([queries, out_grad], *spans[0])] + [([keys, values, queries, out_grad], *span) for span in spans[1:]]
    rest = first_parts(rest, [near_keep])
    near_theirs = swapped(near_send)
    kv_parts = [None]
    qg_parts = [(rest[0][1], swapped(rest[0][0]), 0)]
    for send, own in rest[1:]:
        paired = swapped(send)
        kv_parts.append((own, paired, 0))
        qg_parts.append((own, paired, 2))
    count = len(spans)
    kv_sends, qg_sends, kv, qg, kv_own, own_earlier = [], [], [], [], [], []
    for index in range(count):
        if index:
            kv_sends.append(head_parts(*kv_parts[index], others, kv[index - 1] + own_earlier[index - 1:index]))
            kv.append([round_sub(value, by) for by, value in zip(others, kv_sends[index])])
            kv_own.append(head_parts(*kv_parts[index], [0], own_earlier[index - 1:index]))
        else:
            kv_sends.append([])
            kv_own.append(both_rows([near_keep], near_theirs.reshape(1, *near_theirs.shape)))
            kv.append(both_rows(kv_far, swapped(other_side(kv_far))))
        own_earlier.append(along_blocks(kv_own[index][0], 1, True))
        qg_sends.append(head_parts(*qg_parts[index], others, qg[index - 1] if index else []))
        qg.append([round_sub(value, by) for by, value in zip(others, qg_sends[index])])
    kept, paired, first_dq, back = [], [], [], []
    for index, (low, high) in enumerate(spans):
        last = index == count - 1
        forward = [relayed(value, first_dq) if index else value for value in kv[index]]
        earlier = [own_earlier[index]] + [along_blocks(value, 1, not last) for value in forward]
        qg_all = head_parts(*qg_parts[index], [0], []) + qg[index]
        kv_all = kv_own[index] + kv[index]
        heads = (high - low) // HD
        if last:
            grads, dq, early = attention_grads(bias, kv_all, earlier, qg_all, True, 0, heads, back)
            dq = [dq[0]] + [round_sub(dq[by], by) for by in others]
            later = [along_blocks(value, -1, False) for value in early[1:]]
            dkv = summed([grads], later, others, dq[1:])
            near = along_blocks(relayed(early[0], dq[1:]), -1, False)
            dkv = summed([grads], [near], [0], []) + [round_sub(value, by) for by, value in zip(others, dkv)]
        else:
            groups, turn = [], []
            for head in range(heads):
                groups.append(attention_grads(bias, kv_all, earlier, qg_all, False, head, 1, turn))
                turn = groups[-1][1][:1]
                first_dq = first_dq or turn
            later = [along_blocks(early[0], -1, False) for _, _, early in groups]
            dq = side_by_side([dq for _, dq, _ in groups]) if heads > 1 else groups[0][1]
            dq = [dq[0]] + [round_sub(dq[by], by) for by in others]
            back = later[:1] + dq[1:]
            dkv = summed([grads for grads, _, _ in groups], later, [0] + others, dq[1:])
            dkv = [dkv[0]] + [round_sub(dkv[by], by) for by in others]
        send, keep = rows_for_pair(dq, dkv)
        kept.append(keep)
        paired.append(swapped(send))
    return tuple(laid_out(kept, paired, spans))


def solution(mesh):
    spread = P(("grp", "blk", "pair", "sub"), None)
    return jax.shard_map(
        shards, mesh=mesh, in_specs=(spread,) * 4 + (P("grp"),), out_specs=(spread,) * 3, check_vma=False
    )
```

```python
import math

import jax
import jax.numpy as jnp
from jax import lax
from jax.experimental import pallas as pl
from jax.experimental.pallas import tpu as pltpu
from jax.sharding import PartitionSpec as P

HD = 128
NEG_FILL = -1e30
LOW = jnp.bfloat16
WIDE = jnp.float32
MIB = 1024 * 1024
TO_BITS = HD ** (-0.5) / math.log(2.0)
SCALE = HD ** (-0.5)
ROWS_BY_ROWS = (((1,), (1,)), ((), ()))


def chunks_of(heads):
    return [heads // 2, heads - heads // 2]


def along_blocks(value, by, ring):
    peers = lax.axis_size("blk")
    pairs = [(i, (i + by) % peers) for i in range(peers) if ring or 0 <= i + by < peers]
    return lax.ppermute(value, "blk", pairs)


def round_sub(value, by):
    peers = lax.axis_size("sub")
    return lax.ppermute(value, "sub", [(i, (i + by) % peers) for i in range(peers)])


def swapped(value):
    return lax.ppermute(value, "pair", [(0, 1), (1, 0)])


def run_moves(moves, sems):
    copies = [pltpu.make_async_copy(src, dst, sems.at[at]) for at, (src, dst) in enumerate(moves)]
    for copy in copies:
        copy.start()
    for copy in copies:
        copy.wait()


def call(kernel, ins, outs, scratch, name, whole=False, flops=0, room=8 * MIB):
    spec = pl.BlockSpec(memory_space=pltpu.VMEM if whole else pl.ANY)
    moved = sum(math.prod(a.shape) * a.dtype.itemsize for a in list(ins) + list(outs))
    return list(
        pl.pallas_call(
            kernel,
            out_shape=outs,
            in_specs=[spec] * len(ins),
            out_specs=[spec] * len(outs),
            scratch_shapes=scratch,
            name=name,
            cost_estimate=pl.CostEstimate(flops=flops, bytes_accessed=moved, transcendentals=0),
            compiler_params=pltpu.CompilerParams(vmem_limit_bytes=room),
        )(*ins)
    )


def shape(*dims, dtype=LOW):
    return jax.ShapeDtypeStruct(dims, dtype)


def first_parts(groups, after):
    held, wanted, outs = [], [], []
    for arrays, low, high in groups:
        rows, width = arrays[0].shape
        peers = lax.axis_size("sub")
        half = width // 2
        part = half // peers
        wanted.append((len(held), len(arrays), low, high))
        held += [pltpu.with_memory_space_constraint(array, pltpu.HBM) for array in arrays]
        outs += [pltpu.VMEM((len(arrays), peers, rows, high - low), LOW)] * 2

    def kernel(*refs):
        out_refs, sems = refs[-1 - len(outs):-1], refs[-1]
        p = lax.axis_index("pair")
        moves = []
        for group, (first, count, low, high) in enumerate(wanted):
            for side, out in zip((1 - p, p), out_refs[2 * group:2 * group + 2]):
                for at in range(peers):
                    start = pl.multiple_of(side * half + at * part + low, HD)
                    for i in range(count):
                        moves.append((refs[first + i].at[:, pl.ds(start, high - low)], out.at[i, at]))
        run_moves(moves, sems)

    spec = pl.BlockSpec(memory_space=pl.ANY)
    parts = pl.pallas_call(
        kernel,
        out_shape=outs,
        in_specs=[spec] * (len(held) + len(after)),
        out_specs=[spec] * len(outs),
        scratch_shapes=[pltpu.SemaphoreType.DMA((2 * peers * len(held),))],
        name="first_parts",
        compiler_params=pltpu.CompilerParams(vmem_limit_bytes=8 * MIB),
    )(*held, *after)
    return [(parts[2 * i], parts[2 * i + 1]) for i in range(len(groups))]


def first_keys(arrays, low, high):
    rows, width = arrays[0].shape
    half = width // 2
    peers = lax.axis_size("sub")
    part = half // peers
    cut = high - low

    def kernel(*refs):
        ins, far, (send, keep), sems = refs[:2], refs[2:1 + peers], refs[1 + peers:-1], refs[-1]
        p, s = lax.axis_index("pair"), lax.axis_index("sub")
        moves = []
        for i, ref in enumerate(ins):
            for by in range(1, peers):
                for side in range(2):
                    start = pl.multiple_of(side * half + lax.rem(s + by, peers) * part + low, HD)
                    moves.append((ref.at[:, pl.ds(start, cut)], far[by - 1].at[i, side]))
            for out, side in ((send, 1 - p), (keep, p)):
                start = pl.multiple_of(side * half + s * part + low, HD)
                moves.append((ref.at[:, pl.ds(start, cut)], out.at[i]))
        run_moves(moves, sems)

    spec = pl.BlockSpec(memory_space=pl.ANY)
    outs = [pltpu.VMEM((2, 2, rows, cut), LOW)] * (peers - 1) + [pltpu.VMEM((2, rows, cut), LOW)] * 2
    parts = pl.pallas_call(
        kernel,
        out_shape=outs,
        in_specs=[spec] * 2,
        out_specs=[spec] * len(outs),
        scratch_shapes=[pltpu.SemaphoreType.DMA((4 * peers,))],
        name="first_keys",
        compiler_params=pltpu.CompilerParams(vmem_limit_bytes=8 * MIB),
    )(*[pltpu.with_memory_space_constraint(array, pltpu.HBM) for array in arrays])
    return list(parts[:-2]), parts[-2], parts[-1]


def other_side(received):
    count = len(received)

    def kernel(*refs):
        p = lax.axis_index("pair")
        run_moves([(ref.at[:, 1 - p], refs[-2].at[by]) for by, ref in enumerate(refs[:count])], refs[-1])

    _, _, rows, cut = received[0].shape
    scratch = [pltpu.SemaphoreType.DMA((count,))]
    return call(kernel, received, [shape(count, 2, rows, cut)], scratch, "other_side")[0]


def both_rows(mine, theirs):
    count = len(mine)
    _, _, rows, cut = theirs.shape

    def kernel(*refs):
        ins, theirs_ref, outs, sems = refs[:count], refs[count], refs[count + 1:-1], refs[-1]
        p = lax.axis_index("pair")
        moves = []
        for by, (ref, out) in enumerate(zip(ins, outs)):
            source = ref.at[:, p] if len(ref.shape) == 4 else ref
            moves += [(source, out.at[:, p]), (theirs_ref.at[by], out.at[:, 1 - p])]
        run_moves(moves, sems)

    outs = [shape(2, 2, rows, cut)] * count
    scratch = [pltpu.SemaphoreType.DMA((2 * count,))]
    return call(kernel, mine + [theirs], outs, scratch, "both_rows")


def head_parts(own, paired, which, turns, after):
    _, peers, rows, cut = own.shape
    chosen = pl.ds(which, 2)

    def kernel(own_ref, pair_ref, *refs):
        outs, sems = refs[len(after):-1], refs[-1]
        p, s = lax.axis_index("pair"), lax.axis_index("sub")
        moves = []
        for by, out in zip(turns, outs):
            at = lax.rem(s + by, peers)
            moves += [(own_ref.at[chosen, at], out.at[:, p]), (pair_ref.at[chosen, at], out.at[:, 1 - p])]
        run_moves(moves, sems)

    outs = [shape(2, 2, rows, cut)] * len(turns)
    scratch = [pltpu.SemaphoreType.DMA((2 * len(turns),))]
    return call(kernel, [own, paired] + after, outs, scratch, "head_parts")


def relayed(value, after):
    def kernel(value_ref, *refs):
        run_moves([(value_ref, refs[-2])], refs[-1])

    scratch = [pltpu.SemaphoreType.DMA((1,))]
    return call(kernel, [value] + after, [shape(*value.shape)], scratch, "relayed")[0]


def attention_grads(bias, kv, kv_earlier, qg, split, first, heads, after):
    peers = len(kv)
    rows, cut = kv[0].shape[2], heads * HD
    chosen = pl.ds(first * HD, cut)
    strip = rows * peers
    early_count = peers if split else 1

    def kernel(*refs):
        bias_ref = refs[0]
        kv_in, early_in, qg_in = refs[1:1 + peers], refs[1 + peers:1 + 2 * peers], refs[1 + 2 * peers:1 + 3 * peers]
        outs = refs[1 + 3 * peers + len(after):-5]
        own_out, dq_outs, early_outs = outs[0], outs[1:1 + peers], outs[1 + peers:]
        kv_all, qg_all, early, dq_all, sems = refs[-5:]
        s = lax.axis_index("sub")
        moves = []
        for by in range(peers):
            at = lax.rem(s - by + peers, peers)
            moves += [
                (early_in[by].at[:, :, :, chosen], kv_all.at[:, 0:2, at]),
                (kv_in[by].at[:, :, :, chosen], kv_all.at[:, 2:4, at]),
                (qg_in[by].at[:, :, :, chosen], qg_all.at[:, :, at]),
            ]
        run_moves(moves, sems)
        strips = [(head, tile) for head in range(heads) for tile in range(2)]
        products, terms = {}, {}

        def flat(ref, which, tiles, head):
            block = ref[which, tiles, :, :, pl.ds(head * HD, HD)]
            return block.reshape(block.shape[0] * strip, HD)

        def multiply(head, tile):
            at, span = pl.ds(tile, 1), pl.ds(tile, 3)
            q, g = flat(qg_all, 0, at, head), flat(qg_all, 1, at, head)
            k, v = flat(kv_all, 0, span, head), flat(kv_all, 1, span, head)
            scores = lax.dot_general(k, q, ROWS_BY_ROWS, preferred_element_type=WIDE)
            grad_prob = lax.dot_general(v, g, ROWS_BY_ROWS, preferred_element_type=WIDE)
            products[head, tile] = q, g, k, scores, grad_prob

        def finish(head, tile):
            q, g, k, scores, grad_prob = products.pop((head, tile))
            scores = scores * TO_BITS + bias_ref[tile]
            peak = jnp.max(scores, axis=0, keepdims=True)
            weight = jnp.exp2(scores - peak)
            prob = weight * (1.0 / jnp.sum(weight, axis=0, keepdims=True))
            prob_low = prob.astype(LOW)
            row_dot = jnp.sum(prob_low.astype(WIDE) * grad_prob, axis=0, keepdims=True)
            score_low = (prob * (grad_prob - row_dot)).astype(LOW)
            dq = jnp.dot(k.T, score_low, preferred_element_type=WIDE) * SCALE
            dq_all[tile, :, :, pl.ds(head * HD, HD)] = dq.T.astype(LOW).reshape(peers, rows, HD)
            dk = jnp.dot(score_low, q, preferred_element_type=WIDE) * SCALE
            dv = jnp.dot(prob_low, g, preferred_element_type=WIDE)
            terms[head, tile] = dk, dv

        def gather(head):
            for which in range(2):
                low, high = terms[head, 0][which], terms[head, 1][which]
                sums = (
                    low[:strip],
                    low[strip:2 * strip] + high[:strip],
                    low[2 * strip:] + high[strip:2 * strip],
                    high[2 * strip:],
                )
                for tile, total in enumerate(sums):
                    total = total.reshape(peers, rows, HD)
                    if tile < 2:
                        early[which, tile, :, :, pl.ds(head * HD, HD)] = total.astype(LOW)
                    else:
                        own_out[which, tile - 2, :, :, pl.ds(head * HD, HD)] = total

        multiply(*strips[0])
        for at, (head, tile) in enumerate(strips):
            if at + 1 < len(strips):
                multiply(*strips[at + 1])
            finish(head, tile)
            if tile == 1:
                gather(head)
        moves = [] if split else [(early, early_outs[0])]
        for by in range(peers):
            at = lax.rem(s + by, peers)
            moves.append((dq_all.at[:, at], dq_outs[by]))
            if split:
                moves.append((early.at[:, :, at], early_outs[by]))
        run_moves(moves, sems)

    outs = [shape(2, 2, peers, rows, cut, dtype=WIDE)] + [shape(2, rows, cut)] * peers
    outs += [shape(2, 2, rows, cut)] * peers if split else [shape(2, 2, peers, rows, cut)]
    scratch = [
        pltpu.VMEM((2, 4, peers, rows, cut), LOW),
        pltpu.VMEM((2, 2, peers, rows, cut), LOW),
        pltpu.VMEM((2, 2, peers, rows, cut), LOW),
        pltpu.VMEM((2, peers, rows, cut), LOW),
        pltpu.SemaphoreType.DMA((3 * peers,)),
    ]
    flops = heads * 2 * 5 * 2 * strip * 3 * strip * HD
    ins = [bias] + kv + kv_earlier + qg + after
    outs = call(kernel, ins, outs, scratch, "attention_grads", whole=True, flops=flops, room=40 * MIB)
    return outs[0], outs[1:1 + peers], outs[1 + peers:]


def summed(own, later, turns, after):
    _, _, peers, rows, _ = own[0].shape
    widths = [array.shape[-1] for array in own]
    split = later[0].ndim == 4

    def kernel(*refs):
        own_refs, later_refs = refs[:len(own)], refs[len(own):len(own) + len(later)]
        outs = refs[len(own) + len(later) + len(after):]
        s = lax.axis_index("sub")
        for place, (by, out) in enumerate(zip(turns, outs)):
            at = lax.rem(s + by, peers)
            start = 0
            for group, width in enumerate(widths):
                for which in range(2):
                    for row in range(2):
                        term = later_refs[place][which, row] if split else later_refs[group][which, row, at]
                        total = own_refs[group][which, row, at] + term.astype(WIDE)
                        out[which, row, :, pl.ds(start, width)] = total.astype(LOW)
                start += width

    outs = [shape(2, 2, rows, sum(widths))] * len(turns)
    return call(kernel, own + later + after, outs, [], "summed", whole=True)


def rows_for_pair(dq, dkv):
    peers = len(dq)
    _, rows, cut = dq[0].shape

    def kernel(*refs):
        dq_refs, dkv_refs, (send, keep) = refs[:peers], refs[peers:2 * peers], refs[-2:]
        p, s = lax.axis_index("pair"), lax.axis_index("sub")
        for by in range(peers):
            at = lax.rem(s - by + peers, peers)
            for out, row in ((send, 1 - p), (keep, p)):
                out[0, at] = dq_refs[by][row]
                for which in range(2):
                    out[1 + which, at] = dkv_refs[by][which, row]

    outs = [shape(3, peers, rows, cut)] * 2
    return call(kernel, dq + dkv, outs, [], "rows_for_pair", whole=True)


def laid_out(kept, paired, spans):
    _, peers, rows, _ = kept[0].shape
    part = spans[-1][1]
    half = part * peers
    count = len(spans)

    def kernel(*refs):
        keep, rec, outs, sems = refs[:count], refs[count:2 * count], refs[2 * count:-1], refs[-1]
        p = lax.axis_index("pair")
        moves = []
        for mine, theirs, (low, high) in zip(keep, rec, spans):
            for source, side in ((mine, p), (theirs, 1 - p)):
                for at in range(peers):
                    columns = pl.ds(pl.multiple_of(side * half + at * part + low, HD), high - low)
                    moves += [(source.at[which, at], out.at[:, columns]) for which, out in enumerate(outs)]
        run_moves(moves, sems)

    outs = [shape(rows, 2 * half)] * 3
    return call(kernel, kept + paired, outs, [pltpu.SemaphoreType.DMA((6 * count * peers,))], "laid_out")


def allowed_bias(session, rows):
    strip = rows * lax.axis_size("sub")
    block = 2 * strip
    at_block = lax.axis_index("blk")
    window = jnp.concatenate([jnp.zeros((block,), jnp.int32), session])
    sess = lax.dynamic_slice_in_dim(window, at_block * block, 2 * block)
    place = (at_block - 1) * block + jnp.arange(2 * block, dtype=jnp.int32)

    def tile_bias(tile):
        q_at = slice(block + tile * strip, block + (tile + 1) * strip)
        k_at = slice(tile * strip, (tile + 3) * strip)
        k_place, q_place = place[k_at, None], place[None, q_at]
        allowed = (sess[None, q_at] == sess[k_at, None]) & (k_place <= q_place) & (k_place >= 0)
        return jnp.where(allowed, 0.0, NEG_FILL)

    return jnp.stack([tile_bias(0), tile_bias(1)])


def shards(queries, keys, values, out_grad, session):
    peers = lax.axis_size("sub")
    others = list(range(1, peers))
    part = queries.shape[1] // (2 * peers)
    spans, at = [], 0
    for heads in chunks_of(part // HD):
        spans.append((at, at + heads * HD))
        at += heads * HD
    bias = allowed_bias(session, queries.shape[0])
    kv_far, near_send, near_keep = first_keys([keys, values], *spans[0])
    kv_far = [round_sub(value, by) for by, value in zip(others, kv_far)]
    rest = [([queries, out_grad], *spans[0])] + [([keys, values, queries, out_grad], *span) for span in spans[1:]]
    rest = first_parts(rest, [near_keep])
    near_theirs = swapped(near_send)
    kv_parts = [None]
    qg_parts = [(rest[0][1], swapped(rest[0][0]), 0)]
    for send, own in rest[1:]:
        paired = swapped(send)
        kv_parts.append((own, paired, 0))
        qg_parts.append((own, paired, 2))
    count = len(spans)
    kv_sends, qg_sends, kv, qg, kv_own, own_earlier = [], [], [], [], [], []
    for index in range(count):
        if index:
            kv_sends.append(head_parts(*kv_parts[index], others, kv[index - 1] + own_earlier[index - 1:index]))
            kv.append([round_sub(value, by) for by, value in zip(others, kv_sends[index])])
            kv_own.append(head_parts(*kv_parts[index], [0], own_earlier[index - 1:index]))
        else:
            kv_sends.append([])
            kv_own.append(both_rows([near_keep], near_theirs.reshape(1, *near_theirs.shape)))
            kv.append(both_rows(kv_far, swapped(other_side(kv_far))))
        own_earlier.append(along_blocks(kv_own[index][0], 1, True))
        qg_sends.append(head_parts(*qg_parts[index], others, qg[index - 1] if index else []))
        qg.append([round_sub(value, by) for by, value in zip(others, qg_sends[index])])
    kept, paired, first_dq, back, release = [], [], [], [], []
    for index, (low, high) in enumerate(spans):
        last = index == count - 1
        forward = [relayed(value, first_dq) if index else value for value in kv[index]]
        earlier = [own_earlier[index]] + [along_blocks(value, 1, not last) for value in forward]
        qg_all = head_parts(*qg_parts[index], [0], []) + qg[index]
        kv_all = kv_own[index] + kv[index]
        heads = (high - low) // HD
        if last:
            grads, dq, early = attention_grads(bias, kv_all, earlier, qg_all, True, 0, heads, back)
            dq = [dq[0]] + [round_sub(dq[by], by) for by in others]
            later = [along_blocks(value, -1, False) for value in early[1:]]
            dkv = summed([grads], later, others, dq[1:])
            near = along_blocks(relayed(early[0], release), -1, False)
            dkv = summed([grads], [near], [0], []) + [round_sub(value, by) for by, value in zip(others, dkv)]
        else:
            grads, dq, early = attention_grads(bias, kv_all, earlier, qg_all, False, 0, heads, [])
            first_dq = dq[:1]
            dq = [dq[0]] + [round_sub(dq[by], by) for by in others]
            back = dq[1:]
            dkv = summed([grads], [along_blocks(early[0], -1, False)], [0] + others, dq[1:])
            release = dkv[:1]
            dkv = [dkv[0]] + [round_sub(dkv[by], by) for by in others]
        send, keep = rows_for_pair(dq, dkv)
        kept.append(keep)
        paired.append(swapped(send))
    return tuple(laid_out(kept, paired, spans))


def solution(mesh):
    spread = P(("grp", "blk", "pair", "sub"), None)
    return jax.shard_map(
        shards, mesh=mesh, in_specs=(spread,) * 4 + (P("grp"),), out_specs=(spread,) * 3, check_vma=False
    )
```

```python
import math

import jax
import jax.numpy as jnp
from jax import lax
from jax.experimental import pallas as pl
from jax.experimental.pallas import tpu as pltpu
from jax.sharding import PartitionSpec as P

HD = 128
NEG_FILL = -1e30
LOW = jnp.bfloat16
WIDE = jnp.float32
MIB = 1024 * 1024
TO_BITS = HD ** (-0.5) / math.log(2.0)
SCALE = HD ** (-0.5)
ROWS_BY_ROWS = (((1,), (1,)), ((), ()))


def chunks_of(heads):
    return [heads // 2, heads - heads // 2]


def along_blocks(value, by, ring):
    peers = lax.axis_size("blk")
    pairs = [(i, (i + by) % peers) for i in range(peers) if ring or 0 <= i + by < peers]
    return lax.ppermute(value, "blk", pairs)


def round_sub(value, by):
    peers = lax.axis_size("sub")
    return lax.ppermute(value, "sub", [(i, (i + by) % peers) for i in range(peers)])


def swapped(value):
    return lax.ppermute(value, "pair", [(0, 1), (1, 0)])


def run_moves(moves, sems):
    copies = [pltpu.make_async_copy(src, dst, sems.at[at]) for at, (src, dst) in enumerate(moves)]
    for copy in copies:
        copy.start()
    for copy in copies:
        copy.wait()


def call(kernel, ins, outs, scratch, name, whole=False, flops=0, room=8 * MIB):
    spec = pl.BlockSpec(memory_space=pltpu.VMEM if whole else pl.ANY)
    moved = sum(math.prod(a.shape) * a.dtype.itemsize for a in list(ins) + list(outs))
    return list(
        pl.pallas_call(
            kernel,
            out_shape=outs,
            in_specs=[spec] * len(ins),
            out_specs=[spec] * len(outs),
            scratch_shapes=scratch,
            name=name,
            cost_estimate=pl.CostEstimate(flops=flops, bytes_accessed=moved, transcendentals=0),
            compiler_params=pltpu.CompilerParams(vmem_limit_bytes=room),
        )(*ins)
    )


def shape(*dims, dtype=LOW):
    return jax.ShapeDtypeStruct(dims, dtype)


def first_parts(groups, after):
    held, wanted, outs = [], [], []
    for arrays, low, high in groups:
        rows, width = arrays[0].shape
        peers = lax.axis_size("sub")
        half = width // 2
        part = half // peers
        wanted.append((len(held), len(arrays), low, high))
        held += [pltpu.with_memory_space_constraint(array, pltpu.HBM) for array in arrays]
        outs += [pltpu.VMEM((len(arrays), peers, rows, high - low), LOW)] * 2

    def kernel(*refs):
        out_refs, sems = refs[-1 - len(outs):-1], refs[-1]
        p = lax.axis_index("pair")
        moves = []
        for group, (first, count, low, high) in enumerate(wanted):
            for side, out in zip((1 - p, p), out_refs[2 * group:2 * group + 2]):
                for at in range(peers):
                    start = pl.multiple_of(side * half + at * part + low, HD)
                    for i in range(count):
                        moves.append((refs[first + i].at[:, pl.ds(start, high - low)], out.at[i, at]))
        run_moves(moves, sems)

    spec = pl.BlockSpec(memory_space=pl.ANY)
    parts = pl.pallas_call(
        kernel,
        out_shape=outs,
        in_specs=[spec] * (len(held) + len(after)),
        out_specs=[spec] * len(outs),
        scratch_shapes=[pltpu.SemaphoreType.DMA((2 * peers * len(held),))],
        name="first_parts",
        compiler_params=pltpu.CompilerParams(vmem_limit_bytes=8 * MIB),
    )(*held, *after)
    return [(parts[2 * i], parts[2 * i + 1]) for i in range(len(groups))]


def first_keys(arrays, low, high):
    rows, width = arrays[0].shape
    half = width // 2
    peers = lax.axis_size("sub")
    part = half // peers
    cut = high - low

    def kernel(*refs):
        ins, far, (send, keep), sems = refs[:2], refs[2:1 + peers], refs[1 + peers:-1], refs[-1]
        p, s = lax.axis_index("pair"), lax.axis_index("sub")
        moves = []
        for i, ref in enumerate(ins):
            for by in range(1, peers):
                for side in range(2):
                    start = pl.multiple_of(side * half + lax.rem(s + by, peers) * part + low, HD)
                    moves.append((ref.at[:, pl.ds(start, cut)], far[by - 1].at[i, side]))
            for out, side in ((send, 1 - p), (keep, p)):
                start = pl.multiple_of(side * half + s * part + low, HD)
                moves.append((ref.at[:, pl.ds(start, cut)], out.at[i]))
        run_moves(moves, sems)

    spec = pl.BlockSpec(memory_space=pl.ANY)
    outs = [pltpu.VMEM((2, 2, rows, cut), LOW)] * (peers - 1) + [pltpu.VMEM((2, rows, cut), LOW)] * 2
    parts = pl.pallas_call(
        kernel,
        out_shape=outs,
        in_specs=[spec] * 2,
        out_specs=[spec] * len(outs),
        scratch_shapes=[pltpu.SemaphoreType.DMA((4 * peers,))],
        name="first_keys",
        compiler_params=pltpu.CompilerParams(vmem_limit_bytes=8 * MIB),
    )(*[pltpu.with_memory_space_constraint(array, pltpu.HBM) for array in arrays])
    return list(parts[:-2]), parts[-2], parts[-1]


def other_side(received):
    count = len(received)

    def kernel(*refs):
        p = lax.axis_index("pair")
        run_moves([(ref.at[:, 1 - p], refs[-2].at[by]) for by, ref in enumerate(refs[:count])], refs[-1])

    _, _, rows, cut = received[0].shape
    scratch = [pltpu.SemaphoreType.DMA((count,))]
    return call(kernel, received, [shape(count, 2, rows, cut)], scratch, "other_side")[0]


def both_rows(mine, theirs):
    count = len(mine)
    _, _, rows, cut = theirs.shape

    def kernel(*refs):
        ins, theirs_ref, outs, sems = refs[:count], refs[count], refs[count + 1:-1], refs[-1]
        p = lax.axis_index("pair")
        moves = []
        for by, (ref, out) in enumerate(zip(ins, outs)):
            source = ref.at[:, p] if len(ref.shape) == 4 else ref
            moves += [(source, out.at[:, p]), (theirs_ref.at[by], out.at[:, 1 - p])]
        run_moves(moves, sems)

    outs = [shape(2, 2, rows, cut)] * count
    scratch = [pltpu.SemaphoreType.DMA((2 * count,))]
    return call(kernel, mine + [theirs], outs, scratch, "both_rows")


def head_parts(own, paired, which, turns, after):
    _, peers, rows, cut = own.shape
    chosen = pl.ds(which, 2)

    def kernel(own_ref, pair_ref, *refs):
        outs, sems = refs[len(after):-1], refs[-1]
        p, s = lax.axis_index("pair"), lax.axis_index("sub")
        moves = []
        for by, out in zip(turns, outs):
            at = lax.rem(s + by, peers)
            moves += [(own_ref.at[chosen, at], out.at[:, p]), (pair_ref.at[chosen, at], out.at[:, 1 - p])]
        run_moves(moves, sems)

    outs = [shape(2, 2, rows, cut)] * len(turns)
    scratch = [pltpu.SemaphoreType.DMA((2 * len(turns),))]
    return call(kernel, [own, paired] + after, outs, scratch, "head_parts")


def relayed(value, after):
    def kernel(value_ref, *refs):
        run_moves([(value_ref, refs[-2])], refs[-1])

    scratch = [pltpu.SemaphoreType.DMA((1,))]
    return call(kernel, [value] + after, [shape(*value.shape)], scratch, "relayed")[0]


def attention_grads(bias, kv, kv_earlier, qg, split, first, heads, after):
    peers = len(kv)
    rows, cut = kv[0].shape[2], heads * HD
    chosen = pl.ds(first * HD, cut)
    strip = rows * peers
    early_count = peers if split else 1

    def kernel(*refs):
        bias_ref = refs[0]
        kv_in, early_in, qg_in = refs[1:1 + peers], refs[1 + peers:1 + 2 * peers], refs[1 + 2 * peers:1 + 3 * peers]
        outs = refs[1 + 3 * peers + len(after):-5]
        own_out, dq_outs, early_outs = outs[0], outs[1:1 + peers], outs[1 + peers:]
        kv_all, qg_all, early, dq_all, sems = refs[-5:]
        s = lax.axis_index("sub")
        moves = []
        for by in range(peers):
            at = lax.rem(s - by + peers, peers)
            moves += [
                (early_in[by].at[:, :, :, chosen], kv_all.at[:, 0:2, at]),
                (kv_in[by].at[:, :, :, chosen], kv_all.at[:, 2:4, at]),
                (qg_in[by].at[:, :, :, chosen], qg_all.at[:, :, at]),
            ]
        run_moves(moves, sems)
        strips = [(head, tile) for head in range(heads) for tile in range(2)]
        products, terms = {}, {}

        def flat(ref, which, tiles, head):
            block = ref[which, tiles, :, :, pl.ds(head * HD, HD)]
            return block.reshape(block.shape[0] * strip, HD)

        def multiply(head, tile):
            at, span = pl.ds(tile, 1), pl.ds(tile, 3)
            q, g = flat(qg_all, 0, at, head), flat(qg_all, 1, at, head)
            k, v = flat(kv_all, 0, span, head), flat(kv_all, 1, span, head)
            scores = lax.dot_general(k, q, ROWS_BY_ROWS, preferred_element_type=WIDE)
            grad_prob = lax.dot_general(v, g, ROWS_BY_ROWS, preferred_element_type=WIDE)
            products[head, tile] = q, g, k, scores, grad_prob

        def finish(head, tile):
            q, g, k, scores, grad_prob = products.pop((head, tile))
            scores = scores * TO_BITS + bias_ref[tile]
            peak = jnp.max(scores, axis=0, keepdims=True)
            weight = jnp.exp2(scores - peak)
            prob = weight * (1.0 / jnp.sum(weight, axis=0, keepdims=True))
            prob_low = prob.astype(LOW)
            row_dot = jnp.sum(prob_low.astype(WIDE) * grad_prob, axis=0, keepdims=True)
            score_low = (prob * (grad_prob - row_dot)).astype(LOW)
            dq = jnp.dot(k.T, score_low, preferred_element_type=WIDE) * SCALE
            dq_all[tile, :, :, pl.ds(head * HD, HD)] = dq.T.astype(LOW).reshape(peers, rows, HD)
            dk = jnp.dot(score_low, q, preferred_element_type=WIDE) * SCALE
            dv = jnp.dot(prob_low, g, preferred_element_type=WIDE)
            terms[head, tile] = dk, dv

        def gather(head):
            for which in range(2):
                low, high = terms[head, 0][which], terms[head, 1][which]
                sums = (
                    low[:strip],
                    low[strip:2 * strip] + high[:strip],
                    low[2 * strip:] + high[strip:2 * strip],
                    high[2 * strip:],
                )
                for tile, total in enumerate(sums):
                    total = total.reshape(peers, rows, HD)
                    if tile < 2:
                        early[which, tile, :, :, pl.ds(head * HD, HD)] = total.astype(LOW)
                    else:
                        own_out[which, tile - 2, :, :, pl.ds(head * HD, HD)] = total

        multiply(*strips[0])
        for at, (head, tile) in enumerate(strips):
            if at + 1 < len(strips):
                multiply(*strips[at + 1])
            finish(head, tile)
            if tile == 1:
                gather(head)
        moves = [] if split else [(early, early_outs[0])]
        for by in range(peers):
            at = lax.rem(s + by, peers)
            moves.append((dq_all.at[:, at], dq_outs[by]))
            if split:
                moves.append((early.at[:, :, at], early_outs[by]))
        run_moves(moves, sems)

    outs = [shape(2, 2, peers, rows, cut, dtype=WIDE)] + [shape(2, rows, cut)] * peers
    outs += [shape(2, 2, rows, cut)] * peers if split else [shape(2, 2, peers, rows, cut)]
    scratch = [
        pltpu.VMEM((2, 4, peers, rows, cut), LOW),
        pltpu.VMEM((2, 2, peers, rows, cut), LOW),
        pltpu.VMEM((2, 2, peers, rows, cut), LOW),
        pltpu.VMEM((2, peers, rows, cut), LOW),
        pltpu.SemaphoreType.DMA((3 * peers,)),
    ]
    flops = heads * 2 * 5 * 2 * strip * 3 * strip * HD
    ins = [bias] + kv + kv_earlier + qg + after
    outs = call(kernel, ins, outs, scratch, "attention_grads", whole=True, flops=flops, room=40 * MIB)
    return outs[0], outs[1:1 + peers], outs[1 + peers:]


def summed(own, later, turns, after):
    _, _, peers, rows, _ = own[0].shape
    widths = [array.shape[-1] for array in own]
    split = later[0].ndim == 4

    def kernel(*refs):
        own_refs, later_refs = refs[:len(own)], refs[len(own):len(own) + len(later)]
        outs = refs[len(own) + len(later) + len(after):]
        s = lax.axis_index("sub")
        for place, (by, out) in enumerate(zip(turns, outs)):
            at = lax.rem(s + by, peers)
            start = 0
            for group, width in enumerate(widths):
                for which in range(2):
                    for row in range(2):
                        term = later_refs[place][which, row] if split else later_refs[group][which, row, at]
                        total = own_refs[group][which, row, at] + term.astype(WIDE)
                        out[which, row, :, pl.ds(start, width)] = total.astype(LOW)
                start += width

    outs = [shape(2, 2, rows, sum(widths))] * len(turns)
    return call(kernel, own + later + after, outs, [], "summed", whole=True)


def rows_for_pair(dq, dkv):
    peers = len(dq)
    _, rows, cut = dq[0].shape

    def kernel(*refs):
        dq_refs, dkv_refs, (send, keep) = refs[:peers], refs[peers:2 * peers], refs[-2:]
        p, s = lax.axis_index("pair"), lax.axis_index("sub")
        for by in range(peers):
            at = lax.rem(s - by + peers, peers)
            for out, row in ((send, 1 - p), (keep, p)):
                out[0, at] = dq_refs[by][row]
                for which in range(2):
                    out[1 + which, at] = dkv_refs[by][which, row]

    outs = [shape(3, peers, rows, cut)] * 2
    return call(kernel, dq + dkv, outs, [], "rows_for_pair", whole=True)


def laid_out(kept, paired, spans):
    _, peers, rows, _ = kept[0].shape
    part = spans[-1][1]
    half = part * peers
    count = len(spans)

    def kernel(*refs):
        keep, rec, outs, sems = refs[:count], refs[count:2 * count], refs[2 * count:-1], refs[-1]
        p = lax.axis_index("pair")
        moves = []
        for mine, theirs, (low, high) in zip(keep, rec, spans):
            for source, side in ((mine, p), (theirs, 1 - p)):
                for at in range(peers):
                    columns = pl.ds(pl.multiple_of(side * half + at * part + low, HD), high - low)
                    moves += [(source.at[which, at], out.at[:, columns]) for which, out in enumerate(outs)]
        run_moves(moves, sems)

    outs = [shape(rows, 2 * half)] * 3
    return call(kernel, kept + paired, outs, [pltpu.SemaphoreType.DMA((6 * count * peers,))], "laid_out")


def allowed_bias(session, rows):
    strip = rows * lax.axis_size("sub")
    block = 2 * strip
    at_block = lax.axis_index("blk")
    window = jnp.concatenate([jnp.zeros((block,), jnp.int32), session])
    sess = lax.dynamic_slice_in_dim(window, at_block * block, 2 * block)
    place = (at_block - 1) * block + jnp.arange(2 * block, dtype=jnp.int32)

    def tile_bias(tile):
        q_at = slice(block + tile * strip, block + (tile + 1) * strip)
        k_at = slice(tile * strip, (tile + 3) * strip)
        k_place, q_place = place[k_at, None], place[None, q_at]
        allowed = (sess[None, q_at] == sess[k_at, None]) & (k_place <= q_place) & (k_place >= 0)
        return jnp.where(allowed, 0.0, NEG_FILL)

    return jnp.stack([tile_bias(0), tile_bias(1)])


def shards(queries, keys, values, out_grad, session):
    peers = lax.axis_size("sub")
    others = list(range(1, peers))
    part = queries.shape[1] // (2 * peers)
    spans, at = [], 0
    for heads in chunks_of(part // HD):
        spans.append((at, at + heads * HD))
        at += heads * HD
    bias = allowed_bias(session, queries.shape[0])
    kv_far, near_send, near_keep = first_keys([keys, values], *spans[0])
    kv_far = [round_sub(value, by) for by, value in zip(others, kv_far)]
    rest = [([queries, out_grad], *spans[0])] + [([keys, values, queries, out_grad], *span) for span in spans[1:]]
    rest = first_parts(rest, [near_keep])
    near_theirs = swapped(near_send)
    kv_parts = [None]
    qg_parts = [(rest[0][1], swapped(rest[0][0]), 0)]
    for send, own in rest[1:]:
        paired = swapped(send)
        kv_parts.append((own, paired, 0))
        qg_parts.append((own, paired, 2))
    count = len(spans)
    kv_sends, qg_sends, kv, qg, kv_own, own_earlier = [], [], [], [], [], []
    for index in range(count):
        if index:
            kv_sends.append(head_parts(*kv_parts[index], others, kv[index - 1] + own_earlier[index - 1:index]))
            kv.append([round_sub(value, by) for by, value in zip(others, kv_sends[index])])
            kv_own.append(head_parts(*kv_parts[index], [0], own_earlier[index - 1:index]))
        else:
            kv_sends.append([])
            kv_own.append(both_rows([near_keep], near_theirs.reshape(1, *near_theirs.shape)))
            kv.append(both_rows(kv_far, swapped(other_side(kv_far))))
        own_earlier.append(along_blocks(kv_own[index][0], 1, True))
        qg_sends.append(head_parts(*qg_parts[index], others, qg[index - 1] if index else []))
        qg.append([round_sub(value, by) for by, value in zip(others, qg_sends[index])])
    kept, paired, first_dq, back, release = [], [], [], [], []
    for index, (low, high) in enumerate(spans):
        last = index == count - 1
        forward = [relayed(value, first_dq) if index else value for value in kv[index]]
        earlier = [own_earlier[index]] + [along_blocks(value, 1, not last) for value in forward]
        qg_all = head_parts(*qg_parts[index], [0], []) + qg[index]
        kv_all = kv_own[index] + kv[index]
        heads = (high - low) // HD
        if last:
            grads, dq, early = attention_grads(bias, kv_all, earlier, qg_all, True, 0, heads, [])
            dq = [dq[0]] + [round_sub(dq[by], by) for by in others]
            later = [along_blocks(relayed(value, back), -1, False) for value in early[1:]]
            dkv = summed([grads], later, others, dq[1:])
            near = along_blocks(relayed(early[0], release), -1, False)
            dkv = summed([grads], [near], [0], []) + [round_sub(value, by) for by, value in zip(others, dkv)]
        else:
            grads, dq, early = attention_grads(bias, kv_all, earlier, qg_all, False, 0, heads, [])
            first_dq = dq[:1]
            dq = [dq[0]] + [round_sub(dq[by], by) for by in others]
            back = dq[1:]
            dkv = summed([grads], [along_blocks(early[0], -1, False)], [0] + others, dq[1:])
            release = dkv[:1]
            dkv = [dkv[0]] + [round_sub(dkv[by], by) for by in others]
        send, keep = rows_for_pair(dq, dkv)
        kept.append(keep)
        paired.append(swapped(send))
    return tuple(laid_out(kept, paired, spans))


def solution(mesh):
    spread = P(("grp", "blk", "pair", "sub"), None)
    return jax.shard_map(
        shards, mesh=mesh, in_specs=(spread,) * 4 + (P("grp"),), out_specs=(spread,) * 3, check_vma=False
    )
```

```python
import math

import jax
import jax.numpy as jnp
from jax import lax
from jax.experimental import pallas as pl
from jax.experimental.pallas import tpu as pltpu
from jax.sharding import PartitionSpec as P

HD = 128
NEG_FILL = -1e30
LOW = jnp.bfloat16
WIDE = jnp.float32
MIB = 1024 * 1024
TO_BITS = HD ** (-0.5) / math.log(2.0)
SCALE = HD ** (-0.5)
ROWS_BY_ROWS = (((1,), (1,)), ((), ()))


def chunks_of(heads):
    return [heads // 2, heads - heads // 2]


def along_blocks(value, by, ring):
    peers = lax.axis_size("blk")
    pairs = [(i, (i + by) % peers) for i in range(peers) if ring or 0 <= i + by < peers]
    return lax.ppermute(value, "blk", pairs)


def round_sub(value, by):
    peers = lax.axis_size("sub")
    return lax.ppermute(value, "sub", [(i, (i + by) % peers) for i in range(peers)])


def cross_sub(value, by):
    peers = lax.axis_size("sub")
    pairs = [(2 * s + p, 2 * ((s + by) % peers) + 1 - p) for p in range(2) for s in range(peers)]
    return lax.ppermute(value, ("sub", "pair"), pairs)


def swapped(value):
    return lax.ppermute(value, "pair", [(0, 1), (1, 0)])


def run_moves(moves, sems):
    copies = [pltpu.make_async_copy(src, dst, sems.at[at]) for at, (src, dst) in enumerate(moves)]
    for copy in copies:
        copy.start()
    for copy in copies:
        copy.wait()


def call(kernel, ins, outs, scratch, name, whole=False, flops=0, room=8 * MIB):
    spec = pl.BlockSpec(memory_space=pltpu.VMEM if whole else pl.ANY)
    moved = sum(math.prod(a.shape) * a.dtype.itemsize for a in list(ins) + list(outs))
    return list(
        pl.pallas_call(
            kernel,
            out_shape=outs,
            in_specs=[spec] * len(ins),
            out_specs=[spec] * len(outs),
            scratch_shapes=scratch,
            name=name,
            cost_estimate=pl.CostEstimate(flops=flops, bytes_accessed=moved, transcendentals=0),
            compiler_params=pltpu.CompilerParams(vmem_limit_bytes=room),
        )(*ins)
    )


def shape(*dims, dtype=LOW):
    return jax.ShapeDtypeStruct(dims, dtype)


def first_parts(groups, after):
    held, wanted, outs = [], [], []
    for arrays, low, high in groups:
        rows, width = arrays[0].shape
        peers = lax.axis_size("sub")
        half = width // 2
        part = half // peers
        wanted.append((len(held), len(arrays), low, high))
        held += [pltpu.with_memory_space_constraint(array, pltpu.HBM) for array in arrays]
        outs += [pltpu.VMEM((len(arrays), peers, rows, high - low), LOW)] * 2

    def kernel(*refs):
        out_refs, sems = refs[-1 - len(outs):-1], refs[-1]
        p = lax.axis_index("pair")
        moves = []
        for group, (first, count, low, high) in enumerate(wanted):
            for side, out in zip((1 - p, p), out_refs[2 * group:2 * group + 2]):
                for at in range(peers):
                    start = pl.multiple_of(side * half + at * part + low, HD)
                    for i in range(count):
                        moves.append((refs[first + i].at[:, pl.ds(start, high - low)], out.at[i, at]))
        run_moves(moves, sems)

    spec = pl.BlockSpec(memory_space=pl.ANY)
    parts = pl.pallas_call(
        kernel,
        out_shape=outs,
        in_specs=[spec] * (len(held) + len(after)),
        out_specs=[spec] * len(outs),
        scratch_shapes=[pltpu.SemaphoreType.DMA((2 * peers * len(held),))],
        name="first_parts",
        compiler_params=pltpu.CompilerParams(vmem_limit_bytes=8 * MIB),
    )(*held, *after)
    return [(parts[2 * i], parts[2 * i + 1]) for i in range(len(groups))]


def first_keys(arrays, low, high, after):
    rows, width = arrays[0].shape
    half = width // 2
    peers = lax.axis_size("sub")
    part = half // peers
    cut = high - low

    def kernel(*refs):
        ins, far, (send, keep), sems = refs[:2], refs[2 + len(after):1 + peers + len(after)], refs[-3:-1], refs[-1]
        p, s = lax.axis_index("pair"), lax.axis_index("sub")
        moves = []
        for i, ref in enumerate(ins):
            for by in range(1, peers):
                for side in range(2):
                    start = pl.multiple_of(side * half + lax.rem(s + by, peers) * part + low, HD)
                    moves.append((ref.at[:, pl.ds(start, cut)], far[by - 1].at[i, side]))
            for out, side in ((send, 1 - p), (keep, p)):
                start = pl.multiple_of(side * half + s * part + low, HD)
                moves.append((ref.at[:, pl.ds(start, cut)], out.at[i]))
        run_moves(moves, sems)

    spec = pl.BlockSpec(memory_space=pl.ANY)
    outs = [pltpu.VMEM((2, 2, rows, cut), LOW)] * (peers - 1) + [pltpu.VMEM((2, rows, cut), LOW)] * 2
    parts = pl.pallas_call(
        kernel,
        out_shape=outs,
        in_specs=[spec] * (2 + len(after)),
        out_specs=[spec] * len(outs),
        scratch_shapes=[pltpu.SemaphoreType.DMA((4 * peers,))],
        name="first_keys",
        compiler_params=pltpu.CompilerParams(vmem_limit_bytes=8 * MIB),
    )(*[pltpu.with_memory_space_constraint(array, pltpu.HBM) for array in arrays], *after)
    return list(parts[:-2]), parts[-2], parts[-1]


def other_side(received):
    count = len(received)

    def kernel(*refs):
        p = lax.axis_index("pair")
        run_moves([(ref.at[:, 1 - p], refs[-2].at[by]) for by, ref in enumerate(refs[:count])], refs[-1])

    _, _, rows, cut = received[0].shape
    scratch = [pltpu.SemaphoreType.DMA((count,))]
    return call(kernel, received, [shape(count, 2, rows, cut)], scratch, "other_side")[0]


def both_rows(mine, theirs):
    count = len(mine)
    _, _, rows, cut = theirs.shape

    def kernel(*refs):
        ins, theirs_ref, outs, sems = refs[:count], refs[count], refs[count + 1:-1], refs[-1]
        p = lax.axis_index("pair")
        moves = []
        for by, (ref, out) in enumerate(zip(ins, outs)):
            source = ref.at[:, p] if len(ref.shape) == 4 else ref
            moves += [(source, out.at[:, p]), (theirs_ref.at[by], out.at[:, 1 - p])]
        run_moves(moves, sems)

    outs = [shape(2, 2, rows, cut)] * count
    scratch = [pltpu.SemaphoreType.DMA((2 * count,))]
    return call(kernel, mine + [theirs], outs, scratch, "both_rows")


def head_parts(own, paired, which, turns, after):
    _, peers, rows, cut = own.shape
    chosen = pl.ds(which, 2)

    def kernel(own_ref, pair_ref, *refs):
        outs, sems = refs[len(after):-1], refs[-1]
        p, s = lax.axis_index("pair"), lax.axis_index("sub")
        moves = []
        for by, out in zip(turns, outs):
            at = lax.rem(s + by, peers)
            moves += [(own_ref.at[chosen, at], out.at[:, p]), (pair_ref.at[chosen, at], out.at[:, 1 - p])]
        run_moves(moves, sems)

    outs = [shape(2, 2, rows, cut)] * len(turns)
    scratch = [pltpu.SemaphoreType.DMA((2 * len(turns),))]
    return call(kernel, [own, paired] + after, outs, scratch, "head_parts")


def relayed(value, after):
    def kernel(value_ref, *refs):
        run_moves([(value_ref, refs[-2])], refs[-1])

    scratch = [pltpu.SemaphoreType.DMA((1,))]
    return call(kernel, [value] + after, [shape(*value.shape)], scratch, "relayed")[0]


def attention_grads(bias, kv, kv_earlier, qg, split, first, heads, after):
    peers = len(kv)
    rows, cut = kv[0].shape[2], heads * HD
    chosen = pl.ds(first * HD, cut)
    strip = rows * peers
    early_count = peers if split else 1

    def kernel(*refs):
        bias_ref = refs[0]
        kv_in, early_in, qg_in = refs[1:1 + peers], refs[1 + peers:1 + 2 * peers], refs[1 + 2 * peers:1 + 3 * peers]
        outs = refs[1 + 3 * peers + len(after):-5]
        own_out, dq_outs, early_outs = outs[0], outs[1:1 + peers], outs[1 + peers:]
        kv_all, qg_all, early, dq_all, sems = refs[-5:]
        s = lax.axis_index("sub")
        moves = []
        for by in range(peers):
            at = lax.rem(s - by + peers, peers)
            moves += [
                (early_in[by].at[:, :, :, chosen], kv_all.at[:, 0:2, at]),
                (kv_in[by].at[:, :, :, chosen], kv_all.at[:, 2:4, at]),
                (qg_in[by].at[:, :, :, chosen], qg_all.at[:, :, at]),
            ]
        run_moves(moves, sems)
        strips = [(head, tile) for head in range(heads) for tile in range(2)]
        products, terms = {}, {}

        def flat(ref, which, tiles, head):
            block = ref[which, tiles, :, :, pl.ds(head * HD, HD)]
            return block.reshape(block.shape[0] * strip, HD)

        def multiply(head, tile):
            at, span = pl.ds(tile, 1), pl.ds(tile, 3)
            q, g = flat(qg_all, 0, at, head), flat(qg_all, 1, at, head)
            k, v = flat(kv_all, 0, span, head), flat(kv_all, 1, span, head)
            scores = lax.dot_general(k, q, ROWS_BY_ROWS, preferred_element_type=WIDE)
            grad_prob = lax.dot_general(v, g, ROWS_BY_ROWS, preferred_element_type=WIDE)
            products[head, tile] = q, g, k, scores, grad_prob

        def finish(head, tile):
            q, g, k, scores, grad_prob = products.pop((head, tile))
            scores = scores * TO_BITS + bias_ref[tile]
            peak = jnp.max(scores, axis=0, keepdims=True)
            weight = jnp.exp2(scores - peak)
            prob = weight * (1.0 / jnp.sum(weight, axis=0, keepdims=True))
            prob_low = prob.astype(LOW)
            row_dot = jnp.sum(prob_low.astype(WIDE) * grad_prob, axis=0, keepdims=True)
            score_low = (prob * (grad_prob - row_dot)).astype(LOW)
            dq = jnp.dot(k.T, score_low, preferred_element_type=WIDE) * SCALE
            dq_all[tile, :, :, pl.ds(head * HD, HD)] = dq.T.astype(LOW).reshape(peers, rows, HD)
            dk = jnp.dot(score_low, q, preferred_element_type=WIDE) * SCALE
            dv = jnp.dot(prob_low, g, preferred_element_type=WIDE)
            terms[head, tile] = dk, dv

        def gather(head):
            for which in range(2):
                low, high = terms[head, 0][which], terms[head, 1][which]
                sums = (
                    low[:strip],
                    low[strip:2 * strip] + high[:strip],
                    low[2 * strip:] + high[strip:2 * strip],
                    high[2 * strip:],
                )
                for tile, total in enumerate(sums):
                    total = total.reshape(peers, rows, HD)
                    if tile < 2:
                        early[which, tile, :, :, pl.ds(head * HD, HD)] = total.astype(LOW)
                    else:
                        own_out[which, tile - 2, :, :, pl.ds(head * HD, HD)] = total

        multiply(*strips[0])
        for at, (head, tile) in enumerate(strips):
            if at + 1 < len(strips):
                multiply(*strips[at + 1])
            finish(head, tile)
            if tile == 1:
                gather(head)
        moves = [] if split else [(early, early_outs[0])]
        for by in range(peers):
            at = lax.rem(s + by, peers)
            moves.append((dq_all.at[:, at], dq_outs[by]))
            if split:
                moves.append((early.at[:, :, at], early_outs[by]))
        run_moves(moves, sems)

    outs = [shape(2, 2, peers, rows, cut, dtype=WIDE)] + [shape(2, rows, cut)] * peers
    outs += [shape(2, 2, rows, cut)] * peers if split else [shape(2, 2, peers, rows, cut)]
    scratch = [
        pltpu.VMEM((2, 4, peers, rows, cut), LOW),
        pltpu.VMEM((2, 2, peers, rows, cut), LOW),
        pltpu.VMEM((2, 2, peers, rows, cut), LOW),
        pltpu.VMEM((2, peers, rows, cut), LOW),
        pltpu.SemaphoreType.DMA((3 * peers,)),
    ]
    flops = heads * 2 * 5 * 2 * strip * 3 * strip * HD
    ins = [bias] + kv + kv_earlier + qg + after
    outs = call(kernel, ins, outs, scratch, "attention_grads", whole=True, flops=flops, room=40 * MIB)
    return outs[0], outs[1:1 + peers], outs[1 + peers:]


def summed(own, later, turns, after):
    _, _, peers, rows, _ = own[0].shape
    widths = [array.shape[-1] for array in own]
    split = later[0].ndim == 4

    def kernel(*refs):
        own_refs, later_refs = refs[:len(own)], refs[len(own):len(own) + len(later)]
        outs = refs[len(own) + len(later) + len(after):]
        s = lax.axis_index("sub")
        for place, (by, out) in enumerate(zip(turns, outs)):
            at = lax.rem(s + by, peers)
            start = 0
            for group, width in enumerate(widths):
                for which in range(2):
                    for row in range(2):
                        term = later_refs[place][which, row] if split else later_refs[group][which, row, at]
                        total = own_refs[group][which, row, at] + term.astype(WIDE)
                        out[which, row, :, pl.ds(start, width)] = total.astype(LOW)
                start += width

    outs = [shape(2, 2, rows, sum(widths))] * len(turns)
    return call(kernel, own + later + after, outs, [], "summed", whole=True)


def rows_for_pair(dq, dkv):
    peers = len(dq)
    _, rows, cut = dq[0].shape

    def kernel(*refs):
        dq_refs, dkv_refs, (send, keep) = refs[:peers], refs[peers:2 * peers], refs[-2:]
        p, s = lax.axis_index("pair"), lax.axis_index("sub")
        for by in range(peers):
            at = lax.rem(s - by + peers, peers)
            for out, row in ((send, 1 - p), (keep, p)):
                out[0, at] = dq_refs[by][row]
                for which in range(2):
                    out[1 + which, at] = dkv_refs[by][which, row]

    outs = [shape(3, peers, rows, cut)] * 2
    return call(kernel, dq + dkv, outs, [], "rows_for_pair", whole=True)


def last_sums(own, later, after):
    _, _, peers, rows, cut = own.shape

    def kernel(own_ref, *refs):
        later_refs, outs = refs[:peers - 1], refs[len(later) + len(after):]
        p, s = lax.axis_index("pair"), lax.axis_index("sub")
        for by in range(1, peers):
            at = lax.rem(s + by, peers)
            for out, row in ((outs[2 * by - 2], p), (outs[2 * by - 1], 1 - p)):
                for which in range(2):
                    total = own_ref[which, row, at] + later_refs[by - 1][which, row].astype(WIDE)
                    out[which] = total.astype(LOW)

    return call(kernel, [own] + later + after, [shape(2, rows, cut)] * (2 * peers - 2), [], "last_sums", whole=True)


def last_rows(own, later):
    _, _, peers, rows, cut = own.shape

    def kernel(own_ref, later_ref, send_k, send_v, keep):
        p, s = lax.axis_index("pair"), lax.axis_index("sub")
        for which, send in enumerate((send_k, send_v)):
            for out, at, row in ((send, 0, 1 - p), (keep, which, p)):
                out[at] = (own_ref[which, row, s] + later_ref[which, row].astype(WIDE)).astype(LOW)

    outs = [shape(1, rows, cut), shape(1, rows, cut), shape(2, rows, cut)]
    return call(kernel, [own, later], outs, [], "last_rows", whole=True)


def query_rows(dq):
    peers = len(dq)
    _, rows, cut = dq[0].shape

    def kernel(*refs):
        p = lax.axis_index("pair")
        for out, row in zip(refs[peers:], (1 - p, p)):
            for by in range(peers):
                out[by] = refs[by][row]

    return call(kernel, dq, [shape(peers, rows, cut)] * 2, [], "query_rows", whole=True)


def stacked(parts):
    _, rows, cut = parts[0].shape

    def kernel(*refs):
        at = 0
        for ref in refs[:-1]:
            for i in range(ref.shape[0]):
                refs[-1][at + i] = ref[i]
            at += ref.shape[0]

    outs = [shape(sum(part.shape[0] for part in parts), rows, cut)]
    return call(kernel, parts, outs, [], "stacked", whole=True)[0]


def laid_out(whole, last, straight, crossed, spans):
    peers = lax.axis_size("sub")
    rows = last[0].shape[1]
    part = spans[-1][1]
    half = part * peers
    ins = [array for both in whole for array in both] + list(last) + straight + crossed

    def kernel(*refs):
        outs, sems = refs[len(ins):-1], refs[-1]
        p, s = lax.axis_index("pair"), lax.axis_index("sub")
        moves = []

        def place(source, which, side, at, span):
            columns = pl.ds(pl.multiple_of(side * half + at * part + span[0], HD), span[1] - span[0])
            moves.append((source, outs[which].at[:, columns]))

        for i, side in enumerate((p, 1 - p)):
            for chunk in range(len(whole)):
                for at in range(peers):
                    for which in range(3):
                        place(refs[2 * chunk + i].at[which, at], which, side, at, spans[chunk])
            ours = refs[2 * len(whole) + i]
            far = refs[2 * len(whole) + 2 + i * (peers - 1):]
            for by in range(peers):
                at = lax.rem(s - by + peers, peers)
                place(ours.at[2 + by], 0, side, at, spans[-1])
                for which in range(2):
                    source = ours.at[which] if by == 0 else far[by - 1].at[which]
                    place(source, 1 + which, side, at, spans[-1])
        run_moves(moves, sems)

    outs = [shape(rows, 2 * half)] * 3
    scratch = [pltpu.SemaphoreType.DMA((6 * len(spans) * peers,))]
    return call(kernel, ins, outs, scratch, "laid_out")


def allowed_bias(session, rows):
    strip = rows * lax.axis_size("sub")
    block = 2 * strip
    at_block = lax.axis_index("blk")
    window = jnp.concatenate([jnp.zeros((block,), jnp.int32), session])
    sess = lax.dynamic_slice_in_dim(window, at_block * block, 2 * block)
    place = (at_block - 1) * block + jnp.arange(2 * block, dtype=jnp.int32)

    def tile_bias(tile):
        q_at = slice(block + tile * strip, block + (tile + 1) * strip)
        k_at = slice(tile * strip, (tile + 3) * strip)
        k_place, q_place = place[k_at, None], place[None, q_at]
        allowed = (sess[None, q_at] == sess[k_at, None]) & (k_place <= q_place) & (k_place >= 0)
        return jnp.where(allowed, 0.0, NEG_FILL)

    return jnp.stack([tile_bias(0), tile_bias(1)])


def shards(queries, keys, values, out_grad, session):
    peers = lax.axis_size("sub")
    others = list(range(1, peers))
    part = queries.shape[1] // (2 * peers)
    spans, at = [], 0
    for heads in chunks_of(part // HD):
        spans.append((at, at + heads * HD))
        at += heads * HD
    bias = allowed_bias(session, queries.shape[0])
    kv_far, near_send, near_keep = first_keys([keys, values], *spans[0], [])
    kv_far = [round_sub(value, by) for by, value in zip(others, kv_far)]
    rest = [([queries, out_grad], *spans[0])] + [([keys, values], *span) for span in spans[1:]]
    rest = first_parts(rest, [near_keep])
    near_theirs = swapped(near_send)
    paired = [(own, swapped(send), 0) for send, own in rest]
    qg_parts, kv_parts = paired[:1], [None] + paired[1:]
    later_reads = [first_keys([queries, out_grad], *span, [rest[0][1]]) for span in spans[1:]]
    count = len(spans)
    kv_sends, qg_own, kv, qg, kv_own, own_earlier = [], [], [], [], [], []
    for index in range(count):
        if index:
            kv_sends.append(head_parts(*kv_parts[index], others, kv[index - 1] + own_earlier[index - 1:index]))
            kv.append([round_sub(value, by) for by, value in zip(others, kv_sends[index])])
            kv_own.append(head_parts(*kv_parts[index], [0], own_earlier[index - 1:index]))
        else:
            kv_sends.append([])
            kv_own.append(both_rows([near_keep], near_theirs.reshape(1, *near_theirs.shape)))
            kv.append(both_rows(kv_far, swapped(other_side(kv_far))))
        own_earlier.append(along_blocks(kv_own[index][0], 1, True))
        if index:
            far, send, keep = later_reads[index - 1]
            far = [round_sub(relayed(value, qg[index - 1]), by) for by, value in zip(others, far)]
            qg.append(both_rows(far, swapped(other_side(far))))
            qg_own.append(both_rows([keep], swapped(send).reshape(1, *send.shape)))
        else:
            sends = head_parts(*qg_parts[index], others, [])
            qg.append([round_sub(value, by) for by, value in zip(others, sends)])
            qg_own.append(head_parts(*qg_parts[index], [0], []))
    done, first_dq = [], []
    for index, (low, high) in enumerate(spans):
        last = index == count - 1
        forward = [relayed(value, first_dq) if index else value for value in kv[index]]
        earlier = [own_earlier[index]] + [along_blocks(value, 1, not last) for value in forward]
        qg_all = qg_own[index] + qg[index]
        after = [] if last else own_earlier[index + 1:index + 2] + [later_reads[index][2]]
        done.append(attention_grads(bias, kv_own[index] + kv[index], earlier, qg_all, last, 0, (high - low) // HD, after))
        first_dq = done[-1][1][:1]
    whole, back, release = [], [], []
    for index, (grads, dq, early) in enumerate(done):
        near_dq = dq[:1]
        dq = near_dq + [round_sub(dq[by], by) for by in others]
        if index == count - 1:
            later = [along_blocks(relayed(value, back), -1, False) for value in early[1:]]
            sums = last_sums(grads, later, dq[1:])
            straight = [round_sub(sums[2 * by - 2], by) for by in others]
            crossed = [cross_sub(sums[2 * by - 1], by) for by in others]
            near = along_blocks(relayed(early[0], sums[:1]), -1, False)
            send_k, send_v, keep = last_rows(grads, near)
            send, keep_dq = query_rows(dq)
            theirs = [swapped(send_k), swapped(send_v), swapped(send)]
            ours = (stacked([keep, keep_dq]), stacked(theirs))
        else:
            back = dq[1:]
            dkv = summed([grads], [along_blocks(early[0], -1, False)], [0] + others, dq[1:] + first_dq)
            release = dkv[:1]
            dkv = [dkv[0]] + [round_sub(dkv[by], by) for by in others]
            send, keep = rows_for_pair(dq, dkv)
            whole.append((keep, swapped(send)))
    return tuple(laid_out(whole, ours, straight, crossed, spans))


def solution(mesh):
    spread = P(("grp", "blk", "pair", "sub"), None)
    return jax.shard_map(
        shards, mesh=mesh, in_specs=(spread,) * 4 + (P("grp"),), out_specs=(spread,) * 3, check_vma=False
    )
```

```python
import math

import jax
import jax.numpy as jnp
from jax import lax
from jax.experimental import pallas as pl
from jax.experimental.pallas import tpu as pltpu
from jax.sharding import PartitionSpec as P

HD = 128
NEG_FILL = -1e30
LOW = jnp.bfloat16
WIDE = jnp.float32
MIB = 1024 * 1024
TO_BITS = HD ** (-0.5) / math.log(2.0)
SCALE = HD ** (-0.5)
ROWS_BY_ROWS = (((1,), (1,)), ((), ()))


def chunks_of(heads):
    return [heads // 2, heads - heads // 2]


def along_blocks(value, by, ring):
    peers = lax.axis_size("blk")
    pairs = [(i, (i + by) % peers) for i in range(peers) if ring or 0 <= i + by < peers]
    return lax.ppermute(value, "blk", pairs)


def round_sub(value, by):
    peers = lax.axis_size("sub")
    return lax.ppermute(value, "sub", [(i, (i + by) % peers) for i in range(peers)])


def swapped(value):
    return lax.ppermute(value, "pair", [(0, 1), (1, 0)])


def run_moves(moves, sems):
    copies = [pltpu.make_async_copy(src, dst, sems.at[at]) for at, (src, dst) in enumerate(moves)]
    for copy in copies:
        copy.start()
    for copy in copies:
        copy.wait()


def call(kernel, ins, outs, scratch, name, whole=False, flops=0, room=8 * MIB):
    spec = pl.BlockSpec(memory_space=pltpu.VMEM if whole else pl.ANY)
    moved = sum(math.prod(a.shape) * a.dtype.itemsize for a in list(ins) + list(outs))
    return list(
        pl.pallas_call(
            kernel,
            out_shape=outs,
            in_specs=[spec] * len(ins),
            out_specs=[spec] * len(outs),
            scratch_shapes=scratch,
            name=name,
            cost_estimate=pl.CostEstimate(flops=flops, bytes_accessed=moved, transcendentals=0),
            compiler_params=pltpu.CompilerParams(vmem_limit_bytes=room),
        )(*ins)
    )


def shape(*dims, dtype=LOW):
    return jax.ShapeDtypeStruct(dims, dtype)


def first_parts(groups, after):
    held, wanted, outs = [], [], []
    for arrays, low, high in groups:
        rows, width = arrays[0].shape
        peers = lax.axis_size("sub")
        half = width // 2
        part = half // peers
        wanted.append((len(held), len(arrays), low, high))
        held += [pltpu.with_memory_space_constraint(array, pltpu.HBM) for array in arrays]
        outs += [pltpu.VMEM((len(arrays), peers, rows, high - low), LOW)] * 2

    def kernel(*refs):
        out_refs, sems = refs[-1 - len(outs):-1], refs[-1]
        p = lax.axis_index("pair")
        moves = []
        for group, (first, count, low, high) in enumerate(wanted):
            for side, out in zip((1 - p, p), out_refs[2 * group:2 * group + 2]):
                for at in range(peers):
                    start = pl.multiple_of(side * half + at * part + low, HD)
                    for i in range(count):
                        moves.append((refs[first + i].at[:, pl.ds(start, high - low)], out.at[i, at]))
        run_moves(moves, sems)

    spec = pl.BlockSpec(memory_space=pl.ANY)
    parts = pl.pallas_call(
        kernel,
        out_shape=outs,
        in_specs=[spec] * (len(held) + len(after)),
        out_specs=[spec] * len(outs),
        scratch_shapes=[pltpu.SemaphoreType.DMA((2 * peers * len(held),))],
        name="first_parts",
        compiler_params=pltpu.CompilerParams(vmem_limit_bytes=8 * MIB),
    )(*held, *after)
    return [(parts[2 * i], parts[2 * i + 1]) for i in range(len(groups))]


def first_keys(arrays, low, high):
    rows, width = arrays[0].shape
    half = width // 2
    peers = lax.axis_size("sub")
    part = half // peers
    cut = high - low

    def kernel(*refs):
        ins, far, (send, keep), sems = refs[:2], refs[2:1 + peers], refs[1 + peers:-1], refs[-1]
        p, s = lax.axis_index("pair"), lax.axis_index("sub")
        moves = []
        for i, ref in enumerate(ins):
            for by in range(1, peers):
                for side in range(2):
                    start = pl.multiple_of(side * half + lax.rem(s + by, peers) * part + low, HD)
                    moves.append((ref.at[:, pl.ds(start, cut)], far[by - 1].at[i, side]))
            for out, side in ((send, 1 - p), (keep, p)):
                start = pl.multiple_of(side * half + s * part + low, HD)
                moves.append((ref.at[:, pl.ds(start, cut)], out.at[i]))
        run_moves(moves, sems)

    spec = pl.BlockSpec(memory_space=pl.ANY)
    outs = [pltpu.VMEM((2, 2, rows, cut), LOW)] * (peers - 1) + [pltpu.VMEM((2, rows, cut), LOW)] * 2
    parts = pl.pallas_call(
        kernel,
        out_shape=outs,
        in_specs=[spec] * 2,
        out_specs=[spec] * len(outs),
        scratch_shapes=[pltpu.SemaphoreType.DMA((4 * peers,))],
        name="first_keys",
        compiler_params=pltpu.CompilerParams(vmem_limit_bytes=8 * MIB),
    )(*[pltpu.with_memory_space_constraint(array, pltpu.HBM) for array in arrays])
    return list(parts[:-2]), parts[-2], parts[-1]


def other_side(received):
    count = len(received)

    def kernel(*refs):
        p = lax.axis_index("pair")
        run_moves([(ref.at[:, 1 - p], refs[-2].at[by]) for by, ref in enumerate(refs[:count])], refs[-1])

    _, _, rows, cut = received[0].shape
    scratch = [pltpu.SemaphoreType.DMA((count,))]
    return call(kernel, received, [shape(count, 2, rows, cut)], scratch, "other_side")[0]


def both_rows(mine, theirs):
    count = len(mine)
    _, _, rows, cut = theirs.shape

    def kernel(*refs):
        ins, theirs_ref, outs, sems = refs[:count], refs[count], refs[count + 1:-1], refs[-1]
        p = lax.axis_index("pair")
        moves = []
        for by, (ref, out) in enumerate(zip(ins, outs)):
            source = ref.at[:, p] if len(ref.shape) == 4 else ref
            moves += [(source, out.at[:, p]), (theirs_ref.at[by], out.at[:, 1 - p])]
        run_moves(moves, sems)

    outs = [shape(2, 2, rows, cut)] * count
    scratch = [pltpu.SemaphoreType.DMA((2 * count,))]
    return call(kernel, mine + [theirs], outs, scratch, "both_rows")


def head_parts(own, paired, which, turns, after):
    _, peers, rows, cut = own.shape
    chosen = pl.ds(which, 2)

    def kernel(own_ref, pair_ref, *refs):
        outs, sems = refs[len(after):-1], refs[-1]
        p, s = lax.axis_index("pair"), lax.axis_index("sub")
        moves = []
        for by, out in zip(turns, outs):
            at = lax.rem(s + by, peers)
            moves += [(own_ref.at[chosen, at], out.at[:, p]), (pair_ref.at[chosen, at], out.at[:, 1 - p])]
        run_moves(moves, sems)

    outs = [shape(2, 2, rows, cut)] * len(turns)
    scratch = [pltpu.SemaphoreType.DMA((2 * len(turns),))]
    return call(kernel, [own, paired] + after, outs, scratch, "head_parts")


def relayed(value, after):
    def kernel(value_ref, *refs):
        run_moves([(value_ref, refs[-2])], refs[-1])

    scratch = [pltpu.SemaphoreType.DMA((1,))]
    return call(kernel, [value] + after, [shape(*value.shape)], scratch, "relayed")[0]


def attention_grads(bias, kv, kv_earlier, qg, split, first, heads, after):
    peers = len(kv)
    rows, cut = kv[0].shape[2], heads * HD
    chosen = pl.ds(first * HD, cut)
    strip = rows * peers
    early_count = peers if split else 1

    def kernel(*refs):
        bias_ref = refs[0]
        kv_in, early_in, qg_in = refs[1:1 + peers], refs[1 + peers:1 + 2 * peers], refs[1 + 2 * peers:1 + 3 * peers]
        outs = refs[1 + 3 * peers + len(after):-5]
        own_out, dq_outs, early_outs = outs[0], outs[1:1 + peers], outs[1 + peers:]
        kv_all, qg_all, early, dq_all, sems = refs[-5:]
        s = lax.axis_index("sub")
        moves = []
        for by in range(peers):
            at = lax.rem(s - by + peers, peers)
            moves += [
                (early_in[by].at[:, :, :, chosen], kv_all.at[:, 0:2, at]),
                (kv_in[by].at[:, :, :, chosen], kv_all.at[:, 2:4, at]),
                (qg_in[by].at[:, :, :, chosen], qg_all.at[:, :, at]),
            ]
        run_moves(moves, sems)
        strips = [(head, tile) for head in range(heads) for tile in range(2)]
        products, terms = {}, {}

        def flat(ref, which, tiles, head):
            block = ref[which, tiles, :, :, pl.ds(head * HD, HD)]
            return block.reshape(block.shape[0] * strip, HD)

        def multiply(head, tile):
            at, span = pl.ds(tile, 1), pl.ds(tile, 3)
            q, g = flat(qg_all, 0, at, head), flat(qg_all, 1, at, head)
            k, v = flat(kv_all, 0, span, head), flat(kv_all, 1, span, head)
            scores = lax.dot_general(k, q, ROWS_BY_ROWS, preferred_element_type=WIDE)
            grad_prob = lax.dot_general(v, g, ROWS_BY_ROWS, preferred_element_type=WIDE)
            products[head, tile] = q, g, k, scores, grad_prob

        def finish(head, tile):
            q, g, k, scores, grad_prob = products.pop((head, tile))
            scores = scores * TO_BITS + bias_ref[tile]
            peak = jnp.max(scores, axis=0, keepdims=True)
            weight = jnp.exp2(scores - peak)
            prob = weight * (1.0 / jnp.sum(weight, axis=0, keepdims=True))
            prob_low = prob.astype(LOW)
            row_dot = jnp.sum(prob_low.astype(WIDE) * grad_prob, axis=0, keepdims=True)
            score_low = (prob * (grad_prob - row_dot)).astype(LOW)
            dq = jnp.dot(k.T, score_low, preferred_element_type=WIDE) * SCALE
            dq_all[tile, :, :, pl.ds(head * HD, HD)] = dq.T.astype(LOW).reshape(peers, rows, HD)
            dk = jnp.dot(score_low, q, preferred_element_type=WIDE) * SCALE
            dv = jnp.dot(prob_low, g, preferred_element_type=WIDE)
            terms[head, tile] = dk, dv

        def gather(head):
            for which in range(2):
                low, high = terms[head, 0][which], terms[head, 1][which]
                sums = (
                    low[:strip],
                    low[strip:2 * strip] + high[:strip],
                    low[2 * strip:] + high[strip:2 * strip],
                    high[2 * strip:],
                )
                for tile, total in enumerate(sums):
                    total = total.reshape(peers, rows, HD)
                    if tile < 2:
                        early[which, tile, :, :, pl.ds(head * HD, HD)] = total.astype(LOW)
                    else:
                        own_out[which, tile - 2, :, :, pl.ds(head * HD, HD)] = total

        multiply(*strips[0])
        for at, (head, tile) in enumerate(strips):
            if at + 1 < len(strips):
                multiply(*strips[at + 1])
            finish(head, tile)
            if tile == 1:
                gather(head)
        moves = [] if split else [(early, early_outs[0])]
        for by in range(peers):
            at = lax.rem(s + by, peers)
            moves.append((dq_all.at[:, at], dq_outs[by]))
            if split:
                moves.append((early.at[:, :, at], early_outs[by]))
        run_moves(moves, sems)

    outs = [shape(2, 2, peers, rows, cut, dtype=WIDE)] + [shape(2, rows, cut)] * peers
    outs += [shape(2, 2, rows, cut)] * peers if split else [shape(2, 2, peers, rows, cut)]
    scratch = [
        pltpu.VMEM((2, 4, peers, rows, cut), LOW),
        pltpu.VMEM((2, 2, peers, rows, cut), LOW),
        pltpu.VMEM((2, 2, peers, rows, cut), LOW),
        pltpu.VMEM((2, peers, rows, cut), LOW),
        pltpu.SemaphoreType.DMA((3 * peers,)),
    ]
    flops = heads * 2 * 5 * 2 * strip * 3 * strip * HD
    ins = [bias] + kv + kv_earlier + qg + after
    outs = call(kernel, ins, outs, scratch, "attention_grads", whole=True, flops=flops, room=40 * MIB)
    return outs[0], outs[1:1 + peers], outs[1 + peers:]


def summed(own, later, turns, after):
    _, _, peers, rows, _ = own[0].shape
    widths = [array.shape[-1] for array in own]
    split = later[0].ndim == 4

    def kernel(*refs):
        own_refs, later_refs = refs[:len(own)], refs[len(own):len(own) + len(later)]
        outs = refs[len(own) + len(later) + len(after):]
        s = lax.axis_index("sub")
        for place, (by, out) in enumerate(zip(turns, outs)):
            at = lax.rem(s + by, peers)
            start = 0
            for group, width in enumerate(widths):
                for which in range(2):
                    for row in range(2):
                        term = later_refs[place][which, row] if split else later_refs[group][which, row, at]
                        total = own_refs[group][which, row, at] + term.astype(WIDE)
                        out[which, row, :, pl.ds(start, width)] = total.astype(LOW)
                start += width

    outs = [shape(2, 2, rows, sum(widths))] * len(turns)
    return call(kernel, own + later + after, outs, [], "summed", whole=True)


def last_rows(own, later):
    _, _, peers, rows, cut = own.shape

    def kernel(own_ref, later_ref, send_k, send_v, keep):
        p, s = lax.axis_index("pair"), lax.axis_index("sub")
        for which, send in enumerate((send_k, send_v)):
            for out, at, row in ((send, 0, 1 - p), (keep, which, p)):
                out[at] = (own_ref[which, row, s] + later_ref[which, row].astype(WIDE)).astype(LOW)

    outs = [shape(1, rows, cut), shape(1, rows, cut), shape(2, rows, cut)]
    return call(kernel, [own, later], outs, [], "last_rows", whole=True)


def query_rows(dq):
    peers = len(dq)
    _, rows, cut = dq[0].shape

    def kernel(*refs):
        p = lax.axis_index("pair")
        for out, row in zip(refs[peers:], (1 - p, p)):
            for by in range(peers):
                out[by] = refs[by][row]

    return call(kernel, dq, [shape(peers, rows, cut)] * 2, [], "query_rows", whole=True)


def stacked(parts):
    _, rows, cut = parts[0].shape

    def kernel(*refs):
        at = 0
        for ref in refs[:-1]:
            for i in range(ref.shape[0]):
                refs[-1][at + i] = ref[i]
            at += ref.shape[0]

    outs = [shape(sum(part.shape[0] for part in parts), rows, cut)]
    return call(kernel, parts, outs, [], "stacked", whole=True)[0]


def far_rows(received):
    peers = len(received) + 1
    _, _, rows, cut = received[0].shape

    def kernel(*refs):
        p = lax.axis_index("pair")
        for out, row in zip(refs[-2:], (1 - p, p)):
            for by in range(peers - 1):
                for which in range(2):
                    out[which, by] = refs[by][which, row]

    return call(kernel, received, [shape(2, peers - 1, rows, cut)] * 2, [], "far_rows", whole=True)


def laid_out(chunks, spans):
    peers = lax.axis_size("sub")
    rows = chunks[0][0].shape[1]
    part = spans[-1][1]
    half = part * peers
    ins = [array for chunk in chunks for array in chunk]

    def kernel(*refs):
        outs, sems = refs[len(ins):-1], refs[-1]
        p, s = lax.axis_index("pair"), lax.axis_index("sub")
        moves = []

        def place(source, which, side, at, span):
            columns = pl.ds(pl.multiple_of(side * half + at * part + span[0], HD), span[1] - span[0])
            moves.append((source, outs[which].at[:, columns]))

        for chunk, span in enumerate(spans):
            for i, side in enumerate((p, 1 - p)):
                near_ref, far_ref = refs[4 * chunk + i], refs[4 * chunk + 2 + i]
                for by in range(peers):
                    at = lax.rem(s - by + peers, peers)
                    place(near_ref.at[2 + by], 0, side, at, span)
                    for which in range(2):
                        source = far_ref.at[which, by - 1] if by else near_ref.at[which]
                        place(source, 1 + which, side, at, span)
        run_moves(moves, sems)

    outs = [shape(rows, 2 * half)] * 3
    scratch = [pltpu.SemaphoreType.DMA((6 * len(spans) * peers,))]
    return call(kernel, ins, outs, scratch, "laid_out")


def allowed_bias(session, rows):
    strip = rows * lax.axis_size("sub")
    block = 2 * strip
    at_block = lax.axis_index("blk")
    window = jnp.concatenate([jnp.zeros((block,), jnp.int32), session])
    sess = lax.dynamic_slice_in_dim(window, at_block * block, 2 * block)
    place = (at_block - 1) * block + jnp.arange(2 * block, dtype=jnp.int32)

    def tile_bias(tile):
        q_at = slice(block + tile * strip, block + (tile + 1) * strip)
        k_at = slice(tile * strip, (tile + 3) * strip)
        k_place, q_place = place[k_at, None], place[None, q_at]
        allowed = (sess[None, q_at] == sess[k_at, None]) & (k_place <= q_place) & (k_place >= 0)
        return jnp.where(allowed, 0.0, NEG_FILL)

    return jnp.stack([tile_bias(0), tile_bias(1)])


def shards(queries, keys, values, out_grad, session):
    peers = lax.axis_size("sub")
    others = list(range(1, peers))
    part = queries.shape[1] // (2 * peers)
    spans, at = [], 0
    for heads in chunks_of(part // HD):
        spans.append((at, at + heads * HD))
        at += heads * HD
    bias = allowed_bias(session, queries.shape[0])
    kv_far, near_send, near_keep = first_keys([keys, values], *spans[0])
    kv_far = [round_sub(value, by) for by, value in zip(others, kv_far)]
    rest = [([queries, out_grad], *spans[0])] + [([keys, values, queries, out_grad], *span) for span in spans[1:]]
    rest = first_parts(rest, [near_keep])
    near_theirs = swapped(near_send)
    kv_parts = [None]
    qg_parts = [(rest[0][1], swapped(rest[0][0]), 0)]
    for send, own in rest[1:]:
        paired = swapped(send)
        kv_parts.append((own, paired, 0))
        qg_parts.append((own, paired, 2))
    count = len(spans)
    kv_sends, qg_sends, kv, qg, kv_own, own_earlier = [], [], [], [], [], []
    for index in range(count):
        if index:
            kv_sends.append(head_parts(*kv_parts[index], others, kv[index - 1] + own_earlier[index - 1:index]))
            kv.append([round_sub(value, by) for by, value in zip(others, kv_sends[index])])
            kv_own.append(head_parts(*kv_parts[index], [0], own_earlier[index - 1:index]))
        else:
            kv_sends.append([])
            kv_own.append(both_rows([near_keep], near_theirs.reshape(1, *near_theirs.shape)))
            kv.append(both_rows(kv_far, swapped(other_side(kv_far))))
        own_earlier.append(along_blocks(kv_own[index][0], 1, True))
        qg_sends.append(head_parts(*qg_parts[index], others, qg[index - 1] if index else []))
        qg.append([round_sub(value, by) for by, value in zip(others, qg_sends[index])])
    chunks, first_dq, back = [], [], []
    for index, (low, high) in enumerate(spans):
        last = index == count - 1
        forward = [relayed(value, first_dq) if index else value for value in kv[index]]
        earlier = [own_earlier[index]] + [along_blocks(value, 1, not last) for value in forward]
        qg_all = head_parts(*qg_parts[index], [0], []) + qg[index]
        kv_all = kv_own[index] + kv[index]
        heads = (high - low) // HD
        if last:
            grads, dq, early = attention_grads(bias, kv_all, earlier, qg_all, True, 0, heads, [])
            dq = [dq[0]] + [round_sub(dq[by], by) for by in others]
            later = [along_blocks(relayed(value, back), -1, False) for value in early[1:]]
            dkv = summed([grads], later, others, dq[1:])
            own_later = along_blocks(relayed(early[0], dkv), -1, False)
            send_k, send_v, keep = last_rows(grads, own_later)
            send, keep_dq = query_rows(dq)
            theirs = [swapped(send_k), swapped(send_v), swapped(send)]
            near = [stacked([keep, keep_dq]), stacked(theirs)]
        else:
            grads, dq, early = attention_grads(bias, kv_all, earlier, qg_all, False, 0, heads, [])
            first_dq = dq[:1]
            dq = [dq[0]] + [round_sub(dq[by], by) for by in others]
            back = dq[1:]
            dkv = summed([grads], [along_blocks(early[0], -1, False)], [0] + others, dq[1:])
            send, keep = far_rows(dkv[:1])
            send_dq, keep_dq = query_rows(dq)
            two = (2,) + keep.shape[2:]
            near = [stacked([keep.reshape(two), keep_dq]), stacked([swapped(send).reshape(two), swapped(send_dq)])]
            dkv = dkv[1:]
        send, keep = far_rows([round_sub(value, by) for by, value in zip(others, dkv)])
        chunks.append(near + [keep, swapped(send)])
    return tuple(laid_out(chunks, spans))


def solution(mesh):
    spread = P(("grp", "blk", "pair", "sub"), None)
    return jax.shard_map(
        shards, mesh=mesh, in_specs=(spread,) * 4 + (P("grp"),), out_specs=(spread,) * 3, check_vma=False
    )
```

```python
import math

import jax
import jax.numpy as jnp
from jax import lax
from jax.experimental import pallas as pl
from jax.experimental.pallas import tpu as pltpu
from jax.sharding import PartitionSpec as P

HD = 128
NEG_FILL = -1e30
LOW = jnp.bfloat16
WIDE = jnp.float32
MIB = 1024 * 1024
TO_BITS = HD ** (-0.5) / math.log(2.0)
SCALE = HD ** (-0.5)
ROWS_BY_ROWS = (((1,), (1,)), ((), ()))


def chunks_of(heads):
    return [heads // 2, heads - heads // 2]


def along_blocks(value, by, ring):
    peers = lax.axis_size("blk")
    pairs = [(i, (i + by) % peers) for i in range(peers) if ring or 0 <= i + by < peers]
    return lax.ppermute(value, "blk", pairs)


def round_sub(value, by):
    peers = lax.axis_size("sub")
    return lax.ppermute(value, "sub", [(i, (i + by) % peers) for i in range(peers)])


def swapped(value):
    return lax.ppermute(value, "pair", [(0, 1), (1, 0)])


def run_moves(moves, sems):
    copies = [pltpu.make_async_copy(src, dst, sems.at[at]) for at, (src, dst) in enumerate(moves)]
    for copy in copies:
        copy.start()
    for copy in copies:
        copy.wait()


def call(kernel, ins, outs, scratch, name, whole=False, flops=0, room=8 * MIB):
    spec = pl.BlockSpec(memory_space=pltpu.VMEM if whole else pl.ANY)
    moved = sum(math.prod(a.shape) * a.dtype.itemsize for a in list(ins) + list(outs))
    return list(
        pl.pallas_call(
            kernel,
            out_shape=outs,
            in_specs=[spec] * len(ins),
            out_specs=[spec] * len(outs),
            scratch_shapes=scratch,
            name=name,
            cost_estimate=pl.CostEstimate(flops=flops, bytes_accessed=moved, transcendentals=0),
            compiler_params=pltpu.CompilerParams(vmem_limit_bytes=room),
        )(*ins)
    )


def shape(*dims, dtype=LOW):
    return jax.ShapeDtypeStruct(dims, dtype)


def first_parts(groups, after):
    held, wanted, outs = [], [], []
    for arrays, low, high in groups:
        rows, width = arrays[0].shape
        peers = lax.axis_size("sub")
        half = width // 2
        part = half // peers
        wanted.append((len(held), len(arrays), low, high))
        held += [pltpu.with_memory_space_constraint(array, pltpu.HBM) for array in arrays]
        outs += [pltpu.VMEM((len(arrays), peers, rows, high - low), LOW)] * 2

    def kernel(*refs):
        out_refs, sems = refs[-1 - len(outs):-1], refs[-1]
        p = lax.axis_index("pair")
        moves = []
        for group, (first, count, low, high) in enumerate(wanted):
            for side, out in zip((1 - p, p), out_refs[2 * group:2 * group + 2]):
                for at in range(peers):
                    start = pl.multiple_of(side * half + at * part + low, HD)
                    for i in range(count):
                        moves.append((refs[first + i].at[:, pl.ds(start, high - low)], out.at[i, at]))
        run_moves(moves, sems)

    spec = pl.BlockSpec(memory_space=pl.ANY)
    parts = pl.pallas_call(
        kernel,
        out_shape=outs,
        in_specs=[spec] * (len(held) + len(after)),
        out_specs=[spec] * len(outs),
        scratch_shapes=[pltpu.SemaphoreType.DMA((2 * peers * len(held),))],
        name="first_parts",
        compiler_params=pltpu.CompilerParams(vmem_limit_bytes=8 * MIB),
    )(*held, *after)
    return [(parts[2 * i], parts[2 * i + 1]) for i in range(len(groups))]


def first_keys(arrays, low, high):
    rows, width = arrays[0].shape
    half = width // 2
    peers = lax.axis_size("sub")
    part = half // peers
    cut = high - low

    def kernel(*refs):
        ins, far, (send, keep), sems = refs[:2], refs[2:1 + peers], refs[1 + peers:-1], refs[-1]
        p, s = lax.axis_index("pair"), lax.axis_index("sub")
        moves = []
        for i, ref in enumerate(ins):
            for by in range(1, peers):
                for side in range(2):
                    start = pl.multiple_of(side * half + lax.rem(s + by, peers) * part + low, HD)
                    moves.append((ref.at[:, pl.ds(start, cut)], far[by - 1].at[i, side]))
            for out, side in ((send, 1 - p), (keep, p)):
                start = pl.multiple_of(side * half + s * part + low, HD)
                moves.append((ref.at[:, pl.ds(start, cut)], out.at[i]))
        run_moves(moves, sems)

    spec = pl.BlockSpec(memory_space=pl.ANY)
    outs = [pltpu.VMEM((2, 2, rows, cut), LOW)] * (peers - 1) + [pltpu.VMEM((2, rows, cut), LOW)] * 2
    parts = pl.pallas_call(
        kernel,
        out_shape=outs,
        in_specs=[spec] * 2,
        out_specs=[spec] * len(outs),
        scratch_shapes=[pltpu.SemaphoreType.DMA((4 * peers,))],
        name="first_keys",
        compiler_params=pltpu.CompilerParams(vmem_limit_bytes=8 * MIB),
    )(*[pltpu.with_memory_space_constraint(array, pltpu.HBM) for array in arrays])
    return list(parts[:-2]), parts[-2], parts[-1]


def other_side(received):
    count = len(received)

    def kernel(*refs):
        p = lax.axis_index("pair")
        run_moves([(ref.at[:, 1 - p], refs[-2].at[by]) for by, ref in enumerate(refs[:count])], refs[-1])

    _, _, rows, cut = received[0].shape
    scratch = [pltpu.SemaphoreType.DMA((count,))]
    return call(kernel, received, [shape(count, 2, rows, cut)], scratch, "other_side")[0]


def both_rows(mine, theirs):
    count = len(mine)
    _, _, rows, cut = theirs.shape

    def kernel(*refs):
        ins, theirs_ref, outs, sems = refs[:count], refs[count], refs[count + 1:-1], refs[-1]
        p = lax.axis_index("pair")
        moves = []
        for by, (ref, out) in enumerate(zip(ins, outs)):
            source = ref.at[:, p] if len(ref.shape) == 4 else ref
            moves += [(source, out.at[:, p]), (theirs_ref.at[by], out.at[:, 1 - p])]
        run_moves(moves, sems)

    outs = [shape(2, 2, rows, cut)] * count
    scratch = [pltpu.SemaphoreType.DMA((2 * count,))]
    return call(kernel, mine + [theirs], outs, scratch, "both_rows")


def head_parts(own, paired, which, turns, after):
    _, peers, rows, cut = own.shape
    chosen = pl.ds(which, 2)

    def kernel(own_ref, pair_ref, *refs):
        outs, sems = refs[len(after):-1], refs[-1]
        p, s = lax.axis_index("pair"), lax.axis_index("sub")
        moves = []
        for by, out in zip(turns, outs):
            at = lax.rem(s + by, peers)
            moves += [(own_ref.at[chosen, at], out.at[:, p]), (pair_ref.at[chosen, at], out.at[:, 1 - p])]
        run_moves(moves, sems)

    outs = [shape(2, 2, rows, cut)] * len(turns)
    scratch = [pltpu.SemaphoreType.DMA((2 * len(turns),))]
    return call(kernel, [own, paired] + after, outs, scratch, "head_parts")


def relayed(value, after):
    def kernel(value_ref, *refs):
        run_moves([(value_ref, refs[-2])], refs[-1])

    scratch = [pltpu.SemaphoreType.DMA((1,))]
    return call(kernel, [value] + after, [shape(*value.shape)], scratch, "relayed")[0]


def attention_grads(bias, kv, kv_earlier, qg, split, first, heads, after):
    peers = len(kv)
    rows, cut = kv[0].shape[2], heads * HD
    chosen = pl.ds(first * HD, cut)
    strip = rows * peers
    early_count = peers if split else 1

    def kernel(*refs):
        bias_ref = refs[0]
        kv_in, early_in, qg_in = refs[1:1 + peers], refs[1 + peers:1 + 2 * peers], refs[1 + 2 * peers:1 + 3 * peers]
        outs = refs[1 + 3 * peers + len(after):-5]
        own_out, dq_outs, early_outs = outs[0], outs[1:1 + peers], outs[1 + peers:]
        kv_all, qg_all, early, dq_all, sems = refs[-5:]
        s = lax.axis_index("sub")
        moves = []
        for by in range(peers):
            at = lax.rem(s - by + peers, peers)
            moves += [
                (early_in[by].at[:, :, :, chosen], kv_all.at[:, 0:2, at]),
                (kv_in[by].at[:, :, :, chosen], kv_all.at[:, 2:4, at]),
                (qg_in[by].at[:, :, :, chosen], qg_all.at[:, :, at]),
            ]
        run_moves(moves, sems)
        strips = [(head, tile) for head in range(heads) for tile in range(2)]
        products, terms = {}, {}

        def flat(ref, which, tiles, head):
            block = ref[which, tiles, :, :, pl.ds(head * HD, HD)]
            return block.reshape(block.shape[0] * strip, HD)

        def multiply(head, tile):
            at, span = pl.ds(tile, 1), pl.ds(tile, 3)
            q, g = flat(qg_all, 0, at, head), flat(qg_all, 1, at, head)
            k, v = flat(kv_all, 0, span, head), flat(kv_all, 1, span, head)
            scores = lax.dot_general(k, q, ROWS_BY_ROWS, preferred_element_type=WIDE)
            grad_prob = lax.dot_general(v, g, ROWS_BY_ROWS, preferred_element_type=WIDE)
            products[head, tile] = q, g, k, scores, grad_prob

        def finish(head, tile):
            q, g, k, scores, grad_prob = products.pop((head, tile))
            scores = scores * TO_BITS + bias_ref[tile]
            peak = jnp.max(scores, axis=0, keepdims=True)
            weight = jnp.exp2(scores - peak)
            prob = weight * (1.0 / jnp.sum(weight, axis=0, keepdims=True))
            prob_low = prob.astype(LOW)
            row_dot = jnp.sum(prob_low.astype(WIDE) * grad_prob, axis=0, keepdims=True)
            score_low = (prob * (grad_prob - row_dot)).astype(LOW)
            dq = jnp.dot(k.T, score_low, preferred_element_type=WIDE) * SCALE
            dq_all[tile, :, :, pl.ds(head * HD, HD)] = dq.T.astype(LOW).reshape(peers, rows, HD)
            dk = jnp.dot(score_low, q, preferred_element_type=WIDE) * SCALE
            dv = jnp.dot(prob_low, g, preferred_element_type=WIDE)
            terms[head, tile] = dk, dv

        def gather(head):
            for which in range(2):
                low, high = terms[head, 0][which], terms[head, 1][which]
                sums = (
                    low[:strip],
                    low[strip:2 * strip] + high[:strip],
                    low[2 * strip:] + high[strip:2 * strip],
                    high[2 * strip:],
                )
                for tile, total in enumerate(sums):
                    total = total.reshape(peers, rows, HD)
                    if tile < 2:
                        early[which, tile, :, :, pl.ds(head * HD, HD)] = total.astype(LOW)
                    else:
                        own_out[which, tile - 2, :, :, pl.ds(head * HD, HD)] = total

        multiply(*strips[0])
        for at, (head, tile) in enumerate(strips):
            if at + 1 < len(strips):
                multiply(*strips[at + 1])
            finish(head, tile)
            if tile == 1:
                gather(head)
        moves = [] if split else [(early, early_outs[0])]
        for by in range(peers):
            at = lax.rem(s + by, peers)
            moves.append((dq_all.at[:, at], dq_outs[by]))
            if split:
                moves.append((early.at[:, :, at], early_outs[by]))
        run_moves(moves, sems)

    outs = [shape(2, 2, peers, rows, cut, dtype=WIDE)] + [shape(2, rows, cut)] * peers
    outs += [shape(2, 2, rows, cut)] * peers if split else [shape(2, 2, peers, rows, cut)]
    scratch = [
        pltpu.VMEM((2, 4, peers, rows, cut), LOW),
        pltpu.VMEM((2, 2, peers, rows, cut), LOW),
        pltpu.VMEM((2, 2, peers, rows, cut), LOW),
        pltpu.VMEM((2, peers, rows, cut), LOW),
        pltpu.SemaphoreType.DMA((3 * peers,)),
    ]
    flops = heads * 2 * 5 * 2 * strip * 3 * strip * HD
    ins = [bias] + kv + kv_earlier + qg + after
    outs = call(kernel, ins, outs, scratch, "attention_grads", whole=True, flops=flops, room=40 * MIB)
    return outs[0], outs[1:1 + peers], outs[1 + peers:]


def summed(own, later, turns, after):
    _, _, peers, rows, _ = own[0].shape
    widths = [array.shape[-1] for array in own]
    split = later[0].ndim == 4

    def kernel(*refs):
        own_refs, later_refs = refs[:len(own)], refs[len(own):len(own) + len(later)]
        outs = refs[len(own) + len(later) + len(after):]
        s = lax.axis_index("sub")
        for place, (by, out) in enumerate(zip(turns, outs)):
            at = lax.rem(s + by, peers)
            start = 0
            for group, width in enumerate(widths):
                for which in range(2):
                    for row in range(2):
                        term = later_refs[place][which, row] if split else later_refs[group][which, row, at]
                        total = own_refs[group][which, row, at] + term.astype(WIDE)
                        out[which, row, :, pl.ds(start, width)] = total.astype(LOW)
                start += width

    outs = [shape(2, 2, rows, sum(widths))] * len(turns)
    return call(kernel, own + later + after, outs, [], "summed", whole=True)


def last_rows(own, later, dq):
    _, _, _, rows, cut = own.shape

    def kernel(own_ref, later_ref, *refs):
        dq_refs, outs = refs[:len(dq)], refs[len(dq):]
        p, s = lax.axis_index("pair"), lax.axis_index("sub")
        for out, row in zip(outs, (1 - p, p)):
            for which in range(2):
                total = own_ref[which, row, s] + later_ref[which, row].astype(WIDE)
                out[which] = total.astype(LOW)
            for by in range(len(dq)):
                out[2 + by] = dq_refs[by][row]

    return call(kernel, [own, later] + dq, [shape(2 + len(dq), rows, cut)] * 2, [], "last_rows", whole=True)


def query_rows(dq):
    peers = len(dq)
    _, rows, cut = dq[0].shape

    def kernel(*refs):
        p = lax.axis_index("pair")
        for out, row in zip(refs[peers:], (1 - p, p)):
            for by in range(peers):
                out[by] = refs[by][row]

    return call(kernel, dq, [shape(peers, rows, cut)] * 2, [], "query_rows", whole=True)


def stacked(parts):
    _, rows, cut = parts[0].shape

    def kernel(*refs):
        at = 0
        for ref in refs[:-1]:
            for i in range(ref.shape[0]):
                refs[-1][at + i] = ref[i]
            at += ref.shape[0]

    outs = [shape(sum(part.shape[0] for part in parts), rows, cut)]
    return call(kernel, parts, outs, [], "stacked", whole=True)[0]


def far_rows(received):
    peers = len(received) + 1
    _, _, rows, cut = received[0].shape

    def kernel(*refs):
        p = lax.axis_index("pair")
        for out, row in zip(refs[-2:], (1 - p, p)):
            for by in range(peers - 1):
                for which in range(2):
                    out[which, by] = refs[by][which, row]

    return call(kernel, received, [shape(2, peers - 1, rows, cut)] * 2, [], "far_rows", whole=True)


def laid_out(chunks, spans):
    peers = lax.axis_size("sub")
    rows = chunks[0][0].shape[1]
    part = spans[-1][1]
    half = part * peers
    ins = [array for chunk in chunks for array in chunk]

    def kernel(*refs):
        outs, sems = refs[len(ins):-1], refs[-1]
        p, s = lax.axis_index("pair"), lax.axis_index("sub")
        moves = []

        def place(source, which, side, at, span):
            columns = pl.ds(pl.multiple_of(side * half + at * part + span[0], HD), span[1] - span[0])
            moves.append((source, outs[which].at[:, columns]))

        for chunk, span in enumerate(spans):
            for i, side in enumerate((p, 1 - p)):
                near_ref, far_ref = refs[4 * chunk + i], refs[4 * chunk + 2 + i]
                for by in range(peers):
                    at = lax.rem(s - by + peers, peers)
                    place(near_ref.at[2 + by], 0, side, at, span)
                    for which in range(2):
                        source = far_ref.at[which, by - 1] if by else near_ref.at[which]
                        place(source, 1 + which, side, at, span)
        run_moves(moves, sems)

    outs = [shape(rows, 2 * half)] * 3
    scratch = [pltpu.SemaphoreType.DMA((6 * len(spans) * peers,))]
    return call(kernel, ins, outs, scratch, "laid_out")


def allowed_bias(session, rows):
    strip = rows * lax.axis_size("sub")
    block = 2 * strip
    at_block = lax.axis_index("blk")
    window = jnp.concatenate([jnp.zeros((block,), jnp.int32), session])
    sess = lax.dynamic_slice_in_dim(window, at_block * block, 2 * block)
    place = (at_block - 1) * block + jnp.arange(2 * block, dtype=jnp.int32)

    def tile_bias(tile):
        q_at = slice(block + tile * strip, block + (tile + 1) * strip)
        k_at = slice(tile * strip, (tile + 3) * strip)
        k_place, q_place = place[k_at, None], place[None, q_at]
        allowed = (sess[None, q_at] == sess[k_at, None]) & (k_place <= q_place) & (k_place >= 0)
        return jnp.where(allowed, 0.0, NEG_FILL)

    return jnp.stack([tile_bias(0), tile_bias(1)])


def shards(queries, keys, values, out_grad, session):
    peers = lax.axis_size("sub")
    others = list(range(1, peers))
    part = queries.shape[1] // (2 * peers)
    spans, at = [], 0
    for heads in chunks_of(part // HD):
        spans.append((at, at + heads * HD))
        at += heads * HD
    bias = allowed_bias(session, queries.shape[0])
    kv_far, near_send, near_keep = first_keys([keys, values], *spans[0])
    kv_far = [round_sub(value, by) for by, value in zip(others, kv_far)]
    rest = [([queries, out_grad], *spans[0])] + [([keys, values, queries, out_grad], *span) for span in spans[1:]]
    rest = first_parts(rest, [near_keep])
    near_theirs = swapped(near_send)
    kv_parts = [None]
    qg_parts = [(rest[0][1], swapped(rest[0][0]), 0)]
    for send, own in rest[1:]:
        paired = swapped(send)
        kv_parts.append((own, paired, 0))
        qg_parts.append((own, paired, 2))
    count = len(spans)
    kv_sends, qg_sends, kv, qg, kv_own, own_earlier = [], [], [], [], [], []
    for index in range(count):
        if index:
            kv_sends.append(head_parts(*kv_parts[index], others, kv[index - 1] + own_earlier[index - 1:index]))
            kv.append([round_sub(value, by) for by, value in zip(others, kv_sends[index])])
            kv_own.append(head_parts(*kv_parts[index], [0], own_earlier[index - 1:index]))
        else:
            kv_sends.append([])
            kv_own.append(both_rows([near_keep], near_theirs.reshape(1, *near_theirs.shape)))
            kv.append(both_rows(kv_far, swapped(other_side(kv_far))))
        own_earlier.append(along_blocks(kv_own[index][0], 1, True))
        qg_sends.append(head_parts(*qg_parts[index], others, qg[index - 1] if index else []))
        qg.append([round_sub(value, by) for by, value in zip(others, qg_sends[index])])
    chunks, first_dq, back, release = [], [], [], []
    for index, (low, high) in enumerate(spans):
        last = index == count - 1
        forward = [relayed(value, first_dq) if index else value for value in kv[index]]
        earlier = [own_earlier[index]] + [along_blocks(value, 1, not last) for value in forward]
        qg_all = head_parts(*qg_parts[index], [0], []) + qg[index]
        kv_all = kv_own[index] + kv[index]
        heads = (high - low) // HD
        if last:
            grads, dq, early = attention_grads(bias, kv_all, earlier, qg_all, True, 0, heads, [])
            dq = [dq[0]] + [round_sub(dq[by], by) for by in others]
            later = [along_blocks(relayed(value, back), -1, False) for value in early[1:]]
            dkv = summed([grads], later, others, dq[1:])
            own_later = along_blocks(relayed(early[0], release), -1, False)
            send, keep = last_rows(grads, own_later, [])
            send_dq, keep_dq = query_rows(dq)
            near = [stacked([keep, keep_dq]), stacked([swapped(send), swapped(send_dq)])]
        else:
            grads, dq, early = attention_grads(bias, kv_all, earlier, qg_all, False, 0, heads, [])
            first_dq = dq[:1]
            dq = [dq[0]] + [round_sub(dq[by], by) for by in others]
            back = dq[1:]
            dkv = summed([grads], [along_blocks(early[0], -1, False)], [0] + others, dq[1:])
            release = dkv[:1]
            send, keep = far_rows(dkv[:1])
            send_dq, keep_dq = query_rows(dq)
            two = (2,) + keep.shape[2:]
            near = [stacked([keep.reshape(two), keep_dq]), stacked([swapped(send).reshape(two), swapped(send_dq)])]
            dkv = dkv[1:]
        send, keep = far_rows([round_sub(value, by) for by, value in zip(others, dkv)])
        chunks.append(near + [keep, swapped(send)])
    return tuple(laid_out(chunks, spans))


def solution(mesh):
    spread = P(("grp", "blk", "pair", "sub"), None)
    return jax.shard_map(
        shards, mesh=mesh, in_specs=(spread,) * 4 + (P("grp"),), out_specs=(spread,) * 3, check_vma=False
    )
```

```python
import math

import jax
import jax.numpy as jnp
from jax import lax
from jax.experimental import pallas as pl
from jax.experimental.pallas import tpu as pltpu
from jax.sharding import PartitionSpec as P

HD = 128
NEG_FILL = -1e30
LOW = jnp.bfloat16
WIDE = jnp.float32
MIB = 1024 * 1024
TO_BITS = HD ** (-0.5) / math.log(2.0)
SCALE = HD ** (-0.5)
ROWS_BY_ROWS = (((1,), (1,)), ((), ()))


def chunks_of(heads):
    return [heads // 2, heads - heads // 2]


def along_blocks(value, by, ring):
    peers = lax.axis_size("blk")
    pairs = [(i, (i + by) % peers) for i in range(peers) if ring or 0 <= i + by < peers]
    return lax.ppermute(value, "blk", pairs)


def round_sub(value, by):
    peers = lax.axis_size("sub")
    return lax.ppermute(value, "sub", [(i, (i + by) % peers) for i in range(peers)])


def swapped(value):
    return lax.ppermute(value, "pair", [(0, 1), (1, 0)])


def run_moves(moves, sems):
    copies = [pltpu.make_async_copy(src, dst, sems.at[at]) for at, (src, dst) in enumerate(moves)]
    for copy in copies:
        copy.start()
    for copy in copies:
        copy.wait()


def call(kernel, ins, outs, scratch, name, whole=False, flops=0, room=8 * MIB):
    spec = pl.BlockSpec(memory_space=pltpu.VMEM if whole else pl.ANY)
    moved = sum(math.prod(a.shape) * a.dtype.itemsize for a in list(ins) + list(outs))
    return list(
        pl.pallas_call(
            kernel,
            out_shape=outs,
            in_specs=[spec] * len(ins),
            out_specs=[spec] * len(outs),
            scratch_shapes=scratch,
            name=name,
            cost_estimate=pl.CostEstimate(flops=flops, bytes_accessed=moved, transcendentals=0),
            compiler_params=pltpu.CompilerParams(vmem_limit_bytes=room),
        )(*ins)
    )


def shape(*dims, dtype=LOW):
    return jax.ShapeDtypeStruct(dims, dtype)


def first_parts(groups, after):
    held, wanted, outs = [], [], []
    for arrays, low, high in groups:
        rows, width = arrays[0].shape
        peers = lax.axis_size("sub")
        half = width // 2
        part = half // peers
        wanted.append((len(held), len(arrays), low, high))
        held += [pltpu.with_memory_space_constraint(array, pltpu.HBM) for array in arrays]
        outs += [pltpu.VMEM((len(arrays), peers, rows, high - low), LOW)] * 2

    def kernel(*refs):
        out_refs, sems = refs[-1 - len(outs):-1], refs[-1]
        p = lax.axis_index("pair")
        moves = []
        for group, (first, count, low, high) in enumerate(wanted):
            for side, out in zip((1 - p, p), out_refs[2 * group:2 * group + 2]):
                for at in range(peers):
                    start = pl.multiple_of(side * half + at * part + low, HD)
                    for i in range(count):
                        moves.append((refs[first + i].at[:, pl.ds(start, high - low)], out.at[i, at]))
        run_moves(moves, sems)

    spec = pl.BlockSpec(memory_space=pl.ANY)
    parts = pl.pallas_call(
        kernel,
        out_shape=outs,
        in_specs=[spec] * (len(held) + len(after)),
        out_specs=[spec] * len(outs),
        scratch_shapes=[pltpu.SemaphoreType.DMA((2 * peers * len(held),))],
        name="first_parts",
        compiler_params=pltpu.CompilerParams(vmem_limit_bytes=8 * MIB),
    )(*held, *after)
    return [(parts[2 * i], parts[2 * i + 1]) for i in range(len(groups))]


def head_parts(own, paired, which, turns, after):
    _, peers, rows, cut = own.shape
    chosen = pl.ds(which, 2)

    def kernel(own_ref, pair_ref, *refs):
        outs, sems = refs[len(after):-1], refs[-1]
        p, s = lax.axis_index("pair"), lax.axis_index("sub")
        moves = []
        for by, out in zip(turns, outs):
            at = lax.rem(s + by, peers)
            moves += [(own_ref.at[chosen, at], out.at[:, p]), (pair_ref.at[chosen, at], out.at[:, 1 - p])]
        run_moves(moves, sems)

    outs = [shape(2, 2, rows, cut)] * len(turns)
    scratch = [pltpu.SemaphoreType.DMA((2 * len(turns),))]
    return call(kernel, [own, paired] + after, outs, scratch, "head_parts")


def relayed(value, after):
    def kernel(value_ref, *refs):
        run_moves([(value_ref, refs[-2])], refs[-1])

    scratch = [pltpu.SemaphoreType.DMA((1,))]
    return call(kernel, [value] + after, [shape(*value.shape)], scratch, "relayed")[0]


def attention_grads(bias, kv, kv_earlier, qg, split, after):
    peers = len(kv)
    _, _, rows, cut = kv[0].shape
    heads = cut // HD
    strip = rows * peers
    early_count = peers if split else 1

    def kernel(*refs):
        bias_ref = refs[0]
        kv_in, early_in, qg_in = refs[1:1 + peers], refs[1 + peers:1 + 2 * peers], refs[1 + 2 * peers:1 + 3 * peers]
        outs = refs[1 + 3 * peers + len(after):-5]
        own_out, dq_outs, early_outs = outs[0], outs[1:1 + peers], outs[1 + peers:]
        kv_all, qg_all, early, dq_all, sems = refs[-5:]
        s = lax.axis_index("sub")
        moves = []
        for by in range(peers):
            at = lax.rem(s - by + peers, peers)
            moves += [
                (early_in[by], kv_all.at[:, 0:2, at]),
                (kv_in[by], kv_all.at[:, 2:4, at]),
                (qg_in[by], qg_all.at[:, :, at]),
            ]
        run_moves(moves, sems)
        strips = [(head, tile) for head in range(heads) for tile in range(2)]
        products, terms = {}, {}

        def flat(ref, which, tiles, head):
            block = ref[which, tiles, :, :, pl.ds(head * HD, HD)]
            return block.reshape(block.shape[0] * strip, HD)

        def multiply(head, tile):
            at, span = pl.ds(tile, 1), pl.ds(tile, 3)
            q, g = flat(qg_all, 0, at, head), flat(qg_all, 1, at, head)
            k, v = flat(kv_all, 0, span, head), flat(kv_all, 1, span, head)
            scores = lax.dot_general(k, q, ROWS_BY_ROWS, preferred_element_type=WIDE)
            grad_prob = lax.dot_general(v, g, ROWS_BY_ROWS, preferred_element_type=WIDE)
            products[head, tile] = q, g, k, scores, grad_prob

        def finish(head, tile):
            q, g, k, scores, grad_prob = products.pop((head, tile))
            scores = scores * TO_BITS + bias_ref[tile]
            peak = jnp.max(scores, axis=0, keepdims=True)
            weight = jnp.exp2(scores - peak)
            prob = weight * (1.0 / jnp.sum(weight, axis=0, keepdims=True))
            prob_low = prob.astype(LOW)
            row_dot = jnp.sum(prob_low.astype(WIDE) * grad_prob, axis=0, keepdims=True)
            score_low = (prob * (grad_prob - row_dot)).astype(LOW)
            dq = jnp.dot(k.T, score_low, preferred_element_type=WIDE) * SCALE
            dq_all[tile, :, :, pl.ds(head * HD, HD)] = dq.T.astype(LOW).reshape(peers, rows, HD)
            dk = jnp.dot(score_low, q, preferred_element_type=WIDE) * SCALE
            dv = jnp.dot(prob_low, g, preferred_element_type=WIDE)
            terms[head, tile] = dk, dv

        def gather(head):
            for which in range(2):
                low, high = terms[head, 0][which], terms[head, 1][which]
                sums = (
                    low[:strip],
                    low[strip:2 * strip] + high[:strip],
                    low[2 * strip:] + high[strip:2 * strip],
                    high[2 * strip:],
                )
                for tile, total in enumerate(sums):
                    total = total.reshape(peers, rows, HD)
                    if tile < 2:
                        early[which, tile, :, :, pl.ds(head * HD, HD)] = total.astype(LOW)
                    else:
                        own_out[which, tile - 2, :, :, pl.ds(head * HD, HD)] = total

        multiply(*strips[0])
        for at, (head, tile) in enumerate(strips):
            if at + 1 < len(strips):
                multiply(*strips[at + 1])
            finish(head, tile)
            if tile == 1:
                gather(head)
        moves = [] if split else [(early, early_outs[0])]
        for by in range(peers):
            at = lax.rem(s + by, peers)
            moves.append((dq_all.at[:, at], dq_outs[by]))
            if split:
                moves.append((early.at[:, :, at], early_outs[by]))
        run_moves(moves, sems)

    outs = [shape(2, 2, peers, rows, cut, dtype=WIDE)] + [shape(2, rows, cut)] * peers
    outs += [shape(2, 2, rows, cut)] * peers if split else [shape(2, 2, peers, rows, cut)]
    scratch = [
        pltpu.VMEM((2, 4, peers, rows, cut), LOW),
        pltpu.VMEM((2, 2, peers, rows, cut), LOW),
        pltpu.VMEM((2, 2, peers, rows, cut), LOW),
        pltpu.VMEM((2, peers, rows, cut), LOW),
        pltpu.SemaphoreType.DMA((3 * peers,)),
    ]
    flops = heads * 2 * 5 * 2 * strip * 3 * strip * HD
    ins = [bias] + kv + kv_earlier + qg + after
    outs = call(kernel, ins, outs, scratch, "attention_grads", whole=True, flops=flops, room=40 * MIB)
    return outs[0], outs[1:1 + peers], outs[1 + peers:]


def summed(own, later, turns, after):
    _, _, peers, rows, cut = own.shape
    split = len(later) > 1 or later[0].ndim == 4

    def kernel(own_ref, *refs):
        later_refs, outs = refs[:len(later)], refs[len(later) + len(after):]
        s = lax.axis_index("sub")
        for place, (by, out) in enumerate(zip(turns, outs)):
            at = lax.rem(s + by, peers)
            for which in range(2):
                for row in range(2):
                    term = later_refs[place][which, row] if split else later_refs[0][which, row, at]
                    out[which, row] = (own_ref[which, row, at] + term.astype(WIDE)).astype(LOW)

    outs = [shape(2, 2, rows, cut)] * len(turns)
    return call(kernel, [own] + later + after, outs, [], "summed", whole=True)


def rows_for_pair(dq, dkv):
    peers = len(dq)
    _, rows, cut = dq[0].shape

    def kernel(*refs):
        dq_refs, dkv_refs, (send, keep) = refs[:peers], refs[peers:2 * peers], refs[-2:]
        p, s = lax.axis_index("pair"), lax.axis_index("sub")
        for by in range(peers):
            at = lax.rem(s - by + peers, peers)
            for out, row in ((send, 1 - p), (keep, p)):
                out[0, at] = dq_refs[by][row]
                for which in range(2):
                    out[1 + which, at] = dkv_refs[by][which, row]

    outs = [shape(3, peers, rows, cut)] * 2
    return call(kernel, dq + dkv, outs, [], "rows_for_pair", whole=True)


def laid_out(kept, paired, spans):
    _, peers, rows, _ = kept[0].shape
    part = spans[-1][1]
    half = part * peers
    count = len(spans)

    def kernel(*refs):
        keep, rec, outs, sems = refs[:count], refs[count:2 * count], refs[2 * count:-1], refs[-1]
        p = lax.axis_index("pair")
        moves = []
        for mine, theirs, (low, high) in zip(keep, rec, spans):
            for source, side in ((mine, p), (theirs, 1 - p)):
                for at in range(peers):
                    columns = pl.ds(pl.multiple_of(side * half + at * part + low, HD), high - low)
                    moves += [(source.at[which, at], out.at[:, columns]) for which, out in enumerate(outs)]
        run_moves(moves, sems)

    outs = [shape(rows, 2 * half)] * 3
    return call(kernel, kept + paired, outs, [pltpu.SemaphoreType.DMA((6 * count * peers,))], "laid_out")


def allowed_bias(session, rows):
    strip = rows * lax.axis_size("sub")
    block = 2 * strip
    at_block = lax.axis_index("blk")
    window = jnp.concatenate([jnp.zeros((block,), jnp.int32), session])
    sess = lax.dynamic_slice_in_dim(window, at_block * block, 2 * block)
    place = (at_block - 1) * block + jnp.arange(2 * block, dtype=jnp.int32)

    def tile_bias(tile):
        q_at = slice(block + tile * strip, block + (tile + 1) * strip)
        k_at = slice(tile * strip, (tile + 3) * strip)
        k_place, q_place = place[k_at, None], place[None, q_at]
        allowed = (sess[None, q_at] == sess[k_at, None]) & (k_place <= q_place) & (k_place >= 0)
        return jnp.where(allowed, 0.0, NEG_FILL)

    return jnp.stack([tile_bias(0), tile_bias(1)])


def shards(queries, keys, values, out_grad, session):
    peers = lax.axis_size("sub")
    others = list(range(1, peers))
    part = queries.shape[1] // (2 * peers)
    spans, at = [], 0
    for heads in chunks_of(part // HD):
        spans.append((at, at + heads * HD))
        at += heads * HD
    bias = allowed_bias(session, queries.shape[0])
    (kv_send, kv_first), = first_parts([([keys, values], *spans[0])], [])
    rest = [([queries, out_grad], *spans[0])] + [([keys, values, queries, out_grad], *span) for span in spans[1:]]
    rest = first_parts(rest, [kv_first])
    kv_parts = [(kv_first, swapped(kv_send), 0)]
    qg_parts = [(rest[0][1], swapped(rest[0][0]), 0)]
    for send, own in rest[1:]:
        paired = swapped(send)
        kv_parts.append((own, paired, 0))
        qg_parts.append((own, paired, 2))
    count = len(spans)
    kv_sends, qg_sends, kv, qg, kv_own, own_earlier = [], [], [], [], [], []
    for index in range(count):
        kv_sends.append(head_parts(*kv_parts[index], others, kv[index - 1] if index else []))
        kv.append([round_sub(value, by) for by, value in zip(others, kv_sends[index])])
        kv_own.append(head_parts(*kv_parts[index], [0], own_earlier[index - 1:index]))
        own_earlier.append(along_blocks(kv_own[index][0], 1, True))
        qg_sends.append(head_parts(*qg_parts[index], others, qg[index - 1] if index else []))
        qg.append([round_sub(value, by) for by, value in zip(others, qg_sends[index])])
    kept, paired, back, release = [], [], [], []
    for index in range(count):
        last = index == count - 1
        forward = [relayed(value, [first_dq]) if index else value for value in kv[index]]
        earlier = [own_earlier[index]] + [along_blocks(value, 1, not last) for value in forward]
        qg_all = head_parts(*qg_parts[index], [0], []) + qg[index]
        grads, dq, early = attention_grads(bias, kv_own[index] + kv[index], earlier, qg_all, last, [])
        first_dq = dq[0]
        dq = [dq[0]] + [round_sub(dq[by], by) for by in others]
        if last:
            later = [along_blocks(relayed(value, back), -1, False) for value in early[1:]]
            dkv = summed(grads, later, others, dq[1:])
            near = along_blocks(relayed(early[0], release), -1, False)
            dkv = summed(grads, [near], [0], []) + [round_sub(value, by) for by, value in zip(others, dkv)]
        else:
            back = dq[1:]
            dkv = summed(grads, [along_blocks(early[0], -1, False)], [0] + others, dq[1:])
            release = dkv[:1]
            dkv = [dkv[0]] + [round_sub(dkv[by], by) for by in others]
        send, keep = rows_for_pair(dq, dkv)
        kept.append(keep)
        paired.append(swapped(send))
    return tuple(laid_out(kept, paired, spans))


def solution(mesh):
    spread = P(("grp", "blk", "pair", "sub"), None)
    return jax.shard_map(
        shards, mesh=mesh, in_specs=(spread,) * 4 + (P("grp"),), out_specs=(spread,) * 3, check_vma=False
    )
```

```python
import functools
import math

import jax
import jax.numpy as jnp
from jax import lax
from jax.experimental import pallas as pl
from jax.experimental.pallas import tpu as pltpu
from jax.sharding import PartitionSpec as P

HD = 128
NEG_FILL = -1e30
LOW = jnp.bfloat16
WIDE = jnp.float32
MIB = 1024 * 1024
TO_BITS = HD ** (-0.5) / math.log(2.0)
SCALE = HD ** (-0.5)
ROWS_BY_ROWS = (((1,), (1,)), ((), ()))


def chunks_of(heads):
    return [heads // 2, heads - heads // 2]


def along_blocks(value, by, ring):
    peers = lax.axis_size("blk")
    pairs = [(i, (i + by) % peers) for i in range(peers) if ring or 0 <= i + by < peers]
    return lax.ppermute(value, "blk", pairs)


def round_sub(value, by):
    peers = lax.axis_size("sub")
    return lax.ppermute(value, "sub", [(i, (i + by) % peers) for i in range(peers)])


def swapped(value):
    return lax.ppermute(value, "pair", [(0, 1), (1, 0)])


def run_moves(moves, sems):
    copies = [pltpu.make_async_copy(src, dst, sems.at[at]) for at, (src, dst) in enumerate(moves)]
    for copy in copies:
        copy.start()
    for copy in copies:
        copy.wait()


def call(kernel, ins, outs, scratch, name, whole=False, flops=0, room=8 * MIB):
    spec = pl.BlockSpec(memory_space=pltpu.VMEM if whole else pl.ANY)
    moved = sum(math.prod(a.shape) * a.dtype.itemsize for a in list(ins) + list(outs))
    return list(
        pl.pallas_call(
            kernel,
            out_shape=outs,
            in_specs=[spec] * len(ins),
            out_specs=[spec] * len(outs),
            scratch_shapes=scratch,
            name=name,
            cost_estimate=pl.CostEstimate(flops=flops, bytes_accessed=moved, transcendentals=0),
            compiler_params=pltpu.CompilerParams(vmem_limit_bytes=room),
        )(*ins)
    )


def shape(*dims, dtype=LOW):
    return jax.ShapeDtypeStruct(dims, dtype)


def first_parts(groups, after):
    held, wanted, outs = [], [], []
    for arrays, low, high in groups:
        rows, width = arrays[0].shape
        peers = lax.axis_size("sub")
        half = width // 2
        part = half // peers
        wanted.append((len(held), len(arrays), low, high))
        held += [pltpu.with_memory_space_constraint(array, pltpu.HBM) for array in arrays]
        outs += [pltpu.VMEM((len(arrays), peers, rows, high - low), LOW)] * 2

    def kernel(*refs):
        out_refs, sems = refs[-1 - len(outs):-1], refs[-1]
        p = lax.axis_index("pair")
        moves = []
        for group, (first, count, low, high) in enumerate(wanted):
            for side, out in zip((1 - p, p), out_refs[2 * group:2 * group + 2]):
                for at in range(peers):
                    start = pl.multiple_of(side * half + at * part + low, HD)
                    for i in range(count):
                        moves.append((refs[first + i].at[:, pl.ds(start, high - low)], out.at[i, at]))
        run_moves(moves, sems)

    spec = pl.BlockSpec(memory_space=pl.ANY)
    parts = pl.pallas_call(
        kernel,
        out_shape=outs,
        in_specs=[spec] * (len(held) + len(after)),
        out_specs=[spec] * len(outs),
        scratch_shapes=[pltpu.SemaphoreType.DMA((2 * peers * len(held),))],
        name="first_parts",
        compiler_params=pltpu.CompilerParams(vmem_limit_bytes=8 * MIB),
    )(*held, *after)
    return [(parts[2 * i], parts[2 * i + 1]) for i in range(len(groups))]


def head_parts(own, paired, which, turns, after):
    _, peers, rows, cut = own.shape
    chosen = pl.ds(which, 2)

    def kernel(own_ref, pair_ref, *refs):
        outs, sems = refs[len(after):-1], refs[-1]
        p, s = lax.axis_index("pair"), lax.axis_index("sub")
        moves = []
        for by, out in zip(turns, outs):
            at = lax.rem(s + by, peers)
            moves += [(own_ref.at[chosen, at], out.at[:, p]), (pair_ref.at[chosen, at], out.at[:, 1 - p])]
        run_moves(moves, sems)

    outs = [shape(2, 2, rows, cut)] * len(turns)
    scratch = [pltpu.SemaphoreType.DMA((2 * len(turns),))]
    return call(kernel, [own, paired] + after, outs, scratch, "head_parts")


def relayed(value, after):
    def kernel(value_ref, *refs):
        run_moves([(value_ref, refs[-2])], refs[-1])

    scratch = [pltpu.SemaphoreType.DMA((1,))]
    return call(kernel, [value] + after, [shape(*value.shape)], scratch, "relayed")[0]


def attention_grads(bias, kv, kv_earlier, qg, split, after):
    peers = len(kv)
    _, _, rows, cut = kv[0].shape
    heads = cut // HD
    strip = rows * peers
    early_count = peers if split else 1

    def kernel(*refs):
        bias_ref = refs[0]
        kv_in, early_in, qg_in = refs[1:1 + peers], refs[1 + peers:1 + 2 * peers], refs[1 + 2 * peers:1 + 3 * peers]
        outs = refs[1 + 3 * peers + len(after):-5]
        own_out, dq_outs, early_outs = outs[0], outs[1:1 + peers], outs[1 + peers:]
        kv_all, qg_all, early, dq_all, sems = refs[-5:]
        s = lax.axis_index("sub")
        moves = []
        for by in range(peers):
            at = lax.rem(s - by + peers, peers)
            moves += [
                (early_in[by], kv_all.at[:, 0:2, at]),
                (kv_in[by], kv_all.at[:, 2:4, at]),
                (qg_in[by], qg_all.at[:, :, at]),
            ]
        run_moves(moves, sems)
        strips = [(head, tile) for head in range(heads) for tile in range(2)]
        products, terms = {}, {}

        def flat(ref, which, tiles, head):
            block = ref[which, tiles, :, :, pl.ds(head * HD, HD)]
            return block.reshape(block.shape[0] * strip, HD)

        def multiply(head, tile):
            at, span = pl.ds(tile, 1), pl.ds(tile, 3)
            q, g = flat(qg_all, 0, at, head), flat(qg_all, 1, at, head)
            k, v = flat(kv_all, 0, span, head), flat(kv_all, 1, span, head)
            scores = lax.dot_general(k, q, ROWS_BY_ROWS, preferred_element_type=WIDE)
            grad_prob = lax.dot_general(v, g, ROWS_BY_ROWS, preferred_element_type=WIDE)
            products[head, tile] = q, g, k, scores, grad_prob

        def finish(head, tile):
            q, g, k, scores, grad_prob = products.pop((head, tile))
            cuts = [slice(at, at + HD) for at in range(0, 3 * strip, HD)]
            scaled = [scores[cut] * TO_BITS + bias_ref[tile, cut] for cut in cuts]
            peak = jnp.max(functools.reduce(jnp.maximum, scaled), axis=0, keepdims=True)
            weight = [jnp.exp2(piece - peak) for piece in scaled]
            inverse = 1.0 / jnp.sum(functools.reduce(jnp.add, weight), axis=0, keepdims=True)
            prob = [piece * inverse for piece in weight]
            low = [piece.astype(LOW) for piece in prob]
            dots = [piece.astype(WIDE) * grad_prob[cut] for piece, cut in zip(low, cuts)]
            row_dot = jnp.sum(functools.reduce(jnp.add, dots), axis=0, keepdims=True)
            score_low = [(piece * (grad_prob[cut] - row_dot)).astype(LOW) for piece, cut in zip(prob, cuts)]
            prob_low, score_low = jnp.concatenate(low, axis=0), jnp.concatenate(score_low, axis=0)
            dq = jnp.dot(k.T, score_low, preferred_element_type=WIDE) * SCALE
            dq_all[tile, :, :, pl.ds(head * HD, HD)] = dq.T.astype(LOW).reshape(peers, rows, HD)
            dk = jnp.dot(score_low, q, preferred_element_type=WIDE) * SCALE
            dv = jnp.dot(prob_low, g, preferred_element_type=WIDE)
            terms[head, tile] = dk, dv

        def gather(head):
            for which in range(2):
                low, high = terms[head, 0][which], terms[head, 1][which]
                sums = (
                    low[:strip],
                    low[strip:2 * strip] + high[:strip],
                    low[2 * strip:] + high[strip:2 * strip],
                    high[2 * strip:],
                )
                for tile, total in enumerate(sums):
                    total = total.reshape(peers, rows, HD)
                    if tile < 2:
                        early[which, tile, :, :, pl.ds(head * HD, HD)] = total.astype(LOW)
                    else:
                        own_out[which, tile - 2, :, :, pl.ds(head * HD, HD)] = total

        multiply(*strips[0])
        for at, (head, tile) in enumerate(strips):
            if at + 1 < len(strips):
                multiply(*strips[at + 1])
            finish(head, tile)
            if tile == 1:
                gather(head)
        moves = [] if split else [(early, early_outs[0])]
        for by in range(peers):
            at = lax.rem(s + by, peers)
            moves.append((dq_all.at[:, at], dq_outs[by]))
            if split:
                moves.append((early.at[:, :, at], early_outs[by]))
        run_moves(moves, sems)

    outs = [shape(2, 2, peers, rows, cut, dtype=WIDE)] + [shape(2, rows, cut)] * peers
    outs += [shape(2, 2, rows, cut)] * peers if split else [shape(2, 2, peers, rows, cut)]
    scratch = [
        pltpu.VMEM((2, 4, peers, rows, cut), LOW),
        pltpu.VMEM((2, 2, peers, rows, cut), LOW),
        pltpu.VMEM((2, 2, peers, rows, cut), LOW),
        pltpu.VMEM((2, peers, rows, cut), LOW),
        pltpu.SemaphoreType.DMA((3 * peers,)),
    ]
    flops = heads * 2 * 5 * 2 * strip * 3 * strip * HD
    ins = [bias] + kv + kv_earlier + qg + after
    outs = call(kernel, ins, outs, scratch, "attention_grads", whole=True, flops=flops, room=40 * MIB)
    return outs[0], outs[1:1 + peers], outs[1 + peers:]


def summed(own, later, turns, after):
    _, _, peers, rows, cut = own.shape
    split = len(later) > 1 or later[0].ndim == 4

    def kernel(own_ref, *refs):
        later_refs, outs = refs[:len(later)], refs[len(later) + len(after):]
        s = lax.axis_index("sub")
        for place, (by, out) in enumerate(zip(turns, outs)):
            at = lax.rem(s + by, peers)
            for which in range(2):
                for row in range(2):
                    term = later_refs[place][which, row] if split else later_refs[0][which, row, at]
                    out[which, row] = (own_ref[which, row, at] + term.astype(WIDE)).astype(LOW)

    outs = [shape(2, 2, rows, cut)] * len(turns)
    return call(kernel, [own] + later + after, outs, [], "summed", whole=True)


def rows_for_pair(dq, dkv):
    peers = len(dq)
    _, rows, cut = dq[0].shape

    def kernel(*refs):
        dq_refs, dkv_refs, (send, keep) = refs[:peers], refs[peers:2 * peers], refs[-2:]
        p, s = lax.axis_index("pair"), lax.axis_index("sub")
        for by in range(peers):
            at = lax.rem(s - by + peers, peers)
            for out, row in ((send, 1 - p), (keep, p)):
                out[0, at] = dq_refs[by][row]
                for which in range(2):
                    out[1 + which, at] = dkv_refs[by][which, row]

    outs = [shape(3, peers, rows, cut)] * 2
    return call(kernel, dq + dkv, outs, [], "rows_for_pair", whole=True)


def laid_out(kept, paired, spans):
    _, peers, rows, _ = kept[0].shape
    part = spans[-1][1]
    half = part * peers
    count = len(spans)

    def kernel(*refs):
        keep, rec, outs, sems = refs[:count], refs[count:2 * count], refs[2 * count:-1], refs[-1]
        p = lax.axis_index("pair")
        moves = []
        for mine, theirs, (low, high) in zip(keep, rec, spans):
            for source, side in ((mine, p), (theirs, 1 - p)):
                for at in range(peers):
                    columns = pl.ds(pl.multiple_of(side * half + at * part + low, HD), high - low)
                    moves += [(source.at[which, at], out.at[:, columns]) for which, out in enumerate(outs)]
        run_moves(moves, sems)

    outs = [shape(rows, 2 * half)] * 3
    return call(kernel, kept + paired, outs, [pltpu.SemaphoreType.DMA((6 * count * peers,))], "laid_out")


def allowed_bias(session, rows):
    strip = rows * lax.axis_size("sub")
    block = 2 * strip
    at_block = lax.axis_index("blk")
    window = jnp.concatenate([jnp.zeros((block,), jnp.int32), session])
    sess = lax.dynamic_slice_in_dim(window, at_block * block, 2 * block)
    place = (at_block - 1) * block + jnp.arange(2 * block, dtype=jnp.int32)

    def tile_bias(tile):
        q_at = slice(block + tile * strip, block + (tile + 1) * strip)
        k_at = slice(tile * strip, (tile + 3) * strip)
        k_place, q_place = place[k_at, None], place[None, q_at]
        allowed = (sess[None, q_at] == sess[k_at, None]) & (k_place <= q_place) & (k_place >= 0)
        return jnp.where(allowed, 0.0, NEG_FILL)

    return jnp.stack([tile_bias(0), tile_bias(1)])


def shards(queries, keys, values, out_grad, session):
    peers = lax.axis_size("sub")
    others = list(range(1, peers))
    part = queries.shape[1] // (2 * peers)
    spans, at = [], 0
    for heads in chunks_of(part // HD):
        spans.append((at, at + heads * HD))
        at += heads * HD
    bias = allowed_bias(session, queries.shape[0])
    (kv_send, kv_first), = first_parts([([keys, values], *spans[0])], [])
    rest = [([queries, out_grad], *spans[0])] + [([keys, values, queries, out_grad], *span) for span in spans[1:]]
    rest = first_parts(rest, [kv_first])
    kv_parts = [(kv_first, swapped(kv_send), 0)]
    qg_parts = [(rest[0][1], swapped(rest[0][0]), 0)]
    for send, own in rest[1:]:
        paired = swapped(send)
        kv_parts.append((own, paired, 0))
        qg_parts.append((own, paired, 2))
    count = len(spans)
    kv_sends, qg_sends, kv, qg, kv_own, own_earlier = [], [], [], [], [], []
    for index in range(count):
        kv_sends.append(head_parts(*kv_parts[index], others, kv[index - 1] if index else []))
        kv.append([round_sub(value, by) for by, value in zip(others, kv_sends[index])])
        kv_own.append(head_parts(*kv_parts[index], [0], own_earlier[index - 1:index]))
        own_earlier.append(along_blocks(kv_own[index][0], 1, True))
        qg_sends.append(head_parts(*qg_parts[index], others, qg[index - 1] if index else []))
        qg.append([round_sub(value, by) for by, value in zip(others, qg_sends[index])])
    kept, paired = [], []
    for index in range(count):
        last = index == count - 1
        forward = [relayed(value, [first_dq]) if index else value for value in kv[index]]
        earlier = [own_earlier[index]] + [along_blocks(value, 1, not last) for value in forward]
        qg_all = head_parts(*qg_parts[index], [0], []) + qg[index]
        grads, dq, early = attention_grads(bias, kv_own[index] + kv[index], earlier, qg_all, last, [])
        first_dq = dq[0]
        dq = [dq[0]] + [round_sub(dq[by], by) for by in others]
        if last:
            later = [along_blocks(value, -1, False) for value in early[1:]]
            dkv = summed(grads, later, others, dq[1:])
            near = along_blocks(relayed(early[0], dkv), -1, False)
            dkv = summed(grads, [near], [0], []) + [round_sub(value, by) for by, value in zip(others, dkv)]
        else:
            dkv = summed(grads, [along_blocks(early[0], -1, False)], [0] + others, dq[1:])
            dkv = [dkv[0]] + [round_sub(dkv[by], by) for by in others]
        send, keep = rows_for_pair(dq, dkv)
        kept.append(keep)
        paired.append(swapped(send))
    return tuple(laid_out(kept, paired, spans))


def solution(mesh):
    spread = P(("grp", "blk", "pair", "sub"), None)
    return jax.shard_map(
        shards, mesh=mesh, in_specs=(spread,) * 4 + (P("grp"),), out_specs=(spread,) * 3, check_vma=False
    )
```

```python
import functools
import math

import jax
import jax.numpy as jnp
from jax import lax
from jax.experimental import pallas as pl
from jax.experimental.pallas import tpu as pltpu
from jax.sharding import PartitionSpec as P

HD = 128
NEG_FILL = -1e30
LOW = jnp.bfloat16
WIDE = jnp.float32
MIB = 1024 * 1024
TO_BITS = HD ** (-0.5) / math.log(2.0)
SCALE = HD ** (-0.5)
ROWS_BY_ROWS = (((1,), (1,)), ((), ()))


def chunks_of(heads):
    return [heads // 2, heads - heads // 2]


def along_blocks(value, by, ring):
    peers = lax.axis_size("blk")
    pairs = [(i, (i + by) % peers) for i in range(peers) if ring or 0 <= i + by < peers]
    return lax.ppermute(value, "blk", pairs)


def round_sub(value, by):
    peers = lax.axis_size("sub")
    return lax.ppermute(value, "sub", [(i, (i + by) % peers) for i in range(peers)])


def swapped(value):
    return lax.ppermute(value, "pair", [(0, 1), (1, 0)])


def run_moves(moves, sems):
    copies = [pltpu.make_async_copy(src, dst, sems.at[at]) for at, (src, dst) in enumerate(moves)]
    for copy in copies:
        copy.start()
    for copy in copies:
        copy.wait()


def call(kernel, ins, outs, scratch, name, whole=False, flops=0, room=8 * MIB):
    spec = pl.BlockSpec(memory_space=pltpu.VMEM if whole else pl.ANY)
    moved = sum(math.prod(a.shape) * a.dtype.itemsize for a in list(ins) + list(outs))
    return list(
        pl.pallas_call(
            kernel,
            out_shape=outs,
            in_specs=[spec] * len(ins),
            out_specs=[spec] * len(outs),
            scratch_shapes=scratch,
            name=name,
            cost_estimate=pl.CostEstimate(flops=flops, bytes_accessed=moved, transcendentals=0),
            compiler_params=pltpu.CompilerParams(vmem_limit_bytes=room),
        )(*ins)
    )


def shape(*dims, dtype=LOW):
    return jax.ShapeDtypeStruct(dims, dtype)


def first_parts(groups, after):
    held, wanted, outs = [], [], []
    for arrays, low, high in groups:
        rows, width = arrays[0].shape
        peers = lax.axis_size("sub")
        half = width // 2
        part = half // peers
        wanted.append((len(held), len(arrays), low, high))
        held += [pltpu.with_memory_space_constraint(array, pltpu.HBM) for array in arrays]
        outs += [pltpu.VMEM((len(arrays), peers, rows, high - low), LOW)] * 2

    def kernel(*refs):
        out_refs, sems = refs[-1 - len(outs):-1], refs[-1]
        p = lax.axis_index("pair")
        moves = []
        for group, (first, count, low, high) in enumerate(wanted):
            for side, out in zip((1 - p, p), out_refs[2 * group:2 * group + 2]):
                for at in range(peers):
                    start = pl.multiple_of(side * half + at * part + low, HD)
                    for i in range(count):
                        moves.append((refs[first + i].at[:, pl.ds(start, high - low)], out.at[i, at]))
        run_moves(moves, sems)

    spec = pl.BlockSpec(memory_space=pl.ANY)
    parts = pl.pallas_call(
        kernel,
        out_shape=outs,
        in_specs=[spec] * (len(held) + len(after)),
        out_specs=[spec] * len(outs),
        scratch_shapes=[pltpu.SemaphoreType.DMA((2 * peers * len(held),))],
        name="first_parts",
        compiler_params=pltpu.CompilerParams(vmem_limit_bytes=8 * MIB),
    )(*held, *after)
    return [(parts[2 * i], parts[2 * i + 1]) for i in range(len(groups))]


def head_parts(own, paired, which, turns, after):
    _, peers, rows, cut = own.shape
    chosen = pl.ds(which, 2)

    def kernel(own_ref, pair_ref, *refs):
        outs, sems = refs[len(after):-1], refs[-1]
        p, s = lax.axis_index("pair"), lax.axis_index("sub")
        moves = []
        for by, out in zip(turns, outs):
            at = lax.rem(s + by, peers)
            moves += [(own_ref.at[chosen, at], out.at[:, p]), (pair_ref.at[chosen, at], out.at[:, 1 - p])]
        run_moves(moves, sems)

    outs = [shape(2, 2, rows, cut)] * len(turns)
    scratch = [pltpu.SemaphoreType.DMA((2 * len(turns),))]
    return call(kernel, [own, paired] + after, outs, scratch, "head_parts")


def relayed(value, after):
    def kernel(value_ref, *refs):
        run_moves([(value_ref, refs[-2])], refs[-1])

    scratch = [pltpu.SemaphoreType.DMA((1,))]
    return call(kernel, [value] + after, [shape(*value.shape)], scratch, "relayed")[0]


def attention_grads(bias, kv, kv_earlier, qg, split, after):
    peers = len(kv)
    _, _, rows, cut = kv[0].shape
    heads = cut // HD
    strip = rows * peers
    early_count = peers if split else 1

    def kernel(*refs):
        bias_ref = refs[0]
        kv_in, early_in, qg_in = refs[1:1 + peers], refs[1 + peers:1 + 2 * peers], refs[1 + 2 * peers:1 + 3 * peers]
        outs = refs[1 + 3 * peers + len(after):-5]
        own_out, dq_outs, early_outs = outs[0], outs[1:1 + peers], outs[1 + peers:]
        kv_all, qg_all, early, dq_all, sems = refs[-5:]
        s = lax.axis_index("sub")
        moves = []
        for by in range(peers):
            at = lax.rem(s - by + peers, peers)
            moves += [
                (early_in[by], kv_all.at[:, 0:2, at]),
                (kv_in[by], kv_all.at[:, 2:4, at]),
                (qg_in[by], qg_all.at[:, :, at]),
            ]
        run_moves(moves, sems)
        strips = [(head, tile) for head in range(heads) for tile in range(2)]
        products, terms, turned = {}, {}, {}

        def flat(ref, which, tiles, head):
            block = ref[which, tiles, :, :, pl.ds(head * HD, HD)]
            return block.reshape(block.shape[0] * strip, HD)

        def multiply(head, tile):
            at, span = pl.ds(tile, 1), pl.ds(tile, 3)
            q, g = flat(qg_all, 0, at, head), flat(qg_all, 1, at, head)
            k, v = flat(kv_all, 0, span, head), flat(kv_all, 1, span, head)
            scores = lax.dot_general(k, q, ROWS_BY_ROWS, preferred_element_type=WIDE)
            grad_prob = lax.dot_general(v, g, ROWS_BY_ROWS, preferred_element_type=WIDE)
            products[head, tile] = q, g, k, scores, grad_prob

        def finish(head, tile):
            q, g, k, scores, grad_prob = products.pop((head, tile))
            cuts = [slice(at, at + HD) for at in range(0, 3 * strip, HD)]
            scaled = [scores[cut] * TO_BITS + bias_ref[tile, cut] for cut in cuts]
            peak = jnp.max(functools.reduce(jnp.maximum, scaled), axis=0, keepdims=True)
            weight = [jnp.exp2(piece - peak) for piece in scaled]
            inverse = 1.0 / jnp.sum(functools.reduce(jnp.add, weight), axis=0, keepdims=True)
            prob = [piece * inverse for piece in weight]
            low = [piece.astype(LOW) for piece in prob]
            dots = [piece.astype(WIDE) * grad_prob[cut] for piece, cut in zip(low, cuts)]
            row_dot = jnp.sum(functools.reduce(jnp.add, dots), axis=0, keepdims=True)
            score_low = [(piece * (grad_prob[cut] - row_dot)).astype(LOW) for piece, cut in zip(prob, cuts)]
            prob_low, score_low = jnp.concatenate(low, axis=0), jnp.concatenate(score_low, axis=0)
            if tile == 0:
                turned[head] = flat(kv_all, 0, pl.ds(0, 4), head).T
            k_turned = turned[head][:, tile * strip:(tile + 3) * strip]
            dq = jnp.dot(k_turned, score_low, preferred_element_type=WIDE) * SCALE
            dq_all[tile, :, :, pl.ds(head * HD, HD)] = dq.T.astype(LOW).reshape(peers, rows, HD)
            dk = jnp.dot(score_low, q, preferred_element_type=WIDE) * SCALE
            dv = jnp.dot(prob_low, g, preferred_element_type=WIDE)
            terms[head, tile] = dk, dv

        def gather(head):
            for which in range(2):
                low, high = terms[head, 0][which], terms[head, 1][which]
                sums = (
                    low[:strip],
                    low[strip:2 * strip] + high[:strip],
                    low[2 * strip:] + high[strip:2 * strip],
                    high[2 * strip:],
                )
                for tile, total in enumerate(sums):
                    total = total.reshape(peers, rows, HD)
                    if tile < 2:
                        early[which, tile, :, :, pl.ds(head * HD, HD)] = total.astype(LOW)
                    else:
                        own_out[which, tile - 2, :, :, pl.ds(head * HD, HD)] = total

        multiply(*strips[0])
        for at, (head, tile) in enumerate(strips):
            if at + 1 < len(strips):
                multiply(*strips[at + 1])
            finish(head, tile)
            if tile == 1:
                gather(head)
        moves = [] if split else [(early, early_outs[0])]
        for by in range(peers):
            at = lax.rem(s + by, peers)
            moves.append((dq_all.at[:, at], dq_outs[by]))
            if split:
                moves.append((early.at[:, :, at], early_outs[by]))
        run_moves(moves, sems)

    outs = [shape(2, 2, peers, rows, cut, dtype=WIDE)] + [shape(2, rows, cut)] * peers
    outs += [shape(2, 2, rows, cut)] * peers if split else [shape(2, 2, peers, rows, cut)]
    scratch = [
        pltpu.VMEM((2, 4, peers, rows, cut), LOW),
        pltpu.VMEM((2, 2, peers, rows, cut), LOW),
        pltpu.VMEM((2, 2, peers, rows, cut), LOW),
        pltpu.VMEM((2, peers, rows, cut), LOW),
        pltpu.SemaphoreType.DMA((3 * peers,)),
    ]
    flops = heads * 2 * 5 * 2 * strip * 3 * strip * HD
    ins = [bias] + kv + kv_earlier + qg + after
    outs = call(kernel, ins, outs, scratch, "attention_grads", whole=True, flops=flops, room=40 * MIB)
    return outs[0], outs[1:1 + peers], outs[1 + peers:]


def summed(own, later, turns, after):
    _, _, peers, rows, cut = own.shape
    split = len(later) > 1 or later[0].ndim == 4

    def kernel(own_ref, *refs):
        later_refs, outs = refs[:len(later)], refs[len(later) + len(after):]
        s = lax.axis_index("sub")
        for place, (by, out) in enumerate(zip(turns, outs)):
            at = lax.rem(s + by, peers)
            for which in range(2):
                for row in range(2):
                    term = later_refs[place][which, row] if split else later_refs[0][which, row, at]
                    out[which, row] = (own_ref[which, row, at] + term.astype(WIDE)).astype(LOW)

    outs = [shape(2, 2, rows, cut)] * len(turns)
    return call(kernel, [own] + later + after, outs, [], "summed", whole=True)


def rows_for_pair(dq, dkv):
    peers = len(dq)
    _, rows, cut = dq[0].shape

    def kernel(*refs):
        dq_refs, dkv_refs, (send, keep) = refs[:peers], refs[peers:2 * peers], refs[-2:]
        p, s = lax.axis_index("pair"), lax.axis_index("sub")
        for by in range(peers):
            at = lax.rem(s - by + peers, peers)
            for out, row in ((send, 1 - p), (keep, p)):
                out[0, at] = dq_refs[by][row]
                for which in range(2):
                    out[1 + which, at] = dkv_refs[by][which, row]

    outs = [shape(3, peers, rows, cut)] * 2
    return call(kernel, dq + dkv, outs, [], "rows_for_pair", whole=True)


def laid_out(kept, paired, spans):
    _, peers, rows, _ = kept[0].shape
    part = spans[-1][1]
    half = part * peers
    count = len(spans)

    def kernel(*refs):
        keep, rec, outs, sems = refs[:count], refs[count:2 * count], refs[2 * count:-1], refs[-1]
        p = lax.axis_index("pair")
        moves = []
        for mine, theirs, (low, high) in zip(keep, rec, spans):
            for source, side in ((mine, p), (theirs, 1 - p)):
                for at in range(peers):
                    columns = pl.ds(pl.multiple_of(side * half + at * part + low, HD), high - low)
                    moves += [(source.at[which, at], out.at[:, columns]) for which, out in enumerate(outs)]
        run_moves(moves, sems)

    outs = [shape(rows, 2 * half)] * 3
    return call(kernel, kept + paired, outs, [pltpu.SemaphoreType.DMA((6 * count * peers,))], "laid_out")


def allowed_bias(session, rows):
    strip = rows * lax.axis_size("sub")
    block = 2 * strip
    at_block = lax.axis_index("blk")
    window = jnp.concatenate([jnp.zeros((block,), jnp.int32), session])
    sess = lax.dynamic_slice_in_dim(window, at_block * block, 2 * block)
    place = (at_block - 1) * block + jnp.arange(2 * block, dtype=jnp.int32)

    def tile_bias(tile):
        q_at = slice(block + tile * strip, block + (tile + 1) * strip)
        k_at = slice(tile * strip, (tile + 3) * strip)
        k_place, q_place = place[k_at, None], place[None, q_at]
        allowed = (sess[None, q_at] == sess[k_at, None]) & (k_place <= q_place) & (k_place >= 0)
        return jnp.where(allowed, 0.0, NEG_FILL)

    return jnp.stack([tile_bias(0), tile_bias(1)])


def shards(queries, keys, values, out_grad, session):
    peers = lax.axis_size("sub")
    others = list(range(1, peers))
    part = queries.shape[1] // (2 * peers)
    spans, at = [], 0
    for heads in chunks_of(part // HD):
        spans.append((at, at + heads * HD))
        at += heads * HD
    bias = allowed_bias(session, queries.shape[0])
    (kv_send, kv_first), = first_parts([([keys, values], *spans[0])], [])
    rest = [([queries, out_grad], *spans[0])] + [([keys, values, queries, out_grad], *span) for span in spans[1:]]
    rest = first_parts(rest, [kv_first])
    kv_parts = [(kv_first, swapped(kv_send), 0)]
    qg_parts = [(rest[0][1], swapped(rest[0][0]), 0)]
    for send, own in rest[1:]:
        paired = swapped(send)
        kv_parts.append((own, paired, 0))
        qg_parts.append((own, paired, 2))
    count = len(spans)
    kv_sends, qg_sends, kv, qg, kv_own, own_earlier = [], [], [], [], [], []
    for index in range(count):
        kv_sends.append(head_parts(*kv_parts[index], others, kv[index - 1] if index else []))
        kv.append([round_sub(value, by) for by, value in zip(others, kv_sends[index])])
        kv_own.append(head_parts(*kv_parts[index], [0], own_earlier[index - 1:index]))
        own_earlier.append(along_blocks(kv_own[index][0], 1, True))
        qg_sends.append(head_parts(*qg_parts[index], others, qg[index - 1] if index else []))
        qg.append([round_sub(value, by) for by, value in zip(others, qg_sends[index])])
    kept, paired = [], []
    for index in range(count):
        last = index == count - 1
        forward = [relayed(value, [first_dq]) if index else value for value in kv[index]]
        earlier = [own_earlier[index]] + [along_blocks(value, 1, not last) for value in forward]
        qg_all = head_parts(*qg_parts[index], [0], []) + qg[index]
        grads, dq, early = attention_grads(bias, kv_own[index] + kv[index], earlier, qg_all, last, [])
        first_dq = dq[0]
        dq = [dq[0]] + [round_sub(dq[by], by) for by in others]
        if last:
            later = [along_blocks(value, -1, False) for value in early[1:]]
            dkv = summed(grads, later, others, dq[1:])
            near = along_blocks(relayed(early[0], dkv), -1, False)
            dkv = summed(grads, [near], [0], []) + [round_sub(value, by) for by, value in zip(others, dkv)]
        else:
            dkv = summed(grads, [along_blocks(early[0], -1, False)], [0] + others, dq[1:])
            dkv = [dkv[0]] + [round_sub(dkv[by], by) for by in others]
        send, keep = rows_for_pair(dq, dkv)
        kept.append(keep)
        paired.append(swapped(send))
    return tuple(laid_out(kept, paired, spans))


def solution(mesh):
    spread = P(("grp", "blk", "pair", "sub"), None)
    return jax.shard_map(
        shards, mesh=mesh, in_specs=(spread,) * 4 + (P("grp"),), out_specs=(spread,) * 3, check_vma=False
    )
```
